32 devices in a mesh: wide: 8 (over z, y), narrow: 4 (over x, core).
Axes of the slice: x: 2, y: 2, z: 4, core: 2. Of those that a mesh axis runs over, the one named last changes fastest.
Arguments:
- inputs: bfloat16 [16384, 768], P(('wide', 'narrow')), may hold values from -6 to 6
- gain_attn: bfloat16 [768], P(('wide', 'narrow')), may hold values from 0.5 to 1.5
- w_query: bfloat16 [768, 768], P(('wide', 'narrow')), may hold values from -0.21875 to 0.21875
- w_key: bfloat16 [768, 768], P(('wide', 'narrow')), may hold values from -0.21875 to 0.21875
- w_value: bfloat16 [768, 768], P(('wide', 'narrow')), may hold values from -0.21875 to 0.21875
- w_output: bfloat16 [768, 768], P(('wide', 'narrow')), may hold values from -2.5 to 2.5
- rel_bias: float32 [32, 12], replicated, may hold values from -4 to 4
- gain_ffn: bfloat16 [768], P(('wide', 'narrow')), may hold values from 0.5 to 1.5
- w_router: bfloat16 [768, 32], P(('wide', 'narrow')), may hold values from -0.21875 to 0.21875
- expert_in: bfloat16 [32, 768, 3072], P('wide', None, 'narrow'), may hold values from -0.21875 to 0.21875
- expert_out: bfloat16 [32, 3072, 768], P('wide', 'narrow'), may hold values from -6 to 6
- routes: int32 [16384, 1], P(('wide', 'narrow')), may hold values from 0 to 31
- capacity: int32 [32], P(('wide', 'narrow')), may hold values from 1 to 2, as said below
- cotangent: bfloat16 [16384, 768], P(('wide', 'narrow')), may hold values from -6 to 6
Outputs:
- result: bfloat16 [16384, 768], P(('wide', 'narrow'))
- grad_inputs: float32 [16384, 768], P(('wide', 'narrow'))
- grad_gain_attn: float32 [768], P(('wide', 'narrow'))
- grad_query: float32 [768, 768], P(('wide', 'narrow'))
- grad_key: float32 [768, 768], P(('wide', 'narrow'))
- grad_value: float32 [768, 768], P(('wide', 'narrow'))
- grad_output: float32 [768, 768], P(('wide', 'narrow'))
- grad_rel_bias: float32 [32, 12], replicated
- grad_gain_ffn: float32 [768], P(('wide', 'narrow'))
- grad_router: float32 [768, 32], P(('wide', 'narrow'))
- grad_expert_in: float32 [32, 768, 3072], P('wide', None, 'narrow')
- grad_expert_out: float32 [32, 3072, 768], P('wide', 'narrow')
The draws below stay inside these ranges and needn't reach their ends.
Inputs may be any that keep to these rules, and one draw needn't show every extreme that they name: `capacity`: each group of 512 tokens has its own factor; both values occur.
All inputs are finite; a program needn't handle non-finite values.
Results may differ from the reference program's by a relative error of at most 0.019.
Values may be sent and summed in bfloat16 or wider, within the bound.
A program may use at most 320 MiB of HBM per device.

```python
import jax
import jax.numpy as jnp
import numpy as np
from jax import lax

D = 768
HEADS = 12
HEAD_DIM = 64
FF = 3072
BUCKETS = 32
SEQ_LEN = 512
TOK_DEV = 512
EXPERTS = 32
RANKS = 32
TOKENS = 16384
SLOTS = 32


def draw_capacity(key, part):
    key_one, key_two, key_three = jax.random.split(key, 3)
    factors = jax.random.randint(key_one, (RANKS,), 1, 3)
    high_rank = jax.random.randint(key_two, (), 0, RANKS)
    low_rank = (high_rank + 1 + jax.random.randint(key_three, (), 0, RANKS - 1)) % RANKS
    ranks_seen = jnp.arange(RANKS)
    return jnp.where(ranks_seen == high_rank, 2, jnp.where(ranks_seen == low_rank, 1, factors)).astype(jnp.int32)


def shard_levels(key, dims, shards, low, largest):
    level, own = 1.0, jax.random.fold_in(key, 6)
    for axis_at, parts in shards:
        steps = jnp.exp(jax.random.uniform(jax.random.fold_in(own, axis_at), (parts,), jnp.float32, low / len(shards), largest / len(shards)))
        level = level * jnp.repeat(steps, dims[axis_at] // parts).reshape([-1 if axis == axis_at else 1 for axis in range(len(dims))])
    return level


def picks_of(key, rows, number_of, top, lift):
    ranking = jax.random.permutation(jax.random.fold_in(key, 1), number_of)
    boost = ranking
    for power in range(3):
        boost = boost * boost // number_of
    boost = boost * lift // number_of
    tickets = jax.random.randint(jax.random.fold_in(key, 2), (rows, number_of), 0, 4096) + boost
    holders = jax.random.permutation(jax.random.fold_in(key, 3), rows)[jnp.arange(number_of) % rows]
    tickets = jnp.where(jnp.arange(rows)[:, None] == holders[None, :], 1 << 14, tickets)
    score = tickets * number_of + jnp.arange(number_of)
    return lax.top_k(score.astype(jnp.int32), top)[1].astype(jnp.int32)


def noise(own_key, extent, spread, most, pieces=(), kind=jnp.bfloat16):
    entries = spread * jax.random.normal(own_key, extent, jnp.float32)
    if pieces:
        entries = entries * shard_levels(own_key, extent, pieces, -0.22, 0.18)
    return jnp.clip(entries, -most, most).astype(kind)


def setup_inputs(seed: int = 0) -> dict:
    key_list = jax.random.split(jax.random.key(seed), 15)
    inputs = noise(key_list[0], (TOKENS, D), 1.0, 6.0, ((0, 32),))
    gain_attn = jnp.clip(1.0 + 0.1 * jax.random.normal(key_list[1], (D,), jnp.float32), 0.5, 1.5).astype(jnp.bfloat16)
    w_query = noise(key_list[2], (D, D), D ** -0.5, 0.21875, ((0, 32),))
    w_key = noise(key_list[3], (D, D), D ** -0.5, 0.21875, ((0, 32),))
    w_value = noise(key_list[4], (D, D), D ** -0.5, 0.21875, ((0, 32),))
    w_output = noise(key_list[5], (D, D), (4 * D // SEQ_LEN) ** -0.5, 2.5, ((0, 32),))
    rel_bias = noise(key_list[6], (BUCKETS, HEADS), 1.0, 4.0, (), jnp.float32)
    gain_ffn = jnp.clip(1.0 + 0.1 * jax.random.normal(key_list[7], (D,), jnp.float32), 0.5, 1.5).astype(jnp.bfloat16)
    w_router = noise(key_list[8], (D, EXPERTS), D ** -0.5, 0.21875, ((0, 32),))
    expert_in = noise(key_list[9], (EXPERTS, D, FF), D ** -0.5, 0.21875, ((0, 8), (2, 4)))
    expert_out = noise(key_list[10], (EXPERTS, FF, D), (max(1, EXPERTS // 32)), 6.0, ((0, 8), (1, 4)))
    routes = picks_of(key_list[11], TOKENS, EXPERTS, 1, 512)
    capacity = draw_capacity(jax.random.fold_in(key_list[14], 71), 0)
    cotangent = noise(key_list[13], (TOKENS, D), 1.0, 6.0, ((0, 32),))
    return {"inputs": inputs, "gain_attn": gain_attn, "w_query": w_query, "w_key": w_key, "w_value": w_value, "w_output": w_output, "rel_bias": rel_bias, "gain_ffn": gain_ffn, "w_router": w_router, "expert_in": expert_in, "expert_out": expert_out, "routes": routes, "capacity": capacity, "cotangent": cotangent}


EPSILON = 1e-06
HIGHEST = lax.Precision.HIGHEST

@jax.custom_vjp
def low(v):
    return lax.optimization_barrier(v.astype(jnp.bfloat16)).astype(jnp.float32)

@jax.custom_vjp
def low_back(v):
    return v

def low_keep(v):
    return (low(v), None)

def low_pass(kept, grad):
    return (grad,)

def back_keep(v):
    return (v, None)

def back_low(kept, grad):
    return (low(grad),)
low.defvjp(low_keep, low_pass)
low_back.defvjp(back_keep, back_low)

def bucket_offsets(length, bucket_count):
    offsets = np.arange(-(length - 1), length)
    half_count = bucket_count // 2
    exact_count = half_count // 2
    distance = np.abs(offsets)
    scaled = exact_count + np.floor(np.log(np.maximum(distance, 1) / exact_count) / np.log(128.0 / exact_count) * (half_count - exact_count)).astype(np.int64)
    scaled = np.minimum(scaled, half_count - 1)
    return ((offsets > 0) * half_count + np.where(distance < exact_count, distance, scaled)).astype(np.int32)

def offset_index(row_start, row_count, length):
    return (np.arange(length)[None, :] - np.arange(row_start, row_start + row_count)[:, None] + length - 1).astype(np.int32)

def matmul(left, right):
    return jnp.dot(left, right, precision=HIGHEST)

def normalize(values, gain):
    inverse = lax.rsqrt(lax.optimization_barrier(jnp.mean(values * values, axis=-1, keepdims=True)) + EPSILON)
    return values * inverse * gain

def softmax_rows(scores):
    row_peak = lax.optimization_barrier(jnp.max(scores, axis=-1, keepdims=True))
    exponent = jnp.exp(scores - row_peak)
    return exponent / lax.optimization_barrier(jnp.sum(exponent, axis=-1, keepdims=True))

def layer(inputs, gain_attn, w_query, w_key, w_value, w_output, rel_bias, gain_ffn, w_router, expert_in, expert_out, routes, capacity):
    normed_attn = low(normalize(inputs, gain_attn))
    query_rows = low_back(low(matmul(normed_attn, w_query)))
    key_rows = low_back(low(matmul(normed_attn, w_key)))
    value_rows = low_back(low(matmul(normed_attn, w_value)))
    seq_shape = (TOKENS // SEQ_LEN, SEQ_LEN, HEADS, HEAD_DIM)
    table = jnp.asarray(bucket_offsets(SEQ_LEN, BUCKETS)[offset_index(0, SEQ_LEN, SEQ_LEN)]).astype(jnp.int32)
    bias_full = jnp.transpose(rel_bias[table], (2, 0, 1))

    def attend_one(packed):
        query_seq, key_seq, value_seq = packed
        scores = jnp.einsum('ihd,jhd->hij', query_seq, key_seq, precision=HIGHEST) * 0.125 + bias_full
        weights = low(softmax_rows(low_back(scores)))
        return jnp.einsum('hij,jhd->ihd', weights, value_seq, precision=HIGHEST)
    attended = lax.map(jax.checkpoint(attend_one), (query_rows.reshape(seq_shape), key_rows.reshape(seq_shape), value_rows.reshape(seq_shape)))
    attended = low_back(low(attended.reshape(TOKENS, D)))
    mixed = inputs + low_back(matmul(attended, w_output))
    normed_ffn = low(normalize(mixed, gain_ffn))
    logits = low_back(matmul(normed_ffn, w_router))
    router_probs = softmax_rows(logits)
    choice_ids = routes[:, 0].astype(jnp.int32)
    chosen = choice_ids[:, None] == jnp.arange(EXPERTS, dtype=jnp.int32)[None, :]
    gate = lax.optimization_barrier(jnp.sum(jnp.where(chosen, router_probs, 0.0), axis=-1))
    grouped = chosen.astype(jnp.int32).reshape(RANKS, TOK_DEV, EXPERTS)
    running = jnp.cumsum(grouped, axis=1, dtype=jnp.int32).astype(jnp.int32)
    position = (lax.optimization_barrier(jnp.sum(running * grouped, axis=-1, dtype=jnp.int32)) - 1).astype(jnp.int32)
    limit = (capacity.astype(jnp.int32)[:, None] * TOK_DEV // EXPERTS).astype(jnp.int32)
    kept = position < limit
    slot_ids = jnp.where(kept, choice_ids.reshape(RANKS, TOK_DEV) * SLOTS + position, EXPERTS * SLOTS).astype(jnp.int32)
    flat_ids = (slot_ids + jnp.arange(RANKS, dtype=jnp.int32)[:, None] * (EXPERTS * SLOTS + 1)).reshape(TOKENS).astype(jnp.int32)
    buffer = jnp.zeros((RANKS * (EXPERTS * SLOTS + 1), D), jnp.float32).at[flat_ids].add(normed_ffn)
    buffer = buffer.reshape(RANKS, EXPERTS * SLOTS + 1, D)[:, :-1]
    dispatched = low_back(buffer.reshape(RANKS, EXPERTS, SLOTS, D))
    per_expert = jnp.transpose(dispatched, (1, 0, 2, 3)).reshape(EXPERTS, RANKS * SLOTS, D)

    def expert_one(packed):
        rows_in, weight_in, weight_out = packed
        pre = low_back(matmul(rows_in, weight_in))
        hidden = low(jax.nn.gelu(pre, approximate=True))
        return low_back(low(matmul(hidden, weight_out)))
    outputs = lax.map(jax.checkpoint(expert_one), (per_expert, expert_in, expert_out))
    outputs = jnp.transpose(outputs.reshape(EXPERTS, RANKS, SLOTS, D), (1, 0, 2, 3)).reshape(RANKS, EXPERTS * SLOTS, D)
    padded = jnp.concatenate([outputs, jnp.zeros((RANKS, 1, D), jnp.float32)], axis=1).reshape(RANKS * (EXPERTS * SLOTS + 1), D)
    combined = padded[flat_ids]
    return mixed + gate[:, None] * combined

def reference(inputs, gain_attn, w_query, w_key, w_value, w_output, rel_bias, gain_ffn, w_router, expert_in, expert_out, routes, capacity, cotangent):
    floats = (inputs.astype(jnp.float32), gain_attn.astype(jnp.float32), w_query.astype(jnp.float32), w_key.astype(jnp.float32), w_value.astype(jnp.float32), w_output.astype(jnp.float32), rel_bias.astype(jnp.float32), gain_ffn.astype(jnp.float32), w_router.astype(jnp.float32), expert_in.astype(jnp.float32), expert_out.astype(jnp.float32))

    def wrapped(*values):
        return layer(*values, routes, capacity)
    result, pullback = jax.vjp(wrapped, *floats)
    grads = pullback(cotangent.astype(jnp.float32))
    return (result.astype(jnp.bfloat16), grads[0], grads[1], grads[2], grads[3], grads[4], grads[5], grads[6], grads[7], grads[8], grads[9], grads[10])
```

```python
import jax
import jax.numpy as jnp
import numpy as np
from jax import lax
from jax.experimental import pallas as pl
from jax.experimental.pallas import tpu as pltpu
from jax.sharding import PartitionSpec as P

HEADS = 12
SEQ_LEN = 512
BLOCK = 128
EPSILON = 1e-06
HIGHEST = lax.Precision.HIGHEST
ROOT_TWO_PI = 0.7978845608028654
CUBIC = 0.044715
BOTH = ("wide", "narrow")
F32 = jnp.float32
BF16 = jnp.bfloat16


def bucket_of(offsets, bucket_count):
    half_count = bucket_count // 2
    exact_count = half_count // 2
    distance = np.abs(offsets)
    scaled = exact_count + np.floor(
        np.log(np.maximum(distance, 1) / exact_count)
        / np.log(128.0 / exact_count)
        * (half_count - exact_count)
    ).astype(np.int64)
    scaled = np.minimum(scaled, half_count - 1)
    return ((offsets > 0) * half_count + np.where(distance < exact_count, distance, scaled)).astype(
        np.int32
    )


def near_picks(bucket_count, sign):
    offsets = sign * (np.arange(4 * BLOCK) - (2 * BLOCK - 1))
    picks = (bucket_of(offsets, bucket_count)[:, None] == np.arange(bucket_count)[None, :]).astype(
        np.float32
    )
    picks[-1] = 0.0
    return picks


def dot_nn(left, right):
    return lax.dot_general(left, right, (((1,), (0,)), ((), ())), preferred_element_type=F32)


def dot_nt(left, right):
    return lax.dot_general(left, right, (((1,), (1,)), ((), ())), preferred_element_type=F32)


def dot_tn(left, right):
    return lax.dot_general(left, right, (((0,), (0,)), ((), ())), preferred_element_type=F32)


def inverse_rms(values):
    return lax.rsqrt(jnp.mean(values * values, axis=-1, keepdims=True) + EPSILON)


def norm_backward(values, inverse, gain, grad_normed):
    scaled = grad_normed * gain
    grad_gain = jnp.sum(grad_normed * values * inverse, axis=0, keepdims=True)
    inner = jnp.mean(scaled * values, axis=-1, keepdims=True)
    return (inverse * (scaled - values * inverse * inverse * inner), grad_gain)


def softmax_lanes(logits):
    peak = jnp.max(logits, axis=-1, keepdims=True)
    exponent = jnp.exp(logits - peak)
    return exponent / jnp.sum(exponent, axis=-1, keepdims=True)


def toeplitz_near(near_row):
    spread = jnp.broadcast_to(near_row, (BLOCK, 4 * BLOCK))
    return pltpu.roll(spread, 3 * BLOCK + 1, 1, stride=1, stride_axis=0)[:, : 3 * BLOCK]


def bias_rows(near, far_low, far_high, row, blocks):
    pieces = []
    for column in range(blocks):
        distance = column - row
        if distance <= -2:
            pieces.append(jnp.full((BLOCK, BLOCK), far_low, F32))
        elif distance >= 2:
            pieces.append(jnp.full((BLOCK, BLOCK), far_high, F32))
        else:
            pieces.append(near[:, (distance + 1) * BLOCK : (distance + 2) * BLOCK])
    return jnp.concatenate(pieces, axis=1)


def diagonal_sums(near_sum):
    padded = jnp.concatenate([near_sum, jnp.zeros((BLOCK, BLOCK), F32)], axis=1)
    groups = jnp.zeros((8, 4 * BLOCK), F32)
    for at in range(0, BLOCK, 8):
        groups = groups + pltpu.roll(padded[at : at + 8, :], BLOCK - 8 - at, 1)
    sums = groups[7:8, :]
    for at in range(7):
        sums = sums + pltpu.roll(groups[at : at + 1, :], 7 - at, 1)
    return sums


def slot_places(routes_ref, row_ref, limit, experts, slots, count):
    lower = lax.broadcasted_iota(jnp.int32, (count, count), 0)
    upper = lax.broadcasted_iota(jnp.int32, (count, count), 1)
    col = routes_ref[...]
    chosen = lax.broadcasted_iota(jnp.int32, (count, experts), 1) == col
    running = dot_nn((upper <= lower).astype(BF16), chosen.astype(BF16))
    place = jnp.sum(jnp.where(chosen, running, 0.0), axis=1, keepdims=True).astype(jnp.int32) - 1
    slot_col = jnp.where(place < limit, col * slots + place, -1)
    row = row_ref[...]
    chosen_t = lax.broadcasted_iota(jnp.int32, (experts, count), 0) == row
    running_t = dot_nn(chosen_t.astype(BF16), (lower <= upper).astype(BF16))
    place_t = (
        jnp.sum(jnp.where(chosen_t, running_t, 0.0), axis=0, keepdims=True).astype(jnp.int32) - 1
    )
    slot_row = jnp.where(place_t < limit, row * slots + place_t, -1)
    return slot_col, slot_row


def place_kernel(slots, experts, capacity_ref, routes_ref, row_ref, cot_ref, slot_col, slot_row, cot_out):
    count = routes_ref.shape[0]
    limit = capacity_ref[0] * count // experts
    col, row = slot_places(routes_ref, row_ref, limit, experts, slots, count)
    slot_col[...] = col
    slot_row[...] = row
    picks = (lax.broadcasted_iota(jnp.int32, (experts * slots, count), 0) == row).astype(BF16)
    cot_out[...] = dot_nn(picks, cot_ref[...]).astype(BF16)


def forward_kernel(
    rel_ref, x_ref, w_ref, gain_a, gain_f, router_ref, near_ref, slot_row,
    normed_ref, q_ref, k_ref, v_ref, att_ref, lse_ref, mixed_ref, normed_f, sent_ref,
):
    count, width = x_ref.shape
    head_dim = width // HEADS
    blocks = count // BLOCK
    bucket_count = rel_ref.shape[0]
    tokens = x_ref[...].astype(F32)
    normed = (tokens * inverse_rms(tokens) * gain_a[...]).astype(BF16)
    normed_ref[...] = normed
    for out, at in ((q_ref, 0), (k_ref, 1), (v_ref, 2)):
        out[...] = dot_nn(normed, w_ref[:, at * width : (at + 1) * width]).astype(BF16)
    lse_ref[...] = jnp.zeros_like(lse_ref)
    first = lax.broadcasted_iota(jnp.int32, (1, BLOCK), 1) < head_dim
    lanes = lax.broadcasted_iota(jnp.int32, (1, BLOCK), 1)

    def pair(at, carry):
        cols = pl.ds(pl.multiple_of(at * BLOCK, BLOCK), BLOCK)
        k_pair, v_pair = k_ref[:, cols], v_ref[:, cols]
        nears = [toeplitz_near(near_ref[pl.ds(2 * at + half, 1), :]) for half in range(2)]
        for row in range(blocks):
            rows = slice(row * BLOCK, (row + 1) * BLOCK)
            q_rows = q_ref[rows, cols] * jnp.asarray(head_dim**-0.5, BF16)
            found = []
            log_sums = lse_ref[rows, :]
            for half in range(2):
                head = 2 * at + half
                low, high = rel_ref[bucket_count // 2 - 1, head], rel_ref[bucket_count - 1, head]
                mask = first if half == 0 else jnp.logical_not(first)
                scores = dot_nt(jnp.where(mask, q_rows, jnp.zeros_like(q_rows)), k_pair)
                scores = scores + bias_rows(nears[half], low, high, row, blocks)
                peak = jnp.max(scores, axis=-1, keepdims=True)
                exponent = jnp.exp(scores - peak)
                total = jnp.sum(exponent, axis=-1, keepdims=True)
                found.append(dot_nn((exponent * (1.0 / total)).astype(BF16), v_pair))
                log_sums = jnp.where(lanes == head, peak + jnp.log(total), log_sums)
            lse_ref[rows, :] = log_sums
            att_ref[rows, cols] = jnp.where(first, found[0], found[1]).astype(BF16)
        return carry

    lax.fori_loop(0, HEADS // 2, pair, 0)
    mixed = tokens + dot_nn(att_ref[...], w_ref[:, 3 * width : 4 * width])
    mixed_ref[...] = mixed
    normed_2 = (mixed * inverse_rms(mixed) * gain_f[...]).astype(BF16)
    normed_f[...] = normed_2
    total_slots = sent_ref.shape[0]
    picks = (lax.broadcasted_iota(jnp.int32, (total_slots, count), 0) == slot_row[...]).astype(BF16)
    sent_ref[...] = dot_nn(picks, normed_2).astype(BF16)


def expert_kernel(
    first_ref, rows_ref, cot_ref, in_ref, out_ref, router_ref,
    back_ref, grows_ref, gin_ref, gout_ref, hidden_ref, gpre_ref, sg_ref,
):
    sources, _, slots, width = rows_ref.shape
    total = sources * slots
    step = min(256, total)
    expert = first_ref[0] + pl.program_id(0)

    def chunk(at, carry):
        these = pl.ds(pl.multiple_of(at * (step // slots), step // slots), step // slots)
        flat = pl.ds(pl.multiple_of(at * step, step), step)
        rows = rows_ref[these, 0].reshape(step, width)
        probs = softmax_lanes(dot_nn(rows, router_ref[...]))
        here = lax.broadcasted_iota(jnp.int32, probs.shape, 1) == expert
        gate = jnp.sum(jnp.where(here, probs, 0.0), axis=-1, keepdims=True)
        sg = (cot_ref[these, 0].reshape(step, width).astype(F32) * gate).astype(BF16)
        sg_ref[flat, :] = sg
        pre = dot_nn(rows, in_ref[0])
        square = pre * pre
        inner = jnp.tanh(pre * (ROOT_TWO_PI + ROOT_TWO_PI * CUBIC * square))
        half = 0.5 * (1.0 + inner)
        hidden = (pre * half).astype(BF16)
        hidden_ref[flat, :] = hidden
        slope = half + 0.5 * pre * (1.0 - inner * inner) * (
            ROOT_TWO_PI + 3.0 * ROOT_TWO_PI * CUBIC * square
        )
        gpre = (dot_nt(sg, out_ref[0]) * slope).astype(BF16)
        gpre_ref[flat, :] = gpre
        back_ref[these, 0] = dot_nn(hidden, out_ref[0]).astype(BF16).reshape(-1, slots, width)
        grows_ref[these, 0] = dot_nt(gpre, in_ref[0]).astype(BF16).reshape(-1, slots, width)
        return carry

    lax.fori_loop(0, total // step, chunk, 0)
    gout_ref[0] = dot_tn(hidden_ref[...], sg_ref[...])
    gin_ref[0] = dot_tn(rows_ref[:, 0].reshape(total, width), gpre_ref[...])


def backward_kernel(
    rel_ref, x_ref, w_ref, gain_a, gain_f, router_ref, near_ref, slot_col, routes_ref,
    normed_ref, q_ref, k_ref, v_ref, att_ref, lse_ref, mixed_ref, normed_f, cot_ref, outs_ref, grows_ref,
    result_ref, gx_ref, gw_ref, grouter_ref, gnear_ref, gfar_ref, ggain_ref,
    q_t, k_t, normed_t, datt, datt_t, delta, lse_t, gq, gk, gv, gmixed, dst,
):
    count, width = x_ref.shape
    head_dim = width // HEADS
    blocks = count // BLOCK
    bucket_count = rel_ref.shape[0]
    experts = router_ref.shape[1]
    picks = (
        lax.broadcasted_iota(jnp.int32, (count, outs_ref.shape[0]), 1) == slot_col[...]
    ).astype(BF16)
    combined = dot_nn(picks, outs_ref[...])
    mixed = mixed_ref[...]
    cot = cot_ref[...].astype(F32)
    probs = softmax_lanes(dot_nn(normed_f[...], router_ref[...]))
    chosen = lax.broadcasted_iota(jnp.int32, (count, experts), 1) == routes_ref[...]
    gate = jnp.sum(jnp.where(chosen, probs, 0.0), axis=-1, keepdims=True)
    result_ref[...] = (mixed + gate * combined).astype(BF16)
    grad_gate = jnp.sum(cot * combined, axis=-1, keepdims=True)
    grad_logits = (probs * (jnp.where(chosen, grad_gate, 0.0) - gate * grad_gate)).astype(BF16)
    grouter_ref[...] = dot_tn(normed_f[...], grad_logits)
    grad_normed = dot_nt(grad_logits, router_ref[...]) + dot_nn(picks, grows_ref[...])
    grad_norm, ggain_ref[1:2, :] = norm_backward(mixed, inverse_rms(mixed), gain_f[...], grad_normed)
    grad_mixed = cot + grad_norm
    gmixed[...] = grad_mixed
    branch = grad_mixed.astype(BF16)
    gw_ref[:, 3 * width : 4 * width] = dot_tn(att_ref[...], branch).astype(BF16)
    datt[...] = dot_nt(branch, w_ref[:, 3 * width : 4 * width]).astype(BF16)
    datt_t[...] = datt[...].T
    q_t[...] = (q_ref[...] * jnp.asarray(head_dim**-0.5, BF16)).T
    k_t[...] = k_ref[...].T
    normed_t[...] = normed_ref[...].T
    products = datt_t[...].astype(F32) * att_ref[...].T.astype(F32)
    delta[...] = jnp.sum(products.reshape(HEADS, head_dim, count), axis=1)
    lse_t[...] = lse_ref[...].T
    first = lax.broadcasted_iota(jnp.int32, (1, BLOCK), 1) < head_dim

    def pair(at, carry):
        cols = pl.ds(pl.multiple_of(at * BLOCK, BLOCK), BLOCK)
        q_pair, datt_pair = q_ref[:, cols], datt[:, cols]
        gq_parts, gk_parts, gv_parts = [], [], []
        for half in range(2):
            head = 2 * at + half
            low, high = rel_ref[bucket_count // 2 - 1, head], rel_ref[bucket_count - 1, head]
            mask = first if half == 0 else jnp.logical_not(first)
            near = toeplitz_near(near_ref[pl.ds(head, 1), :])
            lse_row, delta_row = lse_t[pl.ds(head, 1), :], delta[pl.ds(head, 1), :]
            near_sum = jnp.zeros((BLOCK, 3 * BLOCK), F32)
            low_sum, high_sum = jnp.zeros((BLOCK, BLOCK), F32), jnp.zeros((BLOCK, BLOCK), F32)
            gk_rows, gv_rows = [], []
            for row in range(blocks):
                rows = slice(row * BLOCK, (row + 1) * BLOCK)
                k_rows, v_rows = k_ref[rows, cols], v_ref[rows, cols]
                zeros = jnp.zeros_like(k_rows)
                scores = dot_nn(jnp.where(mask, k_rows, zeros), q_t[cols, :])
                scores = scores + bias_rows(near, high, low, row, blocks)
                weights = jnp.exp(scores - lse_row)
                grad_weights = dot_nn(jnp.where(mask, v_rows, zeros), datt_t[cols, :])
                grad_scores = weights * (grad_weights - delta_row)
                gv_rows.append(dot_nn(weights.astype(BF16), datt_pair))
                low_bits = grad_scores.astype(BF16)
                dst[rows, :] = low_bits
                gk_rows.append(dot_nn(low_bits, q_pair))
                for column in range(blocks):
                    piece = grad_scores[:, column * BLOCK : (column + 1) * BLOCK]
                    distance = column - row
                    if distance <= -2:
                        high_sum = high_sum + piece
                    elif distance >= 2:
                        low_sum = low_sum + piece
                    else:
                        pads = [jnp.zeros((BLOCK, BLOCK), F32)] * 3
                        pads[distance + 1] = piece
                        near_sum = near_sum + jnp.concatenate(pads, axis=1)
            gq_parts.append(
                dot_nn(k_t[pl.ds(pl.multiple_of(head * head_dim, head_dim), head_dim), :], dst[...])
            )
            gk_parts.append(jnp.concatenate(gk_rows, axis=0))
            gv_parts.append(jnp.concatenate(gv_rows, axis=0))
            gnear_ref[pl.ds(head, 1), :] = diagonal_sums(near_sum)
            gfar_ref[pl.ds(head, 1), :] = jnp.concatenate(
                [jnp.sum(low_sum, axis=0, keepdims=True), jnp.sum(high_sum, axis=0, keepdims=True)], axis=1
            )
        scale = head_dim**-0.5
        gq[:, cols] = (jnp.concatenate(gq_parts, axis=0).T * scale).astype(BF16)
        gk[:, cols] = (jnp.where(first, gk_parts[0], gk_parts[1]) * scale).astype(BF16)
        gv[:, cols] = jnp.where(first, gv_parts[0], gv_parts[1]).astype(BF16)
        return carry

    lax.fori_loop(0, HEADS // 2, pair, 0)
    grad_normed = jnp.zeros((count, width), F32)
    for at, grad in enumerate((gq, gk, gv)):
        gw_ref[:, at * width : (at + 1) * width] = dot_nn(normed_t[...], grad[...]).astype(BF16)
        grad_normed = grad_normed + dot_nt(grad[...], w_ref[:, at * width : (at + 1) * width])
    tokens = x_ref[...].astype(F32)
    grad_norm, ggain_ref[0:1, :] = norm_backward(tokens, inverse_rms(tokens), gain_a[...], grad_normed)
    gx_ref[...] = gmixed[...] + grad_norm


def in_vmem(count):
    return [pl.BlockSpec(memory_space=pltpu.VMEM)] * count


def shards(
    inputs, gain_attn, w_query, w_key, w_value, w_output, rel_bias, gain_ffn, w_router,
    expert_in, expert_out, routes, capacity, cotangent,
):
    count, width = inputs.shape
    experts = w_router.shape[1]
    local, _, hidden_width = expert_in.shape
    wide, narrow = lax.axis_size("wide"), lax.axis_size("narrow")
    slots = 2 * count // experts
    total = experts * slots
    bucket_count = rel_bias.shape[0]
    params = pltpu.CompilerParams(vmem_limit_bytes=60 << 20)
    smem = pl.BlockSpec(memory_space=pltpu.SMEM)

    packed = jnp.concatenate([w_query, w_key, w_value, w_output], axis=1)
    weights = lax.all_gather(packed, BOTH, axis=0, tiled=True)
    small = lax.all_gather(
        jnp.concatenate([w_router, gain_attn[:, None], gain_ffn[:, None]], axis=1), BOTH, axis=0, tiled=True
    )
    router = small[:, :experts]
    gain_a = small[:, experts].astype(F32)[None, :]
    gain_f = small[:, experts + 1].astype(F32)[None, :]
    near = jnp.dot(near_picks(bucket_count, 1), rel_bias, precision=HIGHEST).T
    near_back = jnp.dot(near_picks(bucket_count, -1), rel_bias, precision=HIGHEST).T

    slot_col, slot_row, cot_sent = pl.pallas_call(
        lambda *refs: place_kernel(slots, experts, *refs),
        out_shape=(
            jax.ShapeDtypeStruct((count, 1), jnp.int32),
            jax.ShapeDtypeStruct((1, count), jnp.int32),
            jax.ShapeDtypeStruct((total, width), BF16),
        ),
        in_specs=[smem] + in_vmem(3),
        out_specs=tuple(in_vmem(3)),
        compiler_params=params,
        name="places",
    )(capacity, routes, routes.reshape(1, count), cotangent)

    def spread(rows):
        taken = lax.all_to_all(
            rows.reshape(wide, local * slots, width), "wide", split_axis=0, concat_axis=0, tiled=True
        )
        held = lax.all_gather(taken, "narrow", axis=0, tiled=True)
        return held.reshape(wide * narrow, local, slots, width)

    def collect(rows):
        own = lax.psum_scatter(
            rows.reshape(wide * narrow, local * slots, width), "narrow", scatter_dimension=0, tiled=True
        )
        back = lax.all_to_all(own, "wide", split_axis=0, concat_axis=0, tiled=True)
        return back.reshape(total, width)

    cot_all = spread(cot_sent)

    rows_t = lambda dtype, cols=width: jax.ShapeDtypeStruct((count, cols), dtype)
    normed, q, k, v, att, lse, mixed, normed_f, sent = pl.pallas_call(
        forward_kernel,
        out_shape=(
            rows_t(BF16), rows_t(BF16), rows_t(BF16), rows_t(BF16), rows_t(BF16), rows_t(F32, BLOCK),
            rows_t(F32), rows_t(BF16), jax.ShapeDtypeStruct((total, width), BF16),
        ),
        in_specs=[smem] + in_vmem(7),
        out_specs=tuple(in_vmem(9)),
        compiler_params=params,
        name="forward",
    )(rel_bias, inputs, weights, gain_a, gain_f, router, near, slot_row)

    rows_all = spread(sent)
    sources = wide * narrow
    block = pl.BlockSpec((sources, 1, slots, width), lambda e: (0, e, 0, 0))
    w_in_spec = pl.BlockSpec((1, width, hidden_width), lambda e: (e, 0, 0))
    w_out_spec = pl.BlockSpec((1, hidden_width, width), lambda e: (e, 0, 0))
    first_expert = (lax.axis_index("wide") * local).astype(jnp.int32)[None]
    back, grows, gin, gout = pl.pallas_call(
        expert_kernel,
        grid=(local,),
        out_shape=(
            jax.ShapeDtypeStruct(rows_all.shape, BF16),
            jax.ShapeDtypeStruct(rows_all.shape, BF16),
            jax.ShapeDtypeStruct(expert_in.shape, F32),
            jax.ShapeDtypeStruct(expert_out.shape, F32),
        ),
        in_specs=[
            smem, block, block, w_in_spec, w_out_spec, pl.BlockSpec((width, experts), lambda e: (0, 0)),
        ],
        out_specs=(block, block, w_in_spec, w_out_spec),
        scratch_shapes=[
            pltpu.VMEM((sources * slots, hidden_width), BF16),
            pltpu.VMEM((sources * slots, hidden_width), BF16),
            pltpu.VMEM((sources * slots, width), BF16),
        ],
        compiler_params=params,
        name="experts",
    )(first_expert, rows_all, cot_all, expert_in, expert_out, router)
    outs_back = collect(back)
    grows_back = collect(grows)

    wide_t = lambda dtype: pltpu.VMEM((width, count), dtype)
    tall = lambda dtype: pltpu.VMEM((count, width), dtype)
    result, grad_inputs, gw, grouter, gnear, gfar, ggain = pl.pallas_call(
        backward_kernel,
        out_shape=(
            rows_t(BF16), rows_t(F32), jax.ShapeDtypeStruct((width, 4 * width), BF16),
            jax.ShapeDtypeStruct((width, experts), F32), jax.ShapeDtypeStruct((HEADS, 4 * BLOCK), F32),
            jax.ShapeDtypeStruct((HEADS, 2 * BLOCK), F32), jax.ShapeDtypeStruct((2, width), F32),
        ),
        in_specs=[smem] + in_vmem(19),
        out_specs=tuple(in_vmem(7)),
        scratch_shapes=[
            wide_t(BF16), wide_t(BF16), wide_t(BF16), tall(BF16), wide_t(BF16),
            pltpu.VMEM((HEADS, count), F32), pltpu.VMEM((BLOCK, count), F32),
            tall(BF16), tall(BF16), tall(BF16), tall(F32), pltpu.VMEM((count, count), BF16),
        ],
        compiler_params=params,
        name="backward",
    )(
        rel_bias, inputs, weights, gain_a, gain_f, router, near_back, slot_col, routes,
        normed, q, k, v, att, lse, mixed, normed_f, cotangent, outs_back, grows_back,
    )

    gw = lax.psum_scatter(gw, BOTH, scatter_dimension=0, tiled=True).astype(F32)
    grad_query, grad_key, grad_value, grad_output = (gw[:, i * width : (i + 1) * width] for i in range(4))
    gsmall = lax.psum_scatter(
        jnp.concatenate([grouter, ggain.T], axis=1), BOTH, scatter_dimension=0, tiled=True
    )
    grad_rel = jnp.dot(near_picks(bucket_count, -1).T, gnear.T, precision=HIGHEST)
    low, high = jnp.sum(gfar[:, :BLOCK], axis=1), jnp.sum(gfar[:, BLOCK:], axis=1)
    grad_rel = grad_rel.at[bucket_count // 2 - 1].add(low).at[bucket_count - 1].add(high)
    grad_rel = lax.psum(grad_rel, BOTH)
    return (
        result, grad_inputs, gsmall[:, experts], grad_query, grad_key, grad_value, grad_output,
        grad_rel, gsmall[:, experts + 1], gsmall[:, :experts], gin, gout,
    )


def solution(mesh):
    return jax.shard_map(
        shards,
        mesh=mesh,
        in_specs=(
            P(BOTH, None),
            P(BOTH),
            P(BOTH, None),
            P(BOTH, None),
            P(BOTH, None),
            P(BOTH, None),
            P(),
            P(BOTH),
            P(BOTH, None),
            P("wide", None, "narrow"),
            P("wide", "narrow", None),
            P(BOTH, None),
            P(BOTH),
            P(BOTH, None),
        ),
        out_specs=(
            P(BOTH, None),
            P(BOTH, None),
            P(BOTH),
            P(BOTH, None),
            P(BOTH, None),
            P(BOTH, None),
            P(BOTH, None),
            P(),
            P(BOTH),
            P(BOTH, None),
            P("wide", None, "narrow"),
            P("wide", "narrow", None),
        ),
        check_vma=False,
    )
```

```python
import jax
import jax.numpy as jnp
import numpy as np
from jax import lax
from jax.experimental import pallas as pl
from jax.experimental.pallas import tpu as pltpu
from jax.sharding import PartitionSpec as P

HEADS = 12
SEQ_LEN = 512
BLOCK = 128
EPSILON = 1e-06
HIGHEST = lax.Precision.HIGHEST
ROOT_TWO_PI = 0.7978845608028654
CUBIC = 0.044715
BOTH = ("wide", "narrow")
F32 = jnp.float32
BF16 = jnp.bfloat16


def bucket_of(offsets, bucket_count):
    half_count = bucket_count // 2
    exact_count = half_count // 2
    distance = np.abs(offsets)
    scaled = exact_count + np.floor(
        np.log(np.maximum(distance, 1) / exact_count)
        / np.log(128.0 / exact_count)
        * (half_count - exact_count)
    ).astype(np.int64)
    scaled = np.minimum(scaled, half_count - 1)
    return ((offsets > 0) * half_count + np.where(distance < exact_count, distance, scaled)).astype(
        np.int32
    )


def near_picks(bucket_count, sign):
    offsets = sign * (np.arange(4 * BLOCK) - (2 * BLOCK - 1))
    picks = (bucket_of(offsets, bucket_count)[:, None] == np.arange(bucket_count)[None, :]).astype(
        np.float32
    )
    picks[-1] = 0.0
    return picks


def dot_nn(left, right):
    return lax.dot_general(left, right, (((1,), (0,)), ((), ())), preferred_element_type=F32)


def dot_nt(left, right):
    return lax.dot_general(left, right, (((1,), (1,)), ((), ())), preferred_element_type=F32)


def dot_tn(left, right):
    return lax.dot_general(left, right, (((0,), (0,)), ((), ())), preferred_element_type=F32)


def inverse_rms(values):
    return lax.rsqrt(jnp.mean(values * values, axis=-1, keepdims=True) + EPSILON)


def norm_backward(values, inverse, gain, grad_normed):
    scaled = grad_normed * gain
    grad_gain = jnp.sum(grad_normed * values * inverse, axis=0, keepdims=True)
    inner = jnp.mean(scaled * values, axis=-1, keepdims=True)
    return (inverse * (scaled - values * inverse * inverse * inner), grad_gain)


def softmax_lanes(logits):
    peak = jnp.max(logits, axis=-1, keepdims=True)
    exponent = jnp.exp(logits - peak)
    return exponent / jnp.sum(exponent, axis=-1, keepdims=True)


def toeplitz_near(near_row):
    spread = jnp.broadcast_to(near_row, (BLOCK, 4 * BLOCK))
    return pltpu.roll(spread, 3 * BLOCK + 1, 1, stride=1, stride_axis=0)[:, : 3 * BLOCK]


def bias_rows(near, far_low, far_high, row, blocks):
    pieces = []
    for column in range(blocks):
        distance = column - row
        if distance <= -2:
            pieces.append(jnp.full((BLOCK, BLOCK), far_low, F32))
        elif distance >= 2:
            pieces.append(jnp.full((BLOCK, BLOCK), far_high, F32))
        else:
            pieces.append(near[:, (distance + 1) * BLOCK : (distance + 2) * BLOCK])
    return jnp.concatenate(pieces, axis=1)


def diagonal_sums(near_sum):
    padded = jnp.concatenate([near_sum, jnp.zeros((BLOCK, BLOCK), F32)], axis=1)
    groups = jnp.zeros((8, 4 * BLOCK), F32)
    for at in range(0, BLOCK, 8):
        groups = groups + pltpu.roll(padded[at : at + 8, :], BLOCK - 8 - at, 1)
    sums = groups[7:8, :]
    for at in range(7):
        sums = sums + pltpu.roll(groups[at : at + 1, :], 7 - at, 1)
    return sums


def slot_places(routes_ref, row_ref, limit, experts, slots, count):
    lower = lax.broadcasted_iota(jnp.int32, (count, count), 0)
    upper = lax.broadcasted_iota(jnp.int32, (count, count), 1)
    col = routes_ref[...]
    chosen = lax.broadcasted_iota(jnp.int32, (count, experts), 1) == col
    running = dot_nn((upper <= lower).astype(BF16), chosen.astype(BF16))
    place = jnp.sum(jnp.where(chosen, running, 0.0), axis=1, keepdims=True).astype(jnp.int32) - 1
    slot_col = jnp.where(place < limit, col * slots + place, -1)
    row = row_ref[...]
    chosen_t = lax.broadcasted_iota(jnp.int32, (experts, count), 0) == row
    running_t = dot_nn(chosen_t.astype(BF16), (lower <= upper).astype(BF16))
    place_t = (
        jnp.sum(jnp.where(chosen_t, running_t, 0.0), axis=0, keepdims=True).astype(jnp.int32) - 1
    )
    slot_row = jnp.where(place_t < limit, row * slots + place_t, -1)
    return slot_col, slot_row


def place_kernel(slots, experts, capacity_ref, routes_ref, row_ref, cot_ref, slot_col, slot_row, cot_out):
    count = routes_ref.shape[0]
    limit = capacity_ref[0] * count // experts
    col, row = slot_places(routes_ref, row_ref, limit, experts, slots, count)
    slot_col[...] = col
    slot_row[...] = row
    picks = (lax.broadcasted_iota(jnp.int32, (experts * slots, count), 0) == row).astype(BF16)
    cot_out[...] = dot_nn(picks, cot_ref[...]).astype(BF16)


def forward_kernel(
    rel_ref, x_ref, w_ref, gain_a, gain_f, router_ref, near_ref, slot_row,
    normed_ref, q_ref, k_ref, v_ref, att_ref, lse_ref, mixed_ref, normed_f, sent_ref,
):
    count, width = x_ref.shape
    head_dim = width // HEADS
    blocks = count // BLOCK
    bucket_count = rel_ref.shape[0]
    tokens = x_ref[...].astype(F32)
    normed = (tokens * inverse_rms(tokens) * gain_a[...]).astype(BF16)
    normed_ref[...] = normed
    for out, at in ((q_ref, 0), (k_ref, 1), (v_ref, 2)):
        out[...] = dot_nn(normed, w_ref[:, at * width : (at + 1) * width]).astype(BF16)
    lse_ref[...] = jnp.zeros_like(lse_ref)
    first = lax.broadcasted_iota(jnp.int32, (1, BLOCK), 1) < head_dim
    lanes = lax.broadcasted_iota(jnp.int32, (1, BLOCK), 1)

    def pair(at, carry):
        cols = pl.ds(pl.multiple_of(at * BLOCK, BLOCK), BLOCK)
        k_pair, v_pair = k_ref[:, cols], v_ref[:, cols]
        nears = [toeplitz_near(near_ref[pl.ds(2 * at + half, 1), :]) for half in range(2)]
        for row in range(blocks):
            rows = slice(row * BLOCK, (row + 1) * BLOCK)
            q_rows = q_ref[rows, cols] * jnp.asarray(head_dim**-0.5, BF16)
            found = []
            log_sums = lse_ref[rows, :]
            for half in range(2):
                head = 2 * at + half
                low, high = rel_ref[bucket_count // 2 - 1, head], rel_ref[bucket_count - 1, head]
                mask = first if half == 0 else jnp.logical_not(first)
                scores = dot_nt(jnp.where(mask, q_rows, jnp.zeros_like(q_rows)), k_pair)
                scores = scores + bias_rows(nears[half], low, high, row, blocks)
                peak = jnp.max(scores, axis=-1, keepdims=True)
                exponent = jnp.exp(scores - peak)
                total = jnp.sum(exponent, axis=-1, keepdims=True)
                found.append(dot_nn((exponent * (1.0 / total)).astype(BF16), v_pair))
                log_sums = jnp.where(lanes == head, peak + jnp.log(total), log_sums)
            lse_ref[rows, :] = log_sums
            att_ref[rows, cols] = jnp.where(first, found[0], found[1]).astype(BF16)
        return carry

    lax.fori_loop(0, HEADS // 2, pair, 0)
    mixed = tokens + dot_nn(att_ref[...], w_ref[:, 3 * width : 4 * width])
    mixed_ref[...] = mixed
    normed_2 = (mixed * inverse_rms(mixed) * gain_f[...]).astype(BF16)
    normed_f[...] = normed_2
    total_slots = sent_ref.shape[0]
    picks = (lax.broadcasted_iota(jnp.int32, (total_slots, count), 0) == slot_row[...]).astype(BF16)
    sent_ref[...] = dot_nn(picks, normed_2).astype(BF16)


def expert_kernel(
    first_ref, rows_ref, cot_ref, in_ref, out_ref, router_ref,
    back_ref, grows_ref, gin_ref, gout_ref, hidden_ref, gpre_ref, sg_ref,
):
    sources, _, slots, width = rows_ref.shape
    total = sources * slots
    step = min(256, total)
    expert = first_ref[0] + pl.program_id(0)

    def chunk(at, carry):
        these = pl.ds(pl.multiple_of(at * (step // slots), step // slots), step // slots)
        flat = pl.ds(pl.multiple_of(at * step, step), step)
        rows = rows_ref[these, 0].reshape(step, width)
        probs = softmax_lanes(dot_nn(rows, router_ref[...]))
        here = lax.broadcasted_iota(jnp.int32, probs.shape, 1) == expert
        gate = jnp.sum(jnp.where(here, probs, 0.0), axis=-1, keepdims=True)
        sg = (cot_ref[these, 0].reshape(step, width).astype(F32) * gate).astype(BF16)
        sg_ref[flat, :] = sg
        pre = dot_nn(rows, in_ref[0])
        square = pre * pre
        inner = jnp.tanh(pre * (ROOT_TWO_PI + ROOT_TWO_PI * CUBIC * square))
        half = 0.5 * (1.0 + inner)
        hidden = (pre * half).astype(BF16)
        hidden_ref[flat, :] = hidden
        slope = half + 0.5 * pre * (1.0 - inner * inner) * (
            ROOT_TWO_PI + 3.0 * ROOT_TWO_PI * CUBIC * square
        )
        gpre = (dot_nt(sg, out_ref[0]) * slope).astype(BF16)
        gpre_ref[flat, :] = gpre
        back_ref[these, 0] = dot_nn(hidden, out_ref[0]).astype(BF16).reshape(-1, slots, width)
        grows_ref[these, 0] = dot_nt(gpre, in_ref[0]).astype(BF16).reshape(-1, slots, width)
        return carry

    lax.fori_loop(0, total // step, chunk, 0)
    gout_ref[0] = dot_tn(hidden_ref[...], sg_ref[...])
    gin_ref[0] = dot_tn(rows_ref[:, 0].reshape(total, width), gpre_ref[...])


def remote(source, target, send, receive, device):
    return pltpu.make_async_remote_copy(
        src_ref=source,
        dst_ref=target,
        send_sem=send,
        recv_sem=receive,
        device_id=device,
        device_id_type=pl.DeviceIdType.MESH,
    )


def greet(devices):
    barrier = pltpu.get_barrier_semaphore()
    for device in devices:
        pl.semaphore_signal(barrier, inc=1, device_id=device, device_id_type=pl.DeviceIdType.MESH)
    pl.semaphore_wait(barrier, len(devices))


class Place:
    def __init__(self, wide):
        self.wide = wide
        self.w, self.n = lax.axis_index("wide"), lax.axis_index("narrow")
        self.x, self.c = self.n // 2, lax.rem(self.n, 2)
        self.core = (self.w, self.x * 2 + 1 - self.c)
        self.side = (self.w, (1 - self.x) * 2 + self.c)

    def at(self, step):
        return lax.rem(self.w + step, self.wide)

    def peer(self, step):
        return (self.at(step), self.n)

    def partners(self):
        return [self.peer(k) for k in range(1, self.wide)] + [self.core, self.side]


class Spread:
    def __init__(self, place, sent, held, wide_s, wide_r, side_s, side_r, core_s, core_r):
        self.place, self.sent, self.held = place, sent, held
        self.wide_s, self.wide_r, self.side_s, self.side_r = wide_s, wide_r, side_s, side_r
        self.core_s, self.core_r = core_s, core_r

    def hop(self, e, k):
        p = self.place
        return remote(
            self.sent.at[p.at(k), e], self.held.at[e, p.n, p.w], self.wide_s.at[e, k], self.wide_r.at[e, k], p.peer(k)
        )

    def start(self, e):
        for k in range(1, self.place.wide):
            self.hop(e, k).start()

    def half(self, e, h):
        p = self.place
        run = p.wide // 2
        rows = self.held.at[e, p.n, pl.ds(h * run, run)]
        return remote(rows, rows, self.side_s.at[e, h], self.side_r.at[e, h], p.side)

    def over(self, e, far):
        p = self.place
        m = (1 - p.x) * 2 + p.c if far else p.n
        return remote(
            self.held.at[e, m], self.held.at[e, m], self.core_s.at[e, far], self.core_r.at[e, far], p.core
        )

    def forward(self, e):
        p = self.place
        run = p.wide // 2
        for other in range(2):
            h = p.w // run
            h = 1 - h if other else h
            for k in range(1, p.wide):
                mine = (p.at(p.wide - k) // run) == h

                @pl.when(mine)
                def _():
                    self.hop(e, k).wait_recv()

            self.half(e, h).start()
        self.over(e, 0).start()

    def pass_on(self, e):
        for h in range(2):
            self.half(e, h).wait_recv()
        self.over(e, 1).start()

    def arrive(self, e):
        self.over(e, 0).wait_recv()
        self.over(e, 1).wait_recv()

    def drain(self, e):
        for k in range(1, self.place.wide):
            self.hop(e, k).wait_send()
        for h in range(2):
            self.half(e, h).wait_send()
            self.over(e, h).wait_send()


def moving_expert_kernel(
    sent, cot_hbm, in_hbm, out_hbm, router_ref,
    rows_o, sg_o, hidden_o, gpre_o, outs_o, back_o, gate_o,
    held, cot, w_in, w_out, sg, hidden, gpre, outs, to_core, from_core, to_side, from_side, near_sum, ready,
    gate_sum, gate_core, gate_from_core, gate_side, gate_from_side, gate_ready,
    load_s, store_s, wide_s, wide_r, side_s, side_r, core_s, core_r,
    rc_s, rc_r, rx_s, rx_r, rw_s, rw_r, gc_s, gc_r, gx_s, gx_r, gw_s, gw_r,
):
    wide, local, slots, width = sent.shape
    narrow = held.shape[1]
    step = wide * slots
    p = Place(wide)
    moves = Spread(p, sent, held, wide_s, wide_r, side_s, side_r, core_s, core_r)
    greet(p.partners())
    for e in range(local):
        moves.start(e)

    def loads(e):
        return [
            pltpu.make_async_copy(in_hbm.at[e], w_in.at[e], load_s.at[e, 0]),
            pltpu.make_async_copy(out_hbm.at[e], w_out.at[e], load_s.at[e, 1]),
            pltpu.make_async_copy(cot_hbm.at[e], cot.at[e], load_s.at[e, 2]),
        ]

    def stores(e):
        b = lax.rem(e, 2)
        return [
            pltpu.make_async_copy(held.at[e], rows_o.at[e], store_s.at[e, 0]),
            pltpu.make_async_copy(sg.at[b], sg_o.at[e], store_s.at[e, 1]),
            pltpu.make_async_copy(hidden.at[b], hidden_o.at[e], store_s.at[e, 2]),
            pltpu.make_async_copy(gpre.at[b], gpre_o.at[e], store_s.at[e, 3]),
            pltpu.make_async_copy(outs.at[b], outs_o.at[e], store_s.at[e, 4]),
        ]

    for e in range(local):
        for copy in loads(e):
            copy.start()
        held[e, p.n, p.w] = sent[p.w, e]
    gate_sum[...] = jnp.zeros_like(gate_sum)
    moves.forward(0)
    moves.pass_on(0)

    def chunk(e, m):
        b = lax.rem(e, 2)
        rows = held[e, m].reshape(step, width)
        probs = softmax_lanes(dot_nn(rows, router_ref[...]))
        here = lax.broadcasted_iota(jnp.int32, probs.shape, 1) == p.w * local + e
        gate = jnp.sum(jnp.where(here, probs, 0.0), axis=-1, keepdims=True)
        cot_rows = cot[e, m].reshape(step, width).astype(F32)
        sg_rows = (cot_rows * gate).astype(BF16)
        sg[b, m] = sg_rows
        pre = dot_nn(rows, w_in[e])
        square = pre * pre
        inner = jnp.tanh(pre * (ROOT_TWO_PI + ROOT_TWO_PI * CUBIC * square))
        half = 0.5 * (1.0 + inner)
        hidden_rows = (pre * half).astype(BF16)
        hidden[b, m] = hidden_rows
        slope = half + 0.5 * pre * (1.0 - inner * inner) * (
            ROOT_TWO_PI + 3.0 * ROOT_TWO_PI * CUBIC * square
        )
        gpre_rows = (dot_nt(sg_rows, w_out[e]) * slope).astype(BF16)
        gpre[b, m] = gpre_rows
        out_rows = dot_nn(hidden_rows, w_out[e])
        outs[b, m] = out_rows.astype(BF16)
        gate_rows = jnp.sum(out_rows * cot_rows, axis=-1, keepdims=True)
        row = lax.broadcasted_iota(jnp.int32, (step, local * slots), 0)
        lane = lax.broadcasted_iota(jnp.int32, (step, local * slots), 1)
        spread = jnp.where(lane == e * slots + lax.rem(row, slots), gate_rows, 0.0)
        gate_sum[m] += jnp.sum(spread.reshape(wide, slots, local * slots), axis=1)
        return dot_nt(gpre_rows, w_in[e])

    def core_copy(e, far):
        return remote(to_core.at[e, far], from_core.at[e, far], rc_s.at[e, far], rc_r.at[e, far], p.core)

    def side_copy(e):
        return remote(to_side.at[e], from_side.at[e], rx_s.at[e], rx_r.at[e], p.side)

    def back_copy(e, k):
        return remote(ready.at[e, p.at(k)], back_o.at[p.w, e], rw_s.at[e, k], rw_r.at[e, k], p.peer(k))

    def finish(e):
        side_copy(e).wait_recv()
        ready[e] = (near_sum[...] + from_side[e].astype(F32)).astype(BF16).reshape(wide, slots, width)
        for k in range(1, wide):
            back_copy(e, k).start()
        back_o[p.w, e] = ready[e, p.w]

    far_x = (1 - p.x) * 2

    def expert(e, carry):
        for copy in loads(e):
            copy.wait()

        @pl.when(e >= 2)
        def _():
            for copy in stores(e - 2)[1:]:
                copy.wait()

        moves.arrive(e)
        to_core[e, 1] = chunk(e, far_x + 1 - p.c).astype(BF16)
        core_copy(e, 1).start()

        @pl.when(e + 1 < local)
        def _():
            moves.forward(e + 1)

        far_part = chunk(e, far_x + p.c)
        core_copy(e, 1).wait_recv()
        to_side[e] = (far_part + from_core[e, 1].astype(F32)).astype(BF16)
        side_copy(e).start()

        @pl.when(e > 0)
        def _():
            finish(e - 1)

        to_core[e, 0] = chunk(e, p.x * 2 + 1 - p.c).astype(BF16)
        core_copy(e, 0).start()

        @pl.when(e + 1 < local)
        def _():
            moves.pass_on(e + 1)

        near_part = chunk(e, p.n)
        core_copy(e, 0).wait_recv()
        near_sum[...] = near_part + from_core[e, 0].astype(F32)
        for copy in stores(e):
            copy.start()
        return carry

    lax.fori_loop(0, local, expert, 0)
    gate_core[0] = gate_sum[p.x * 2 + 1 - p.c]
    gate_core[1] = gate_sum[far_x + 1 - p.c]
    gates_core = remote(gate_core, gate_from_core, gc_s, gc_r, p.core)
    gates_core.start()
    gates_core.wait_recv()
    gate_side[...] = gate_sum[far_x + p.c] + gate_from_core[1]
    gates_side = remote(gate_side, gate_from_side, gx_s, gx_r, p.side)
    gates_side.start()
    finish(local - 1)
    gates_side.wait_recv()
    gates = gate_sum[p.n] + gate_from_core[0] + gate_from_side[...]
    for v in range(wide):
        gate_ready[v] = gates[v : v + 1, :]
    gates_wide = [
        remote(gate_ready.at[p.at(k)], gate_o.at[p.w], gw_s.at[k], gw_r.at[k], p.peer(k)) for k in range(1, wide)
    ]
    for copy in gates_wide:
        copy.start()
    gate_o[p.w] = gate_ready[p.w]
    gates_core.wait_send()
    gates_side.wait_send()

    def drain(e, carry):
        moves.drain(e)
        core_copy(e, 0).wait_send()
        core_copy(e, 1).wait_send()
        side_copy(e).wait_send()
        stores(e)[0].wait()

        @pl.when(e >= local - 2)
        def _():
            for copy in stores(e)[1:]:
                copy.wait()

        for k in range(1, wide):
            back_copy(e, k).wait()
        return carry

    lax.fori_loop(0, local, drain, 0)
    for copy in gates_wide:
        copy.wait()


def weight_grad_kernel(rows_ref, sg_ref, hidden_ref, gpre_ref, gin_ref, gout_ref):
    gout_ref[0] = dot_tn(hidden_ref[0], sg_ref[0])
    gin_ref[0] = dot_tn(rows_ref[0], gpre_ref[0])


def moving_experts(sent, cot_all, expert_in, expert_out, router, wide, narrow):
    _, local, slots, width = sent.shape
    hidden_width = expert_in.shape[2]
    step = wide * slots
    sds = jax.ShapeDtypeStruct
    any_spec, vmem_spec = pl.BlockSpec(memory_space=pl.ANY), pl.BlockSpec(memory_space=pltpu.VMEM)
    dma = pltpu.SemaphoreType.DMA
    rows, sg, hidden, gpre, outs, back, gates = pl.pallas_call(
        moving_expert_kernel,
        out_shape=(
            sds((local, narrow, wide, slots, width), BF16),
            sds((local, narrow, step, width), BF16),
            sds((local, narrow, step, hidden_width), BF16),
            sds((local, narrow, step, hidden_width), BF16),
            sds((local, narrow, step, width), BF16),
            sds((wide, local, slots, width), BF16),
            sds((wide, 1, local * slots), F32),
        ),
        in_specs=[vmem_spec, any_spec, any_spec, any_spec, vmem_spec],
        out_specs=(any_spec,) * 5 + (vmem_spec,) * 2,
        scratch_shapes=[
            pltpu.VMEM((local, narrow, wide, slots, width), BF16),
            pltpu.VMEM((local, narrow, wide, slots, width), BF16),
            pltpu.VMEM(expert_in.shape, BF16),
            pltpu.VMEM(expert_out.shape, BF16),
            pltpu.VMEM((2, narrow, step, width), BF16),
            pltpu.VMEM((2, narrow, step, hidden_width), BF16),
            pltpu.VMEM((2, narrow, step, hidden_width), BF16),
            pltpu.VMEM((2, narrow, step, width), BF16),
            pltpu.VMEM((local, 2, step, width), BF16),
            pltpu.VMEM((local, 2, step, width), BF16),
            pltpu.VMEM((local, step, width), BF16),
            pltpu.VMEM((local, step, width), BF16),
            pltpu.VMEM((step, width), F32),
            pltpu.VMEM((local, wide, slots, width), BF16),
            pltpu.VMEM((narrow, wide, local * slots), F32),
            pltpu.VMEM((2, wide, local * slots), F32),
            pltpu.VMEM((2, wide, local * slots), F32),
            pltpu.VMEM((wide, local * slots), F32),
            pltpu.VMEM((wide, local * slots), F32),
            pltpu.VMEM((wide, 1, local * slots), F32),
            dma((local, 3)), dma((local, 5)), dma((local, wide)), dma((local, wide)),
            dma((local, 2)), dma((local, 2)), dma((local, 2)), dma((local, 2)),
            dma((local, 2)), dma((local, 2)), dma((local,)), dma((local,)), dma((local, wide)), dma((local, wide)),
            dma, dma, dma, dma, dma((wide,)), dma((wide,)),
        ],
        compiler_params=pltpu.CompilerParams(
            collective_id=2, has_side_effects=True, vmem_limit_bytes=62 << 20
        ),
        name="experts",
    )(sent, cot_all, expert_in, expert_out, router)
    total = narrow * step
    spec = lambda cols: pl.BlockSpec((1, total, cols), lambda e: (e, 0, 0))
    gin, gout = pl.pallas_call(
        weight_grad_kernel,
        grid=(local,),
        out_shape=(sds(expert_in.shape, F32), sds(expert_out.shape, F32)),
        in_specs=[spec(width), spec(width), spec(hidden_width), spec(hidden_width)],
        out_specs=(
            pl.BlockSpec((1, width, hidden_width), lambda e: (e, 0, 0)),
            pl.BlockSpec((1, hidden_width, width), lambda e: (e, 0, 0)),
        ),
        compiler_params=pltpu.CompilerParams(vmem_limit_bytes=60 << 20),
        name="weight_grads",
    )(
        rows.reshape(local, total, width), sg.reshape(local, total, width),
        hidden.reshape(local, total, hidden_width), gpre.reshape(local, total, hidden_width),
    )
    return outs, back, gates, gin, gout


def backward_kernel(
    rel_ref, x_ref, w_ref, gain_a, gain_f, router_ref, near_ref, slot_col, routes_ref,
    normed_ref, q_ref, k_ref, v_ref, att_ref, lse_ref, mixed_ref, normed_f, cot_ref, outs_ref, grows_ref, gates_ref,
    result_ref, gx_ref, gw_ref, grouter_ref, gnear_ref, gfar_ref, ggain_ref,
    q_t, k_t, normed_t, datt, datt_t, delta, lse_t, gq, gk, gv, gmixed, dst,
):
    count, width = x_ref.shape
    head_dim = width // HEADS
    blocks = count // BLOCK
    bucket_count = rel_ref.shape[0]
    experts = router_ref.shape[1]
    owned = lax.broadcasted_iota(jnp.int32, (count, outs_ref.shape[0]), 1) == slot_col[...]
    picks = owned.astype(BF16)
    combined = dot_nn(picks, outs_ref[...])
    mixed = mixed_ref[...]
    cot = cot_ref[...].astype(F32)
    probs = softmax_lanes(dot_nn(normed_f[...], router_ref[...]))
    chosen = lax.broadcasted_iota(jnp.int32, (count, experts), 1) == routes_ref[...]
    gate = jnp.sum(jnp.where(chosen, probs, 0.0), axis=-1, keepdims=True)
    result_ref[...] = (mixed + gate * combined).astype(BF16)
    grad_gate = jnp.sum(jnp.where(owned, gates_ref[...], 0.0), axis=-1, keepdims=True)
    grad_logits = (probs * (jnp.where(chosen, grad_gate, 0.0) - gate * grad_gate)).astype(BF16)
    grouter_ref[...] = dot_tn(normed_f[...], grad_logits)
    grad_normed = dot_nt(grad_logits, router_ref[...]) + dot_nn(picks, grows_ref[...])
    grad_norm, ggain_ref[1:2, :] = norm_backward(mixed, inverse_rms(mixed), gain_f[...], grad_normed)
    grad_mixed = cot + grad_norm
    gmixed[...] = grad_mixed
    branch = grad_mixed.astype(BF16)
    gw_ref[:, 3 * width : 4 * width] = dot_tn(att_ref[...], branch).astype(BF16)
    datt[...] = dot_nt(branch, w_ref[:, 3 * width : 4 * width]).astype(BF16)
    datt_t[...] = datt[...].T
    q_t[...] = (q_ref[...] * jnp.asarray(head_dim**-0.5, BF16)).T
    k_t[...] = k_ref[...].T
    normed_t[...] = normed_ref[...].T
    products = datt_t[...].astype(F32) * att_ref[...].T.astype(F32)
    delta[...] = jnp.sum(products.reshape(HEADS, head_dim, count), axis=1)
    lse_t[...] = lse_ref[...].T
    first = lax.broadcasted_iota(jnp.int32, (1, BLOCK), 1) < head_dim

    def pair(at, carry):
        cols = pl.ds(pl.multiple_of(at * BLOCK, BLOCK), BLOCK)
        q_pair, datt_pair = q_ref[:, cols], datt[:, cols]
        gq_parts, gk_parts, gv_parts = [], [], []
        for half in range(2):
            head = 2 * at + half
            low, high = rel_ref[bucket_count // 2 - 1, head], rel_ref[bucket_count - 1, head]
            mask = first if half == 0 else jnp.logical_not(first)
            near = toeplitz_near(near_ref[pl.ds(head, 1), :])
            lse_row, delta_row = lse_t[pl.ds(head, 1), :], delta[pl.ds(head, 1), :]
            near_sum = jnp.zeros((BLOCK, 3 * BLOCK), F32)
            low_sum, high_sum = jnp.zeros((BLOCK, BLOCK), F32), jnp.zeros((BLOCK, BLOCK), F32)
            gk_rows, gv_rows = [], []
            for row in range(blocks):
                rows = slice(row * BLOCK, (row + 1) * BLOCK)
                k_rows, v_rows = k_ref[rows, cols], v_ref[rows, cols]
                zeros = jnp.zeros_like(k_rows)
                scores = dot_nn(jnp.where(mask, k_rows, zeros), q_t[cols, :])
                scores = scores + bias_rows(near, high, low, row, blocks)
                weights = jnp.exp(scores - lse_row)
                grad_weights = dot_nn(jnp.where(mask, v_rows, zeros), datt_t[cols, :])
                grad_scores = weights * (grad_weights - delta_row)
                gv_rows.append(dot_nn(weights.astype(BF16), datt_pair))
                low_bits = grad_scores.astype(BF16)
                dst[rows, :] = low_bits
                gk_rows.append(dot_nn(low_bits, q_pair))
                for column in range(blocks):
                    piece = grad_scores[:, column * BLOCK : (column + 1) * BLOCK]
                    distance = column - row
                    if distance <= -2:
                        high_sum = high_sum + piece
                    elif distance >= 2:
                        low_sum = low_sum + piece
                    else:
                        pads = [jnp.zeros((BLOCK, BLOCK), F32)] * 3
                        pads[distance + 1] = piece
                        near_sum = near_sum + jnp.concatenate(pads, axis=1)
            gq_parts.append(
                dot_nn(k_t[pl.ds(pl.multiple_of(head * head_dim, head_dim), head_dim), :], dst[...])
            )
            gk_parts.append(jnp.concatenate(gk_rows, axis=0))
            gv_parts.append(jnp.concatenate(gv_rows, axis=0))
            gnear_ref[pl.ds(head, 1), :] = diagonal_sums(near_sum)
            gfar_ref[pl.ds(head, 1), :] = jnp.concatenate(
                [jnp.sum(low_sum, axis=0, keepdims=True), jnp.sum(high_sum, axis=0, keepdims=True)], axis=1
            )
        scale = head_dim**-0.5
        gq[:, cols] = (jnp.concatenate(gq_parts, axis=0).T * scale).astype(BF16)
        gk[:, cols] = (jnp.where(first, gk_parts[0], gk_parts[1]) * scale).astype(BF16)
        gv[:, cols] = jnp.where(first, gv_parts[0], gv_parts[1]).astype(BF16)
        return carry

    lax.fori_loop(0, HEADS // 2, pair, 0)
    grad_normed = jnp.zeros((count, width), F32)
    for at, grad in enumerate((gq, gk, gv)):
        gw_ref[:, at * width : (at + 1) * width] = dot_nn(normed_t[...], grad[...]).astype(BF16)
        grad_normed = grad_normed + dot_nt(grad[...], w_ref[:, at * width : (at + 1) * width])
    tokens = x_ref[...].astype(F32)
    grad_norm, ggain_ref[0:1, :] = norm_backward(tokens, inverse_rms(tokens), gain_a[...], grad_normed)
    gx_ref[...] = gmixed[...] + grad_norm


def in_vmem(count):
    return [pl.BlockSpec(memory_space=pltpu.VMEM)] * count


def shards(
    inputs, gain_attn, w_query, w_key, w_value, w_output, rel_bias, gain_ffn, w_router,
    expert_in, expert_out, routes, capacity, cotangent,
):
    count, width = inputs.shape
    experts = w_router.shape[1]
    local, _, hidden_width = expert_in.shape
    wide, narrow = lax.axis_size("wide"), lax.axis_size("narrow")
    slots = 2 * count // experts
    total = experts * slots
    bucket_count = rel_bias.shape[0]
    params = pltpu.CompilerParams(vmem_limit_bytes=60 << 20)
    smem = pl.BlockSpec(memory_space=pltpu.SMEM)

    packed = jnp.concatenate([w_query, w_key, w_value, w_output], axis=1)
    weights = lax.all_gather(packed, BOTH, axis=0, tiled=True)
    small = lax.all_gather(
        jnp.concatenate([w_router, gain_attn[:, None], gain_ffn[:, None]], axis=1), BOTH, axis=0, tiled=True
    )
    router = small[:, :experts]
    gain_a = small[:, experts].astype(F32)[None, :]
    gain_f = small[:, experts + 1].astype(F32)[None, :]
    near = jnp.dot(near_picks(bucket_count, 1), rel_bias, precision=HIGHEST).T
    near_back = jnp.dot(near_picks(bucket_count, -1), rel_bias, precision=HIGHEST).T

    slot_col, slot_row, cot_sent = pl.pallas_call(
        lambda *refs: place_kernel(slots, experts, *refs),
        out_shape=(
            jax.ShapeDtypeStruct((count, 1), jnp.int32),
            jax.ShapeDtypeStruct((1, count), jnp.int32),
            jax.ShapeDtypeStruct((total, width), BF16),
        ),
        in_specs=[smem] + in_vmem(3),
        out_specs=tuple(in_vmem(3)),
        compiler_params=params,
        name="places",
    )(capacity, routes, routes.reshape(1, count), cotangent)

    def spread(rows):
        taken = lax.all_to_all(
            rows.reshape(wide, local * slots, width), "wide", split_axis=0, concat_axis=0, tiled=True
        )
        held = lax.all_gather(taken, "narrow", axis=0, tiled=True)
        return held.reshape(wide * narrow, local, slots, width)

    def collect(rows):
        own = lax.psum_scatter(
            rows.reshape(wide * narrow, local * slots, width), "narrow", scatter_dimension=0, tiled=True
        )
        back = lax.all_to_all(own, "wide", split_axis=0, concat_axis=0, tiled=True)
        return back.reshape(total, width)

    cot_all = spread(cot_sent)

    rows_t = lambda dtype, cols=width: jax.ShapeDtypeStruct((count, cols), dtype)
    normed, q, k, v, att, lse, mixed, normed_f, sent = pl.pallas_call(
        forward_kernel,
        out_shape=(
            rows_t(BF16), rows_t(BF16), rows_t(BF16), rows_t(BF16), rows_t(BF16), rows_t(F32, BLOCK),
            rows_t(F32), rows_t(BF16), jax.ShapeDtypeStruct((total, width), BF16),
        ),
        in_specs=[smem] + in_vmem(7),
        out_specs=tuple(in_vmem(9)),
        compiler_params=params,
        name="forward",
    )(rel_bias, inputs, weights, gain_a, gain_f, router, near, slot_row)

    if narrow == 4 and wide % 2 == 0 and slots % 16 == 0 and local * slots % BLOCK == 0:
        outs, back, gates, gin, gout = moving_experts(
            sent.reshape(wide, local, slots, width),
            jnp.moveaxis(cot_all.reshape(narrow, wide, local, slots, width), 2, 0),
            expert_in, expert_out, router, wide, narrow,
        )
        grows_back = back.reshape(total, width)
        gates = gates.reshape(1, total)
        outs_back = collect(
            jnp.moveaxis(outs.reshape(local, narrow * wide, slots, width), 0, 1)
        )
    else:
        rows_all = spread(sent)
        sources = wide * narrow
        block = pl.BlockSpec((sources, 1, slots, width), lambda e: (0, e, 0, 0))
        w_in_spec = pl.BlockSpec((1, width, hidden_width), lambda e: (e, 0, 0))
        w_out_spec = pl.BlockSpec((1, hidden_width, width), lambda e: (e, 0, 0))
        first_expert = (lax.axis_index("wide") * local).astype(jnp.int32)[None]
        back, grows, gin, gout = pl.pallas_call(
            expert_kernel,
            grid=(local,),
            out_shape=(
                jax.ShapeDtypeStruct(rows_all.shape, BF16),
                jax.ShapeDtypeStruct(rows_all.shape, BF16),
                jax.ShapeDtypeStruct(expert_in.shape, F32),
                jax.ShapeDtypeStruct(expert_out.shape, F32),
            ),
            in_specs=[
                smem, block, block, w_in_spec, w_out_spec, pl.BlockSpec((width, experts), lambda e: (0, 0)),
            ],
            out_specs=(block, block, w_in_spec, w_out_spec),
            scratch_shapes=[
                pltpu.VMEM((sources * slots, hidden_width), BF16),
                pltpu.VMEM((sources * slots, hidden_width), BF16),
                pltpu.VMEM((sources * slots, width), BF16),
            ],
            compiler_params=params,
            name="experts",
        )(first_expert, rows_all, cot_all, expert_in, expert_out, router)
        outs_back = collect(back)
        grows_back = collect(grows)
        gates = jnp.sum(outs_back.astype(F32) * cot_sent.astype(F32), axis=1)[None, :]

    wide_t = lambda dtype: pltpu.VMEM((width, count), dtype)
    tall = lambda dtype: pltpu.VMEM((count, width), dtype)
    result, grad_inputs, gw, grouter, gnear, gfar, ggain = pl.pallas_call(
        backward_kernel,
        out_shape=(
            rows_t(BF16), rows_t(F32), jax.ShapeDtypeStruct((width, 4 * width), BF16),
            jax.ShapeDtypeStruct((width, experts), F32), jax.ShapeDtypeStruct((HEADS, 4 * BLOCK), F32),
            jax.ShapeDtypeStruct((HEADS, 2 * BLOCK), F32), jax.ShapeDtypeStruct((2, width), F32),
        ),
        in_specs=[smem] + in_vmem(20),
        out_specs=tuple(in_vmem(7)),
        scratch_shapes=[
            wide_t(BF16), wide_t(BF16), wide_t(BF16), tall(BF16), wide_t(BF16),
            pltpu.VMEM((HEADS, count), F32), pltpu.VMEM((BLOCK, count), F32),
            tall(BF16), tall(BF16), tall(BF16), tall(F32), pltpu.VMEM((count, count), BF16),
        ],
        compiler_params=params,
        name="backward",
    )(
        rel_bias, inputs, weights, gain_a, gain_f, router, near_back, slot_col, routes,
        normed, q, k, v, att, lse, mixed, normed_f, cotangent, outs_back, grows_back, gates,
    )

    gw = lax.psum_scatter(gw, BOTH, scatter_dimension=0, tiled=True).astype(F32)
    grad_query, grad_key, grad_value, grad_output = (gw[:, i * width : (i + 1) * width] for i in range(4))
    gsmall = lax.psum_scatter(
        jnp.concatenate([grouter, ggain.T], axis=1), BOTH, scatter_dimension=0, tiled=True
    )
    grad_rel = jnp.dot(near_picks(bucket_count, -1).T, gnear.T, precision=HIGHEST)
    low, high = jnp.sum(gfar[:, :BLOCK], axis=1), jnp.sum(gfar[:, BLOCK:], axis=1)
    grad_rel = grad_rel.at[bucket_count // 2 - 1].add(low).at[bucket_count - 1].add(high)
    grad_rel = lax.psum(grad_rel, BOTH)
    return (
        result, grad_inputs, gsmall[:, experts], grad_query, grad_key, grad_value, grad_output,
        grad_rel, gsmall[:, experts + 1], gsmall[:, :experts], gin, gout,
    )


def solution(mesh):
    return jax.shard_map(
        shards,
        mesh=mesh,
        in_specs=(
            P(BOTH, None),
            P(BOTH),
            P(BOTH, None),
            P(BOTH, None),
            P(BOTH, None),
            P(BOTH, None),
            P(),
            P(BOTH),
            P(BOTH, None),
            P("wide", None, "narrow"),
            P("wide", "narrow", None),
            P(BOTH, None),
            P(BOTH),
            P(BOTH, None),
        ),
        out_specs=(
            P(BOTH, None),
            P(BOTH, None),
            P(BOTH),
            P(BOTH, None),
            P(BOTH, None),
            P(BOTH, None),
            P(BOTH, None),
            P(),
            P(BOTH),
            P(BOTH, None),
            P("wide", None, "narrow"),
            P("wide", "narrow", None),
        ),
        check_vma=False,
    )
```

```python
import jax
import jax.numpy as jnp
import numpy as np
from jax import lax
from jax.experimental import pallas as pl
from jax.experimental.pallas import tpu as pltpu
from jax.sharding import PartitionSpec as P

HEADS = 12
SEQ_LEN = 512
BLOCK = 128
EPSILON = 1e-06
HIGHEST = lax.Precision.HIGHEST
ROOT_TWO_PI = 0.7978845608028654
CUBIC = 0.044715
BOTH = ("wide", "narrow")
F32 = jnp.float32
BF16 = jnp.bfloat16


def bucket_of(offsets, bucket_count):
    half_count = bucket_count // 2
    exact_count = half_count // 2
    distance = np.abs(offsets)
    scaled = exact_count + np.floor(
        np.log(np.maximum(distance, 1) / exact_count)
        / np.log(128.0 / exact_count)
        * (half_count - exact_count)
    ).astype(np.int64)
    scaled = np.minimum(scaled, half_count - 1)
    return ((offsets > 0) * half_count + np.where(distance < exact_count, distance, scaled)).astype(
        np.int32
    )


def near_picks(bucket_count, sign):
    offsets = sign * (np.arange(4 * BLOCK) - (2 * BLOCK - 1))
    picks = (bucket_of(offsets, bucket_count)[:, None] == np.arange(bucket_count)[None, :]).astype(
        np.float32
    )
    picks[-1] = 0.0
    return picks


def dot_nn(left, right):
    return lax.dot_general(left, right, (((1,), (0,)), ((), ())), preferred_element_type=F32)


def dot_nt(left, right):
    return lax.dot_general(left, right, (((1,), (1,)), ((), ())), preferred_element_type=F32)


def dot_tn(left, right):
    return lax.dot_general(left, right, (((0,), (0,)), ((), ())), preferred_element_type=F32)


def inverse_rms(values):
    return lax.rsqrt(jnp.mean(values * values, axis=-1, keepdims=True) + EPSILON)


def norm_backward(values, inverse, gain, grad_normed):
    scaled = grad_normed * gain
    grad_gain = jnp.sum(grad_normed * values * inverse, axis=0, keepdims=True)
    inner = jnp.mean(scaled * values, axis=-1, keepdims=True)
    return (inverse * (scaled - values * inverse * inverse * inner), grad_gain)


def softmax_lanes(logits):
    peak = jnp.max(logits, axis=-1, keepdims=True)
    exponent = jnp.exp(logits - peak)
    return exponent / jnp.sum(exponent, axis=-1, keepdims=True)


def toeplitz_near(near_row):
    spread = jnp.broadcast_to(near_row, (BLOCK, 4 * BLOCK))
    return pltpu.roll(spread, 3 * BLOCK + 1, 1, stride=1, stride_axis=0)[:, : 3 * BLOCK]


def bias_rows(near, far_low, far_high, row, blocks):
    pieces = []
    for column in range(blocks):
        distance = column - row
        if distance <= -2:
            pieces.append(jnp.full((BLOCK, BLOCK), far_low, F32))
        elif distance >= 2:
            pieces.append(jnp.full((BLOCK, BLOCK), far_high, F32))
        else:
            pieces.append(near[:, (distance + 1) * BLOCK : (distance + 2) * BLOCK])
    return jnp.concatenate(pieces, axis=1)


def diagonal_sums(near_sum):
    padded = jnp.concatenate([near_sum, jnp.zeros((BLOCK, BLOCK), F32)], axis=1)
    groups = jnp.zeros((8, 4 * BLOCK), F32)
    for at in range(0, BLOCK, 8):
        groups = groups + pltpu.roll(padded[at : at + 8, :], BLOCK - 8 - at, 1)
    sums = groups[7:8, :]
    for at in range(7):
        sums = sums + pltpu.roll(groups[at : at + 1, :], 7 - at, 1)
    return sums


def slot_places(routes_ref, row_ref, limit, experts, slots, count):
    lower = lax.broadcasted_iota(jnp.int32, (count, count), 0)
    upper = lax.broadcasted_iota(jnp.int32, (count, count), 1)
    col = routes_ref[...]
    chosen = lax.broadcasted_iota(jnp.int32, (count, experts), 1) == col
    running = dot_nn((upper <= lower).astype(BF16), chosen.astype(BF16))
    place = jnp.sum(jnp.where(chosen, running, 0.0), axis=1, keepdims=True).astype(jnp.int32) - 1
    slot_col = jnp.where(place < limit, col * slots + place, -1)
    row = row_ref[...]
    chosen_t = lax.broadcasted_iota(jnp.int32, (experts, count), 0) == row
    running_t = dot_nn(chosen_t.astype(BF16), (lower <= upper).astype(BF16))
    place_t = (
        jnp.sum(jnp.where(chosen_t, running_t, 0.0), axis=0, keepdims=True).astype(jnp.int32) - 1
    )
    slot_row = jnp.where(place_t < limit, row * slots + place_t, -1)
    return slot_col, slot_row


def place_kernel(slots, experts, capacity_ref, routes_ref, row_ref, cot_ref, slot_col, slot_row, cot_out):
    count = routes_ref.shape[0]
    limit = capacity_ref[0] * count // experts
    col, row = slot_places(routes_ref, row_ref, limit, experts, slots, count)
    slot_col[...] = col
    slot_row[...] = row
    picks = (lax.broadcasted_iota(jnp.int32, (experts * slots, count), 0) == row).astype(BF16)
    cot_out[...] = dot_nn(picks, cot_ref[...]).astype(BF16)


def forward_kernel(
    rel_ref, x_ref, w_ref, gain_a, gain_f, router_ref, near_ref, slot_row,
    normed_ref, q_ref, k_ref, v_ref, att_ref, lse_ref, mixed_ref, normed_f, sent_ref,
):
    count, width = x_ref.shape
    head_dim = width // HEADS
    blocks = count // BLOCK
    bucket_count = rel_ref.shape[0]
    tokens = x_ref[...].astype(F32)
    normed = (tokens * inverse_rms(tokens) * gain_a[...]).astype(BF16)
    normed_ref[...] = normed
    for out, at in ((q_ref, 0), (k_ref, 1), (v_ref, 2)):
        out[...] = dot_nn(normed, w_ref[:, at * width : (at + 1) * width]).astype(BF16)
    lse_ref[...] = jnp.zeros_like(lse_ref)
    first = lax.broadcasted_iota(jnp.int32, (1, BLOCK), 1) < head_dim
    lanes = lax.broadcasted_iota(jnp.int32, (1, BLOCK), 1)

    def pair(at, carry):
        cols = pl.ds(pl.multiple_of(at * BLOCK, BLOCK), BLOCK)
        k_pair, v_pair = k_ref[:, cols], v_ref[:, cols]
        nears = [toeplitz_near(near_ref[pl.ds(2 * at + half, 1), :]) for half in range(2)]
        for row in range(blocks):
            rows = slice(row * BLOCK, (row + 1) * BLOCK)
            q_rows = q_ref[rows, cols] * jnp.asarray(head_dim**-0.5, BF16)
            found = []
            log_sums = lse_ref[rows, :]
            for half in range(2):
                head = 2 * at + half
                low, high = rel_ref[bucket_count // 2 - 1, head], rel_ref[bucket_count - 1, head]
                mask = first if half == 0 else jnp.logical_not(first)
                scores = dot_nt(jnp.where(mask, q_rows, jnp.zeros_like(q_rows)), k_pair)
                scores = scores + bias_rows(nears[half], low, high, row, blocks)
                peak = jnp.max(scores, axis=-1, keepdims=True)
                exponent = jnp.exp(scores - peak)
                total = jnp.sum(exponent, axis=-1, keepdims=True)
                found.append(dot_nn((exponent * (1.0 / total)).astype(BF16), v_pair))
                log_sums = jnp.where(lanes == head, peak + jnp.log(total), log_sums)
            lse_ref[rows, :] = log_sums
            att_ref[rows, cols] = jnp.where(first, found[0], found[1]).astype(BF16)
        return carry

    lax.fori_loop(0, HEADS // 2, pair, 0)
    mixed = tokens + dot_nn(att_ref[...], w_ref[:, 3 * width : 4 * width])
    mixed_ref[...] = mixed
    normed_2 = (mixed * inverse_rms(mixed) * gain_f[...]).astype(BF16)
    normed_f[...] = normed_2
    total_slots = sent_ref.shape[0]
    picks = (lax.broadcasted_iota(jnp.int32, (total_slots, count), 0) == slot_row[...]).astype(BF16)
    sent_ref[...] = dot_nn(picks, normed_2).astype(BF16)


def expert_kernel(
    first_ref, rows_ref, cot_ref, in_ref, out_ref, router_ref,
    back_ref, grows_ref, gin_ref, gout_ref, hidden_ref, gpre_ref, sg_ref,
):
    sources, _, slots, width = rows_ref.shape
    total = sources * slots
    step = min(256, total)
    expert = first_ref[0] + pl.program_id(0)

    def chunk(at, carry):
        these = pl.ds(pl.multiple_of(at * (step // slots), step // slots), step // slots)
        flat = pl.ds(pl.multiple_of(at * step, step), step)
        rows = rows_ref[these, 0].reshape(step, width)
        probs = softmax_lanes(dot_nn(rows, router_ref[...]))
        here = lax.broadcasted_iota(jnp.int32, probs.shape, 1) == expert
        gate = jnp.sum(jnp.where(here, probs, 0.0), axis=-1, keepdims=True)
        sg = (cot_ref[these, 0].reshape(step, width).astype(F32) * gate).astype(BF16)
        sg_ref[flat, :] = sg
        pre = dot_nn(rows, in_ref[0])
        square = pre * pre
        inner = jnp.tanh(pre * (ROOT_TWO_PI + ROOT_TWO_PI * CUBIC * square))
        half = 0.5 * (1.0 + inner)
        hidden = (pre * half).astype(BF16)
        hidden_ref[flat, :] = hidden
        slope = half + 0.5 * pre * (1.0 - inner * inner) * (
            ROOT_TWO_PI + 3.0 * ROOT_TWO_PI * CUBIC * square
        )
        gpre = (dot_nt(sg, out_ref[0]) * slope).astype(BF16)
        gpre_ref[flat, :] = gpre
        back_ref[these, 0] = dot_nn(hidden, out_ref[0]).astype(BF16).reshape(-1, slots, width)
        grows_ref[these, 0] = dot_nt(gpre, in_ref[0]).astype(BF16).reshape(-1, slots, width)
        return carry

    lax.fori_loop(0, total // step, chunk, 0)
    gout_ref[0] = dot_tn(hidden_ref[...], sg_ref[...])
    gin_ref[0] = dot_tn(rows_ref[:, 0].reshape(total, width), gpre_ref[...])


def remote(source, target, send, receive, device):
    return pltpu.make_async_remote_copy(
        src_ref=source,
        dst_ref=target,
        send_sem=send,
        recv_sem=receive,
        device_id=device,
        device_id_type=pl.DeviceIdType.MESH,
    )


def greet(devices):
    barrier = pltpu.get_barrier_semaphore()
    for device in devices:
        pl.semaphore_signal(barrier, inc=1, device_id=device, device_id_type=pl.DeviceIdType.MESH)
    pl.semaphore_wait(barrier, len(devices))


class Place:
    def __init__(self, wide):
        self.wide = wide
        self.w, self.n = lax.axis_index("wide"), lax.axis_index("narrow")
        self.x, self.c = self.n // 2, lax.rem(self.n, 2)
        self.core = (self.w, self.x * 2 + 1 - self.c)
        self.side = (self.w, (1 - self.x) * 2 + self.c)
        self.deep = wide // 2
        self.z, self.y = self.w // 2, lax.rem(self.w, 2)
        self.row = (self.z * 2 + 1 - self.y, self.n)

    def at(self, step):
        return lax.rem(self.w + step, self.wide)

    def peer(self, step):
        return (self.at(step), self.n)

    def partners(self):
        return [self.peer(k) for k in range(1, self.wide)] + [self.core, self.side]


class Spread:
    def __init__(self, place, sent, held, wide_s, wide_r, side_s, side_r, core_s, core_r):
        self.place, self.sent, self.held = place, sent, held
        self.wide_s, self.wide_r, self.side_s, self.side_r = wide_s, wide_r, side_s, side_r
        self.core_s, self.core_r = core_s, core_r

    def hop(self, e, k):
        p = self.place
        return remote(
            self.sent.at[p.at(k), e], self.held.at[e, p.n, p.w], self.wide_s.at[e, k], self.wide_r.at[e, k], p.peer(k)
        )

    def start(self, e):
        for k in range(1, self.place.wide):
            self.hop(e, k).start()

    def half(self, e, h):
        p = self.place
        run = p.wide // 2
        rows = self.held.at[e, p.n, pl.ds(h * run, run)]
        return remote(rows, rows, self.side_s.at[e, h], self.side_r.at[e, h], p.side)

    def over(self, e, far):
        p = self.place
        m = (1 - p.x) * 2 + p.c if far else p.n
        return remote(
            self.held.at[e, m], self.held.at[e, m], self.core_s.at[e, far], self.core_r.at[e, far], p.core
        )

    def forward(self, e):
        p = self.place
        run = p.wide // 2
        for other in range(2):
            h = p.w // run
            h = 1 - h if other else h
            for k in range(1, p.wide):
                mine = (p.at(p.wide - k) // run) == h

                @pl.when(mine)
                def _():
                    self.hop(e, k).wait_recv()

            self.half(e, h).start()
        self.over(e, 0).start()

    def pass_on(self, e):
        for h in range(2):
            self.half(e, h).wait_recv()
        self.over(e, 1).start()

    def arrive(self, e):
        self.over(e, 0).wait_recv()
        self.over(e, 1).wait_recv()

    def drain(self, e):
        for k in range(1, self.place.wide):
            self.hop(e, k).wait_send()
        for h in range(2):
            self.half(e, h).wait_send()
            self.over(e, h).wait_send()


def moving_expert_kernel(
    sent, cot_hbm, in_hbm, out_hbm, router_ref,
    rows_o, sg_o, hidden_o, gpre_o, outs_o, back_o, gate_o,
    held, cot, w_in, w_out, sg, hidden, gpre, outs, to_core, from_core, to_side, from_side, near_sum, ready,
    gate_sum, gate_core, gate_from_core, gate_side, gate_from_side, gate_ready,
    load_s, store_s, wide_s, wide_r, side_s, side_r, core_s, core_r,
    rc_s, rc_r, rx_s, rx_r, rw_s, rw_r, gc_s, gc_r, gx_s, gx_r, gw_s, gw_r,
):
    wide, local, slots, width = sent.shape
    narrow = held.shape[1]
    step = wide * slots
    p = Place(wide)
    moves = Spread(p, sent, held, wide_s, wide_r, side_s, side_r, core_s, core_r)
    greet(p.partners())
    for e in range(local):
        moves.start(e)

    def loads(e):
        return [
            pltpu.make_async_copy(in_hbm.at[e], w_in.at[e], load_s.at[e, 0]),
            pltpu.make_async_copy(out_hbm.at[e], w_out.at[e], load_s.at[e, 1]),
            pltpu.make_async_copy(cot_hbm.at[e], cot.at[e], load_s.at[e, 2]),
        ]

    def stores(e):
        b = lax.rem(e, 2)
        return [
            pltpu.make_async_copy(held.at[e], rows_o.at[e], store_s.at[e, 0]),
            pltpu.make_async_copy(sg.at[b], sg_o.at[e], store_s.at[e, 1]),
            pltpu.make_async_copy(hidden.at[b], hidden_o.at[e], store_s.at[e, 2]),
            pltpu.make_async_copy(gpre.at[b], gpre_o.at[e], store_s.at[e, 3]),
            pltpu.make_async_copy(outs.at[b], outs_o.at[e], store_s.at[e, 4]),
        ]

    for e in range(local):
        for copy in loads(e):
            copy.start()
        held[e, p.n, p.w] = sent[p.w, e]
    gate_sum[...] = jnp.zeros_like(gate_sum)
    moves.forward(0)
    moves.pass_on(0)

    def chunk(e, m):
        b = lax.rem(e, 2)
        rows = held[e, m].reshape(step, width)
        probs = softmax_lanes(dot_nn(rows, router_ref[...]))
        here = lax.broadcasted_iota(jnp.int32, probs.shape, 1) == p.w * local + e
        gate = jnp.sum(jnp.where(here, probs, 0.0), axis=-1, keepdims=True)
        cot_rows = cot[e, m].reshape(step, width).astype(F32)
        sg_rows = (cot_rows * gate).astype(BF16)
        sg[b, m] = sg_rows
        pre = dot_nn(rows, w_in[e])
        square = pre * pre
        inner = jnp.tanh(pre * (ROOT_TWO_PI + ROOT_TWO_PI * CUBIC * square))
        half = 0.5 * (1.0 + inner)
        hidden_rows = (pre * half).astype(BF16)
        hidden[b, m] = hidden_rows
        slope = half + 0.5 * pre * (1.0 - inner * inner) * (
            ROOT_TWO_PI + 3.0 * ROOT_TWO_PI * CUBIC * square
        )
        gpre_rows = (dot_nt(sg_rows, w_out[e]) * slope).astype(BF16)
        gpre[b, m] = gpre_rows
        out_rows = dot_nn(hidden_rows, w_out[e])
        outs[b, m] = out_rows.astype(BF16)
        gate_rows = jnp.sum(out_rows * cot_rows, axis=-1, keepdims=True)
        row = lax.broadcasted_iota(jnp.int32, (step, local * slots), 0)
        lane = lax.broadcasted_iota(jnp.int32, (step, local * slots), 1)
        spread = jnp.where(lane == e * slots + lax.rem(row, slots), gate_rows, 0.0)
        gate_sum[m] += jnp.sum(spread.reshape(wide, slots, local * slots), axis=1)
        return dot_nt(gpre_rows, w_in[e])

    def core_copy(e, far):
        return remote(to_core.at[e, far], from_core.at[e, far], rc_s.at[e, far], rc_r.at[e, far], p.core)

    def side_copy(e):
        return remote(to_side.at[e], from_side.at[e], rx_s.at[e], rx_r.at[e], p.side)

    def back_copy(e, k):
        return remote(ready.at[e, p.at(k)], back_o.at[p.w, e], rw_s.at[e, k], rw_r.at[e, k], p.peer(k))

    def finish(e):
        side_copy(e).wait_recv()
        ready[e] = (near_sum[...] + from_side[e].astype(F32)).astype(BF16).reshape(wide, slots, width)
        for k in range(1, wide):
            back_copy(e, k).start()
        back_o[p.w, e] = ready[e, p.w]

    far_x = (1 - p.x) * 2

    def expert(e, carry):
        for copy in loads(e):
            copy.wait()

        @pl.when(e >= 2)
        def _():
            for copy in stores(e - 2)[1:]:
                copy.wait()

        moves.arrive(e)
        to_core[e, 1] = chunk(e, far_x + 1 - p.c).astype(BF16)
        core_copy(e, 1).start()

        @pl.when(e + 1 < local)
        def _():
            moves.forward(e + 1)

        far_part = chunk(e, far_x + p.c)
        core_copy(e, 1).wait_recv()
        to_side[e] = (far_part + from_core[e, 1].astype(F32)).astype(BF16)
        side_copy(e).start()

        @pl.when(e > 0)
        def _():
            finish(e - 1)

        to_core[e, 0] = chunk(e, p.x * 2 + 1 - p.c).astype(BF16)
        core_copy(e, 0).start()

        @pl.when(e + 1 < local)
        def _():
            moves.pass_on(e + 1)

        near_part = chunk(e, p.n)
        core_copy(e, 0).wait_recv()
        near_sum[...] = near_part + from_core[e, 0].astype(F32)
        for copy in stores(e):
            copy.start()
        return carry

    lax.fori_loop(0, local, expert, 0)
    gate_core[0] = gate_sum[p.x * 2 + 1 - p.c]
    gate_core[1] = gate_sum[far_x + 1 - p.c]
    gates_core = remote(gate_core, gate_from_core, gc_s, gc_r, p.core)
    gates_core.start()
    gates_core.wait_recv()
    gate_side[...] = gate_sum[far_x + p.c] + gate_from_core[1]
    gates_side = remote(gate_side, gate_from_side, gx_s, gx_r, p.side)
    gates_side.start()
    finish(local - 1)
    gates_side.wait_recv()
    gates = gate_sum[p.n] + gate_from_core[0] + gate_from_side[...]
    for v in range(wide):
        gate_ready[v] = gates[v : v + 1, :]
    gates_wide = [
        remote(gate_ready.at[p.at(k)], gate_o.at[p.w], gw_s.at[k], gw_r.at[k], p.peer(k)) for k in range(1, wide)
    ]
    for copy in gates_wide:
        copy.start()
    gate_o[p.w] = gate_ready[p.w]
    gates_core.wait_send()
    gates_side.wait_send()

    def drain(e, carry):
        moves.drain(e)
        core_copy(e, 0).wait_send()
        core_copy(e, 1).wait_send()
        side_copy(e).wait_send()
        stores(e)[0].wait()

        @pl.when(e >= local - 2)
        def _():
            for copy in stores(e)[1:]:
                copy.wait()

        for k in range(1, wide):
            back_copy(e, k).wait()
        return carry

    lax.fori_loop(0, local, drain, 0)
    for copy in gates_wide:
        copy.wait()


def weight_grad_kernel(rows_ref, sg_ref, hidden_ref, gpre_ref, gin_ref, gout_ref):
    gout_ref[0] = dot_tn(hidden_ref[0], sg_ref[0])
    gin_ref[0] = dot_tn(rows_ref[0], gpre_ref[0])


def moving_experts(sent, cot_all, expert_in, expert_out, router, wide, narrow):
    _, local, slots, width = sent.shape
    hidden_width = expert_in.shape[2]
    step = wide * slots
    sds = jax.ShapeDtypeStruct
    any_spec, vmem_spec = pl.BlockSpec(memory_space=pl.ANY), pl.BlockSpec(memory_space=pltpu.VMEM)
    dma = pltpu.SemaphoreType.DMA
    rows, sg, hidden, gpre, outs, back, gates = pl.pallas_call(
        moving_expert_kernel,
        out_shape=(
            sds((local, narrow, wide, slots, width), BF16),
            sds((local, narrow, step, width), BF16),
            sds((local, narrow, step, hidden_width), BF16),
            sds((local, narrow, step, hidden_width), BF16),
            sds((local, narrow, step, width), BF16),
            sds((wide, local, slots, width), BF16),
            sds((wide, 1, local * slots), F32),
        ),
        in_specs=[vmem_spec, any_spec, any_spec, any_spec, vmem_spec],
        out_specs=(any_spec,) * 5 + (vmem_spec,) * 2,
        scratch_shapes=[
            pltpu.VMEM((local, narrow, wide, slots, width), BF16),
            pltpu.VMEM((local, narrow, wide, slots, width), BF16),
            pltpu.VMEM(expert_in.shape, BF16),
            pltpu.VMEM(expert_out.shape, BF16),
            pltpu.VMEM((2, narrow, step, width), BF16),
            pltpu.VMEM((2, narrow, step, hidden_width), BF16),
            pltpu.VMEM((2, narrow, step, hidden_width), BF16),
            pltpu.VMEM((2, narrow, step, width), BF16),
            pltpu.VMEM((local, 2, step, width), BF16),
            pltpu.VMEM((local, 2, step, width), BF16),
            pltpu.VMEM((local, step, width), BF16),
            pltpu.VMEM((local, step, width), BF16),
            pltpu.VMEM((step, width), F32),
            pltpu.VMEM((local, wide, slots, width), BF16),
            pltpu.VMEM((narrow, wide, local * slots), F32),
            pltpu.VMEM((2, wide, local * slots), F32),
            pltpu.VMEM((2, wide, local * slots), F32),
            pltpu.VMEM((wide, local * slots), F32),
            pltpu.VMEM((wide, local * slots), F32),
            pltpu.VMEM((wide, 1, local * slots), F32),
            dma((local, 3)), dma((local, 5)), dma((local, wide)), dma((local, wide)),
            dma((local, 2)), dma((local, 2)), dma((local, 2)), dma((local, 2)),
            dma((local, 2)), dma((local, 2)), dma((local,)), dma((local,)), dma((local, wide)), dma((local, wide)),
            dma, dma, dma, dma, dma((wide,)), dma((wide,)),
        ],
        compiler_params=pltpu.CompilerParams(
            collective_id=2, has_side_effects=True, vmem_limit_bytes=62 << 20
        ),
        name="experts",
    )(sent, cot_all, expert_in, expert_out, router)
    total = narrow * step
    spec = lambda cols: pl.BlockSpec((1, total, cols), lambda e: (e, 0, 0))
    gin, gout = pl.pallas_call(
        weight_grad_kernel,
        grid=(local,),
        out_shape=(sds(expert_in.shape, F32), sds(expert_out.shape, F32)),
        in_specs=[spec(width), spec(width), spec(hidden_width), spec(hidden_width)],
        out_specs=(
            pl.BlockSpec((1, width, hidden_width), lambda e: (e, 0, 0)),
            pl.BlockSpec((1, hidden_width, width), lambda e: (e, 0, 0)),
        ),
        compiler_params=pltpu.CompilerParams(vmem_limit_bytes=60 << 20),
        name="weight_grads",
    )(
        rows.reshape(local, total, width), sg.reshape(local, total, width),
        hidden.reshape(local, total, hidden_width), gpre.reshape(local, total, hidden_width),
    )
    return outs, back, gates, gin, gout


def routed_gate(normed_f, router_ref, routes_ref):
    probs = softmax_lanes(dot_nn(normed_f[...], router_ref[...]))
    chosen = lax.broadcasted_iota(jnp.int32, probs.shape, 1) == routes_ref[...]
    return probs, chosen, jnp.sum(jnp.where(chosen, probs, 0.0), axis=-1, keepdims=True)


def slot_owners(slot_col, total):
    return lax.broadcasted_iota(jnp.int32, (slot_col.shape[0], total), 1) == slot_col[...]


def ffn_backward(probs, chosen, gate, owned, gates_ref, normed_f, router_ref, grows_ref, mixed, cot_ref, gain_f):
    grad_gate = jnp.sum(jnp.where(owned, gates_ref[...], 0.0), axis=-1, keepdims=True)
    grad_logits = (probs * (jnp.where(chosen, grad_gate, 0.0) - gate * grad_gate)).astype(BF16)
    grad_router = dot_tn(normed_f[...], grad_logits)
    grad_normed = dot_nt(grad_logits, router_ref[...]) + dot_nn(owned.astype(BF16), grows_ref[...])
    grad_norm, grad_gain = norm_backward(mixed, inverse_rms(mixed), gain_f[...], grad_normed)
    return grad_router, cot_ref[...].astype(F32) + grad_norm, grad_gain


def attention_setup(q_ref, k_ref, normed_ref, att_ref, lse_ref, datt, q_t, k_t, normed_t, datt_t, delta, lse_t):
    count, width = q_ref.shape
    head_dim = width // HEADS
    datt_t[...] = datt[...].T
    q_t[...] = (q_ref[...] * jnp.asarray(head_dim**-0.5, BF16)).T
    k_t[...] = k_ref[...].T
    normed_t[...] = normed_ref[...].T
    products = datt_t[...].astype(F32) * att_ref[...].T.astype(F32)
    delta[...] = jnp.sum(products.reshape(HEADS, head_dim, count), axis=1)
    lse_t[...] = lse_ref[...].T


def pair_backward(
    at, rel_ref, near_ref, q_ref, k_ref, v_ref, q_t, k_t, datt, datt_t, delta, lse_t, dst, gq, gk, gv, gnear_ref, gfar_ref
):
    count, width = q_ref.shape
    head_dim = width // HEADS
    blocks = count // BLOCK
    bucket_count = rel_ref.shape[0]
    first = lax.broadcasted_iota(jnp.int32, (1, BLOCK), 1) < head_dim
    cols = pl.ds(pl.multiple_of(at * BLOCK, BLOCK), BLOCK)
    q_pair, datt_pair = q_ref[:, cols], datt[:, cols]
    gq_parts, gk_parts, gv_parts = [], [], []
    for half in range(2):
        head = 2 * at + half
        low, high = rel_ref[bucket_count // 2 - 1, head], rel_ref[bucket_count - 1, head]
        mask = first if half == 0 else jnp.logical_not(first)
        near = toeplitz_near(near_ref[pl.ds(head, 1), :])
        lse_row, delta_row = lse_t[pl.ds(head, 1), :], delta[pl.ds(head, 1), :]
        near_sum = jnp.zeros((BLOCK, 3 * BLOCK), F32)
        low_sum, high_sum = jnp.zeros((BLOCK, BLOCK), F32), jnp.zeros((BLOCK, BLOCK), F32)
        gk_rows, gv_rows = [], []
        for row in range(blocks):
            rows = slice(row * BLOCK, (row + 1) * BLOCK)
            k_rows, v_rows = k_ref[rows, cols], v_ref[rows, cols]
            zeros = jnp.zeros_like(k_rows)
            scores = dot_nn(jnp.where(mask, k_rows, zeros), q_t[cols, :])
            scores = scores + bias_rows(near, high, low, row, blocks)
            weights = jnp.exp(scores - lse_row)
            grad_weights = dot_nn(jnp.where(mask, v_rows, zeros), datt_t[cols, :])
            grad_scores = weights * (grad_weights - delta_row)
            gv_rows.append(dot_nn(weights.astype(BF16), datt_pair))
            low_bits = grad_scores.astype(BF16)
            dst[rows, :] = low_bits
            gk_rows.append(dot_nn(low_bits, q_pair))
            for column in range(blocks):
                piece = grad_scores[:, column * BLOCK : (column + 1) * BLOCK]
                distance = column - row
                if distance <= -2:
                    high_sum = high_sum + piece
                elif distance >= 2:
                    low_sum = low_sum + piece
                else:
                    pads = [jnp.zeros((BLOCK, BLOCK), F32)] * 3
                    pads[distance + 1] = piece
                    near_sum = near_sum + jnp.concatenate(pads, axis=1)
        gq_parts.append(
            dot_nn(k_t[pl.ds(pl.multiple_of(head * head_dim, head_dim), head_dim), :], dst[...])
        )
        gk_parts.append(jnp.concatenate(gk_rows, axis=0))
        gv_parts.append(jnp.concatenate(gv_rows, axis=0))
        gnear_ref[pl.ds(head, 1), :] = diagonal_sums(near_sum)
        gfar_ref[pl.ds(head, 1), :] = jnp.concatenate(
            [jnp.sum(low_sum, axis=0, keepdims=True), jnp.sum(high_sum, axis=0, keepdims=True)], axis=1
        )
    scale = head_dim**-0.5
    gq[:, cols] = (jnp.concatenate(gq_parts, axis=0).T * scale).astype(BF16)
    gk[:, cols] = (jnp.where(first, gk_parts[0], gk_parts[1]) * scale).astype(BF16)
    gv[:, cols] = jnp.where(first, gv_parts[0], gv_parts[1]).astype(BF16)


def input_backward(x_ref, w_ref, gain_a, gmixed, gq, gk, gv):
    count, width = x_ref.shape
    grad_normed = jnp.zeros((count, width), F32)
    for at, grad in enumerate((gq, gk, gv)):
        grad_normed = grad_normed + dot_nt(grad[...], w_ref[:, at * width : (at + 1) * width])
    tokens = x_ref[...].astype(F32)
    grad_norm, grad_gain = norm_backward(tokens, inverse_rms(tokens), gain_a[...], grad_normed)
    return gmixed[...] + grad_norm, grad_gain


def backward_kernel(
    rel_ref, x_ref, w_ref, gain_a, gain_f, router_ref, near_ref, slot_col, routes_ref,
    normed_ref, q_ref, k_ref, v_ref, att_ref, lse_ref, mixed_ref, normed_f, cot_ref, outs_ref, grows_ref, gates_ref,
    result_ref, gx_ref, gw_ref, grouter_ref, gnear_ref, gfar_ref, ggain_ref,
    q_t, k_t, normed_t, datt, datt_t, delta, lse_t, gq, gk, gv, gmixed, dst,
):
    width = x_ref.shape[1]
    probs, chosen, gate = routed_gate(normed_f, router_ref, routes_ref)
    owned = slot_owners(slot_col, outs_ref.shape[0])
    mixed = mixed_ref[...]
    result_ref[...] = (mixed + gate * dot_nn(owned.astype(BF16), outs_ref[...])).astype(BF16)
    grouter_ref[...], grad_mixed, ggain_ref[1:2, :] = ffn_backward(
        probs, chosen, gate, owned, gates_ref, normed_f, router_ref, grows_ref, mixed, cot_ref, gain_f
    )
    gmixed[...] = grad_mixed
    branch = grad_mixed.astype(BF16)
    gw_ref[:, 3 * width : 4 * width] = dot_tn(att_ref[...], branch).astype(BF16)
    datt[...] = dot_nt(branch, w_ref[:, 3 * width : 4 * width]).astype(BF16)
    attention_setup(q_ref, k_ref, normed_ref, att_ref, lse_ref, datt, q_t, k_t, normed_t, datt_t, delta, lse_t)

    def pair(at, carry):
        pair_backward(
            at, rel_ref, near_ref, q_ref, k_ref, v_ref, q_t, k_t, datt, datt_t, delta, lse_t, dst, gq, gk, gv,
            gnear_ref, gfar_ref,
        )
        return carry

    lax.fori_loop(0, HEADS // 2, pair, 0)
    for at, grad in enumerate((gq, gk, gv)):
        gw_ref[:, at * width : (at + 1) * width] = dot_nn(normed_t[...], grad[...]).astype(BF16)
    gx_ref[...], ggain_ref[0:1, :] = input_backward(x_ref, w_ref, gain_a, gmixed, gq, gk, gv)


class Sums:
    def __init__(self, place, unit, buffers, semaphores, out):
        self.p, self.unit, self.out = place, unit, out
        self.send, self.core, self.kept, self.from_y, self.over_x, self.from_x, self.over_z, self.from_z, self.last = buffers
        self.s, self.r = semaphores
        self.deep = self.send.shape[1]

    def to_core(self):
        u, p = self.unit, self.p
        return remote(self.send.at[u], self.core.at[u], self.s.at[u, 0], self.r.at[u, 0], p.core)

    def to_y(self):
        u, p = self.unit, self.p
        return remote(self.kept.at[u, 1 - p.y], self.from_y.at[u], self.s.at[u, 1], self.r.at[u, 1], p.row)

    def to_x(self):
        u, p = self.unit, self.p
        return remote(self.over_x.at[u, 1 - p.x], self.from_x.at[u], self.s.at[u, 2], self.r.at[u, 2], p.side)

    def to_z(self, k):
        u, p = self.unit, self.p
        z = lax.rem(p.z + k, p.deep)
        return remote(
            self.over_z.at[u, z], self.from_z.at[u, k], self.s.at[u, 3 + k], self.r.at[u, 3 + k], (z * 2 + p.y, p.n)
        )

    def to_last(self):
        u, p = self.unit, self.p
        return remote(self.last.at[u, 1 - p.c], self.out.at[u, p.c], self.s.at[u, 3], self.r.at[u, 3], p.core)

    def begin(self, part):
        self.send[self.unit] = part.astype(BF16).reshape(self.send.shape[1:])
        self.to_core().start()

    def stage_core(self, part):
        u = self.unit
        self.to_core().wait_recv()
        kept = part.reshape(self.core.shape[1:]) + self.core[u].astype(F32)
        self.kept[u] = kept.astype(BF16)
        self.to_y().start()

    def stage_y(self):
        u = self.unit
        self.to_y().wait_recv()
        self.over_x[u] = (self.kept[u, self.p.y].astype(F32) + self.from_y[u].astype(F32)).astype(BF16)
        self.to_x().start()

    def stage_x(self):
        u = self.unit
        self.to_x().wait_recv()
        self.over_z[u] = (self.over_x[u, self.p.x].astype(F32) + self.from_x[u].astype(F32)).astype(BF16)
        for k in range(1, self.p.deep):
            self.to_z(k).start()

    def stage_z(self):
        u = self.unit
        total = self.over_z[u, self.p.z].astype(F32)
        for k in range(1, self.p.deep):
            self.to_z(k).wait_recv()
            total = total + self.from_z[u, k].astype(F32)
        self.last[u] = total.reshape(self.last.shape[1:])
        self.to_last().start()
        self.out[u, self.p.c] = self.last[u, self.p.c]

    def drain(self):
        for copy in (self.to_core(), self.to_y(), self.to_x()):
            copy.wait_send()
        for k in range(1, self.p.deep):
            self.to_z(k).wait_send()
        self.to_last().wait()


def sum_buffers(units, wide, rows, cols):
    deep = wide // 2
    vmem = lambda *shape, dtype=BF16: pltpu.VMEM((units, *shape), dtype)
    return [
        vmem(2, 2, deep, rows, cols), vmem(2, 2, deep, rows, cols), vmem(2, 2, deep, rows, cols),
        vmem(2, deep, rows, cols), vmem(2, deep, rows, cols), vmem(deep, rows, cols), vmem(deep, rows, cols),
        vmem(deep, rows, cols), vmem(2, rows // 2, cols, dtype=F32),
        pltpu.SemaphoreType.DMA((units, 3 + deep)), pltpu.SemaphoreType.DMA((units, 3 + deep)),
    ]


def moving_backward_kernel(
    rel_ref, x_ref, w_ref, gain_a, gain_f, router_ref, near_ref, slot_col, routes_ref,
    normed_ref, q_ref, k_ref, v_ref, att_ref, lse_ref, mixed_ref, normed_f, cot_ref, outs_hbm, grows_ref, gates_ref, picks_ref,
    result_ref, gx_ref, gw_out, go_out, small_out,
    q_t, k_t, normed_t, datt, datt_t, delta, lse_t, gq, gk, gv, gmixed, dst, gnear, gfar,
    own, from_core, to_side, from_side, near_sum, ready, returned, own_s, rc_s, rc_r, rx_s, rx_r, rw_s, rw_r,
    u1, u2, u3, u4, u5, u6, u7, u8, u9, us, ur, o1, o2, o3, o4, o5, o6, o7, o8, o9, os, orr,
    small, small_in, ss, sr,
):
    count, width = x_ref.shape
    local, _, step, _ = outs_hbm.shape
    wide, _, slots, _ = returned.shape
    total = wide * local * slots
    p = Place(wide)
    far_x = (1 - p.x) * 2
    greet(p.partners())

    def core_copy(e, far):
        m = (far_x if far else p.x * 2) + 1 - p.c
        return remote(outs_hbm.at[e, m], from_core.at[e, far], rc_s.at[e, far], rc_r.at[e, far], p.core)

    def own_copy(e, far):
        m = (far_x if far else p.x * 2) + p.c
        return pltpu.make_async_copy(outs_hbm.at[e, m], own.at[e, far], own_s.at[e, far])

    def side_copy(e):
        return remote(to_side.at[e], from_side.at[e], rx_s.at[e], rx_r.at[e], p.side)

    def back_copy(e, k):
        return remote(ready.at[e, p.at(k)], returned.at[p.w, e], rw_s.at[e, k], rw_r.at[e, k], p.peer(k))

    for far in (1, 0):
        for e in range(local):
            core_copy(e, far).start()
            own_copy(e, far).start()

    def over_side(e):
        core_copy(e, 1).wait_recv()
        own_copy(e, 1).wait()
        to_side[e] = (own[e, 1].astype(F32) + from_core[e, 1].astype(F32)).astype(BF16)
        side_copy(e).start()

    def nearby(e):
        core_copy(e, 0).wait_recv()
        own_copy(e, 0).wait()
        near_sum[e] = own[e, 0].astype(F32) + from_core[e, 0].astype(F32)

    def finish(e):
        side_copy(e).wait_recv()
        ready[e] = (near_sum[e] + from_side[e].astype(F32)).astype(BF16).reshape(wide, slots, width)
        for k in range(1, wide):
            back_copy(e, k).start()
        returned[p.w, e] = ready[e, p.w]

    probs, chosen, gate = routed_gate(normed_f, router_ref, routes_ref)
    owned = slot_owners(slot_col, total)
    grad_router, grad_mixed, grad_gain_f = ffn_backward(
        probs, chosen, gate, owned, gates_ref, normed_f, router_ref, grows_ref, mixed_ref[...], cot_ref, gain_f
    )
    gmixed[...] = grad_mixed
    small[0] = jnp.zeros_like(small[0])
    small[0, HEADS : HEADS + 1, :] = grad_gain_f
    for e in range(local):
        over_side(e)
    branch = grad_mixed.astype(BF16)
    o_sums = Sums(p, 0, (o1, o2, o3, o4, o5, o6, o7, o8, o9), (os, orr), go_out)
    half_cols = width // 2
    router_cols = go_out.shape[-1] - half_cols
    router_wide = jnp.concatenate(
        [grad_router, jnp.zeros((width, router_cols - grad_router.shape[1]), F32)], axis=1
    )

    def output_part(core):
        low, high = branch[:, :half_cols], branch[:, half_cols:]
        part = dot_tn(att_ref[...], jnp.where(core == 0, low, high))
        return order_rows(jnp.concatenate([part, jnp.where(core == 0, router_wide, 0.0)], axis=1), p)

    o_sums.begin(output_part(1 - p.c))
    datt[...] = dot_nt(branch, w_ref[:, 3 * width : 4 * width]).astype(BF16)
    for e in range(local):
        nearby(e)
    o_sums.stage_core(output_part(p.c))
    attention_setup(q_ref, k_ref, normed_ref, att_ref, lse_ref, datt, q_t, k_t, normed_t, datt_t, delta, lse_t)

    def pair(at):
        pair_backward(
            at, rel_ref, near_ref, q_ref, k_ref, v_ref, q_t, k_t, datt, datt_t, delta, lse_t, dst, gq, gk, gv,
            gnear, gfar,
        )
        cols = pl.ds(pl.multiple_of(at * BLOCK, BLOCK), BLOCK)
        grads = jnp.concatenate([gq[:, cols], gk[:, cols], gv[:, cols]], axis=1)
        return order_rows(dot_nn(normed_t[...], grads), p)

    def unit(u):
        return Sums(p, u, (u1, u2, u3, u4, u5, u6, u7, u8, u9), (us, ur), gw_out)

    units = HEADS // 4

    def pairs(u, carry):
        unit(u).begin(pair(2 * u + 1 - p.c))

        @pl.when(u == 0)
        def _():
            o_sums.stage_y()

        @pl.when(u == 1)
        def _():
            o_sums.stage_z()

        @pl.when(u >= 1)
        def _():
            unit(u - 1).stage_y()
            finish(u - 1)

        @pl.when(u >= 2)
        def _():
            unit(u - 2).stage_z()

        unit(u).stage_core(pair(2 * u + p.c))

        @pl.when(u == 0)
        def _():
            o_sums.stage_x()

        @pl.when(u >= 1)
        def _():
            unit(u - 1).stage_x()

        return carry

    lax.fori_loop(0, units, pairs, 0)
    near_grads = jnp.dot(gnear[...], picks_ref[...], precision=HIGHEST, preferred_element_type=F32)
    buckets = lax.broadcasted_iota(jnp.int32, near_grads.shape, 1)
    low_sum = jnp.sum(gfar[:, :BLOCK], axis=1, keepdims=True)
    high_sum = jnp.sum(gfar[:, BLOCK:], axis=1, keepdims=True)
    bucket_count = rel_ref.shape[0]
    rel = near_grads + jnp.where(buckets == bucket_count // 2 - 1, low_sum, 0.0)
    small[0, :HEADS, :BLOCK] = rel + jnp.where(buckets == bucket_count - 1, high_sum, 0.0)
    gx_ref[...], grad_gain_a = input_backward(x_ref, w_ref, gain_a, gmixed, gq, gk, gv)
    small[0, HEADS + 1 : HEADS + 2, :] = grad_gain_a

    def small_copy(stage, device, slot):
        return remote(small.at[stage], small_in.at[slot], ss.at[slot], sr.at[slot], device)

    hops = [[p.core], [p.row], [p.side], [(lax.rem(p.z + k, p.deep) * 2 + p.y, p.n) for k in range(1, p.deep)]]
    copies, slot = [], 0
    for stage, devices in enumerate(hops):
        copies.append([small_copy(stage, device, slot + at) for at, device in enumerate(devices)])
        slot += len(devices)

    def small_start(stage):
        for copy in copies[stage]:
            copy.start()

    def small_end(stage):
        slot = sum(len(c) for c in copies[:stage])
        found = small[stage]
        for at, copy in enumerate(copies[stage]):
            copy.wait_recv()
            found = found + small_in[slot + at]
        return found

    small_start(0)
    last = unit(units - 1)
    last.stage_y()
    for e in range(units - 1, local):
        finish(e)
    small[1] = small_end(0)
    small_start(1)
    unit(units - 2).stage_z()
    last.stage_x()
    small[2] = small_end(1)
    small_start(2)
    small[3] = small_end(2)
    small_start(3)
    last.stage_z()
    small_out[...] = small_end(3)
    for e in range(local):
        for k in range(1, wide):
            back_copy(e, k).wait_recv()
    combined = dot_nn(owned.astype(BF16), returned[...].reshape(total, width))
    result_ref[...] = (mixed_ref[...] + gate * combined).astype(BF16)
    for e in range(local):
        core_copy(e, 0).wait_send()
        core_copy(e, 1).wait_send()
        side_copy(e).wait_send()
        for k in range(1, wide):
            back_copy(e, k).wait_send()
    o_sums.drain()
    for u in range(units):
        unit(u).drain()
    for stage in copies:
        for copy in stage:
            copy.wait_send()


def order_rows(part, place):
    width, cols = part.shape
    rows = width // (place.deep * 4)
    blocks = part.reshape(place.deep, 2, 2, rows, cols)
    return jnp.transpose(blocks, (1, 2, 0, 3, 4)).reshape(width, cols)


def moving_backward(
    rel_bias, inputs, weights, gain_a, gain_f, router, near, slot_col, routes,
    normed, q, k, v, att, lse, mixed, normed_f, cotangent, outs, grows, gates, wide, slots,
):
    count, width = inputs.shape
    local, narrow, step, _ = outs.shape
    experts = router.shape[1]
    bucket_count = rel_bias.shape[0]
    deep, rows = wide // 2, width // (wide * 2)
    units = HEADS // 4
    pair_cols, out_cols = 3 * BLOCK, width // 2 + BLOCK * -(-experts // BLOCK)
    sds = jax.ShapeDtypeStruct
    smem = pl.BlockSpec(memory_space=pltpu.SMEM)
    any_spec = pl.BlockSpec(memory_space=pl.ANY)
    picks = np.zeros((4 * BLOCK, BLOCK), np.float32)
    picks[:, :bucket_count] = near_picks(bucket_count, -1)
    wide_t = lambda dtype: pltpu.VMEM((width, count), dtype)
    tall = lambda dtype: pltpu.VMEM((count, width), dtype)
    vmem = lambda *shape, dtype=BF16: pltpu.VMEM(shape, dtype)
    dma = pltpu.SemaphoreType.DMA
    hops = 3 + deep - 1
    result, grad_inputs, gw, go, small = pl.pallas_call(
        moving_backward_kernel,
        out_shape=(
            sds((count, width), BF16), sds((count, width), F32), sds((units, 2, rows // 2, pair_cols), F32),
            sds((1, 2, rows // 2, out_cols), F32), sds((16, width), F32),
        ),
        in_specs=[smem] + in_vmem(17) + [any_spec] + in_vmem(3),
        out_specs=tuple(in_vmem(5)),
        scratch_shapes=[
            wide_t(BF16), wide_t(BF16), wide_t(BF16), tall(BF16), wide_t(BF16),
            vmem(HEADS, count, dtype=F32), vmem(BLOCK, count, dtype=F32),
            tall(BF16), tall(BF16), tall(BF16), tall(F32), vmem(count, count),
            vmem(HEADS, 4 * BLOCK, dtype=F32), vmem(HEADS, 2 * BLOCK, dtype=F32),
            vmem(local, 2, step, width), vmem(local, 2, step, width), vmem(local, step, width), vmem(local, step, width),
            vmem(local, step, width, dtype=F32), vmem(local, wide, slots, width), vmem(wide, local, slots, width),
            dma((local, 2)), dma((local, 2)), dma((local, 2)), dma((local,)), dma((local,)),
            dma((local, wide)), dma((local, wide)),
            *sum_buffers(units, wide, rows, pair_cols), *sum_buffers(1, wide, rows, out_cols),
            vmem(4, 16, width, dtype=F32), vmem(hops, 16, width, dtype=F32), dma((hops,)), dma((hops,)),
        ],
        compiler_params=pltpu.CompilerParams(collective_id=3, has_side_effects=True, vmem_limit_bytes=62 << 20),
        name="backward",
    )(
        rel_bias, inputs, weights, gain_a, gain_f, router, near, slot_col, routes,
        normed, q, k, v, att, lse, mixed, normed_f, cotangent, outs, grows, gates, jnp.asarray(picks),
    )
    kinds = [
        jnp.transpose(gw[..., at * BLOCK : (at + 1) * BLOCK], (2, 0, 1, 3)).reshape(rows // 2, width) for at in range(3)
    ]
    grad_output = jnp.transpose(go[0, :, :, : width // 2], (1, 0, 2)).reshape(rows // 2, width)
    grad_router = go[0, 0, :, width // 2 : width // 2 + experts]
    device = lax.axis_index("wide") * narrow + lax.axis_index("narrow")
    gains = lax.dynamic_slice(small, (HEADS, device * (rows // 2)), (2, rows // 2))
    grad_rel = small[:HEADS, :bucket_count].T
    return result, grad_inputs, kinds, grad_output, grad_router, gains[1], gains[0], grad_rel


def in_vmem(count):
    return [pl.BlockSpec(memory_space=pltpu.VMEM)] * count


def shards(
    inputs, gain_attn, w_query, w_key, w_value, w_output, rel_bias, gain_ffn, w_router,
    expert_in, expert_out, routes, capacity, cotangent,
):
    count, width = inputs.shape
    experts = w_router.shape[1]
    local, _, hidden_width = expert_in.shape
    wide, narrow = lax.axis_size("wide"), lax.axis_size("narrow")
    slots = 2 * count // experts
    total = experts * slots
    bucket_count = rel_bias.shape[0]
    params = pltpu.CompilerParams(vmem_limit_bytes=60 << 20)
    smem = pl.BlockSpec(memory_space=pltpu.SMEM)

    packed = jnp.concatenate([w_query, w_key, w_value, w_output], axis=1)
    weights = lax.all_gather(packed, BOTH, axis=0, tiled=True)
    small = lax.all_gather(
        jnp.concatenate([w_router, gain_attn[:, None], gain_ffn[:, None]], axis=1), BOTH, axis=0, tiled=True
    )
    router = small[:, :experts]
    gain_a = small[:, experts].astype(F32)[None, :]
    gain_f = small[:, experts + 1].astype(F32)[None, :]
    near = jnp.dot(near_picks(bucket_count, 1), rel_bias, precision=HIGHEST).T
    near_back = jnp.dot(near_picks(bucket_count, -1), rel_bias, precision=HIGHEST).T

    slot_col, slot_row, cot_sent = pl.pallas_call(
        lambda *refs: place_kernel(slots, experts, *refs),
        out_shape=(
            jax.ShapeDtypeStruct((count, 1), jnp.int32),
            jax.ShapeDtypeStruct((1, count), jnp.int32),
            jax.ShapeDtypeStruct((total, width), BF16),
        ),
        in_specs=[smem] + in_vmem(3),
        out_specs=tuple(in_vmem(3)),
        compiler_params=params,
        name="places",
    )(capacity, routes, routes.reshape(1, count), cotangent)

    def spread(rows):
        taken = lax.all_to_all(
            rows.reshape(wide, local * slots, width), "wide", split_axis=0, concat_axis=0, tiled=True
        )
        held = lax.all_gather(taken, "narrow", axis=0, tiled=True)
        return held.reshape(wide * narrow, local, slots, width)

    def collect(rows):
        own = lax.psum_scatter(
            rows.reshape(wide * narrow, local * slots, width), "narrow", scatter_dimension=0, tiled=True
        )
        back = lax.all_to_all(own, "wide", split_axis=0, concat_axis=0, tiled=True)
        return back.reshape(total, width)

    cot_all = spread(cot_sent)

    rows_t = lambda dtype, cols=width: jax.ShapeDtypeStruct((count, cols), dtype)
    normed, q, k, v, att, lse, mixed, normed_f, sent = pl.pallas_call(
        forward_kernel,
        out_shape=(
            rows_t(BF16), rows_t(BF16), rows_t(BF16), rows_t(BF16), rows_t(BF16), rows_t(F32, BLOCK),
            rows_t(F32), rows_t(BF16), jax.ShapeDtypeStruct((total, width), BF16),
        ),
        in_specs=[smem] + in_vmem(7),
        out_specs=tuple(in_vmem(9)),
        compiler_params=params,
        name="forward",
    )(rel_bias, inputs, weights, gain_a, gain_f, router, near, slot_row)

    moving = narrow == 4 and wide % 2 == 0 and slots % 16 == 0 and local * slots % BLOCK == 0
    moving = moving and width % (wide * 2 * 16) == 0 and count == SEQ_LEN
    if moving:
        outs, back, gates, gin, gout = moving_experts(
            sent.reshape(wide, local, slots, width),
            jnp.moveaxis(cot_all.reshape(narrow, wide, local, slots, width), 2, 0),
            expert_in, expert_out, router, wide, narrow,
        )
        result, grad_inputs, kinds, grad_output, grad_router, grad_gain_a, grad_gain_f, grad_rel = moving_backward(
            rel_bias, inputs, weights, gain_a, gain_f, router, near_back, slot_col, routes,
            normed, q, k, v, att, lse, mixed, normed_f, cotangent, outs, back.reshape(total, width),
            gates.reshape(1, total), wide, slots,
        )
        return (
            result, grad_inputs, grad_gain_a, *kinds, grad_output, grad_rel, grad_gain_f, grad_router, gin, gout,
        )

    rows_all = spread(sent)
    sources = wide * narrow
    block = pl.BlockSpec((sources, 1, slots, width), lambda e: (0, e, 0, 0))
    w_in_spec = pl.BlockSpec((1, width, hidden_width), lambda e: (e, 0, 0))
    w_out_spec = pl.BlockSpec((1, hidden_width, width), lambda e: (e, 0, 0))
    first_expert = (lax.axis_index("wide") * local).astype(jnp.int32)[None]
    back, grows, gin, gout = pl.pallas_call(
        expert_kernel,
        grid=(local,),
        out_shape=(
            jax.ShapeDtypeStruct(rows_all.shape, BF16),
            jax.ShapeDtypeStruct(rows_all.shape, BF16),
            jax.ShapeDtypeStruct(expert_in.shape, F32),
            jax.ShapeDtypeStruct(expert_out.shape, F32),
        ),
        in_specs=[
            smem, block, block, w_in_spec, w_out_spec, pl.BlockSpec((width, experts), lambda e: (0, 0)),
        ],
        out_specs=(block, block, w_in_spec, w_out_spec),
        scratch_shapes=[
            pltpu.VMEM((sources * slots, hidden_width), BF16),
            pltpu.VMEM((sources * slots, hidden_width), BF16),
            pltpu.VMEM((sources * slots, width), BF16),
        ],
        compiler_params=params,
        name="experts",
    )(first_expert, rows_all, cot_all, expert_in, expert_out, router)
    outs_back = collect(back)
    grows_back = collect(grows)
    gates = jnp.sum(outs_back.astype(F32) * cot_sent.astype(F32), axis=1)[None, :]

    wide_t = lambda dtype: pltpu.VMEM((width, count), dtype)
    tall = lambda dtype: pltpu.VMEM((count, width), dtype)
    result, grad_inputs, gw, grouter, gnear, gfar, ggain = pl.pallas_call(
        backward_kernel,
        out_shape=(
            rows_t(BF16), rows_t(F32), jax.ShapeDtypeStruct((width, 4 * width), BF16),
            jax.ShapeDtypeStruct((width, experts), F32), jax.ShapeDtypeStruct((HEADS, 4 * BLOCK), F32),
            jax.ShapeDtypeStruct((HEADS, 2 * BLOCK), F32), jax.ShapeDtypeStruct((2, width), F32),
        ),
        in_specs=[smem] + in_vmem(20),
        out_specs=tuple(in_vmem(7)),
        scratch_shapes=[
            wide_t(BF16), wide_t(BF16), wide_t(BF16), tall(BF16), wide_t(BF16),
            pltpu.VMEM((HEADS, count), F32), pltpu.VMEM((BLOCK, count), F32),
            tall(BF16), tall(BF16), tall(BF16), tall(F32), pltpu.VMEM((count, count), BF16),
        ],
        compiler_params=params,
        name="backward",
    )(
        rel_bias, inputs, weights, gain_a, gain_f, router, near_back, slot_col, routes,
        normed, q, k, v, att, lse, mixed, normed_f, cotangent, outs_back, grows_back, gates,
    )

    gw = lax.psum_scatter(gw, BOTH, scatter_dimension=0, tiled=True).astype(F32)
    grad_query, grad_key, grad_value, grad_output = (gw[:, i * width : (i + 1) * width] for i in range(4))
    gsmall = lax.psum_scatter(
        jnp.concatenate([grouter, ggain.T], axis=1), BOTH, scatter_dimension=0, tiled=True
    )
    grad_rel = jnp.dot(near_picks(bucket_count, -1).T, gnear.T, precision=HIGHEST)
    low, high = jnp.sum(gfar[:, :BLOCK], axis=1), jnp.sum(gfar[:, BLOCK:], axis=1)
    grad_rel = grad_rel.at[bucket_count // 2 - 1].add(low).at[bucket_count - 1].add(high)
    grad_rel = lax.psum(grad_rel, BOTH)
    return (
        result, grad_inputs, gsmall[:, experts], grad_query, grad_key, grad_value, grad_output,
        grad_rel, gsmall[:, experts + 1], gsmall[:, :experts], gin, gout,
    )


def solution(mesh):
    return jax.shard_map(
        shards,
        mesh=mesh,
        in_specs=(
            P(BOTH, None),
            P(BOTH),
            P(BOTH, None),
            P(BOTH, None),
            P(BOTH, None),
            P(BOTH, None),
            P(),
            P(BOTH),
            P(BOTH, None),
            P("wide", None, "narrow"),
            P("wide", "narrow", None),
            P(BOTH, None),
            P(BOTH),
            P(BOTH, None),
        ),
        out_specs=(
            P(BOTH, None),
            P(BOTH, None),
            P(BOTH),
            P(BOTH, None),
            P(BOTH, None),
            P(BOTH, None),
            P(BOTH, None),
            P(),
            P(BOTH),
            P(BOTH, None),
            P("wide", None, "narrow"),
            P("wide", "narrow", None),
        ),
        check_vma=False,
    )
```

```python
import jax
import jax.numpy as jnp
import numpy as np
from jax import lax
from jax.experimental import pallas as pl
from jax.experimental.pallas import tpu as pltpu
from jax.sharding import PartitionSpec as P

HEADS = 12
SEQ_LEN = 512
BLOCK = 128
EPSILON = 1e-06
HIGHEST = lax.Precision.HIGHEST
ROOT_TWO_PI = 0.7978845608028654
CUBIC = 0.044715
BOTH = ("wide", "narrow")
F32 = jnp.float32
BF16 = jnp.bfloat16


def bucket_of(offsets, bucket_count):
    half_count = bucket_count // 2
    exact_count = half_count // 2
    distance = np.abs(offsets)
    scaled = exact_count + np.floor(
        np.log(np.maximum(distance, 1) / exact_count)
        / np.log(128.0 / exact_count)
        * (half_count - exact_count)
    ).astype(np.int64)
    scaled = np.minimum(scaled, half_count - 1)
    return ((offsets > 0) * half_count + np.where(distance < exact_count, distance, scaled)).astype(
        np.int32
    )


def near_picks(bucket_count, sign):
    offsets = sign * (np.arange(4 * BLOCK) - (2 * BLOCK - 1))
    picks = (bucket_of(offsets, bucket_count)[:, None] == np.arange(bucket_count)[None, :]).astype(
        np.float32
    )
    picks[-1] = 0.0
    return picks


def dot_nn(left, right):
    return lax.dot_general(left, right, (((1,), (0,)), ((), ())), preferred_element_type=F32)


def dot_nt(left, right):
    return lax.dot_general(left, right, (((1,), (1,)), ((), ())), preferred_element_type=F32)


def dot_tn(left, right):
    return lax.dot_general(left, right, (((0,), (0,)), ((), ())), preferred_element_type=F32)


def inverse_rms(values):
    return lax.rsqrt(jnp.mean(values * values, axis=-1, keepdims=True) + EPSILON)


def norm_backward(values, inverse, gain, grad_normed):
    scaled = grad_normed * gain
    grad_gain = jnp.sum(grad_normed * values * inverse, axis=0, keepdims=True)
    inner = jnp.mean(scaled * values, axis=-1, keepdims=True)
    return (inverse * (scaled - values * inverse * inverse * inner), grad_gain)


def softmax_lanes(logits):
    peak = jnp.max(logits, axis=-1, keepdims=True)
    exponent = jnp.exp(logits - peak)
    return exponent / jnp.sum(exponent, axis=-1, keepdims=True)


def toeplitz_near(near_row):
    spread = jnp.broadcast_to(near_row, (BLOCK, 4 * BLOCK))
    return pltpu.roll(spread, 3 * BLOCK + 1, 1, stride=1, stride_axis=0)[:, : 3 * BLOCK]


def bias_rows(near, far_low, far_high, row, blocks):
    pieces = []
    for column in range(blocks):
        distance = column - row
        if distance <= -2:
            pieces.append(jnp.full((BLOCK, BLOCK), far_low, F32))
        elif distance >= 2:
            pieces.append(jnp.full((BLOCK, BLOCK), far_high, F32))
        else:
            pieces.append(near[:, (distance + 1) * BLOCK : (distance + 2) * BLOCK])
    return jnp.concatenate(pieces, axis=1)


def diagonal_sums(near_sum):
    padded = jnp.concatenate([near_sum, jnp.zeros((BLOCK, BLOCK), F32)], axis=1)
    groups = jnp.zeros((8, 4 * BLOCK), F32)
    for at in range(0, BLOCK, 8):
        groups = groups + pltpu.roll(padded[at : at + 8, :], BLOCK - 8 - at, 1)
    sums = groups[7:8, :]
    for at in range(7):
        sums = sums + pltpu.roll(groups[at : at + 1, :], 7 - at, 1)
    return sums


def slot_places(routes_ref, row_ref, limit, experts, slots, count):
    lower = lax.broadcasted_iota(jnp.int32, (count, count), 0)
    upper = lax.broadcasted_iota(jnp.int32, (count, count), 1)
    col = routes_ref[...]
    chosen = lax.broadcasted_iota(jnp.int32, (count, experts), 1) == col
    running = dot_nn((upper <= lower).astype(BF16), chosen.astype(BF16))
    place = jnp.sum(jnp.where(chosen, running, 0.0), axis=1, keepdims=True).astype(jnp.int32) - 1
    slot_col = jnp.where(place < limit, col * slots + place, -1)
    row = row_ref[...]
    chosen_t = lax.broadcasted_iota(jnp.int32, (experts, count), 0) == row
    running_t = dot_nn(chosen_t.astype(BF16), (lower <= upper).astype(BF16))
    place_t = (
        jnp.sum(jnp.where(chosen_t, running_t, 0.0), axis=0, keepdims=True).astype(jnp.int32) - 1
    )
    slot_row = jnp.where(place_t < limit, row * slots + place_t, -1)
    return slot_col, slot_row


def place_kernel(slots, experts, capacity_ref, routes_ref, row_ref, cot_ref, slot_col, slot_row, cot_out):
    count = routes_ref.shape[0]
    limit = capacity_ref[0] * count // experts
    col, row = slot_places(routes_ref, row_ref, limit, experts, slots, count)
    slot_col[...] = col
    slot_row[...] = row
    picks = (lax.broadcasted_iota(jnp.int32, (experts * slots, count), 0) == row).astype(BF16)
    cot_out[...] = dot_nn(picks, cot_ref[...]).astype(BF16)


def pair_forward(at, rel_ref, near_ref, q_ref, k_ref, v_ref, att_ref, lse_ref):
    count, width = q_ref.shape
    head_dim = width // HEADS
    blocks = count // BLOCK
    bucket_count = rel_ref.shape[0]
    lanes = lax.broadcasted_iota(jnp.int32, (1, BLOCK), 1)
    first = lanes < head_dim
    cols = pl.ds(pl.multiple_of(at * BLOCK, BLOCK), BLOCK)
    k_pair, v_pair = k_ref[:, cols], v_ref[:, cols]
    nears = [toeplitz_near(near_ref[pl.ds(2 * at + half, 1), :]) for half in range(2)]
    for row in range(blocks):
        rows = slice(row * BLOCK, (row + 1) * BLOCK)
        q_rows = q_ref[rows, cols] * jnp.asarray(head_dim**-0.5, BF16)
        found = []
        log_sums = lse_ref[rows, :]
        for half in range(2):
            head = 2 * at + half
            low, high = rel_ref[bucket_count // 2 - 1, head], rel_ref[bucket_count - 1, head]
            mask = first if half == 0 else jnp.logical_not(first)
            scores = dot_nt(jnp.where(mask, q_rows, jnp.zeros_like(q_rows)), k_pair)
            scores = scores + bias_rows(nears[half], low, high, row, blocks)
            peak = jnp.max(scores, axis=-1, keepdims=True)
            exponent = jnp.exp(scores - peak)
            total = jnp.sum(exponent, axis=-1, keepdims=True)
            found.append(dot_nn((exponent * (1.0 / total)).astype(BF16), v_pair))
            log_sums = jnp.where(lanes == head, peak + jnp.log(total), log_sums)
        lse_ref[rows, :] = log_sums
        att_ref[rows, cols] = jnp.where(first, found[0], found[1]).astype(BF16)


def slot_rows(slot_row, values, total):
    picks = lax.broadcasted_iota(jnp.int32, (total, slot_row.shape[1]), 0) == slot_row
    return dot_nn(picks.astype(BF16), values).astype(BF16)


def forward_kernel(
    rel_ref, x_ref, w_ref, gain_a, gain_f, router_ref, near_ref, slot_row,
    normed_ref, q_ref, k_ref, v_ref, att_ref, lse_ref, mixed_ref, normed_f, sent_ref,
):
    width = x_ref.shape[1]
    tokens = x_ref[...].astype(F32)
    normed = (tokens * inverse_rms(tokens) * gain_a[...]).astype(BF16)
    normed_ref[...] = normed
    for out, at in ((q_ref, 0), (k_ref, 1), (v_ref, 2)):
        out[...] = dot_nn(normed, w_ref[:, at * width : (at + 1) * width]).astype(BF16)
    lse_ref[...] = jnp.zeros_like(lse_ref)

    def pair(at, carry):
        pair_forward(at, rel_ref, near_ref, q_ref, k_ref, v_ref, att_ref, lse_ref)
        return carry

    lax.fori_loop(0, HEADS // 2, pair, 0)
    mixed = tokens + dot_nn(att_ref[...], w_ref[:, 3 * width : 4 * width])
    mixed_ref[...] = mixed
    normed_2 = (mixed * inverse_rms(mixed) * gain_f[...]).astype(BF16)
    normed_f[...] = normed_2
    sent_ref[...] = slot_rows(slot_row[...], normed_2, sent_ref.shape[0])


def expert_kernel(
    first_ref, rows_ref, cot_ref, in_ref, out_ref, router_ref,
    back_ref, grows_ref, gin_ref, gout_ref, hidden_ref, gpre_ref, sg_ref,
):
    sources, _, slots, width = rows_ref.shape
    total = sources * slots
    step = min(256, total)
    expert = first_ref[0] + pl.program_id(0)

    def chunk(at, carry):
        these = pl.ds(pl.multiple_of(at * (step // slots), step // slots), step // slots)
        flat = pl.ds(pl.multiple_of(at * step, step), step)
        rows = rows_ref[these, 0].reshape(step, width)
        probs = softmax_lanes(dot_nn(rows, router_ref[...]))
        here = lax.broadcasted_iota(jnp.int32, probs.shape, 1) == expert
        gate = jnp.sum(jnp.where(here, probs, 0.0), axis=-1, keepdims=True)
        sg = (cot_ref[these, 0].reshape(step, width).astype(F32) * gate).astype(BF16)
        sg_ref[flat, :] = sg
        pre = dot_nn(rows, in_ref[0])
        square = pre * pre
        inner = jnp.tanh(pre * (ROOT_TWO_PI + ROOT_TWO_PI * CUBIC * square))
        half = 0.5 * (1.0 + inner)
        hidden = (pre * half).astype(BF16)
        hidden_ref[flat, :] = hidden
        slope = half + 0.5 * pre * (1.0 - inner * inner) * (
            ROOT_TWO_PI + 3.0 * ROOT_TWO_PI * CUBIC * square
        )
        gpre = (dot_nt(sg, out_ref[0]) * slope).astype(BF16)
        gpre_ref[flat, :] = gpre
        back_ref[these, 0] = dot_nn(hidden, out_ref[0]).astype(BF16).reshape(-1, slots, width)
        grows_ref[these, 0] = dot_nt(gpre, in_ref[0]).astype(BF16).reshape(-1, slots, width)
        return carry

    lax.fori_loop(0, total // step, chunk, 0)
    gout_ref[0] = dot_tn(hidden_ref[...], sg_ref[...])
    gin_ref[0] = dot_tn(rows_ref[:, 0].reshape(total, width), gpre_ref[...])


def remote(source, target, send, receive, device):
    return pltpu.make_async_remote_copy(
        src_ref=source,
        dst_ref=target,
        send_sem=send,
        recv_sem=receive,
        device_id=device,
        device_id_type=pl.DeviceIdType.MESH,
    )


def greet(devices):
    barrier = pltpu.get_barrier_semaphore()
    for device in devices:
        pl.semaphore_signal(barrier, inc=1, device_id=device, device_id_type=pl.DeviceIdType.MESH)
    pl.semaphore_wait(barrier, len(devices))


class Place:
    def __init__(self, wide):
        self.wide = wide
        self.run = wide // 2
        self.deep = wide // 2
        self.w, self.n = lax.axis_index("wide"), lax.axis_index("narrow")
        self.x, self.c = self.n // 2, lax.rem(self.n, 2)
        self.z, self.y = self.w // 2, lax.rem(self.w, 2)
        self.core = (self.w, self.x * 2 + 1 - self.c)
        self.side = (self.w, (1 - self.x) * 2 + self.c)
        self.row = (self.z * 2 + 1 - self.y, self.n)

    def flip(self, j):
        found, bit = self.w, 1
        while bit <= j:
            if j & bit:
                found = found + bit - 2 * bit * lax.rem(self.w // bit, 2)
            bit *= 2
        return found

    def peer(self, j):
        return (self.flip(j), self.n)

    def span(self, far):
        half = self.w // self.run
        return pl.ds((1 - half if far else half) * self.run, self.run)

    def steps(self, far):
        return range(self.run, self.wide) if far else range(1, self.run)

    def partners(self):
        return [self.peer(j) for j in range(1, self.wide)] + [self.core, self.side]


class Spread:
    def __init__(self, place, sent, held, wide_s, wide_r, side_s, side_r, core_s, core_r):
        self.place, self.sent, self.held = place, sent, held
        self.wide_s, self.wide_r, self.side_s, self.side_r = wide_s, wide_r, side_s, side_r
        self.core_s, self.core_r = core_s, core_r

    def hop(self, e, j):
        p = self.place
        return remote(
            self.sent.at[p.flip(j), e], self.held.at[e, p.n, p.w], self.wide_s.at[e, j], self.wide_r.at[e, j], p.peer(j)
        )

    def start(self, e, far):
        for j in self.place.steps(far):
            self.hop(e, j).start()

    def beside(self, e, far):
        p = self.place
        rows = self.held.at[e, p.n, p.span(far)]
        return remote(rows, rows, self.side_s.at[e, far], self.side_r.at[e, far], p.side)

    def over(self, e, other, far):
        p = self.place
        rows = self.held.at[e, (1 - p.x) * 2 + p.c if other else p.n, p.span(far)]
        at = 2 * other + far
        return remote(rows, rows, self.core_s.at[e, at], self.core_r.at[e, at], p.core)

    def forward(self, e, far):
        for j in self.place.steps(far):
            self.hop(e, j).wait_recv()
        self.beside(e, far).start()
        self.over(e, 0, far).start()

    def pass_on(self, e):
        for far in range(2):
            self.beside(e, far).wait_recv()
            self.over(e, 1, far).start()

    def arrive(self, e):
        for other in range(2):
            for far in range(2):
                self.over(e, other, far).wait_recv()

    def drain(self, e):
        for j in range(1, self.place.wide):
            self.hop(e, j).wait_send()
        for far in range(2):
            self.beside(e, far).wait_send()
            self.over(e, 0, far).wait_send()
            self.over(e, 1, far).wait_send()


class Collect:
    def __init__(self, place, to_core, from_core, from_side, returned, semaphores):
        self.place, self.to_core, self.from_core = place, to_core, from_core
        self.from_side, self.returned = from_side, returned
        self.core_s, self.core_r, self.side_s, self.side_r, self.wide_s, self.wide_r = semaphores

    def core(self, e, other):
        return remote(
            self.to_core(e, other), self.from_core.at[e, other], self.core_s.at[e, other], self.core_r.at[e, other],
            self.place.core,
        )

    def beside(self, e, far):
        rows = self.place.span(far)
        return remote(
            self.from_core.at[e, 1, rows], self.from_side.at[e, rows], self.side_s.at[e, far], self.side_r.at[e, far],
            self.place.side,
        )

    def back(self, e, j):
        p = self.place
        return remote(
            self.from_side.at[e, p.flip(j)], self.returned.at[p.w, e], self.wide_s.at[e, j], self.wide_r.at[e, j], p.peer(j)
        )

    def go_beside(self, e, part):
        self.core(e, 1).wait_recv()
        held = self.from_core[e, 1].astype(F32)
        self.from_core[e, 1] = (part.astype(F32).reshape(held.shape) + held).astype(BF16)
        self.beside(e, 1).start()
        self.beside(e, 0).start()

    def finish(self, e, far, part):
        p = self.place
        rows = p.span(far)
        self.beside(e, far).wait_recv()
        self.from_side[e, rows] = (part(rows) + self.from_side[e, rows].astype(F32)).astype(BF16)
        for j in p.steps(far):
            self.back(e, j).start()
        if not far:
            self.returned[p.w, e] = self.from_side[e, p.w]

    def drain(self, e):
        self.core(e, 0).wait_send()
        self.core(e, 1).wait_send()
        for far in range(2):
            self.beside(e, far).wait_send()
        for j in range(1, self.place.wide):
            self.back(e, j).wait_send()

    def arrive(self, e):
        for j in range(1, self.place.wide):
            self.back(e, j).wait_recv()


class Gather:
    def __init__(self, place, unit, held, halves, semaphores):
        self.p, self.u, self.held, self.halves = place, unit, held, halves
        self.s, self.r = semaphores

    def piece(self, *place):
        return self.held.at[self.u, self.p.c, *place] if self.halves else self.held.at[self.u, *place]

    def column(self, y, x):
        return self.piece(slice(None), y, x)

    def copy(self, piece, slot, device):
        return remote(piece, piece, self.s.at[self.u, slot], self.r.at[self.u, slot], device)

    def to_z(self, k):
        p = self.p
        z = lax.rem(p.z + k, p.deep)
        return self.copy(self.piece(p.z, p.y, p.x), k - 1, (z * 2 + p.y, p.n))

    def to_x(self):
        return self.copy(self.column(self.p.y, self.p.x), 3, self.p.side)

    def to_y(self):
        return self.copy(self.column(self.p.y, self.p.x), 4, self.p.row)

    def corner(self):
        return self.copy(self.column(self.p.y, 1 - self.p.x), 5, self.p.row)

    def to_core(self, at):
        p = self.p
        y, x = ((p.y, p.x), (p.y, 1 - p.x), (1 - p.y, p.x), (1 - p.y, 1 - p.x))[at]
        return self.copy(self.column(y, x), 6 + at, p.core)

    def hand(self, at):
        if self.halves:
            self.to_core(at).start()

    def start(self):
        for k in range(1, self.p.deep):
            self.to_z(k).start()

    def spread(self):
        for k in range(1, self.p.deep):
            self.to_z(k).wait_recv()
        self.to_x().start()
        self.to_y().start()
        self.hand(0)

    def forward(self):
        self.to_x().wait_recv()
        self.corner().start()
        self.hand(1)
        self.to_y().wait_recv()
        self.hand(2)

    def end(self):
        self.corner().wait_recv()
        self.hand(3)

    def arrive(self):
        if self.halves:
            for at in range(4):
                self.to_core(at).wait_recv()

    def drain(self):
        for k in range(1, self.p.deep):
            self.to_z(k).wait_send()
        for copy in (self.to_x(), self.to_y(), self.corner()):
            copy.wait_send()
        if self.halves:
            for at in range(4):
                self.to_core(at).wait_send()


def moving_forward_kernel(
    rel_ref, capacity_ref, x_ref, q_part, k_part, v_part, o_part, small_part, near_ref, routes_ref, row_ref, cot_ref,
    normed_ref, q_ref, k_ref, v_ref, att_ref, lse_ref, mixed_ref, normed_f, sent_ref, slot_col,
    router_out, gains_out, weights_out, cot_out,
    held, small, pair_send, pair_got, small_got, cot_sent, weight_s, pair_s, pair_r,
    gs, gr, hs, hr, wide_s, wide_r, side_s, side_r, core_s, core_r,
):
    count, width = x_ref.shape
    wide, local, slots, _ = cot_sent.shape
    experts = router_out.shape[1]
    total = wide * local * slots
    units = HEADS // 4
    rows = pair_send.shape[2]
    p = Place(wide)
    greet(p.partners())

    def own_cols(u, half):
        if u == units:
            return o_part[:, half * (width // 2) : (half + 1) * (width // 2)]
        cols = slice((2 * u + half) * BLOCK, (2 * u + half + 1) * BLOCK)
        return jnp.concatenate([q_part[:, cols], k_part[:, cols], v_part[:, cols]], axis=1)

    def swap_copies():
        return [
            remote(pair_send.at[0], pair_got.at[0], pair_s.at[0], pair_r.at[0], p.core),
            remote(small_part, small_got, pair_s.at[1], pair_r.at[1], p.core),
        ]

    for u in range(units + 1):
        pair_send[0, u] = jnp.where(p.c == 0, own_cols(u, 1), own_cols(u, 0))
    for copy in swap_copies():
        copy.start()
    for copy in swap_copies():
        copy.wait_recv()

    def joined(mine, other):
        mine, other = mine.astype(F32), other.astype(F32)
        return jnp.concatenate(
            [jnp.where(p.c == 0, mine, other), jnp.where(p.c == 0, other, mine)], axis=0
        ).astype(BF16)

    def gather(u):
        return Gather(p, u, held, True, (gs, gr))

    small_gather = Gather(p, 0, small, False, (hs, hr))
    small[0, p.z, p.y, p.x] = joined(small_part[...], small_got[...])
    small_gather.start()
    for u in range(units + 1):
        mine = jnp.where(p.c == 0, own_cols(u, 0), own_cols(u, 1))
        held[u, p.c, p.z, p.y, p.x] = joined(mine, pair_got[0, u])
        if u < 2:
            gather(u).start()

    limit = capacity_ref[0] * count // experts
    slot_col[...], slot_row = slot_places(routes_ref, row_ref, limit, experts, slots, count)
    cot_sent[...] = slot_rows(slot_row, cot_ref[...], total).reshape(cot_sent.shape)
    moves = Spread(p, cot_sent, cot_out, wide_s, wide_r, side_s, side_r, core_s, core_r)

    def own_rows(e):
        return pltpu.make_async_copy(cot_sent.at[p.w, e], cot_out.at[e, p.n, p.w], weight_s.at[1 + e])

    for e in range(local):
        own_rows(e).start()
    small_gather.spread()
    gather(0).spread()
    gather(2).start()
    gather(1).spread()
    gather(3).start()
    small_gather.forward()
    gather(0).forward()
    for e in range(local):
        moves.start(e, 0)
    moves.start(0, 1)
    small_gather.end()
    small_all = small[0].reshape(width, BLOCK)
    router_out[...] = small_all[:, :experts]
    gains = small_all.astype(F32).T[experts : experts + 8, :]
    gains_out[...] = gains
    tokens = x_ref[...].astype(F32)
    normed_ref[...] = (tokens * inverse_rms(tokens) * gains[0:1, :]).astype(BF16)
    lse_ref[...] = jnp.zeros_like(lse_ref)
    gather(1).forward()
    for e in range(local):
        own_rows(e).wait()
    moves.forward(0, 0)
    moves.start(1, 1)

    def pair(at, weight):
        cols = pl.ds(pl.multiple_of(at * BLOCK, BLOCK), BLOCK)
        found = dot_nn(normed_ref[...], weight.reshape(width, 3 * BLOCK)).astype(BF16)
        q_ref[:, cols], k_ref[:, cols], v_ref[:, cols] = (found[:, i * BLOCK : (i + 1) * BLOCK] for i in range(3))
        pair_forward(at, rel_ref, near_ref, q_ref, k_ref, v_ref, att_ref, lse_ref)

    def pairs(u, carry):
        gather(u).end()
        gather(u).arrive()

        pair(2 * u, held[u, 0])

        @pl.when(u + 2 <= units)
        def _():
            gather(u + 2).spread()

        moves.forward(u, 1)

        @pl.when(u + 2 < local)
        def _():
            moves.start(u + 2, 1)

        moves.forward(u + 1, 0)
        pair(2 * u + 1, held[u, 1])

        @pl.when(u + 2 <= units)
        def _():
            gather(u + 2).forward()

        moves.pass_on(u)
        return carry

    lax.fori_loop(0, units, pairs, 0)
    gather(units).end()
    moves.forward(local - 1, 1)
    gather(units).arrive()
    weights_copy = pltpu.make_async_copy(held, weights_out, weight_s.at[0])
    weights_copy.start()
    mixed = tokens_again(x_ref) + jnp.concatenate(
        [dot_nn(att_ref[...], held[units, half].reshape(width, width // 2)) for half in range(2)], axis=1
    )
    mixed_ref[...] = mixed
    normed_2 = (mixed * inverse_rms(mixed) * gains_out[1:2, :]).astype(BF16)
    normed_f[...] = normed_2
    sent_ref[...] = slot_rows(slot_row, normed_2, total).reshape(sent_ref.shape)
    moves.pass_on(local - 1)
    for copy in swap_copies():
        copy.wait_send()
    small_gather.drain()
    for u in range(units + 1):
        gather(u).drain()
    for e in range(local):
        moves.arrive(e)
        moves.drain(e)
    weights_copy.wait()


def tokens_again(x_ref):
    return x_ref[...].astype(F32)


def moving_forward(
    rel_bias, capacity, inputs, w_query, w_key, w_value, w_output, w_router, gain_attn, gain_ffn, near, routes, cotangent,
    wide, narrow, local, slots,
):
    count, width = inputs.shape
    experts = w_router.shape[1]
    shard = w_query.shape[0]
    deep, units = wide // 2, HEADS // 4
    half = width // 2
    sds = jax.ShapeDtypeStruct
    rows_t = lambda dtype, cols=width: sds((count, cols), dtype)
    smem, any_spec = pl.BlockSpec(memory_space=pltpu.SMEM), pl.BlockSpec(memory_space=pl.ANY)
    vmem = lambda *shape, dtype=BF16: pltpu.VMEM(shape, dtype)
    dma = pltpu.SemaphoreType.DMA
    small = jnp.concatenate(
        [w_router, gain_attn[:, None], gain_ffn[:, None], jnp.zeros((shard, BLOCK - experts - 2), BF16)], axis=1
    )
    return pl.pallas_call(
        moving_forward_kernel,
        out_shape=(
            rows_t(BF16), rows_t(BF16), rows_t(BF16), rows_t(BF16), rows_t(BF16), rows_t(F32, BLOCK), rows_t(F32),
            rows_t(BF16), sds((wide, local, slots, width), BF16), sds((count, 1), jnp.int32),
            sds((width, experts), BF16), sds((8, width), F32),
            sds((units + 1, 2, deep, 2, 2, 2 * shard, half), BF16),
            sds((local, narrow, wide, slots, width), BF16),
        ),
        in_specs=[smem, smem] + in_vmem(10),
        out_specs=tuple(in_vmem(12)) + (any_spec, any_spec),
        scratch_shapes=[
            vmem(units + 1, 2, deep, 2, 2, 2 * shard, half), vmem(1, deep, 2, 2, 2 * shard, BLOCK),
            vmem(1, units + 1, shard, half), vmem(1, units + 1, shard, half), vmem(shard, BLOCK),
            vmem(wide, local, slots, width), dma((1 + local,)), dma((2,)), dma((2,)),
            dma((units + 1, 10)), dma((units + 1, 10)), dma((1, 10)), dma((1, 10)),
            dma((local, wide)), dma((local, wide)), dma((local, 2)), dma((local, 2)), dma((local, 4)), dma((local, 4)),
        ],
        compiler_params=pltpu.CompilerParams(collective_id=1, has_side_effects=True, vmem_limit_bytes=62 << 20),
        name="forward",
    )(
        rel_bias, capacity, inputs, w_query, w_key, w_value, w_output, small, near, routes, routes.reshape(1, count),
        cotangent,
    )


def moving_expert_kernel(
    sent, cot_hbm, in_hbm, out_hbm, router_ref,
    rows_o, sg_o, hidden_o, gpre_o, outs_o, back_o, gate_o,
    held, cot, w_in, w_out, sg, hidden, gpre, outs, to_core, from_core, from_side, near_sum,
    gate_sum, gate_core, gate_from_core, gate_side, gate_from_side, gate_ready,
    load_s, store_s, wide_s, wide_r, side_s, side_r, core_s, core_r,
    rc_s, rc_r, rx_s, rx_r, rw_s, rw_r, gc_s, gc_r, gx_s, gx_r, gw_s, gw_r,
):
    wide, local, slots, width = sent.shape
    narrow = held.shape[1]
    step = wide * slots
    p = Place(wide)
    moves = Spread(p, sent, held, wide_s, wide_r, side_s, side_r, core_s, core_r)
    greet(p.partners())
    moves.start(0, 1)
    moves.start(0, 0)
    moves.start(1, 0)

    def loads(e):
        return [
            pltpu.make_async_copy(in_hbm.at[e], w_in.at[e], load_s.at[e, 0]),
            pltpu.make_async_copy(out_hbm.at[e], w_out.at[e], load_s.at[e, 1]),
            pltpu.make_async_copy(cot_hbm.at[e], cot.at[e], load_s.at[e, 2]),
        ]

    def stores(e):
        b = lax.rem(e, 2)
        return [
            pltpu.make_async_copy(held.at[e], rows_o.at[e], store_s.at[e, 0]),
            pltpu.make_async_copy(sg.at[b], sg_o.at[e], store_s.at[e, 1]),
            pltpu.make_async_copy(hidden.at[b], hidden_o.at[e], store_s.at[e, 2]),
            pltpu.make_async_copy(gpre.at[b], gpre_o.at[e], store_s.at[e, 3]),
            pltpu.make_async_copy(outs.at[b], outs_o.at[e], store_s.at[e, 4]),
        ]

    for e in range(local):
        for copy in loads(e):
            copy.start()
        held[e, p.n, p.w] = sent[p.w, e]
    gate_sum[...] = jnp.zeros_like(gate_sum)
    moves.forward(0, 0)
    moves.forward(1, 0)
    moves.start(1, 1)
    moves.start(2, 0)
    moves.forward(0, 1)
    moves.start(2, 1)
    moves.start(3, 0)
    moves.forward(2, 0)
    moves.pass_on(0)

    def chunk(e, m):
        b = lax.rem(e, 2)
        rows = held[e, m].reshape(step, width)
        probs = softmax_lanes(dot_nn(rows, router_ref[...]))
        here = lax.broadcasted_iota(jnp.int32, probs.shape, 1) == p.w * local + e
        gate = jnp.sum(jnp.where(here, probs, 0.0), axis=-1, keepdims=True)
        cot_rows = cot[e, m].reshape(step, width).astype(F32)
        sg_rows = (cot_rows * gate).astype(BF16)
        sg[b, m] = sg_rows
        pre = dot_nn(rows, w_in[e])
        square = pre * pre
        inner = jnp.tanh(pre * (ROOT_TWO_PI + ROOT_TWO_PI * CUBIC * square))
        half = 0.5 * (1.0 + inner)
        hidden_rows = (pre * half).astype(BF16)
        hidden[b, m] = hidden_rows
        slope = half + 0.5 * pre * (1.0 - inner * inner) * (
            ROOT_TWO_PI + 3.0 * ROOT_TWO_PI * CUBIC * square
        )
        gpre_rows = (dot_nt(sg_rows, w_out[e]) * slope).astype(BF16)
        gpre[b, m] = gpre_rows
        out_rows = dot_nn(hidden_rows, w_out[e])
        outs[b, m] = out_rows.astype(BF16).reshape(wide, slots, width)
        gate_rows = jnp.sum(out_rows * cot_rows, axis=-1, keepdims=True)
        row = lax.broadcasted_iota(jnp.int32, (step, local * slots), 0)
        lane = lax.broadcasted_iota(jnp.int32, (step, local * slots), 1)
        spread = jnp.where(lane == e * slots + lax.rem(row, slots), gate_rows, 0.0)
        gate_sum[m] += jnp.sum(spread.reshape(wide, slots, local * slots), axis=1)
        return dot_nt(gpre_rows, w_in[e])

    back = Collect(
        p, lambda e, other: to_core.at[e, other], from_core, from_side, back_o, (rc_s, rc_r, rx_s, rx_r, rw_s, rw_r)
    )

    def own_sums(rows):
        return near_sum[rows]

    far_x = (1 - p.x) * 2

    def expert(e, carry):
        for copy in loads(e):
            copy.wait()

        @pl.when(e >= 2)
        def _():
            for copy in stores(e - 2)[1:]:
                copy.wait()

        moves.arrive(e)
        to_core[e, 1] = chunk(e, far_x + 1 - p.c).astype(BF16).reshape(wide, slots, width)
        back.core(e, 1).start()

        @pl.when(e + 1 < local)
        def _():
            moves.forward(e + 1, 1)

        @pl.when(e + 3 < local)
        def _():
            moves.start(e + 3, 1)

        back.go_beside(e, chunk(e, far_x + p.c))

        @pl.when(e > 0)
        def _():
            back.finish(e - 1, 1, own_sums)
            back.finish(e - 1, 0, own_sums)

        to_core[e, 0] = chunk(e, p.x * 2 + 1 - p.c).astype(BF16).reshape(wide, slots, width)
        back.core(e, 0).start()

        @pl.when(e + 1 < local)
        def _():
            moves.pass_on(e + 1)

        @pl.when(e + 3 < local)
        def _():
            moves.forward(e + 3, 0)

        near_part = chunk(e, p.n)
        back.core(e, 0).wait_recv()
        near_sum[...] = near_part.reshape(wide, slots, width) + from_core[e, 0].astype(F32)
        for copy in stores(e):
            copy.start()
        return carry

    lax.fori_loop(0, local, expert, 0)
    gate_core[0] = gate_sum[p.x * 2 + 1 - p.c]
    gate_core[1] = gate_sum[far_x + 1 - p.c]
    gates_core = remote(gate_core, gate_from_core, gc_s, gc_r, p.core)
    gates_core.start()
    gates_core.wait_recv()
    gate_side[...] = gate_sum[far_x + p.c] + gate_from_core[1]
    gates_side = remote(gate_side, gate_from_side, gx_s, gx_r, p.side)
    gates_side.start()
    back.finish(local - 1, 1, own_sums)
    back.finish(local - 1, 0, own_sums)
    gates_side.wait_recv()
    gates = gate_sum[p.n] + gate_from_core[0] + gate_from_side[...]
    for v in range(wide):
        gate_ready[v] = gates[v : v + 1, :]
    gates_wide = [
        remote(gate_ready.at[p.flip(j)], gate_o.at[p.w], gw_s.at[j], gw_r.at[j], p.peer(j)) for j in range(1, wide)
    ]
    for copy in gates_wide:
        copy.start()
    gate_o[p.w] = gate_ready[p.w]
    gates_core.wait_send()
    gates_side.wait_send()

    def drain(e, carry):
        moves.drain(e)
        back.drain(e)
        back.arrive(e)
        stores(e)[0].wait()

        @pl.when(e >= local - 2)
        def _():
            for copy in stores(e)[1:]:
                copy.wait()

        return carry

    lax.fori_loop(0, local, drain, 0)
    for copy in gates_wide:
        copy.wait()


def weight_grad_kernel(rows_ref, sg_ref, hidden_ref, gpre_ref, gin_ref, gout_ref):
    gout_ref[0] = dot_tn(hidden_ref[0], sg_ref[0])
    gin_ref[0] = dot_tn(rows_ref[0], gpre_ref[0])


def moving_experts(sent, cot_all, expert_in, expert_out, router, wide, narrow):
    _, local, slots, width = sent.shape
    hidden_width = expert_in.shape[2]
    step = wide * slots
    sds = jax.ShapeDtypeStruct
    any_spec, vmem_spec = pl.BlockSpec(memory_space=pl.ANY), pl.BlockSpec(memory_space=pltpu.VMEM)
    dma = pltpu.SemaphoreType.DMA
    rows, sg, hidden, gpre, outs, back, gates = pl.pallas_call(
        moving_expert_kernel,
        out_shape=(
            sds((local, narrow, wide, slots, width), BF16),
            sds((local, narrow, step, width), BF16),
            sds((local, narrow, step, hidden_width), BF16),
            sds((local, narrow, step, hidden_width), BF16),
            sds((local, narrow, wide, slots, width), BF16),
            sds((wide, local, slots, width), BF16),
            sds((wide, 1, local * slots), F32),
        ),
        in_specs=[vmem_spec, any_spec, any_spec, any_spec, vmem_spec],
        out_specs=(any_spec,) * 5 + (vmem_spec,) * 2,
        scratch_shapes=[
            pltpu.VMEM((local, narrow, wide, slots, width), BF16),
            pltpu.VMEM((local, narrow, wide, slots, width), BF16),
            pltpu.VMEM(expert_in.shape, BF16),
            pltpu.VMEM(expert_out.shape, BF16),
            pltpu.VMEM((2, narrow, step, width), BF16),
            pltpu.VMEM((2, narrow, step, hidden_width), BF16),
            pltpu.VMEM((2, narrow, step, hidden_width), BF16),
            pltpu.VMEM((2, narrow, wide, slots, width), BF16),
            pltpu.VMEM((local, 2, wide, slots, width), BF16),
            pltpu.VMEM((local, 2, wide, slots, width), BF16),
            pltpu.VMEM((local, wide, slots, width), BF16),
            pltpu.VMEM((wide, slots, width), F32),
            pltpu.VMEM((narrow, wide, local * slots), F32),
            pltpu.VMEM((2, wide, local * slots), F32),
            pltpu.VMEM((2, wide, local * slots), F32),
            pltpu.VMEM((wide, local * slots), F32),
            pltpu.VMEM((wide, local * slots), F32),
            pltpu.VMEM((wide, 1, local * slots), F32),
            dma((local, 3)), dma((local, 5)), dma((local, wide)), dma((local, wide)),
            dma((local, 2)), dma((local, 2)), dma((local, 4)), dma((local, 4)),
            dma((local, 2)), dma((local, 2)), dma((local, 2)), dma((local, 2)), dma((local, wide)), dma((local, wide)),
            dma, dma, dma, dma, dma((wide,)), dma((wide,)),
        ],
        compiler_params=pltpu.CompilerParams(
            collective_id=2, has_side_effects=True, vmem_limit_bytes=62 << 20
        ),
        name="experts",
    )(sent, cot_all, expert_in, expert_out, router)
    total = narrow * step
    spec = lambda cols: pl.BlockSpec((1, total, cols), lambda e: (e, 0, 0))
    gin, gout = pl.pallas_call(
        weight_grad_kernel,
        grid=(local,),
        out_shape=(sds(expert_in.shape, F32), sds(expert_out.shape, F32)),
        in_specs=[spec(width), spec(width), spec(hidden_width), spec(hidden_width)],
        out_specs=(
            pl.BlockSpec((1, width, hidden_width), lambda e: (e, 0, 0)),
            pl.BlockSpec((1, hidden_width, width), lambda e: (e, 0, 0)),
        ),
        compiler_params=pltpu.CompilerParams(vmem_limit_bytes=60 << 20),
        name="weight_grads",
    )(
        rows.reshape(local, total, width), sg.reshape(local, total, width),
        hidden.reshape(local, total, hidden_width), gpre.reshape(local, total, hidden_width),
    )
    return outs, back, gates, gin, gout


def routed_gate(normed_f, router_ref, routes_ref):
    probs = softmax_lanes(dot_nn(normed_f[...], router_ref[...]))
    chosen = lax.broadcasted_iota(jnp.int32, probs.shape, 1) == routes_ref[...]
    return probs, chosen, jnp.sum(jnp.where(chosen, probs, 0.0), axis=-1, keepdims=True)


def slot_owners(slot_col, total):
    return lax.broadcasted_iota(jnp.int32, (slot_col.shape[0], total), 1) == slot_col[...]


def ffn_backward(probs, chosen, gate, owned, gates_ref, normed_f, router_ref, grows_ref, mixed, cot_ref, gain_f):
    grad_gate = jnp.sum(jnp.where(owned, gates_ref[...], 0.0), axis=-1, keepdims=True)
    grad_logits = (probs * (jnp.where(chosen, grad_gate, 0.0) - gate * grad_gate)).astype(BF16)
    grad_router = dot_tn(normed_f[...], grad_logits)
    grad_normed = dot_nt(grad_logits, router_ref[...]) + dot_nn(owned.astype(BF16), grows_ref[...])
    grad_norm, grad_gain = norm_backward(mixed, inverse_rms(mixed), gain_f[...], grad_normed)
    return grad_router, cot_ref[...].astype(F32) + grad_norm, grad_gain


def attention_setup(q_ref, k_ref, normed_ref, att_ref, lse_ref, datt, q_t, k_t, normed_t, datt_t, delta, lse_t):
    count, width = q_ref.shape
    head_dim = width // HEADS
    datt_t[...] = datt[...].T
    q_t[...] = (q_ref[...] * jnp.asarray(head_dim**-0.5, BF16)).T
    k_t[...] = k_ref[...].T
    normed_t[...] = normed_ref[...].T
    products = datt_t[...].astype(F32) * att_ref[...].T.astype(F32)
    delta[...] = jnp.sum(products.reshape(HEADS, head_dim, count), axis=1)
    lse_t[...] = lse_ref[...].T


def pair_backward(
    at, rel_ref, near_ref, q_ref, k_ref, v_ref, q_t, k_t, datt, datt_t, delta, lse_t, dst, gq, gk, gv, gnear_ref, gfar_ref
):
    count, width = q_ref.shape
    head_dim = width // HEADS
    blocks = count // BLOCK
    bucket_count = rel_ref.shape[0]
    first = lax.broadcasted_iota(jnp.int32, (1, BLOCK), 1) < head_dim
    cols = pl.ds(pl.multiple_of(at * BLOCK, BLOCK), BLOCK)
    q_pair, datt_pair = q_ref[:, cols], datt[:, cols]
    gq_parts, gk_parts, gv_parts = [], [], []
    for half in range(2):
        head = 2 * at + half
        low, high = rel_ref[bucket_count // 2 - 1, head], rel_ref[bucket_count - 1, head]
        mask = first if half == 0 else jnp.logical_not(first)
        near = toeplitz_near(near_ref[pl.ds(head, 1), :])
        lse_row, delta_row = lse_t[pl.ds(head, 1), :], delta[pl.ds(head, 1), :]
        near_sum = jnp.zeros((BLOCK, 3 * BLOCK), F32)
        low_sum, high_sum = jnp.zeros((BLOCK, BLOCK), F32), jnp.zeros((BLOCK, BLOCK), F32)
        gk_rows, gv_rows = [], []
        for row in range(blocks):
            rows = slice(row * BLOCK, (row + 1) * BLOCK)
            k_rows, v_rows = k_ref[rows, cols], v_ref[rows, cols]
            zeros = jnp.zeros_like(k_rows)
            scores = dot_nn(jnp.where(mask, k_rows, zeros), q_t[cols, :])
            scores = scores + bias_rows(near, high, low, row, blocks)
            weights = jnp.exp(scores - lse_row)
            grad_weights = dot_nn(jnp.where(mask, v_rows, zeros), datt_t[cols, :])
            grad_scores = weights * (grad_weights - delta_row)
            gv_rows.append(dot_nn(weights.astype(BF16), datt_pair))
            low_bits = grad_scores.astype(BF16)
            dst[rows, :] = low_bits
            gk_rows.append(dot_nn(low_bits, q_pair))
            for column in range(blocks):
                piece = grad_scores[:, column * BLOCK : (column + 1) * BLOCK]
                distance = column - row
                if distance <= -2:
                    high_sum = high_sum + piece
                elif distance >= 2:
                    low_sum = low_sum + piece
                else:
                    pads = [jnp.zeros((BLOCK, BLOCK), F32)] * 3
                    pads[distance + 1] = piece
                    near_sum = near_sum + jnp.concatenate(pads, axis=1)
        gq_parts.append(
            dot_nn(k_t[pl.ds(pl.multiple_of(head * head_dim, head_dim), head_dim), :], dst[...])
        )
        gk_parts.append(jnp.concatenate(gk_rows, axis=0))
        gv_parts.append(jnp.concatenate(gv_rows, axis=0))
        gnear_ref[pl.ds(head, 1), :] = diagonal_sums(near_sum)
        gfar_ref[pl.ds(head, 1), :] = jnp.concatenate(
            [jnp.sum(low_sum, axis=0, keepdims=True), jnp.sum(high_sum, axis=0, keepdims=True)], axis=1
        )
    scale = head_dim**-0.5
    gq[:, cols] = (jnp.concatenate(gq_parts, axis=0).T * scale).astype(BF16)
    gk[:, cols] = (jnp.where(first, gk_parts[0], gk_parts[1]) * scale).astype(BF16)
    gv[:, cols] = jnp.where(first, gv_parts[0], gv_parts[1]).astype(BF16)


def input_backward(x_ref, w_ref, gain_a, gmixed, gq, gk, gv):
    count, width = x_ref.shape
    grad_normed = jnp.zeros((count, width), F32)
    for at, grad in enumerate((gq, gk, gv)):
        grad_normed = grad_normed + dot_nt(grad[...], w_ref[:, at * width : (at + 1) * width])
    tokens = x_ref[...].astype(F32)
    grad_norm, grad_gain = norm_backward(tokens, inverse_rms(tokens), gain_a[...], grad_normed)
    return gmixed[...] + grad_norm, grad_gain


def backward_kernel(
    rel_ref, x_ref, w_ref, gain_a, gain_f, router_ref, near_ref, slot_col, routes_ref,
    normed_ref, q_ref, k_ref, v_ref, att_ref, lse_ref, mixed_ref, normed_f, cot_ref, outs_ref, grows_ref, gates_ref,
    result_ref, gx_ref, gw_ref, grouter_ref, gnear_ref, gfar_ref, ggain_ref,
    q_t, k_t, normed_t, datt, datt_t, delta, lse_t, gq, gk, gv, gmixed, dst,
):
    width = x_ref.shape[1]
    probs, chosen, gate = routed_gate(normed_f, router_ref, routes_ref)
    owned = slot_owners(slot_col, outs_ref.shape[0])
    mixed = mixed_ref[...]
    result_ref[...] = (mixed + gate * dot_nn(owned.astype(BF16), outs_ref[...])).astype(BF16)
    grouter_ref[...], grad_mixed, ggain_ref[1:2, :] = ffn_backward(
        probs, chosen, gate, owned, gates_ref, normed_f, router_ref, grows_ref, mixed, cot_ref, gain_f
    )
    gmixed[...] = grad_mixed
    branch = grad_mixed.astype(BF16)
    gw_ref[:, 3 * width : 4 * width] = dot_tn(att_ref[...], branch).astype(BF16)
    datt[...] = dot_nt(branch, w_ref[:, 3 * width : 4 * width]).astype(BF16)
    attention_setup(q_ref, k_ref, normed_ref, att_ref, lse_ref, datt, q_t, k_t, normed_t, datt_t, delta, lse_t)

    def pair(at, carry):
        pair_backward(
            at, rel_ref, near_ref, q_ref, k_ref, v_ref, q_t, k_t, datt, datt_t, delta, lse_t, dst, gq, gk, gv,
            gnear_ref, gfar_ref,
        )
        return carry

    lax.fori_loop(0, HEADS // 2, pair, 0)
    for at, grad in enumerate((gq, gk, gv)):
        gw_ref[:, at * width : (at + 1) * width] = dot_nn(normed_t[...], grad[...]).astype(BF16)
    gx_ref[...], ggain_ref[0:1, :] = input_backward(x_ref, w_ref, gain_a, gmixed, gq, gk, gv)


class Sums:
    def __init__(self, place, unit, buffers, semaphores, out):
        self.p, self.unit, self.out = place, unit, out
        self.send, self.core, self.first_in, self.second_in, self.z_in, self.last = buffers
        self.s, self.r = semaphores
        self.deep = place.deep
        p, c = place, place.c
        self.first, self.second = p.y + c * (p.x - p.y), p.x + c * (p.y - p.x)
        row, side = p.row, p.side
        self.first_peer = tuple(a + c * (b - a) for a, b in zip(row, side))
        self.second_peer = tuple(b + c * (a - b) for a, b in zip(row, side))

    def store(self, buffer, part, core):
        rows, cols = buffer.shape[-2:]
        blocks = part.reshape(self.deep, 2, 2, rows, cols)
        for y in range(2):
            for x in range(2):
                first, second = (y, x) if y == x else (y + core * (x - y), x + core * (y - x))
                buffer[self.unit, first, second] = blocks[:, y, x].astype(buffer.dtype)

    def to_core(self):
        u, p = self.unit, self.p
        return remote(self.send.at[u], self.core.at[u], self.s.at[u, 0], self.r.at[u, 0], p.core)

    def to_y(self):
        u = self.unit
        return remote(self.core.at[u, 1 - self.first], self.first_in.at[u], self.s.at[u, 1], self.r.at[u, 1], self.first_peer)

    def to_x(self):
        u = self.unit
        return remote(self.first_in.at[u, 1 - self.second], self.second_in.at[u], self.s.at[u, 2], self.r.at[u, 2], self.second_peer)

    def to_z(self, k):
        u, p = self.unit, self.p
        z = lax.rem(p.z + k, p.deep)
        return remote(
            self.second_in.at[u, z], self.z_in.at[u, k], self.s.at[u, 3 + k], self.r.at[u, 3 + k], (z * 2 + p.y, p.n)
        )

    def to_last(self):
        u, p = self.unit, self.p
        return remote(self.last.at[u, 1 - p.c], self.out.at[u, p.c], self.s.at[u, 3], self.r.at[u, 3], p.core)

    def begin(self, part):
        self.store(self.send, part, 1 - self.p.c)
        self.to_core().start()

    def stage_core(self, part):
        u = self.unit
        self.to_core().wait_recv()
        rows, cols = self.core.shape[-2:]
        blocks = part.reshape(self.deep, 2, 2, rows, cols)
        c = self.p.c
        for y in range(2):
            for x in range(2):
                first, second = (y, x) if y == x else (y + c * (x - y), x + c * (y - x))
                kept = blocks[:, y, x] + self.core[u, first, second].astype(F32)
                self.core[u, first, second] = kept.astype(BF16)
        self.to_y().start()

    def stage_y(self):
        u = self.unit
        self.to_y().wait_recv()
        self.first_in[u] = (self.core[u, self.first].astype(F32) + self.first_in[u].astype(F32)).astype(BF16)
        self.to_x().start()

    def stage_x(self):
        u = self.unit
        self.to_x().wait_recv()
        self.second_in[u] = (self.first_in[u, self.second].astype(F32) + self.second_in[u].astype(F32)).astype(BF16)
        for k in range(1, self.p.deep):
            self.to_z(k).start()

    def stage_z(self):
        u = self.unit
        total = self.second_in[u, self.p.z].astype(F32)
        for k in range(1, self.p.deep):
            self.to_z(k).wait_recv()
            total = total + self.z_in[u, k].astype(F32)
        self.last[u] = total.reshape(self.last.shape[1:])
        self.to_last().start()
        self.out[u, self.p.c] = self.last[u, self.p.c]

    def drain(self):
        for copy in (self.to_core(), self.to_y(), self.to_x()):
            copy.wait_send()
        for k in range(1, self.p.deep):
            self.to_z(k).wait_send()
        self.to_last().wait()


def sum_buffers(units, wide, rows, cols):
    deep = wide // 2
    vmem = lambda *shape, dtype=BF16: pltpu.VMEM((units, *shape), dtype)
    return [
        vmem(2, 2, deep, rows, cols), vmem(2, 2, deep, rows, cols), vmem(2, deep, rows, cols), vmem(deep, rows, cols),
        vmem(deep, rows, cols), vmem(2, rows // 2, cols, dtype=F32),
        pltpu.SemaphoreType.DMA((units, 3 + deep)), pltpu.SemaphoreType.DMA((units, 3 + deep)),
    ]


def moving_backward_kernel(
    rel_ref, x_hbm, w_hbm, normed_hbm, q_hbm, k_hbm, v_hbm, att_hbm, lse_hbm, outs_hbm,
    gains_ref, router_ref, near_ref, slot_col, routes_ref, mixed_ref, normed_f, cot_ref, grows_ref, gates_ref, picks_ref,
    result_ref, gx_ref, gw_out, go_out, small_out,
    x_ref, w_ref, normed_ref, q_ref, k_ref, v_ref, att_ref, lse_ref, load_s,
    q_t, k_t, normed_t, datt, datt_t, delta, lse_t, gq, gk, gv, gmixed, gnormed, dst, gnear, gfar,
    own, from_core, from_side, returned, own_s, rc_s, rc_r, rx_s, rx_r, rw_s, rw_r,
    u1, u2, u3, u4, u5, u6, us, ur, o1, o2, o3, o4, o5, o6, os, orr,
    small, small_in, ss, sr,
):
    count, width = x_hbm.shape
    wide, local, slots, _ = returned.shape
    total = wide * local * slots
    p = Place(wide)
    far_x = (1 - p.x) * 2
    units = HEADS // 4
    gain_a, gain_f = gains_ref.at[0:1, :], gains_ref.at[1:2, :]
    loads = [
        pltpu.make_async_copy(source, target, load_s.at[at])
        for at, (source, target) in enumerate((
            (att_hbm, att_ref), (w_hbm, w_ref), (q_hbm, q_ref), (k_hbm, k_ref), (normed_hbm, normed_ref),
            (lse_hbm, lse_ref), (v_hbm, v_ref), (x_hbm, x_ref),
        ))
    ]

    def partial(e, other, core):
        return outs_hbm.at[e, (far_x if other else p.x * 2) + core]

    back = Collect(
        p, lambda e, other: partial(e, other, 1 - p.c), from_core, from_side, returned, (rc_s, rc_r, rx_s, rx_r, rw_s, rw_r)
    )

    def own_copy(e, other):
        return pltpu.make_async_copy(partial(e, other, p.c), own.at[e, other], own_s.at[e, other])

    for other in (1, 0):
        for e in range(local):
            own_copy(e, other).start()
    for copy in loads:
        copy.start()
    greet(p.partners())
    for other in (1, 0):
        for e in range(local):
            back.core(e, other).start()

    def over_side(e):
        own_copy(e, 1).wait()
        back.go_beside(e, own[e, 1])

    def finish(e):
        back.core(e, 0).wait_recv()
        own_copy(e, 0).wait()

        def own_sums(rows):
            return own[e, 0, rows].astype(F32) + from_core[e, 0, rows].astype(F32)

        back.finish(e, 1, own_sums)
        back.finish(e, 0, own_sums)

    probs, chosen, gate = routed_gate(normed_f, router_ref, routes_ref)
    over_side(0)
    owned = slot_owners(slot_col, total)
    grad_router, grad_mixed, grad_gain_f = ffn_backward(
        probs, chosen, gate, owned, gates_ref, normed_f, router_ref, grows_ref, mixed_ref[...], cot_ref, gain_f
    )
    gmixed[...] = grad_mixed
    small[0] = jnp.zeros_like(small[0])
    small[0, HEADS : HEADS + 1, :] = grad_gain_f
    over_side(1)
    loads[0].wait()
    branch = grad_mixed.astype(BF16)
    o_sums = Sums(p, 0, (o1, o2, o3, o4, o5, o6), (os, orr), go_out)
    half_cols = width // 2
    router_cols = go_out.shape[-1] - half_cols
    router_wide = jnp.concatenate(
        [grad_router, jnp.zeros((width, router_cols - grad_router.shape[1]), F32)], axis=1
    )

    def output_part(core):
        low, high = branch[:, :half_cols], branch[:, half_cols:]
        part = dot_tn(att_ref[...], jnp.where(core == 0, low, high))
        return jnp.concatenate([part, jnp.where(core == 0, router_wide, 0.0)], axis=1)

    o_sums.begin(output_part(1 - p.c))
    loads[1].wait()
    datt[...] = (
        dot_nt(branch[:, :half_cols], w_ref[units, 0]) + dot_nt(branch[:, half_cols:], w_ref[units, 1])
    ).astype(BF16)
    o_sums.stage_core(output_part(p.c))
    for copy in loads[2:]:
        copy.wait()
    attention_setup(q_ref, k_ref, normed_ref, att_ref, lse_ref, datt, q_t, k_t, normed_t, datt_t, delta, lse_t)

    def pair(at):
        pair_backward(
            at, rel_ref, near_ref, q_ref, k_ref, v_ref, q_t, k_t, datt, datt_t, delta, lse_t, dst, gq, gk, gv,
            gnear, gfar,
        )
        cols = pl.ds(pl.multiple_of(at * BLOCK, BLOCK), BLOCK)
        grads = jnp.concatenate([gq[:, cols], gk[:, cols], gv[:, cols]], axis=1)
        gnormed[...] += dot_nt(grads, w_ref[at // 2, lax.rem(at, 2)])
        return dot_nn(normed_t[...], grads)

    def unit(u):
        return Sums(p, u, (u1, u2, u3, u4, u5, u6), (us, ur), gw_out)

    gnormed[...] = jnp.zeros_like(gnormed)
    finish(0)
    over_side(2)

    def pairs(u, carry):
        unit(u).begin(pair(2 * u + 1 - p.c))

        @pl.when(u == 0)
        def _():
            o_sums.stage_y()

        @pl.when(u == 1)
        def _():
            o_sums.stage_x()

        @pl.when(u == 2)
        def _():
            o_sums.stage_z()

        unit(u).stage_core(pair(2 * u + p.c))
        finish(u + 1)

        @pl.when(u + 3 < local)
        def _():
            over_side(u + 3)

        @pl.when(u >= 1)
        def _():
            unit(u - 1).stage_y()

        @pl.when(u >= 2)
        def _():
            unit(u - 2).stage_x()

        return carry

    lax.fori_loop(0, units, pairs, 0)
    near_grads = jnp.dot(gnear[...], picks_ref[...], precision=HIGHEST, preferred_element_type=F32)
    buckets = lax.broadcasted_iota(jnp.int32, near_grads.shape, 1)
    low_sum = jnp.sum(gfar[:, :BLOCK], axis=1, keepdims=True)
    high_sum = jnp.sum(gfar[:, BLOCK:], axis=1, keepdims=True)
    bucket_count = rel_ref.shape[0]
    rel = near_grads + jnp.where(buckets == bucket_count // 2 - 1, low_sum, 0.0)
    small[0, :HEADS, :BLOCK] = rel + jnp.where(buckets == bucket_count - 1, high_sum, 0.0)
    tokens = x_ref[...].astype(F32)
    grad_norm, grad_gain_a = norm_backward(tokens, inverse_rms(tokens), gain_a[...], gnormed[...])
    gx_ref[...] = gmixed[...] + grad_norm
    small[0, HEADS + 1 : HEADS + 2, :] = grad_gain_a

    def small_copy(stage, device, slot):
        return remote(small.at[stage], small_in.at[slot], ss.at[slot], sr.at[slot], device)

    hops = [[p.core], [p.row], [p.side], [(lax.rem(p.z + k, p.deep) * 2 + p.y, p.n) for k in range(1, p.deep)]]
    copies, slot = [], 0
    for stage, devices in enumerate(hops):
        copies.append([small_copy(stage, device, slot + at) for at, device in enumerate(devices)])
        slot += len(devices)

    def small_start(stage):
        for copy in copies[stage]:
            copy.start()

    def small_end(stage):
        slot = sum(len(c) for c in copies[:stage])
        found = small[stage]
        for at, copy in enumerate(copies[stage]):
            copy.wait_recv()
            found = found + small_in[slot + at]
        return found

    small_start(0)
    last = unit(units - 1)
    last.stage_y()
    unit(units - 2).stage_x()
    small[1] = small_end(0)
    small_start(1)
    unit(units - 3).stage_z()
    small[2] = small_end(1)
    small_start(2)
    last.stage_x()
    unit(units - 2).stage_z()
    small[3] = small_end(2)
    small_start(3)
    for e in range(local):
        back.arrive(e)
    combined = dot_nn(owned.astype(BF16), returned[...].reshape(total, width))
    result_ref[...] = (mixed_ref[...] + gate * combined).astype(BF16)
    last.stage_z()
    small_out[...] = small_end(3)
    for e in range(local):
        back.drain(e)
    o_sums.drain()
    for u in range(units):
        unit(u).drain()
    for stage in copies:
        for copy in stage:
            copy.wait_send()


def moving_backward(
    rel_bias, inputs, weights, gains, router, near, slot_col, routes,
    normed, q, k, v, att, lse, mixed, normed_f, cotangent, outs, grows, gates, wide, slots,
):
    count, width = inputs.shape
    local, narrow = outs.shape[:2]
    experts = router.shape[1]
    bucket_count = rel_bias.shape[0]
    deep, rows = wide // 2, width // (wide * 2)
    units = HEADS // 4
    pair_cols, out_cols = 3 * BLOCK, width // 2 + BLOCK * -(-experts // BLOCK)
    sds = jax.ShapeDtypeStruct
    smem = pl.BlockSpec(memory_space=pltpu.SMEM)
    any_spec = pl.BlockSpec(memory_space=pl.ANY)
    picks = np.zeros((4 * BLOCK, BLOCK), np.float32)
    picks[:, :bucket_count] = near_picks(bucket_count, -1)
    wide_t = lambda dtype: pltpu.VMEM((width, count), dtype)
    tall = lambda dtype: pltpu.VMEM((count, width), dtype)
    vmem = lambda *shape, dtype=BF16: pltpu.VMEM(shape, dtype)
    dma = pltpu.SemaphoreType.DMA
    hops = 3 + deep - 1
    result, grad_inputs, gw, go, small = pl.pallas_call(
        moving_backward_kernel,
        out_shape=(
            sds((count, width), BF16), sds((count, width), F32), sds((units, 2, rows // 2, pair_cols), F32),
            sds((1, 2, rows // 2, out_cols), F32), sds((16, width), F32),
        ),
        in_specs=[smem] + [any_spec] * 9 + in_vmem(11),
        out_specs=tuple(in_vmem(5)),
        scratch_shapes=[
            tall(BF16), pltpu.VMEM(weights.shape, BF16), tall(BF16), tall(BF16), tall(BF16), tall(BF16), tall(BF16),
            vmem(count, BLOCK, dtype=F32), dma((8,)),
            wide_t(BF16), wide_t(BF16), wide_t(BF16), tall(BF16), wide_t(BF16),
            vmem(HEADS, count, dtype=F32), vmem(BLOCK, count, dtype=F32),
            tall(BF16), tall(BF16), tall(BF16), tall(F32), tall(F32), vmem(count, count),
            vmem(HEADS, 4 * BLOCK, dtype=F32), vmem(HEADS, 2 * BLOCK, dtype=F32),
            vmem(local, 2, wide, slots, width), vmem(local, 2, wide, slots, width), vmem(local, wide, slots, width),
            vmem(wide, local, slots, width),
            dma((local, 2)), dma((local, 2)), dma((local, 2)), dma((local, 2)), dma((local, 2)),
            dma((local, wide)), dma((local, wide)),
            *sum_buffers(units, wide, rows, pair_cols), *sum_buffers(1, wide, rows, out_cols),
            vmem(4, 16, width, dtype=F32), vmem(hops, 16, width, dtype=F32), dma((hops,)), dma((hops,)),
        ],
        compiler_params=pltpu.CompilerParams(collective_id=3, has_side_effects=True, vmem_limit_bytes=62 << 20),
        name="backward",
    )(
        rel_bias, inputs, weights, normed, q, k, v, att, lse, outs,
        gains, router, near, slot_col, routes, mixed, normed_f, cotangent, grows, gates, jnp.asarray(picks),
    )
    kinds = [
        jnp.transpose(gw[..., at * BLOCK : (at + 1) * BLOCK], (2, 0, 1, 3)).reshape(rows // 2, width) for at in range(3)
    ]
    grad_output = jnp.transpose(go[0, :, :, : width // 2], (1, 0, 2)).reshape(rows // 2, width)
    grad_router = go[0, 0, :, width // 2 : width // 2 + experts]
    device = lax.axis_index("wide") * narrow + lax.axis_index("narrow")
    gain_grads = lax.dynamic_slice(small, (HEADS, device * (rows // 2)), (2, rows // 2))
    grad_rel = small[:HEADS, :bucket_count].T
    return result, grad_inputs, kinds, grad_output, grad_router, gain_grads[1], gain_grads[0], grad_rel


def in_vmem(count):
    return [pl.BlockSpec(memory_space=pltpu.VMEM)] * count


def shards(
    inputs, gain_attn, w_query, w_key, w_value, w_output, rel_bias, gain_ffn, w_router,
    expert_in, expert_out, routes, capacity, cotangent,
):
    count, width = inputs.shape
    experts = w_router.shape[1]
    local, _, hidden_width = expert_in.shape
    wide, narrow = lax.axis_size("wide"), lax.axis_size("narrow")
    slots = 2 * count // experts
    total = experts * slots
    bucket_count = rel_bias.shape[0]
    params = pltpu.CompilerParams(vmem_limit_bytes=60 << 20)
    smem = pl.BlockSpec(memory_space=pltpu.SMEM)

    near = jnp.dot(near_picks(bucket_count, 1), rel_bias, precision=HIGHEST).T
    near_back = jnp.dot(near_picks(bucket_count, -1), rel_bias, precision=HIGHEST).T

    moving = narrow == 4 and wide & (wide - 1) == 0 and local == HEADS // 4 + 1 and slots % 16 == 0 and local * slots % BLOCK == 0
    moving = moving and width % (wide * 2 * 16) == 0 and count == SEQ_LEN and experts + 8 <= BLOCK
    if moving:
        normed, q, k, v, att, lse, mixed, normed_f, sent, slot_col, router, gains, weights, cot_all = moving_forward(
            rel_bias, capacity, inputs, w_query, w_key, w_value, w_output, w_router, gain_attn, gain_ffn, near, routes,
            cotangent, wide, narrow, local, slots,
        )
        outs, back, gates, gin, gout = moving_experts(sent, cot_all, expert_in, expert_out, router, wide, narrow)
        result, grad_inputs, kinds, grad_output, grad_router, grad_gain_a, grad_gain_f, grad_rel = moving_backward(
            rel_bias, inputs, weights.reshape(HEADS // 4 + 1, 2, width, width // 2), gains, router, near_back,
            slot_col, routes, normed, q, k, v, att, lse, mixed, normed_f, cotangent, outs,
            back.reshape(total, width), gates.reshape(1, total), wide, slots,
        )
        return (
            result, grad_inputs, grad_gain_a, *kinds, grad_output, grad_rel, grad_gain_f, grad_router, gin, gout,
        )

    packed = jnp.concatenate([w_query, w_key, w_value, w_output], axis=1)
    weights = lax.all_gather(packed, BOTH, axis=0, tiled=True)
    small = lax.all_gather(
        jnp.concatenate([w_router, gain_attn[:, None], gain_ffn[:, None]], axis=1), BOTH, axis=0, tiled=True
    )
    router = small[:, :experts]
    gain_a = small[:, experts].astype(F32)[None, :]
    gain_f = small[:, experts + 1].astype(F32)[None, :]
    slot_col, slot_row, cot_sent = pl.pallas_call(
        lambda *refs: place_kernel(slots, experts, *refs),
        out_shape=(
            jax.ShapeDtypeStruct((count, 1), jnp.int32),
            jax.ShapeDtypeStruct((1, count), jnp.int32),
            jax.ShapeDtypeStruct((total, width), BF16),
        ),
        in_specs=[smem] + in_vmem(3),
        out_specs=tuple(in_vmem(3)),
        compiler_params=params,
        name="places",
    )(capacity, routes, routes.reshape(1, count), cotangent)

    def spread(rows):
        taken = lax.all_to_all(
            rows.reshape(wide, local * slots, width), "wide", split_axis=0, concat_axis=0, tiled=True
        )
        held = lax.all_gather(taken, "narrow", axis=0, tiled=True)
        return held.reshape(wide * narrow, local, slots, width)

    def collect(rows):
        own = lax.psum_scatter(
            rows.reshape(wide * narrow, local * slots, width), "narrow", scatter_dimension=0, tiled=True
        )
        back = lax.all_to_all(own, "wide", split_axis=0, concat_axis=0, tiled=True)
        return back.reshape(total, width)

    cot_all = spread(cot_sent)

    rows_t = lambda dtype, cols=width: jax.ShapeDtypeStruct((count, cols), dtype)
    normed, q, k, v, att, lse, mixed, normed_f, sent = pl.pallas_call(
        forward_kernel,
        out_shape=(
            rows_t(BF16), rows_t(BF16), rows_t(BF16), rows_t(BF16), rows_t(BF16), rows_t(F32, BLOCK),
            rows_t(F32), rows_t(BF16), jax.ShapeDtypeStruct((total, width), BF16),
        ),
        in_specs=[smem] + in_vmem(7),
        out_specs=tuple(in_vmem(9)),
        compiler_params=params,
        name="forward",
    )(rel_bias, inputs, weights, gain_a, gain_f, router, near, slot_row)

    rows_all = spread(sent)
    sources = wide * narrow
    block = pl.BlockSpec((sources, 1, slots, width), lambda e: (0, e, 0, 0))
    w_in_spec = pl.BlockSpec((1, width, hidden_width), lambda e: (e, 0, 0))
    w_out_spec = pl.BlockSpec((1, hidden_width, width), lambda e: (e, 0, 0))
    first_expert = (lax.axis_index("wide") * local).astype(jnp.int32)[None]
    back, grows, gin, gout = pl.pallas_call(
        expert_kernel,
        grid=(local,),
        out_shape=(
            jax.ShapeDtypeStruct(rows_all.shape, BF16),
            jax.ShapeDtypeStruct(rows_all.shape, BF16),
            jax.ShapeDtypeStruct(expert_in.shape, F32),
            jax.ShapeDtypeStruct(expert_out.shape, F32),
        ),
        in_specs=[
            smem, block, block, w_in_spec, w_out_spec, pl.BlockSpec((width, experts), lambda e: (0, 0)),
        ],
        out_specs=(block, block, w_in_spec, w_out_spec),
        scratch_shapes=[
            pltpu.VMEM((sources * slots, hidden_width), BF16),
            pltpu.VMEM((sources * slots, hidden_width), BF16),
            pltpu.VMEM((sources * slots, width), BF16),
        ],
        compiler_params=params,
        name="experts",
    )(first_expert, rows_all, cot_all, expert_in, expert_out, router)
    outs_back = collect(back)
    grows_back = collect(grows)
    gates = jnp.sum(outs_back.astype(F32) * cot_sent.astype(F32), axis=1)[None, :]

    wide_t = lambda dtype: pltpu.VMEM((width, count), dtype)
    tall = lambda dtype: pltpu.VMEM((count, width), dtype)
    result, grad_inputs, gw, grouter, gnear, gfar, ggain = pl.pallas_call(
        backward_kernel,
        out_shape=(
            rows_t(BF16), rows_t(F32), jax.ShapeDtypeStruct((width, 4 * width), BF16),
            jax.ShapeDtypeStruct((width, experts), F32), jax.ShapeDtypeStruct((HEADS, 4 * BLOCK), F32),
            jax.ShapeDtypeStruct((HEADS, 2 * BLOCK), F32), jax.ShapeDtypeStruct((2, width), F32),
        ),
        in_specs=[smem] + in_vmem(20),
        out_specs=tuple(in_vmem(7)),
        scratch_shapes=[
            wide_t(BF16), wide_t(BF16), wide_t(BF16), tall(BF16), wide_t(BF16),
            pltpu.VMEM((HEADS, count), F32), pltpu.VMEM((BLOCK, count), F32),
            tall(BF16), tall(BF16), tall(BF16), tall(F32), pltpu.VMEM((count, count), BF16),
        ],
        compiler_params=params,
        name="backward",
    )(
        rel_bias, inputs, weights, gain_a, gain_f, router, near_back, slot_col, routes,
        normed, q, k, v, att, lse, mixed, normed_f, cotangent, outs_back, grows_back, gates,
    )

    gw = lax.psum_scatter(gw, BOTH, scatter_dimension=0, tiled=True).astype(F32)
    grad_query, grad_key, grad_value, grad_output = (gw[:, i * width : (i + 1) * width] for i in range(4))
    gsmall = lax.psum_scatter(
        jnp.concatenate([grouter, ggain.T], axis=1), BOTH, scatter_dimension=0, tiled=True
    )
    grad_rel = jnp.dot(near_picks(bucket_count, -1).T, gnear.T, precision=HIGHEST)
    low, high = jnp.sum(gfar[:, :BLOCK], axis=1), jnp.sum(gfar[:, BLOCK:], axis=1)
    grad_rel = grad_rel.at[bucket_count // 2 - 1].add(low).at[bucket_count - 1].add(high)
    grad_rel = lax.psum(grad_rel, BOTH)
    return (
        result, grad_inputs, gsmall[:, experts], grad_query, grad_key, grad_value, grad_output,
        grad_rel, gsmall[:, experts + 1], gsmall[:, :experts], gin, gout,
    )


def solution(mesh):
    return jax.shard_map(
        shards,
        mesh=mesh,
        in_specs=(
            P(BOTH, None),
            P(BOTH),
            P(BOTH, None),
            P(BOTH, None),
            P(BOTH, None),
            P(BOTH, None),
            P(),
            P(BOTH),
            P(BOTH, None),
            P("wide", None, "narrow"),
            P("wide", "narrow", None),
            P(BOTH, None),
            P(BOTH),
            P(BOTH, None),
        ),
        out_specs=(
            P(BOTH, None),
            P(BOTH, None),
            P(BOTH),
            P(BOTH, None),
            P(BOTH, None),
            P(BOTH, None),
            P(BOTH, None),
            P(),
            P(BOTH),
            P(BOTH, None),
            P("wide", None, "narrow"),
            P("wide", "narrow", None),
        ),
        check_vma=False,
    )
```

```python
import jax
import jax.numpy as jnp
import numpy as np
from jax import lax
from jax.experimental import pallas as pl
from jax.experimental.pallas import tpu as pltpu
from jax.sharding import PartitionSpec as P

HEADS = 12
SEQ_LEN = 512
BLOCK = 128
EPSILON = 1e-06
HIGHEST = lax.Precision.HIGHEST
ROOT_TWO_PI = 0.7978845608028654
CUBIC = 0.044715
BOTH = ("wide", "narrow")
F32 = jnp.float32
BF16 = jnp.bfloat16


def bucket_of(offsets, bucket_count):
    half_count = bucket_count // 2
    exact_count = half_count // 2
    distance = np.abs(offsets)
    scaled = exact_count + np.floor(
        np.log(np.maximum(distance, 1) / exact_count)
        / np.log(128.0 / exact_count)
        * (half_count - exact_count)
    ).astype(np.int64)
    scaled = np.minimum(scaled, half_count - 1)
    return ((offsets > 0) * half_count + np.where(distance < exact_count, distance, scaled)).astype(
        np.int32
    )


def near_picks(bucket_count, sign):
    offsets = sign * (np.arange(4 * BLOCK) - (2 * BLOCK - 1))
    picks = (bucket_of(offsets, bucket_count)[:, None] == np.arange(bucket_count)[None, :]).astype(
        np.float32
    )
    picks[-1] = 0.0
    return picks


def dot_nn(left, right):
    return lax.dot_general(left, right, (((1,), (0,)), ((), ())), preferred_element_type=F32)


def dot_nt(left, right):
    return lax.dot_general(left, right, (((1,), (1,)), ((), ())), preferred_element_type=F32)


def dot_tn(left, right):
    return lax.dot_general(left, right, (((0,), (0,)), ((), ())), preferred_element_type=F32)


def inverse_rms(values):
    return lax.rsqrt(jnp.mean(values * values, axis=-1, keepdims=True) + EPSILON)


def norm_backward(values, inverse, gain, grad_normed):
    scaled = grad_normed * gain
    grad_gain = jnp.sum(grad_normed * values * inverse, axis=0, keepdims=True)
    inner = jnp.mean(scaled * values, axis=-1, keepdims=True)
    return (inverse * (scaled - values * inverse * inverse * inner), grad_gain)


def softmax_lanes(logits):
    peak = jnp.max(logits, axis=-1, keepdims=True)
    exponent = jnp.exp(logits - peak)
    return exponent / jnp.sum(exponent, axis=-1, keepdims=True)


def toeplitz_near(near_row):
    spread = jnp.broadcast_to(near_row, (BLOCK, 4 * BLOCK))
    return pltpu.roll(spread, 3 * BLOCK + 1, 1, stride=1, stride_axis=0)[:, : 3 * BLOCK]


def bias_rows(near, far_low, far_high, row, blocks):
    pieces = []
    for column in range(blocks):
        distance = column - row
        if distance <= -2:
            pieces.append(jnp.full((BLOCK, BLOCK), far_low, F32))
        elif distance >= 2:
            pieces.append(jnp.full((BLOCK, BLOCK), far_high, F32))
        else:
            pieces.append(near[:, (distance + 1) * BLOCK : (distance + 2) * BLOCK])
    return jnp.concatenate(pieces, axis=1)


def diagonal_sums(near_sum):
    padded = jnp.concatenate([near_sum, jnp.zeros((BLOCK, BLOCK), F32)], axis=1)
    groups = jnp.zeros((8, 4 * BLOCK), F32)
    for at in range(0, BLOCK, 8):
        groups = groups + pltpu.roll(padded[at : at + 8, :], BLOCK - 8 - at, 1)
    sums = groups[7:8, :]
    for at in range(7):
        sums = sums + pltpu.roll(groups[at : at + 1, :], 7 - at, 1)
    return sums


def slot_places(routes_ref, row_ref, limit, experts, slots, count):
    lower = lax.broadcasted_iota(jnp.int32, (count, count), 0)
    upper = lax.broadcasted_iota(jnp.int32, (count, count), 1)
    col = routes_ref[...]
    chosen = lax.broadcasted_iota(jnp.int32, (count, experts), 1) == col
    running = dot_nn((upper <= lower).astype(BF16), chosen.astype(BF16))
    place = jnp.sum(jnp.where(chosen, running, 0.0), axis=1, keepdims=True).astype(jnp.int32) - 1
    slot_col = jnp.where(place < limit, col * slots + place, -1)
    row = row_ref[...]
    chosen_t = lax.broadcasted_iota(jnp.int32, (experts, count), 0) == row
    running_t = dot_nn(chosen_t.astype(BF16), (lower <= upper).astype(BF16))
    place_t = (
        jnp.sum(jnp.where(chosen_t, running_t, 0.0), axis=0, keepdims=True).astype(jnp.int32) - 1
    )
    slot_row = jnp.where(place_t < limit, row * slots + place_t, -1)
    return slot_col, slot_row


def place_kernel(slots, experts, capacity_ref, routes_ref, row_ref, cot_ref, slot_col, slot_row, cot_out):
    count = routes_ref.shape[0]
    limit = capacity_ref[0] * count // experts
    col, row = slot_places(routes_ref, row_ref, limit, experts, slots, count)
    slot_col[...] = col
    slot_row[...] = row
    picks = (lax.broadcasted_iota(jnp.int32, (experts * slots, count), 0) == row).astype(BF16)
    cot_out[...] = dot_nn(picks, cot_ref[...]).astype(BF16)


def pair_forward(at, rel_ref, near_ref, q_ref, k_ref, v_ref, att_ref, lse_ref):
    count, width = q_ref.shape
    head_dim = width // HEADS
    blocks = count // BLOCK
    bucket_count = rel_ref.shape[0]
    lanes = lax.broadcasted_iota(jnp.int32, (1, BLOCK), 1)
    first = lanes < head_dim
    cols = pl.ds(pl.multiple_of(at * BLOCK, BLOCK), BLOCK)
    k_pair, v_pair = k_ref[:, cols], v_ref[:, cols]
    nears = [toeplitz_near(near_ref[pl.ds(2 * at + half, 1), :]) for half in range(2)]
    for row in range(blocks):
        rows = slice(row * BLOCK, (row + 1) * BLOCK)
        q_rows = q_ref[rows, cols] * jnp.asarray(head_dim**-0.5, BF16)
        found = []
        log_sums = lse_ref[rows, :]
        for half in range(2):
            head = 2 * at + half
            low, high = rel_ref[bucket_count // 2 - 1, head], rel_ref[bucket_count - 1, head]
            mask = first if half == 0 else jnp.logical_not(first)
            scores = dot_nt(jnp.where(mask, q_rows, jnp.zeros_like(q_rows)), k_pair)
            scores = scores + bias_rows(nears[half], low, high, row, blocks)
            peak = jnp.max(scores, axis=-1, keepdims=True)
            exponent = jnp.exp(scores - peak)
            total = jnp.sum(exponent, axis=-1, keepdims=True)
            found.append(dot_nn((exponent * (1.0 / total)).astype(BF16), v_pair))
            log_sums = jnp.where(lanes == head, peak + jnp.log(total), log_sums)
        lse_ref[rows, :] = log_sums
        att_ref[rows, cols] = jnp.where(first, found[0], found[1]).astype(BF16)


def slot_rows(slot_row, values, total):
    picks = lax.broadcasted_iota(jnp.int32, (total, slot_row.shape[1]), 0) == slot_row
    return dot_nn(picks.astype(BF16), values).astype(BF16)


def forward_kernel(
    rel_ref, x_ref, w_ref, gain_a, gain_f, router_ref, near_ref, slot_row,
    normed_ref, q_ref, k_ref, v_ref, att_ref, lse_ref, mixed_ref, normed_f, sent_ref,
):
    width = x_ref.shape[1]
    tokens = x_ref[...].astype(F32)
    normed = (tokens * inverse_rms(tokens) * gain_a[...]).astype(BF16)
    normed_ref[...] = normed
    for out, at in ((q_ref, 0), (k_ref, 1), (v_ref, 2)):
        out[...] = dot_nn(normed, w_ref[:, at * width : (at + 1) * width]).astype(BF16)
    lse_ref[...] = jnp.zeros_like(lse_ref)

    def pair(at, carry):
        pair_forward(at, rel_ref, near_ref, q_ref, k_ref, v_ref, att_ref, lse_ref)
        return carry

    lax.fori_loop(0, HEADS // 2, pair, 0)
    mixed = tokens + dot_nn(att_ref[...], w_ref[:, 3 * width : 4 * width])
    mixed_ref[...] = mixed
    normed_2 = (mixed * inverse_rms(mixed) * gain_f[...]).astype(BF16)
    normed_f[...] = normed_2
    sent_ref[...] = slot_rows(slot_row[...], normed_2, sent_ref.shape[0])


def expert_kernel(
    first_ref, rows_ref, cot_ref, in_ref, out_ref, router_ref,
    back_ref, grows_ref, gin_ref, gout_ref, hidden_ref, gpre_ref, sg_ref,
):
    sources, _, slots, width = rows_ref.shape
    total = sources * slots
    step = min(256, total)
    expert = first_ref[0] + pl.program_id(0)

    def chunk(at, carry):
        these = pl.ds(pl.multiple_of(at * (step // slots), step // slots), step // slots)
        flat = pl.ds(pl.multiple_of(at * step, step), step)
        rows = rows_ref[these, 0].reshape(step, width)
        probs = softmax_lanes(dot_nn(rows, router_ref[...]))
        here = lax.broadcasted_iota(jnp.int32, probs.shape, 1) == expert
        gate = jnp.sum(jnp.where(here, probs, 0.0), axis=-1, keepdims=True)
        sg = (cot_ref[these, 0].reshape(step, width).astype(F32) * gate).astype(BF16)
        sg_ref[flat, :] = sg
        pre = dot_nn(rows, in_ref[0])
        square = pre * pre
        inner = jnp.tanh(pre * (ROOT_TWO_PI + ROOT_TWO_PI * CUBIC * square))
        half = 0.5 * (1.0 + inner)
        hidden = (pre * half).astype(BF16)
        hidden_ref[flat, :] = hidden
        slope = half + 0.5 * pre * (1.0 - inner * inner) * (
            ROOT_TWO_PI + 3.0 * ROOT_TWO_PI * CUBIC * square
        )
        gpre = (dot_nt(sg, out_ref[0]) * slope).astype(BF16)
        gpre_ref[flat, :] = gpre
        back_ref[these, 0] = dot_nn(hidden, out_ref[0]).astype(BF16).reshape(-1, slots, width)
        grows_ref[these, 0] = dot_nt(gpre, in_ref[0]).astype(BF16).reshape(-1, slots, width)
        return carry

    lax.fori_loop(0, total // step, chunk, 0)
    gout_ref[0] = dot_tn(hidden_ref[...], sg_ref[...])
    gin_ref[0] = dot_tn(rows_ref[:, 0].reshape(total, width), gpre_ref[...])


def remote(source, target, send, receive, device):
    return pltpu.make_async_remote_copy(
        src_ref=source,
        dst_ref=target,
        send_sem=send,
        recv_sem=receive,
        device_id=device,
        device_id_type=pl.DeviceIdType.MESH,
    )


def greet(devices):
    for device in devices:
        pl.semaphore_signal(
            pltpu.get_barrier_semaphore(), inc=1, device_id=device, device_id_type=pl.DeviceIdType.MESH
        )


def meet(devices):
    pl.semaphore_wait(pltpu.get_barrier_semaphore(), len(devices))


FORWARD_STEPS = {
    "first": (("send", 4, 0), ("start", 2, 0), ("start", 3, 0), ("send", 0, 0), ("start", 1, 0), ("spread", 4, 0),
        ("send", 1, 0), ("start", 0, 0), ("spread", 0, 0), ("send", 2, 0), ("start", 0, 2), ("forward", 1, 0),
        ("send", 3, 0), ("start", 1, 1), ("over_x", 4, 0), ("over_y", 4, 0), ("forward", 0, 0), ("spread", 1, 0),
        ("end", 4, 0), ("over_x", 0, 0), ("spread", 2, 0), ("start", 3, 2), ("over_y", 1, 0), ("forward", 3, 0),
        ("start", 3, 1), ("over_x", 1, 0), ("over_x", 2, 0), ("end", 0, 0), ("over_y", 0, 0), ("forward", 1, 1),
        ("start", 2, 2),),
    "N0": (("spread", 3, 0),),
    "A0": (("forward", 2, 0), ("pass", 1, 1), ("forward", 3, 1), ("pass", 3, 0), ("over_y", 2, 0),
        ("start", 1, 2), ("forward", 0, 2), ("forward", 3, 2), ("end", 1, 0),),
    "B0": (("start", 2, 1),),
    "A1": (("forward", 2, 2), ("end", 2, 0), ("start", 0, 1), ("over_x", 3, 0),),
    "A2": (("forward", 2, 1), ("forward", 1, 2), ("pass", 1, 0), ("pass", 2, 0), ("pass", 0, 0), ("pass", 3, 2),
        ("pass", 2, 2), ("pass", 0, 2), ("forward", 0, 1), ("end", 3, 0), ("over_y", 3, 0), ("pass", 3, 1),),
    "M0": (("pass", 1, 2), ("pass", 2, 1), ("pass", 0, 1),),
}

BACKWARD_STEPS = {
    "first": (("core", 3, 1), ("core", 2, 1), ("core", 2, 0),),
    "F0": (("go", 2, 1), ("core", 3, 0), ("near", 2, 0),),
    "O0": (("go", 3, 1),),
    "D0": (("core", 0, 1), ("core", 0, 0),),
    "Q0": (("go", 3, 2), ("near", 3, 0), ("core", 1, 1),),
    "S0": (("go", 2, 0), ("go", 0, 1), ("finish", 3, 1),),
    "A0": (("go", 1, 1), ("go", 0, 2), ("go", 2, 2), ("finish", 2, 1),),
    "B0": (("core", 1, 0),),
    "A1": (("near", 0, 0), ("finish", 3, 2), ("go", 1, 2), ("y", 3, 0), ("near", 1, 0),),
    "B1": (("finish", 0, 1), ("y", 0, 0), ("finish", 2, 2), ("finish", 2, 0), ("go", 0, 0), ("finish", 1, 2),),
    "B2": (("finish", 1, 1),),
    "P0": (("x", 3, 0), ("go", 3, 0), ("y", 1, 0), ("x", 0, 0), ("finish", 0, 2), ("y", 2, 0), ("finish", 0, 0),
        ("finish", 3, 0), ("x", 1, 0), ("x", 2, 0), ("go", 1, 0), ("small", 0, 0), ("small", 1, 0),
        ("small", 2, 0), ("finish", 1, 0), ("z", 0, 0), ("small", 3, 0), ("z", 3, 0), ("z", 1, 0), ("z", 2, 0),),
}

EXPERT_STEPS = {
    "first": (("start", 0, 0), ("start", 0, 2), ("start", 0, 1), ("forward", 0, 0), ("start", 1, 2),
        ("start", 1, 1), ("start", 1, 0), ("forward", 0, 2), ("start", 2, 2), ("forward", 0, 1), ("start", 3, 0),
        ("start", 2, 0), ("forward", 1, 0), ("pass", 0, 2), ("start", 2, 1), ("pass", 0, 1), ("pass", 0, 0),
        ("start", 3, 1), ("forward", 1, 2), ("forward", 1, 1),),
    "A0": (("pass", 1, 0), ("forward", 2, 0),),
    "B0": (("forward", 3, 0),),
    "C0": (("pass", 1, 2), ("forward", 2, 2), ("pass", 1, 1), ("go", 0, 1),),
    "A1": (("start", 3, 2),),
    "W0": (("forward", 2, 1),),
    "C1": (("sum", 0, 0), ("finish", 0, 1), ("pass", 2, 0), ("forward", 3, 1), ("go", 1, 1),),
    "D1": (("forward", 3, 2), ("sum", 1, 0), ("pass", 2, 2), ("pass", 2, 1), ("go", 0, 2),),
    "A2": (("go", 1, 0), ("go", 1, 2),),
    "B2": (("finish", 1, 1), ("go", 0, 0),),
    "W1": (("go", 2, 1), ("pass", 3, 2), ("pass", 3, 0), ("go", 2, 2),),
    "C2": (("finish", 0, 2),),
    "D2": (("pass", 3, 1),),
    "V1": (("sum", 2, 0), ("go", 2, 0), ("finish", 1, 2),),
    "B3": (("go", 3, 1), ("finish", 2, 1), ("go", 3, 2),),
    "W2": (("finish", 2, 2),),
    "D3": (("go", 3, 0), ("finish", 1, 0), ("finish", 0, 0), ("sum", 3, 0), ("finish", 3, 1),),
    "V2": (("finish", 3, 2), ("finish", 2, 0), ("finish", 3, 0),),
}


class Place:
    def __init__(self, wide):
        self.wide = wide
        self.run = wide // 2
        self.deep = wide // 2
        self.w, self.n = lax.axis_index("wide"), lax.axis_index("narrow")
        self.x, self.c = self.n // 2, lax.rem(self.n, 2)
        self.z, self.y = self.w // 2, lax.rem(self.w, 2)
        self.core = (self.w, self.x * 2 + 1 - self.c)
        self.side = (self.w, (1 - self.x) * 2 + self.c)
        self.row = (self.z * 2 + 1 - self.y, self.n)

    def flip(self, j):
        found, bit = self.w, 1
        while bit <= j:
            if j & bit:
                found = found + bit - 2 * bit * lax.rem(self.w // bit, 2)
            bit *= 2
        return found

    def peer(self, j):
        return (self.flip(j), self.n)

    def span(self, piece):
        half = self.w // self.run
        return pl.ds((1 - half if piece else half) * self.run, self.run)

    def steps(self, piece):
        return range(self.run, self.wide) if piece else range(1, self.run)

    def partners(self):
        return [self.peer(j) for j in range(1, self.wide)] + [self.core, self.side]


def slot_part(piece, slots):
    return pl.ds((piece - 1) * (slots // 2), slots // 2) if piece else pl.ds(0, slots)


PIECES = range(3)


class Spread:
    def __init__(self, place, sent, held, wide_s, wide_r, side_s, side_r, core_s, core_r):
        self.place, self.sent, self.held = place, sent, held
        self.wide_s, self.wide_r, self.side_s, self.side_r = wide_s, wide_r, side_s, side_r
        self.core_s, self.core_r = core_s, core_r
        self.slots = sent.shape[2]

    def hop(self, e, j, piece):
        p, part = self.place, slot_part(piece, self.slots)
        at = p.wide + j if piece == 2 else j
        return remote(
            self.sent.at[p.flip(j), e, part], self.held.at[e, p.n, p.w, part],
            self.wide_s.at[e, at], self.wide_r.at[e, at], p.peer(j),
        )

    def start(self, e, piece):
        for j in self.place.steps(piece):
            self.hop(e, j, piece).start()

    def beside(self, e, piece):
        p = self.place
        rows = self.held.at[e, p.n, p.span(piece), slot_part(piece, self.slots)]
        return remote(rows, rows, self.side_s.at[e, piece], self.side_r.at[e, piece], p.side)

    def over(self, e, other, piece):
        p = self.place
        m = (1 - p.x) * 2 + p.c if other else p.n
        rows = self.held.at[e, m, p.span(piece), slot_part(piece, self.slots)]
        at = 3 * other + piece
        return remote(rows, rows, self.core_s.at[e, at], self.core_r.at[e, at], p.core)

    def forward(self, e, piece):
        for j in self.place.steps(piece):
            self.hop(e, j, piece).wait_recv()
        self.beside(e, piece).start()
        self.over(e, 0, piece).start()

    def pass_on(self, e, piece):
        self.beside(e, piece).wait_recv()
        self.over(e, 1, piece).start()

    def arrive(self, e, other):
        for piece in PIECES:
            self.over(e, other, piece).wait_recv()

    def drain(self, e):
        for piece in PIECES:
            for j in self.place.steps(piece):
                self.hop(e, j, piece).wait_send()
            self.beside(e, piece).wait_send()
            self.over(e, 0, piece).wait_send()
            self.over(e, 1, piece).wait_send()

    @staticmethod
    def semaphores(local, wide):
        dma = pltpu.SemaphoreType.DMA
        return [dma((local, n)) for n in (2 * wide, 2 * wide, 3, 3, 6, 6)]


class Collect:
    def __init__(self, place, to_core, from_core, from_side, returned, semaphores):
        self.place, self.to_core, self.from_core = place, to_core, from_core
        self.from_side, self.returned = from_side, returned
        self.core_s, self.core_r, self.side_s, self.side_r, self.wide_s, self.wide_r = semaphores
        self.slots = from_side.shape[2]

    def core(self, e, other):
        return remote(
            self.to_core(e, other), self.from_core.at[e, other], self.core_s.at[e, other], self.core_r.at[e, other],
            self.place.core,
        )

    def beside(self, e, piece):
        rows, part = self.place.span(piece), slot_part(piece, self.slots)
        return remote(
            self.from_core.at[e, 1, rows, part], self.from_side.at[e, rows, part],
            self.side_s.at[e, piece], self.side_r.at[e, piece], self.place.side,
        )

    def back(self, e, j, piece):
        p, part = self.place, slot_part(piece, self.slots)
        at = p.wide + j if piece == 2 else j
        return remote(
            self.from_side.at[e, p.flip(j), part], self.returned.at[p.w, e, part],
            self.wide_s.at[e, at], self.wide_r.at[e, at], p.peer(j),
        )

    def go_beside(self, e, part):
        self.core(e, 1).wait_recv()
        held = self.from_core[e, 1].astype(F32)
        self.from_core[e, 1] = (part.astype(F32).reshape(held.shape) + held).astype(BF16)
        self.beside(e, 1).start()

    def finish(self, e, piece, own):
        p = self.place
        rows, part = p.span(piece), slot_part(piece, self.slots)
        self.beside(e, piece).wait_recv()
        total = own(rows, part) + self.from_side[e, rows, part].astype(F32)
        self.from_side[e, rows, part] = total.astype(BF16)
        for j in p.steps(piece):
            self.back(e, j, piece).start()
        if not piece:
            self.returned[p.w, e] = self.from_side[e, p.w]

    def drain(self, e):
        self.core(e, 0).wait_send()
        self.core(e, 1).wait_send()
        for piece in PIECES:
            self.beside(e, piece).wait_send()
            for j in self.place.steps(piece):
                self.back(e, j, piece).wait_send()

    def arrive(self, e):
        for piece in PIECES:
            for j in self.place.steps(piece):
                self.back(e, j, piece).wait_recv()

    @staticmethod
    def semaphores(local, wide):
        dma = pltpu.SemaphoreType.DMA
        return [dma((local, n)) for n in (2, 2, 3, 3, 2 * wide, 2 * wide)]


class Gather:
    def __init__(self, place, unit, held, halves, semaphores):
        self.p, self.u, self.held, self.halves = place, unit, held, halves
        self.s, self.r = semaphores

    def piece(self, *place):
        return self.held.at[self.u, self.p.c, *place] if self.halves else self.held.at[self.u, *place]

    def column(self, y, x):
        return self.piece(slice(None), y, x)

    def copy(self, piece, slot, device):
        return remote(piece, piece, self.s.at[self.u, slot], self.r.at[self.u, slot], device)

    def to_z(self, k):
        p = self.p
        z = lax.rem(p.z + k, p.deep)
        return self.copy(self.piece(p.z, p.y, p.x), k - 1, (z * 2 + p.y, p.n))

    def to_x(self):
        return self.copy(self.column(self.p.y, self.p.x), 3, self.p.side)

    def to_y(self):
        return self.copy(self.column(self.p.y, self.p.x), 4, self.p.row)

    def corner(self):
        return self.copy(self.column(self.p.y, 1 - self.p.x), 5, self.p.row)

    def to_core(self, at):
        p = self.p
        y, x = ((p.y, p.x), (p.y, 1 - p.x), (1 - p.y, p.x), (1 - p.y, 1 - p.x))[at]
        return self.copy(self.column(y, x), 6 + at, p.core)

    def hand(self, at):
        if self.halves:
            self.to_core(at).start()

    def start(self):
        for k in range(1, self.p.deep):
            self.to_z(k).start()

    def spread(self):
        for k in range(1, self.p.deep):
            self.to_z(k).wait_recv()
        self.to_x().start()
        self.to_y().start()
        self.hand(0)

    def over_x(self):
        self.to_x().wait_recv()
        self.corner().start()
        self.hand(1)

    def over_y(self):
        self.to_y().wait_recv()
        self.hand(2)

    def end(self):
        self.corner().wait_recv()
        self.hand(3)

    def arrive(self):
        if self.halves:
            for at in range(4):
                self.to_core(at).wait_recv()

    def drain(self):
        for k in range(1, self.p.deep):
            self.to_z(k).wait_send()
        for copy in (self.to_x(), self.to_y(), self.corner()):
            copy.wait_send()
        if self.halves:
            for at in range(4):
                self.to_core(at).wait_send()


def moving_forward_kernel(
    rel_ref, capacity_ref, x_ref, q_part, k_part, v_part, o_part, small_part, near_ref, routes_ref, row_ref, cot_ref,
    normed_out, q_out, k_out, v_out, att_out, lse_out, mixed_out, normed_f_out, sent_out, weights_out, cot_out,
    slot_col, router_out, gains_out,
    normed_ref, q_ref, k_ref, v_ref, att_ref, lse_ref, mixed_ref, normed_f, sent_ref, store_s,
    held, small, pair_send, pair_got, small_got, cot_sent, weight_s, pair_s, pair_r,
    gs, gr, hs, hr, wide_s, wide_r, side_s, side_r, core_s, core_r,
):
    count, width = x_ref.shape
    wide, local, slots, _ = cot_sent.shape
    experts = router_out.shape[1]
    total = wide * local * slots
    units = HEADS // 4
    rows = pair_send.shape[2]
    p = Place(wide)
    greet(p.partners())

    def own_cols(u, half):
        if u == units:
            return o_part[:, half * (width // 2) : (half + 1) * (width // 2)]
        cols = slice((2 * u + half) * BLOCK, (2 * u + half + 1) * BLOCK)
        return jnp.concatenate([q_part[:, cols], k_part[:, cols], v_part[:, cols]], axis=1)

    def swap_copies():
        return [
            remote(pair_send.at[0], pair_got.at[0], pair_s.at[0], pair_r.at[0], p.core),
            remote(small_part, small_got, pair_s.at[1], pair_r.at[1], p.core),
        ]

    for u in range(units + 1):
        pair_send[0, u] = jnp.where(p.c == 0, own_cols(u, 1), own_cols(u, 0))
    limit = capacity_ref[0] * count // experts
    slot_col[...], slot_row = slot_places(routes_ref, row_ref, limit, experts, slots, count)
    cot_sent[...] = slot_rows(slot_row, cot_ref[...], total).reshape(cot_sent.shape)
    moves = Spread(p, cot_sent, cot_out, wide_s, wide_r, side_s, side_r, core_s, core_r)

    def own_rows(e):
        return pltpu.make_async_copy(cot_sent.at[p.w, e], cot_out.at[e, p.n, p.w], weight_s.at[1 + e])

    for e in range(local):
        own_rows(e).start()
    lse_ref[...] = jnp.zeros_like(lse_ref)
    for e in range(local):
        own_rows(e).wait()
    meet(p.partners())
    for copy in swap_copies():
        copy.start()
    for copy in swap_copies():
        copy.wait_recv()

    def joined(mine, other):
        mine, other = mine.astype(F32), other.astype(F32)
        return jnp.concatenate(
            [jnp.where(p.c == 0, mine, other), jnp.where(p.c == 0, other, mine)], axis=0
        ).astype(BF16)

    def gather(u):
        if isinstance(u, int) and u > units:
            return small_gather
        return Gather(p, u, held, True, (gs, gr))

    small_gather = Gather(p, 0, small, False, (hs, hr))
    small[0, p.z, p.y, p.x] = joined(small_part[...], small_got[...])
    for u in range(units + 1):
        mine = jnp.where(p.c == 0, own_cols(u, 0), own_cols(u, 1))
        held[u, p.c, p.z, p.y, p.x] = joined(mine, pair_got[0, u])

    acts = {
        "start": moves.start, "forward": moves.forward, "pass": moves.pass_on,
        "send": lambda u, piece: gather(u).start(), "spread": lambda u, piece: gather(u).spread(),
        "over_x": lambda u, piece: gather(u).over_x(), "over_y": lambda u, piece: gather(u).over_y(),
        "end": lambda u, piece: gather(u).end(),
    }

    def act(steps):
        for name, at, piece in steps:
            acts[name](at, piece)

    def after(u, part):
        for at in range(units):
            steps = FORWARD_STEPS.get(part + str(at), ())
            if steps:
                pl.when(u == at)(lambda steps=steps: act(steps))

    act(FORWARD_STEPS["first"])
    small_all = small[0].reshape(width, BLOCK)
    router_out[...] = small_all[:, :experts]
    gains_out[...] = small_all.astype(F32).T[experts : experts + 8, :]
    tokens = x_ref[...].astype(F32)
    normed_ref[...] = (tokens * inverse_rms(tokens) * gains_out[0:1, :]).astype(BF16)
    act(FORWARD_STEPS.get("N0", ()))

    def pair(at, weight):
        cols = pl.ds(pl.multiple_of(at * BLOCK, BLOCK), BLOCK)
        found = dot_nn(normed_ref[...], weight.reshape(width, 3 * BLOCK)).astype(BF16)
        q_ref[:, cols], k_ref[:, cols], v_ref[:, cols] = (found[:, i * BLOCK : (i + 1) * BLOCK] for i in range(3))
        pair_forward(at, rel_ref, near_ref, q_ref, k_ref, v_ref, att_ref, lse_ref)

    def pairs(u, carry):
        gather(u).arrive()
        pair(2 * u, held[u, 0])
        after(u, "A")
        pair(2 * u + 1, held[u, 1])
        after(u, "B")
        return carry

    lax.fori_loop(0, units, pairs, 0)
    stores = [
        pltpu.make_async_copy(source, target, store_s.at[at])
        for at, (source, target) in enumerate((
            (normed_ref, normed_out), (q_ref, q_out), (k_ref, k_out), (v_ref, v_out), (att_ref, att_out),
            (lse_ref, lse_out), (mixed_ref, mixed_out), (normed_f, normed_f_out), (sent_ref, sent_out),
        ))
    ]
    for copy in stores[:6]:
        copy.start()
    gather(units).arrive()
    weights_copy = pltpu.make_async_copy(held, weights_out, weight_s.at[0])
    weights_copy.start()
    mixed = tokens_again(x_ref) + jnp.concatenate(
        [dot_nn(att_ref[...], held[units, half].reshape(width, width // 2)) for half in range(2)], axis=1
    )
    mixed_ref[...] = mixed
    normed_2 = (mixed * inverse_rms(mixed) * gains_out[1:2, :]).astype(BF16)
    normed_f[...] = normed_2
    stores[6].start()
    stores[7].start()
    sent_ref[...] = slot_rows(slot_row, normed_2, total).reshape(sent_ref.shape)
    stores[8].start()
    act(FORWARD_STEPS.get("M0", ()))
    for copy in swap_copies():
        copy.wait_send()
    small_gather.drain()
    for u in range(units + 1):
        gather(u).drain()
    for e in range(local):
        moves.arrive(e, 0)
        moves.arrive(e, 1)
        moves.drain(e)
    weights_copy.wait()
    for copy in stores:
        copy.wait()


def tokens_again(x_ref):
    return x_ref[...].astype(F32)


def moving_forward(
    rel_bias, capacity, inputs, w_query, w_key, w_value, w_output, w_router, gain_attn, gain_ffn, near, routes, cotangent,
    wide, narrow, local, slots,
):
    count, width = inputs.shape
    experts = w_router.shape[1]
    shard = w_query.shape[0]
    deep, units = wide // 2, HEADS // 4
    half = width // 2
    sds = jax.ShapeDtypeStruct
    rows_t = lambda dtype, cols=width: sds((count, cols), dtype)
    smem, any_spec = pl.BlockSpec(memory_space=pltpu.SMEM), pl.BlockSpec(memory_space=pl.ANY)
    vmem = lambda *shape, dtype=BF16: pltpu.VMEM(shape, dtype)
    dma = pltpu.SemaphoreType.DMA
    small = jnp.concatenate(
        [w_router, gain_attn[:, None], gain_ffn[:, None], jnp.zeros((shard, BLOCK - experts - 2), BF16)], axis=1
    )
    return pl.pallas_call(
        moving_forward_kernel,
        out_shape=(
            rows_t(BF16), rows_t(BF16), rows_t(BF16), rows_t(BF16), rows_t(BF16), rows_t(F32, BLOCK), rows_t(F32),
            rows_t(BF16), sds((wide, local, slots, width), BF16),
            sds((units + 1, 2, deep, 2, 2, 2 * shard, half), BF16),
            sds((local, narrow, wide, slots, width), BF16), sds((count, 1), jnp.int32),
            sds((width, experts), BF16), sds((8, width), F32),
        ),
        in_specs=[smem, smem] + in_vmem(10),
        out_specs=(any_spec,) * 11 + tuple(in_vmem(3)),
        scratch_shapes=[
            vmem(count, width), vmem(count, width), vmem(count, width), vmem(count, width), vmem(count, width),
            vmem(count, BLOCK, dtype=F32), vmem(count, width, dtype=F32), vmem(count, width),
            vmem(wide, local, slots, width), dma((9,)),
            vmem(units + 1, 2, deep, 2, 2, 2 * shard, half), vmem(1, deep, 2, 2, 2 * shard, BLOCK),
            vmem(1, units + 1, shard, half), vmem(1, units + 1, shard, half), vmem(shard, BLOCK),
            vmem(wide, local, slots, width), dma((1 + local,)), dma((2,)), dma((2,)),
            dma((units + 1, 10)), dma((units + 1, 10)), dma((1, 10)), dma((1, 10)),
            *Spread.semaphores(local, wide),
        ],
        compiler_params=pltpu.CompilerParams(collective_id=1, has_side_effects=True, vmem_limit_bytes=62 << 20),
        name="forward",
    )(
        rel_bias, capacity, inputs, w_query, w_key, w_value, w_output, small, near, routes, routes.reshape(1, count),
        cotangent,
    )


def moving_expert_kernel(
    sent, cot_hbm, in_hbm, out_hbm, router_ref,
    outs_o, gin_o, gout_o, back_o, gate_o,
    held, cot, w_in, w_out, sg, hidden, gpre, outs, gin, gout, to_core, from_core, from_side, near_sum, far_sum,
    gate_sum, gate_core, gate_from_core, gate_side, gate_from_side, gate_ready,
    load_s, store_s, wide_s, wide_r, side_s, side_r, core_s, core_r,
    rc_s, rc_r, rx_s, rx_r, rw_s, rw_r, gc_s, gc_r, gx_s, gx_r, gw_s, gw_r,
):
    wide, local, slots, width = sent.shape
    narrow = held.shape[1]
    step = wide * slots
    hidden_width = in_hbm.shape[2]
    p = Place(wide)
    moves = Spread(p, sent, held, wide_s, wide_r, side_s, side_r, core_s, core_r)
    greet(p.partners())

    def loads(e):
        return [
            pltpu.make_async_copy(in_hbm.at[e], w_in.at[e], load_s.at[e, 0]),
            pltpu.make_async_copy(out_hbm.at[e], w_out.at[e], load_s.at[e, 1]),
            pltpu.make_async_copy(cot_hbm.at[e], cot.at[e], load_s.at[e, 2]),
        ]

    def store(e, at):
        source = (outs.at[lax.rem(e, 2)], gin, gout)[at]
        return pltpu.make_async_copy(source, (outs_o, gin_o, gout_o)[at].at[e], store_s.at[e, at])

    def grads_out(e):
        b = lax.rem(e, 2)

        @pl.when(e > 0)
        def _():
            store(e - 1, 2).wait()

        rows = narrow * step
        found = dot_tn(hidden[b].reshape(rows, hidden_width), sg[b].reshape(rows, width))
        gout[...] = found.astype(BF16)
        store(e, 2).start()

    def grads_in(e):
        b = lax.rem(e, 2)

        @pl.when(e > 0)
        def _():
            store(e - 1, 1).wait()

        rows = narrow * step
        found = dot_tn(held[e].reshape(rows, width), gpre[b].reshape(rows, hidden_width))
        gin[...] = found.astype(BF16)
        store(e, 1).start()

    for e in range(local):
        for copy in loads(e):
            copy.start()
        held[e, p.n, p.w] = sent[p.w, e]
    gate_sum[...] = jnp.zeros_like(gate_sum)
    meet(p.partners())

    def chunk(e, m):
        b = lax.rem(e, 2)
        rows = held[e, m].reshape(step, width)
        probs = softmax_lanes(dot_nn(rows, router_ref[...]))
        here = lax.broadcasted_iota(jnp.int32, probs.shape, 1) == p.w * local + e
        gate = jnp.sum(jnp.where(here, probs, 0.0), axis=-1, keepdims=True)
        cot_rows = cot[e, m].reshape(step, width).astype(F32)
        sg_rows = (cot_rows * gate).astype(BF16)
        sg[b, m] = sg_rows
        pre = dot_nn(rows, w_in[e])
        square = pre * pre
        inner = jnp.tanh(pre * (ROOT_TWO_PI + ROOT_TWO_PI * CUBIC * square))
        half = 0.5 * (1.0 + inner)
        hidden_rows = (pre * half).astype(BF16)
        hidden[b, m] = hidden_rows
        slope = half + 0.5 * pre * (1.0 - inner * inner) * (
            ROOT_TWO_PI + 3.0 * ROOT_TWO_PI * CUBIC * square
        )
        gpre_rows = (dot_nt(sg_rows, w_out[e]) * slope).astype(BF16)
        gpre[b, m] = gpre_rows
        out_rows = dot_nn(hidden_rows, w_out[e])
        outs[b, m] = out_rows.astype(BF16).reshape(wide, slots, width)
        gate_rows = jnp.sum(out_rows * cot_rows, axis=-1, keepdims=True)
        row = lax.broadcasted_iota(jnp.int32, (step, local * slots), 0)
        lane = lax.broadcasted_iota(jnp.int32, (step, local * slots), 1)
        spread = jnp.where(lane == e * slots + lax.rem(row, slots), gate_rows, 0.0)
        gate_sum[m] += jnp.sum(spread.reshape(wide, slots, local * slots), axis=1)
        return dot_nt(gpre_rows, w_in[e])

    back = Collect(
        p, lambda e, other: to_core.at[e, other], from_core, from_side, back_o, (rc_s, rc_r, rx_s, rx_r, rw_s, rw_r)
    )

    def go(e, piece):
        if piece == 1:
            back.go_beside(e, far_sum[...])
        else:
            back.beside(e, piece).start()

    def add_core(e, piece):
        back.core(e, 0).wait_recv()
        near_sum[e] = near_sum[e] + from_core[e, 0].astype(F32)

    acts = {
        "start": moves.start, "forward": moves.forward, "pass": moves.pass_on, "go": go, "sum": add_core,
        "finish": lambda e, piece: back.finish(e, piece, lambda rows, part: near_sum[e, rows, part]),
    }

    def after(e, part):
        for at in range(local):
            steps = EXPERT_STEPS.get(part + str(at), ())
            if steps:

                def run(steps=steps):
                    for name, expert, piece in steps:
                        acts[name](expert, piece)

                if not isinstance(e, int):
                    pl.when(e == at)(run)
                elif e == at:
                    run()

    for name, expert, piece in EXPERT_STEPS["first"]:
        acts[name](expert, piece)

    far_x = (1 - p.x) * 2

    gates_core = remote(gate_core, gate_from_core, gc_s, gc_r, p.core)

    def gates_core_start():
        gate_core[0] = gate_sum[p.x * 2 + 1 - p.c]
        gate_core[1] = gate_sum[far_x + 1 - p.c]
        gates_core.start()

    def expert(e, carry):
        for copy in loads(e):
            copy.wait()

        @pl.when(e >= 2)
        def _():
            store(e - 2, 0).wait()

        moves.arrive(e, 1)
        to_core[e, 1] = chunk(e, far_x + 1 - p.c).astype(BF16).reshape(wide, slots, width)
        back.core(e, 1).start()
        after(e, "A")
        far_sum[...] = chunk(e, far_x + p.c).reshape(wide, slots, width)
        after(e, "B")

        @pl.when(e > 0)
        def _():
            grads_out(e - 1)
            after(e - 1, "W")

        moves.arrive(e, 0)
        to_core[e, 0] = chunk(e, p.x * 2 + 1 - p.c).astype(BF16).reshape(wide, slots, width)
        back.core(e, 0).start()
        after(e, "C")
        near_sum[e] = chunk(e, p.n).reshape(wide, slots, width)
        store(e, 0).start()

        @pl.when(e == local - 1)
        def _():
            gates_core_start()

        after(e, "D")

        @pl.when(e > 0)
        def _():
            grads_in(e - 1)
            after(e - 1, "V")

        return carry

    lax.fori_loop(0, local, expert, 0)
    gates_core.wait_recv()
    gate_side[...] = gate_sum[far_x + p.c] + gate_from_core[1]
    gates_side = remote(gate_side, gate_from_side, gx_s, gx_r, p.side)
    gates_side.start()
    grads_out(local - 1)
    after(local - 1, "W")
    gates_side.wait_recv()
    gates = gate_sum[p.n] + gate_from_core[0] + gate_from_side[...]
    for v in range(wide):
        gate_ready[v] = gates[v : v + 1, :]
    gates_wide = [
        remote(gate_ready.at[p.flip(j)], gate_o.at[p.w], gw_s.at[j], gw_r.at[j], p.peer(j)) for j in range(1, wide)
    ]
    for copy in gates_wide:
        copy.start()
    gate_o[p.w] = gate_ready[p.w]
    grads_in(local - 1)
    after(local - 1, "V")
    gates_core.wait_send()
    gates_side.wait_send()

    def drain(e, carry):
        moves.drain(e)
        back.drain(e)
        back.arrive(e)

        @pl.when(e >= local - 2)
        def _():
            store(e, 0).wait()

        return carry

    lax.fori_loop(0, local, drain, 0)
    store(local - 1, 1).wait()
    store(local - 1, 2).wait()
    for copy in gates_wide:
        copy.wait()


def moving_experts(sent, cot_all, expert_in, expert_out, router, wide, narrow):
    _, local, slots, width = sent.shape
    hidden_width = expert_in.shape[2]
    step = wide * slots
    sds = jax.ShapeDtypeStruct
    any_spec, vmem_spec = pl.BlockSpec(memory_space=pl.ANY), pl.BlockSpec(memory_space=pltpu.VMEM)
    dma = pltpu.SemaphoreType.DMA
    outs, gin, gout, back, gates = pl.pallas_call(
        moving_expert_kernel,
        out_shape=(
            sds((local, narrow, wide, slots, width), BF16),
            sds(expert_in.shape, BF16),
            sds(expert_out.shape, BF16),
            sds((wide, local, slots, width), BF16),
            sds((wide, 1, local * slots), F32),
        ),
        in_specs=[vmem_spec, any_spec, any_spec, any_spec, vmem_spec],
        out_specs=(any_spec,) * 3 + (vmem_spec,) * 2,
        scratch_shapes=[
            pltpu.VMEM((local, narrow, wide, slots, width), BF16),
            pltpu.VMEM((local, narrow, wide, slots, width), BF16),
            pltpu.VMEM(expert_in.shape, BF16),
            pltpu.VMEM(expert_out.shape, BF16),
            pltpu.VMEM((2, narrow, step, width), BF16),
            pltpu.VMEM((2, narrow, step, hidden_width), BF16),
            pltpu.VMEM((2, narrow, step, hidden_width), BF16),
            pltpu.VMEM((2, narrow, wide, slots, width), BF16),
            pltpu.VMEM(expert_in.shape[1:], BF16),
            pltpu.VMEM(expert_out.shape[1:], BF16),
            pltpu.VMEM((local, 2, wide, slots, width), BF16),
            pltpu.VMEM((local, 2, wide, slots, width), BF16),
            pltpu.VMEM((local, wide, slots, width), BF16),
            pltpu.VMEM((local, wide, slots, width), F32),
            pltpu.VMEM((wide, slots, width), F32),
            pltpu.VMEM((narrow, wide, local * slots), F32),
            pltpu.VMEM((2, wide, local * slots), F32),
            pltpu.VMEM((2, wide, local * slots), F32),
            pltpu.VMEM((wide, local * slots), F32),
            pltpu.VMEM((wide, local * slots), F32),
            pltpu.VMEM((wide, 1, local * slots), F32),
            dma((local, 3)), dma((local, 3)), *Spread.semaphores(local, wide), *Collect.semaphores(local, wide),
            dma, dma, dma, dma, dma((wide,)), dma((wide,)),
        ],
        compiler_params=pltpu.CompilerParams(
            collective_id=2, has_side_effects=True, vmem_limit_bytes=62 << 20
        ),
        name="experts",
    )(sent, cot_all, expert_in, expert_out, router)
    return outs, back, gates, gin.astype(F32), gout.astype(F32)


def routed_gate(normed_f, router_ref, routes_ref):
    probs = softmax_lanes(dot_nn(normed_f[...], router_ref[...]))
    chosen = lax.broadcasted_iota(jnp.int32, probs.shape, 1) == routes_ref[...]
    return probs, chosen, jnp.sum(jnp.where(chosen, probs, 0.0), axis=-1, keepdims=True)


def slot_owners(slot_col, total):
    return lax.broadcasted_iota(jnp.int32, (slot_col.shape[0], total), 1) == slot_col[...]


def ffn_backward(probs, chosen, gate, owned, gates_ref, normed_f, router_ref, grows_ref, mixed, cot_ref, gain_f):
    grad_gate = jnp.sum(jnp.where(owned, gates_ref[...], 0.0), axis=-1, keepdims=True)
    grad_logits = (probs * (jnp.where(chosen, grad_gate, 0.0) - gate * grad_gate)).astype(BF16)
    grad_router = dot_tn(normed_f[...], grad_logits)
    grad_normed = dot_nt(grad_logits, router_ref[...]) + dot_nn(owned.astype(BF16), grows_ref[...])
    grad_norm, grad_gain = norm_backward(mixed, inverse_rms(mixed), gain_f[...], grad_normed)
    return grad_router, cot_ref[...].astype(F32) + grad_norm, grad_gain


def attention_setup(q_ref, k_ref, normed_ref, att_ref, lse_ref, q_t, k_t, normed_t, att_t, lse_t):
    head_dim = q_ref.shape[1] // HEADS
    att_t[...] = att_ref[...].T
    q_t[...] = (q_ref[...] * jnp.asarray(head_dim**-0.5, BF16)).T
    k_t[...] = k_ref[...].T
    normed_t[...] = normed_ref[...].T
    lse_t[...] = lse_ref[...].T


def attention_delta(datt, att_t, datt_t, delta):
    width, count = att_t.shape
    datt_t[...] = datt[...].T
    products = datt_t[...].astype(F32) * att_t[...].astype(F32)
    delta[...] = jnp.sum(products.reshape(HEADS, width // HEADS, count), axis=1)


def pair_backward(
    at, rel_ref, near_ref, q_ref, k_ref, v_ref, q_t, k_t, datt, datt_t, delta, lse_t, dst, gq, gk, gv, gnear_ref, gfar_ref
):
    count, width = q_ref.shape
    head_dim = width // HEADS
    blocks = count // BLOCK
    bucket_count = rel_ref.shape[0]
    first = lax.broadcasted_iota(jnp.int32, (1, BLOCK), 1) < head_dim
    cols = pl.ds(pl.multiple_of(at * BLOCK, BLOCK), BLOCK)
    q_pair, datt_pair = q_ref[:, cols], datt[:, cols]
    gq_parts, gk_parts, gv_parts = [], [], []
    for half in range(2):
        head = 2 * at + half
        low, high = rel_ref[bucket_count // 2 - 1, head], rel_ref[bucket_count - 1, head]
        mask = first if half == 0 else jnp.logical_not(first)
        near = toeplitz_near(near_ref[pl.ds(head, 1), :])
        lse_row, delta_row = lse_t[pl.ds(head, 1), :], delta[pl.ds(head, 1), :]
        near_sum = jnp.zeros((BLOCK, 3 * BLOCK), F32)
        low_sum, high_sum = jnp.zeros((BLOCK, BLOCK), F32), jnp.zeros((BLOCK, BLOCK), F32)
        gk_rows, gv_rows = [], []
        for row in range(blocks):
            rows = slice(row * BLOCK, (row + 1) * BLOCK)
            k_rows, v_rows = k_ref[rows, cols], v_ref[rows, cols]
            zeros = jnp.zeros_like(k_rows)
            scores = dot_nn(jnp.where(mask, k_rows, zeros), q_t[cols, :])
            scores = scores + bias_rows(near, high, low, row, blocks)
            weights = jnp.exp(scores - lse_row)
            grad_weights = dot_nn(jnp.where(mask, v_rows, zeros), datt_t[cols, :])
            grad_scores = weights * (grad_weights - delta_row)
            gv_rows.append(dot_nn(weights.astype(BF16), datt_pair))
            low_bits = grad_scores.astype(BF16)
            dst[rows, :] = low_bits
            gk_rows.append(dot_nn(low_bits, q_pair))
            for column in range(blocks):
                piece = grad_scores[:, column * BLOCK : (column + 1) * BLOCK]
                distance = column - row
                if distance <= -2:
                    high_sum = high_sum + piece
                elif distance >= 2:
                    low_sum = low_sum + piece
                else:
                    pads = [jnp.zeros((BLOCK, BLOCK), F32)] * 3
                    pads[distance + 1] = piece
                    near_sum = near_sum + jnp.concatenate(pads, axis=1)
        gq_parts.append(
            dot_nn(k_t[pl.ds(pl.multiple_of(head * head_dim, head_dim), head_dim), :], dst[...])
        )
        gk_parts.append(jnp.concatenate(gk_rows, axis=0))
        gv_parts.append(jnp.concatenate(gv_rows, axis=0))
        gnear_ref[pl.ds(head, 1), :] = diagonal_sums(near_sum)
        gfar_ref[pl.ds(head, 1), :] = jnp.concatenate(
            [jnp.sum(low_sum, axis=0, keepdims=True), jnp.sum(high_sum, axis=0, keepdims=True)], axis=1
        )
    scale = head_dim**-0.5
    gq[:, cols] = (jnp.concatenate(gq_parts, axis=0).T * scale).astype(BF16)
    gk[:, cols] = (jnp.where(first, gk_parts[0], gk_parts[1]) * scale).astype(BF16)
    gv[:, cols] = jnp.where(first, gv_parts[0], gv_parts[1]).astype(BF16)


def input_backward(x_ref, w_ref, gain_a, gmixed, gq, gk, gv):
    count, width = x_ref.shape
    grad_normed = jnp.zeros((count, width), F32)
    for at, grad in enumerate((gq, gk, gv)):
        grad_normed = grad_normed + dot_nt(grad[...], w_ref[:, at * width : (at + 1) * width])
    tokens = x_ref[...].astype(F32)
    grad_norm, grad_gain = norm_backward(tokens, inverse_rms(tokens), gain_a[...], grad_normed)
    return gmixed[...] + grad_norm, grad_gain


def backward_kernel(
    rel_ref, x_ref, w_ref, gain_a, gain_f, router_ref, near_ref, slot_col, routes_ref,
    normed_ref, q_ref, k_ref, v_ref, att_ref, lse_ref, mixed_ref, normed_f, cot_ref, outs_ref, grows_ref, gates_ref,
    result_ref, gx_ref, gw_ref, grouter_ref, gnear_ref, gfar_ref, ggain_ref,
    q_t, k_t, normed_t, att_t, datt, datt_t, delta, lse_t, gq, gk, gv, gmixed, dst,
):
    width = x_ref.shape[1]
    probs, chosen, gate = routed_gate(normed_f, router_ref, routes_ref)
    owned = slot_owners(slot_col, outs_ref.shape[0])
    mixed = mixed_ref[...]
    result_ref[...] = (mixed + gate * dot_nn(owned.astype(BF16), outs_ref[...])).astype(BF16)
    grouter_ref[...], grad_mixed, ggain_ref[1:2, :] = ffn_backward(
        probs, chosen, gate, owned, gates_ref, normed_f, router_ref, grows_ref, mixed, cot_ref, gain_f
    )
    gmixed[...] = grad_mixed
    branch = grad_mixed.astype(BF16)
    gw_ref[:, 3 * width : 4 * width] = dot_tn(att_ref[...], branch).astype(BF16)
    datt[...] = dot_nt(branch, w_ref[:, 3 * width : 4 * width]).astype(BF16)
    attention_setup(q_ref, k_ref, normed_ref, att_ref, lse_ref, q_t, k_t, normed_t, att_t, lse_t)
    attention_delta(datt, att_t, datt_t, delta)

    def pair(at, carry):
        pair_backward(
            at, rel_ref, near_ref, q_ref, k_ref, v_ref, q_t, k_t, datt, datt_t, delta, lse_t, dst, gq, gk, gv,
            gnear_ref, gfar_ref,
        )
        return carry

    lax.fori_loop(0, HEADS // 2, pair, 0)
    for at, grad in enumerate((gq, gk, gv)):
        gw_ref[:, at * width : (at + 1) * width] = dot_nn(normed_t[...], grad[...]).astype(BF16)
    gx_ref[...], ggain_ref[0:1, :] = input_backward(x_ref, w_ref, gain_a, gmixed, gq, gk, gv)


class Sums:
    def __init__(self, place, unit, buffers, semaphores, out, split):
        self.p, self.unit, self.out, self.split = place, unit, out, split
        self.send, self.core, self.first_in, self.second_in, self.z_in, self.last = buffers
        self.s, self.r = semaphores
        self.deep = place.deep
        p, c = place, place.c * split
        self.first, self.second = p.y + c * (p.x - p.y), p.x + c * (p.y - p.x)
        row, side = p.row, p.side
        self.first_peer = tuple(a + c * (b - a) for a, b in zip(row, side))
        self.second_peer = tuple(b + c * (a - b) for a, b in zip(row, side))

    def store(self, buffer, part, core):
        rows, cols = buffer.shape[-2:]
        blocks = part.reshape(self.deep, 2, 2, rows, cols)
        c = core * self.split
        for y in range(2):
            for x in range(2):
                first, second = (y, x) if y == x else (y + c * (x - y), x + c * (y - x))
                buffer[self.unit, first, second] = blocks[:, y, x].astype(buffer.dtype)

    def to_core(self):
        u, p = self.unit, self.p
        return remote(self.send.at[u], self.core.at[u], self.s.at[u, 0], self.r.at[u, 0], p.core)

    def to_y(self):
        u = self.unit
        return remote(self.core.at[u, 1 - self.first], self.first_in.at[u], self.s.at[u, 1], self.r.at[u, 1], self.first_peer)

    def to_x(self):
        u = self.unit
        return remote(self.first_in.at[u, 1 - self.second], self.second_in.at[u], self.s.at[u, 2], self.r.at[u, 2], self.second_peer)

    def to_z(self, k):
        u, p = self.unit, self.p
        z = lax.rem(p.z + k, p.deep)
        return remote(
            self.second_in.at[u, z], self.z_in.at[u, k], self.s.at[u, 3 + k], self.r.at[u, 3 + k], (z * 2 + p.y, p.n)
        )

    def to_last(self):
        u, p = self.unit, self.p
        return remote(self.last.at[u, 1 - p.c], self.out.at[u, p.c], self.s.at[u, 3], self.r.at[u, 3], p.core)

    def begin(self, part):
        self.store(self.send, part, 1 - self.p.c)
        self.to_core().start()

    def stage_core(self, part):
        u = self.unit
        self.to_core().wait_recv()
        rows, cols = self.core.shape[-2:]
        blocks = part.reshape(self.deep, 2, 2, rows, cols)
        c = self.p.c * self.split
        for y in range(2):
            for x in range(2):
                first, second = (y, x) if y == x else (y + c * (x - y), x + c * (y - x))
                kept = blocks[:, y, x] + self.core[u, first, second].astype(F32)
                self.core[u, first, second] = kept.astype(BF16)
        self.to_y().start()

    def stage_y(self):
        u = self.unit
        self.to_y().wait_recv()
        self.first_in[u] = (self.core[u, self.first].astype(F32) + self.first_in[u].astype(F32)).astype(BF16)
        self.to_x().start()

    def stage_x(self):
        u = self.unit
        self.to_x().wait_recv()
        self.second_in[u] = (self.first_in[u, self.second].astype(F32) + self.second_in[u].astype(F32)).astype(BF16)
        for k in range(1, self.p.deep):
            self.to_z(k).start()

    def stage_z(self):
        u = self.unit
        total = self.second_in[u, self.p.z].astype(F32)
        for k in range(1, self.p.deep):
            self.to_z(k).wait_recv()
            total = total + self.z_in[u, k].astype(F32)
        self.last[u] = total.reshape(self.last.shape[1:])
        self.to_last().start()
        self.out[u, self.p.c] = self.last[u, self.p.c]

    def drain(self):
        for copy in (self.to_core(), self.to_y(), self.to_x()):
            copy.wait_send()
        for k in range(1, self.p.deep):
            self.to_z(k).wait_send()
        self.to_last().wait()


def sum_buffers(units, wide, rows, cols):
    deep = wide // 2
    vmem = lambda *shape, dtype=BF16: pltpu.VMEM((units, *shape), dtype)
    return [
        vmem(2, 2, deep, rows, cols), vmem(2, 2, deep, rows, cols), vmem(2, deep, rows, cols), vmem(deep, rows, cols),
        vmem(deep, rows, cols), vmem(2, rows // 2, cols, dtype=F32),
        pltpu.SemaphoreType.DMA((units, 3 + deep)), pltpu.SemaphoreType.DMA((units, 3 + deep)),
    ]


def moving_backward_kernel(
    rel_ref, x_hbm, w_hbm, normed_hbm, q_hbm, k_hbm, v_hbm, att_hbm, lse_hbm, outs_hbm,
    gains_ref, router_ref, near_ref, slot_col, routes_ref, mixed_ref, normed_f, cot_ref, grows_ref, gates_ref, picks_ref,
    result_ref, gx_ref, gw_out, go_out, small_out,
    x_ref, w_ref, normed_ref, q_ref, k_ref, v_ref, att_ref, lse_ref, load_s,
    q_t, k_t, normed_t, att_t, datt, datt_t, delta, lse_t, gq, gk, gv, gmixed, gnormed, dst, gnear, gfar,
    own, from_core, from_side, returned, own_s, rc_s, rc_r, rx_s, rx_r, rw_s, rw_r,
    u1, u2, u3, u4, u5, u6, us, ur, o1, o2, o3, o4, o5, o6, os, orr,
    small, small_in, ss, sr,
):
    count, width = x_hbm.shape
    wide, local, slots, _ = returned.shape
    total = wide * local * slots
    p = Place(wide)
    far_x = (1 - p.x) * 2
    units = HEADS // 4
    gain_a, gain_f = gains_ref.at[0:1, :], gains_ref.at[1:2, :]
    loads = [
        pltpu.make_async_copy(source, target, load_s.at[at])
        for at, (source, target) in enumerate((
            (att_hbm, att_ref), (q_hbm, q_ref), (k_hbm, k_ref), (normed_hbm, normed_ref), (lse_hbm, lse_ref),
            (w_hbm, w_ref), (v_hbm, v_ref), (x_hbm, x_ref),
        ))
    ]

    def partial(e, other, core):
        return outs_hbm.at[e, (far_x if other else p.x * 2) + core]

    back = Collect(
        p, lambda e, other: partial(e, other, 1 - p.c), from_core, from_side, returned, (rc_s, rc_r, rx_s, rx_r, rw_s, rw_r)
    )

    def own_copy(e, other):
        return pltpu.make_async_copy(partial(e, other, p.c), own.at[e, other], own_s.at[e, other])

    for copy in loads[:5]:
        copy.start()
    greet(p.partners())
    for other in (1, 0):
        for e in range(local):
            own_copy(e, other).start()
    for copy in loads[5:]:
        copy.start()

    def go(e, piece):
        if piece == 1:
            own_copy(e, 1).wait()
            back.go_beside(e, own[e, 1])
        else:
            back.beside(e, piece).start()

    def near(e, piece):
        back.core(e, 0).wait_recv()
        own_copy(e, 0).wait()

    def finish(e, piece):
        back.finish(
            e, piece, lambda rows, part: own[e, 0, rows, part].astype(F32) + from_core[e, 0, rows, part].astype(F32)
        )

    def unit(u):
        if isinstance(u, int) and u == units:
            return Sums(p, 0, (o1, o2, o3, o4, o5, o6), (os, orr), go_out, 0)
        return Sums(p, u, (u1, u2, u3, u4, u5, u6), (us, ur), gw_out, (u + 1) // units)

    hops = [[p.core], [p.row], [p.side], [(lax.rem(p.z + k, p.deep) * 2 + p.y, p.n) for k in range(1, p.deep)]]
    copies, slot = [], 0
    for stage, devices in enumerate(hops):
        copies.append([
            remote(small.at[stage], small_in.at[slot + at], ss.at[slot + at], sr.at[slot + at], device)
            for at, device in enumerate(devices)
        ])
        slot += len(devices)

    def small_end(stage):
        slot = sum(len(c) for c in copies[:stage])
        found = small[stage]
        for at, copy in enumerate(copies[stage]):
            copy.wait_recv()
            found = found + small_in[slot + at]
        return found

    def small_step(stage, piece):
        if stage:
            small[stage] = small_end(stage - 1)
        for copy in copies[stage]:
            copy.start()

    acts = {
        "core": lambda e, other: back.core(e, other).start(), "go": go, "near": near, "finish": finish,
        "y": lambda u, piece: unit(u).stage_y(), "x": lambda u, piece: unit(u).stage_x(),
        "z": lambda u, piece: unit(u).stage_z(), "small": small_step,
    }

    def act(part):
        for name, at, piece in BACKWARD_STEPS.get(part, ()):
            acts[name](at, piece)

    def after(u, part):
        for at in range(units):
            if part + str(at) in BACKWARD_STEPS:
                pl.when(u == at)(lambda at=at: act(part + str(at)))

    probs, chosen, gate = routed_gate(normed_f, router_ref, routes_ref)
    owned = slot_owners(slot_col, total)
    for copy in loads[:5]:
        copy.wait()
    attention_setup(q_ref, k_ref, normed_ref, att_ref, lse_ref, q_t, k_t, normed_t, att_t, lse_t)
    meet(p.partners())
    act("first")
    grad_router, grad_mixed, grad_gain_f = ffn_backward(
        probs, chosen, gate, owned, gates_ref, normed_f, router_ref, grows_ref, mixed_ref[...], cot_ref, gain_f
    )
    gmixed[...] = grad_mixed
    small[0] = jnp.zeros_like(small[0])
    small[0, HEADS : HEADS + 1, :] = grad_gain_f
    act("F0")
    branch = grad_mixed.astype(BF16)
    half_cols = width // 2
    router_cols = go_out.shape[-1] - half_cols
    router_wide = jnp.concatenate(
        [grad_router, jnp.zeros((width, router_cols - grad_router.shape[1]), F32)], axis=1
    )

    def output_part(core):
        low, high = branch[:, :half_cols], branch[:, half_cols:]
        part = dot_nn(att_t[...], jnp.where(core == 0, low, high))
        return jnp.concatenate([part, jnp.where(core == 0, router_wide, 0.0)], axis=1)

    unit(units).begin(output_part(1 - p.c))
    act("O0")
    loads[5].wait()
    datt[...] = (
        dot_nt(branch[:, :half_cols], w_ref[units, 0]) + dot_nt(branch[:, half_cols:], w_ref[units, 1])
    ).astype(BF16)
    act("D0")
    unit(units).stage_core(output_part(p.c))
    act("Q0")
    attention_delta(datt, att_t, datt_t, delta)
    for copy in loads[6:]:
        copy.wait()
    act("S0")

    def pair(at):
        pair_backward(
            at, rel_ref, near_ref, q_ref, k_ref, v_ref, q_t, k_t, datt, datt_t, delta, lse_t, dst, gq, gk, gv,
            gnear, gfar,
        )
        cols = pl.ds(pl.multiple_of(at * BLOCK, BLOCK), BLOCK)
        grads = jnp.concatenate([gq[:, cols], gk[:, cols], gv[:, cols]], axis=1)
        gnormed[...] += dot_nt(grads, w_ref[at // 2, lax.rem(at, 2)])
        return dot_nn(normed_t[...], grads)

    gnormed[...] = jnp.zeros_like(gnormed)

    def pairs(u, carry):
        unit(u).begin(pair(2 * u + 1 - p.c))
        after(u, "A")
        unit(u).stage_core(pair(2 * u + p.c))
        after(u, "B")
        return carry

    lax.fori_loop(0, units, pairs, 0)
    near_grads = jnp.dot(gnear[...], picks_ref[...], precision=HIGHEST, preferred_element_type=F32)
    buckets = lax.broadcasted_iota(jnp.int32, near_grads.shape, 1)
    low_sum = jnp.sum(gfar[:, :BLOCK], axis=1, keepdims=True)
    high_sum = jnp.sum(gfar[:, BLOCK:], axis=1, keepdims=True)
    bucket_count = rel_ref.shape[0]
    rel = near_grads + jnp.where(buckets == bucket_count // 2 - 1, low_sum, 0.0)
    small[0, :HEADS, :BLOCK] = rel + jnp.where(buckets == bucket_count - 1, high_sum, 0.0)
    tokens = x_ref[...].astype(F32)
    grad_norm, grad_gain_a = norm_backward(tokens, inverse_rms(tokens), gain_a[...], gnormed[...])
    gx_ref[...] = gmixed[...] + grad_norm
    small[0, HEADS + 1 : HEADS + 2, :] = grad_gain_a

    act("P0")
    for e in range(local):
        back.arrive(e)
    combined = dot_nn(owned.astype(BF16), returned[...].reshape(total, width))
    result_ref[...] = (mixed_ref[...] + gate * combined).astype(BF16)
    act("R0")
    small_out[...] = small_end(3)
    for e in range(local):
        back.drain(e)
    for u in range(units + 1):
        unit(u).drain()
    for stage in copies:
        for copy in stage:
            copy.wait_send()


def moving_backward(
    rel_bias, inputs, weights, gains, router, near, slot_col, routes,
    normed, q, k, v, att, lse, mixed, normed_f, cotangent, outs, grows, gates, wide, slots,
):
    count, width = inputs.shape
    local, narrow = outs.shape[:2]
    experts = router.shape[1]
    bucket_count = rel_bias.shape[0]
    deep, rows = wide // 2, width // (wide * 2)
    units = HEADS // 4
    pair_cols, out_cols = 3 * BLOCK, width // 2 + BLOCK * -(-experts // BLOCK)
    sds = jax.ShapeDtypeStruct
    smem = pl.BlockSpec(memory_space=pltpu.SMEM)
    any_spec = pl.BlockSpec(memory_space=pl.ANY)
    picks = np.zeros((4 * BLOCK, BLOCK), np.float32)
    picks[:, :bucket_count] = near_picks(bucket_count, -1)
    wide_t = lambda dtype: pltpu.VMEM((width, count), dtype)
    tall = lambda dtype: pltpu.VMEM((count, width), dtype)
    vmem = lambda *shape, dtype=BF16: pltpu.VMEM(shape, dtype)
    dma = pltpu.SemaphoreType.DMA
    hops = 3 + deep - 1
    result, grad_inputs, gw, go, small = pl.pallas_call(
        moving_backward_kernel,
        out_shape=(
            sds((count, width), BF16), sds((count, width), F32), sds((units, 2, rows // 2, pair_cols), F32),
            sds((1, 2, rows // 2, out_cols), F32), sds((16, width), F32),
        ),
        in_specs=[smem] + [any_spec] * 9 + in_vmem(11),
        out_specs=tuple(in_vmem(5)),
        scratch_shapes=[
            tall(BF16), pltpu.VMEM(weights.shape, BF16), tall(BF16), tall(BF16), tall(BF16), tall(BF16), tall(BF16),
            vmem(count, BLOCK, dtype=F32), dma((8,)),
            wide_t(BF16), wide_t(BF16), wide_t(BF16), wide_t(BF16), tall(BF16), wide_t(BF16),
            vmem(HEADS, count, dtype=F32), vmem(BLOCK, count, dtype=F32),
            tall(BF16), tall(BF16), tall(BF16), tall(F32), tall(F32), vmem(count, count),
            vmem(HEADS, 4 * BLOCK, dtype=F32), vmem(HEADS, 2 * BLOCK, dtype=F32),
            vmem(local, 2, wide, slots, width), vmem(local, 2, wide, slots, width), vmem(local, wide, slots, width),
            vmem(wide, local, slots, width),
            dma((local, 2)), *Collect.semaphores(local, wide),
            *sum_buffers(units, wide, rows, pair_cols), *sum_buffers(1, wide, rows, out_cols),
            vmem(4, 16, width, dtype=F32), vmem(hops, 16, width, dtype=F32), dma((hops,)), dma((hops,)),
        ],
        compiler_params=pltpu.CompilerParams(collective_id=3, has_side_effects=True, vmem_limit_bytes=62 << 20),
        name="backward",
    )(
        rel_bias, inputs, weights, normed, q, k, v, att, lse, outs,
        gains, router, near, slot_col, routes, mixed, normed_f, cotangent, grows, gates, jnp.asarray(picks),
    )
    kinds = [
        jnp.transpose(gw[..., at * BLOCK : (at + 1) * BLOCK], (2, 0, 1, 3)).reshape(rows // 2, width) for at in range(3)
    ]
    grad_output = jnp.transpose(go[0, :, :, : width // 2], (1, 0, 2)).reshape(rows // 2, width)
    grad_router = go[0, 0, :, width // 2 : width // 2 + experts]
    device = lax.axis_index("wide") * narrow + lax.axis_index("narrow")
    gain_grads = lax.dynamic_slice(small, (HEADS, device * (rows // 2)), (2, rows // 2))
    grad_rel = small[:HEADS, :bucket_count].T
    return result, grad_inputs, kinds, grad_output, grad_router, gain_grads[1], gain_grads[0], grad_rel


def in_vmem(count):
    return [pl.BlockSpec(memory_space=pltpu.VMEM)] * count


def shards(
    inputs, gain_attn, w_query, w_key, w_value, w_output, rel_bias, gain_ffn, w_router,
    expert_in, expert_out, routes, capacity, cotangent,
):
    count, width = inputs.shape
    experts = w_router.shape[1]
    local, _, hidden_width = expert_in.shape
    wide, narrow = lax.axis_size("wide"), lax.axis_size("narrow")
    slots = 2 * count // experts
    total = experts * slots
    bucket_count = rel_bias.shape[0]
    params = pltpu.CompilerParams(vmem_limit_bytes=60 << 20)
    smem = pl.BlockSpec(memory_space=pltpu.SMEM)

    near = jnp.dot(near_picks(bucket_count, 1), rel_bias, precision=HIGHEST).T
    near_back = jnp.dot(near_picks(bucket_count, -1), rel_bias, precision=HIGHEST).T

    moving = narrow == 4 and wide & (wide - 1) == 0 and local == HEADS // 4 + 1 and slots % 32 == 0 and local * slots % BLOCK == 0
    moving = moving and width % (wide * 2 * 16) == 0 and count == SEQ_LEN and experts + 8 <= BLOCK
    if moving:
        normed, q, k, v, att, lse, mixed, normed_f, sent, weights, cot_all, slot_col, router, gains = moving_forward(
            rel_bias, capacity, inputs, w_query, w_key, w_value, w_output, w_router, gain_attn, gain_ffn, near, routes,
            cotangent, wide, narrow, local, slots,
        )
        outs, back, gates, gin, gout = moving_experts(sent, cot_all, expert_in, expert_out, router, wide, narrow)
        result, grad_inputs, kinds, grad_output, grad_router, grad_gain_a, grad_gain_f, grad_rel = moving_backward(
            rel_bias, inputs, weights.reshape(HEADS // 4 + 1, 2, width, width // 2), gains, router, near_back,
            slot_col, routes, normed, q, k, v, att, lse, mixed, normed_f, cotangent, outs,
            back.reshape(total, width), gates.reshape(1, total), wide, slots,
        )
        return (
            result, grad_inputs, grad_gain_a, *kinds, grad_output, grad_rel, grad_gain_f, grad_router, gin, gout,
        )

    packed = jnp.concatenate([w_query, w_key, w_value, w_output], axis=1)
    weights = lax.all_gather(packed, BOTH, axis=0, tiled=True)
    small = lax.all_gather(
        jnp.concatenate([w_router, gain_attn[:, None], gain_ffn[:, None]], axis=1), BOTH, axis=0, tiled=True
    )
    router = small[:, :experts]
    gain_a = small[:, experts].astype(F32)[None, :]
    gain_f = small[:, experts + 1].astype(F32)[None, :]
    slot_col, slot_row, cot_sent = pl.pallas_call(
        lambda *refs: place_kernel(slots, experts, *refs),
        out_shape=(
            jax.ShapeDtypeStruct((count, 1), jnp.int32),
            jax.ShapeDtypeStruct((1, count), jnp.int32),
            jax.ShapeDtypeStruct((total, width), BF16),
        ),
        in_specs=[smem] + in_vmem(3),
        out_specs=tuple(in_vmem(3)),
        compiler_params=params,
        name="places",
    )(capacity, routes, routes.reshape(1, count), cotangent)

    def spread(rows):
        taken = lax.all_to_all(
            rows.reshape(wide, local * slots, width), "wide", split_axis=0, concat_axis=0, tiled=True
        )
        held = lax.all_gather(taken, "narrow", axis=0, tiled=True)
        return held.reshape(wide * narrow, local, slots, width)

    def collect(rows):
        own = lax.psum_scatter(
            rows.reshape(wide * narrow, local * slots, width), "narrow", scatter_dimension=0, tiled=True
        )
        back = lax.all_to_all(own, "wide", split_axis=0, concat_axis=0, tiled=True)
        return back.reshape(total, width)

    cot_all = spread(cot_sent)

    rows_t = lambda dtype, cols=width: jax.ShapeDtypeStruct((count, cols), dtype)
    normed, q, k, v, att, lse, mixed, normed_f, sent = pl.pallas_call(
        forward_kernel,
        out_shape=(
            rows_t(BF16), rows_t(BF16), rows_t(BF16), rows_t(BF16), rows_t(BF16), rows_t(F32, BLOCK),
            rows_t(F32), rows_t(BF16), jax.ShapeDtypeStruct((total, width), BF16),
        ),
        in_specs=[smem] + in_vmem(7),
        out_specs=tuple(in_vmem(9)),
        compiler_params=params,
        name="forward",
    )(rel_bias, inputs, weights, gain_a, gain_f, router, near, slot_row)

    rows_all = spread(sent)
    sources = wide * narrow
    block = pl.BlockSpec((sources, 1, slots, width), lambda e: (0, e, 0, 0))
    w_in_spec = pl.BlockSpec((1, width, hidden_width), lambda e: (e, 0, 0))
    w_out_spec = pl.BlockSpec((1, hidden_width, width), lambda e: (e, 0, 0))
    first_expert = (lax.axis_index("wide") * local).astype(jnp.int32)[None]
    back, grows, gin, gout = pl.pallas_call(
        expert_kernel,
        grid=(local,),
        out_shape=(
            jax.ShapeDtypeStruct(rows_all.shape, BF16),
            jax.ShapeDtypeStruct(rows_all.shape, BF16),
            jax.ShapeDtypeStruct(expert_in.shape, F32),
            jax.ShapeDtypeStruct(expert_out.shape, F32),
        ),
        in_specs=[
            smem, block, block, w_in_spec, w_out_spec, pl.BlockSpec((width, experts), lambda e: (0, 0)),
        ],
        out_specs=(block, block, w_in_spec, w_out_spec),
        scratch_shapes=[
            pltpu.VMEM((sources * slots, hidden_width), BF16),
            pltpu.VMEM((sources * slots, hidden_width), BF16),
            pltpu.VMEM((sources * slots, width), BF16),
        ],
        compiler_params=params,
        name="experts",
    )(first_expert, rows_all, cot_all, expert_in, expert_out, router)
    outs_back = collect(back)
    grows_back = collect(grows)
    gates = jnp.sum(outs_back.astype(F32) * cot_sent.astype(F32), axis=1)[None, :]

    wide_t = lambda dtype: pltpu.VMEM((width, count), dtype)
    tall = lambda dtype: pltpu.VMEM((count, width), dtype)
    result, grad_inputs, gw, grouter, gnear, gfar, ggain = pl.pallas_call(
        backward_kernel,
        out_shape=(
            rows_t(BF16), rows_t(F32), jax.ShapeDtypeStruct((width, 4 * width), BF16),
            jax.ShapeDtypeStruct((width, experts), F32), jax.ShapeDtypeStruct((HEADS, 4 * BLOCK), F32),
            jax.ShapeDtypeStruct((HEADS, 2 * BLOCK), F32), jax.ShapeDtypeStruct((2, width), F32),
        ),
        in_specs=[smem] + in_vmem(20),
        out_specs=tuple(in_vmem(7)),
        scratch_shapes=[
            wide_t(BF16), wide_t(BF16), wide_t(BF16), wide_t(BF16), tall(BF16), wide_t(BF16),
            pltpu.VMEM((HEADS, count), F32), pltpu.VMEM((BLOCK, count), F32),
            tall(BF16), tall(BF16), tall(BF16), tall(F32), pltpu.VMEM((count, count), BF16),
        ],
        compiler_params=params,
        name="backward",
    )(
        rel_bias, inputs, weights, gain_a, gain_f, router, near_back, slot_col, routes,
        normed, q, k, v, att, lse, mixed, normed_f, cotangent, outs_back, grows_back, gates,
    )

    gw = lax.psum_scatter(gw, BOTH, scatter_dimension=0, tiled=True).astype(F32)
    grad_query, grad_key, grad_value, grad_output = (gw[:, i * width : (i + 1) * width] for i in range(4))
    gsmall = lax.psum_scatter(
        jnp.concatenate([grouter, ggain.T], axis=1), BOTH, scatter_dimension=0, tiled=True
    )
    grad_rel = jnp.dot(near_picks(bucket_count, -1).T, gnear.T, precision=HIGHEST)
    low, high = jnp.sum(gfar[:, :BLOCK], axis=1), jnp.sum(gfar[:, BLOCK:], axis=1)
    grad_rel = grad_rel.at[bucket_count // 2 - 1].add(low).at[bucket_count - 1].add(high)
    grad_rel = lax.psum(grad_rel, BOTH)
    return (
        result, grad_inputs, gsmall[:, experts], grad_query, grad_key, grad_value, grad_output,
        grad_rel, gsmall[:, experts + 1], gsmall[:, :experts], gin, gout,
    )


def solution(mesh):
    return jax.shard_map(
        shards,
        mesh=mesh,
        in_specs=(
            P(BOTH, None),
            P(BOTH),
            P(BOTH, None),
            P(BOTH, None),
            P(BOTH, None),
            P(BOTH, None),
            P(),
            P(BOTH),
            P(BOTH, None),
            P("wide", None, "narrow"),
            P("wide", "narrow", None),
            P(BOTH, None),
            P(BOTH),
            P(BOTH, None),
        ),
        out_specs=(
            P(BOTH, None),
            P(BOTH, None),
            P(BOTH),
            P(BOTH, None),
            P(BOTH, None),
            P(BOTH, None),
            P(BOTH, None),
            P(),
            P(BOTH),
            P(BOTH, None),
            P("wide", None, "narrow"),
            P("wide", "narrow", None),
        ),
        check_vma=False,
    )
```

```python
import jax
import jax.numpy as jnp
import numpy as np
from jax import lax
from jax.experimental import pallas as pl
from jax.experimental.pallas import tpu as pltpu
from jax.sharding import PartitionSpec as P

HEADS = 12
SEQ_LEN = 512
BLOCK = 128
EPSILON = 1e-06
HIGHEST = lax.Precision.HIGHEST
ROOT_TWO_PI = 0.7978845608028654
CUBIC = 0.044715
BOTH = ("wide", "narrow")
F32 = jnp.float32
BF16 = jnp.bfloat16


def bucket_of(offsets, bucket_count):
    half_count = bucket_count // 2
    exact_count = half_count // 2
    distance = np.abs(offsets)
    scaled = exact_count + np.floor(
        np.log(np.maximum(distance, 1) / exact_count)
        / np.log(128.0 / exact_count)
        * (half_count - exact_count)
    ).astype(np.int64)
    scaled = np.minimum(scaled, half_count - 1)
    return ((offsets > 0) * half_count + np.where(distance < exact_count, distance, scaled)).astype(
        np.int32
    )


def near_picks(bucket_count, sign):
    offsets = sign * (np.arange(4 * BLOCK) - (2 * BLOCK - 1))
    picks = (bucket_of(offsets, bucket_count)[:, None] == np.arange(bucket_count)[None, :]).astype(
        np.float32
    )
    picks[-1] = 0.0
    return picks


def dot_nn(left, right):
    return lax.dot_general(left, right, (((1,), (0,)), ((), ())), preferred_element_type=F32)


def dot_nt(left, right):
    return lax.dot_general(left, right, (((1,), (1,)), ((), ())), preferred_element_type=F32)


def dot_tn(left, right):
    return lax.dot_general(left, right, (((0,), (0,)), ((), ())), preferred_element_type=F32)


def inverse_rms(values):
    return lax.rsqrt(jnp.mean(values * values, axis=-1, keepdims=True) + EPSILON)


def norm_backward(values, inverse, gain, grad_normed):
    scaled = grad_normed * gain
    grad_gain = jnp.sum(grad_normed * values * inverse, axis=0, keepdims=True)
    inner = jnp.mean(scaled * values, axis=-1, keepdims=True)
    return (inverse * (scaled - values * inverse * inverse * inner), grad_gain)


def softmax_lanes(logits):
    peak = jnp.max(logits, axis=-1, keepdims=True)
    exponent = jnp.exp(logits - peak)
    return exponent / jnp.sum(exponent, axis=-1, keepdims=True)


def toeplitz_near(near_row):
    spread = jnp.broadcast_to(near_row, (BLOCK, 4 * BLOCK))
    return pltpu.roll(spread, 3 * BLOCK + 1, 1, stride=1, stride_axis=0)[:, : 3 * BLOCK]


def bias_rows(near, near_row, row, blocks):
    far_low, far_high = near_row[:, :1], near_row[:, 4 * BLOCK - 2 : 4 * BLOCK - 1]
    pieces = []
    for column in range(blocks):
        distance = column - row
        if distance <= -2:
            pieces.append(jnp.broadcast_to(far_low, (BLOCK, BLOCK)))
        elif distance >= 2:
            pieces.append(jnp.broadcast_to(far_high, (BLOCK, BLOCK)))
        else:
            pieces.append(near[:, (distance + 1) * BLOCK : (distance + 2) * BLOCK])
    return jnp.concatenate(pieces, axis=1)


def near_biases(rel_ref, picks_ref):
    return lax.dot_general(
        rel_ref[...], picks_ref[...], (((0,), (0,)), ((), ())), precision=HIGHEST, preferred_element_type=F32
    )


def diagonal_sums(near_sum):
    padded = jnp.concatenate([near_sum, jnp.zeros((BLOCK, BLOCK), F32)], axis=1)
    groups = jnp.zeros((8, 4 * BLOCK), F32)
    for at in range(0, BLOCK, 8):
        groups = groups + pltpu.roll(padded[at : at + 8, :], BLOCK - 8 - at, 1)
    sums = groups[7:8, :]
    for at in range(7):
        sums = sums + pltpu.roll(groups[at : at + 1, :], 7 - at, 1)
    return sums


def slot_places(col, row, limit, experts, slots, count):
    lower = lax.broadcasted_iota(jnp.int32, (count, count), 0)
    upper = lax.broadcasted_iota(jnp.int32, (count, count), 1)
    chosen = lax.broadcasted_iota(jnp.int32, (count, experts), 1) == col
    running = dot_nn((upper <= lower).astype(BF16), chosen.astype(BF16))
    place = jnp.sum(jnp.where(chosen, running, 0.0), axis=1, keepdims=True).astype(jnp.int32) - 1
    slot_col = jnp.where(place < limit, col * slots + place, -1)
    chosen_t = lax.broadcasted_iota(jnp.int32, (experts, count), 0) == row
    running_t = dot_nn(chosen_t.astype(BF16), (lower <= upper).astype(BF16))
    place_t = (
        jnp.sum(jnp.where(chosen_t, running_t, 0.0), axis=0, keepdims=True).astype(jnp.int32) - 1
    )
    slot_row = jnp.where(place_t < limit, row * slots + place_t, -1)
    return slot_col, slot_row


def place_kernel(slots, experts, capacity_ref, routes_ref, row_ref, cot_ref, slot_col, slot_row, cot_out):
    count = routes_ref.shape[0]
    limit = capacity_ref[0] * count // experts
    col, row = slot_places(routes_ref[...], row_ref[...], limit, experts, slots, count)
    slot_col[...] = col
    slot_row[...] = row
    picks = (lax.broadcasted_iota(jnp.int32, (experts * slots, count), 0) == row).astype(BF16)
    cot_out[...] = dot_nn(picks, cot_ref[...]).astype(BF16)


def pair_forward(at, near_ref, q_ref, k_ref, v_ref, att_ref, lse_ref):
    count, width = q_ref.shape
    head_dim = width // HEADS
    blocks = count // BLOCK
    lanes = lax.broadcasted_iota(jnp.int32, (1, BLOCK), 1)
    first = lanes < head_dim
    cols = pl.ds(pl.multiple_of(at * BLOCK, BLOCK), BLOCK)
    k_pair, v_pair = k_ref[:, cols], v_ref[:, cols]
    near_rows = [near_ref[pl.ds(2 * at + half, 1), :] for half in range(2)]
    nears = [toeplitz_near(near_row) for near_row in near_rows]
    for row in range(blocks):
        rows = slice(row * BLOCK, (row + 1) * BLOCK)
        q_rows = q_ref[rows, cols] * jnp.asarray(head_dim**-0.5, BF16)
        found = []
        log_sums = lse_ref[rows, :]
        for half in range(2):
            head = 2 * at + half
            mask = first if half == 0 else jnp.logical_not(first)
            scores = dot_nt(jnp.where(mask, q_rows, jnp.zeros_like(q_rows)), k_pair)
            scores = scores + bias_rows(nears[half], near_rows[half], row, blocks)
            peak = jnp.max(scores, axis=-1, keepdims=True)
            exponent = jnp.exp(scores - peak)
            total = jnp.sum(exponent, axis=-1, keepdims=True)
            found.append(dot_nn((exponent * (1.0 / total)).astype(BF16), v_pair))
            log_sums = jnp.where(lanes == head, peak + jnp.log(total), log_sums)
        lse_ref[rows, :] = log_sums
        att_ref[rows, cols] = jnp.where(first, found[0], found[1]).astype(BF16)


def slot_rows(slot_row, values, total):
    picks = lax.broadcasted_iota(jnp.int32, (total, slot_row.shape[1]), 0) == slot_row
    return dot_nn(picks.astype(BF16), values).astype(BF16)


def forward_kernel(
    x_ref, w_ref, gain_a, gain_f, router_ref, near_ref, slot_row,
    normed_ref, q_ref, k_ref, v_ref, att_ref, lse_ref, mixed_ref, normed_f, sent_ref,
):
    width = x_ref.shape[1]
    tokens = x_ref[...].astype(F32)
    normed = (tokens * inverse_rms(tokens) * gain_a[...]).astype(BF16)
    normed_ref[...] = normed
    for out, at in ((q_ref, 0), (k_ref, 1), (v_ref, 2)):
        out[...] = dot_nn(normed, w_ref[:, at * width : (at + 1) * width]).astype(BF16)
    lse_ref[...] = jnp.zeros_like(lse_ref)

    def pair(at, carry):
        pair_forward(at, near_ref, q_ref, k_ref, v_ref, att_ref, lse_ref)
        return carry

    lax.fori_loop(0, HEADS // 2, pair, 0)
    mixed = tokens + dot_nn(att_ref[...], w_ref[:, 3 * width : 4 * width])
    mixed_ref[...] = mixed
    normed_2 = (mixed * inverse_rms(mixed) * gain_f[...]).astype(BF16)
    normed_f[...] = normed_2
    sent_ref[...] = slot_rows(slot_row[...], normed_2, sent_ref.shape[0])


def expert_kernel(
    first_ref, rows_ref, cot_ref, in_ref, out_ref, router_ref,
    back_ref, grows_ref, gin_ref, gout_ref, hidden_ref, gpre_ref, sg_ref,
):
    sources, _, slots, width = rows_ref.shape
    total = sources * slots
    step = min(256, total)
    expert = first_ref[0] + pl.program_id(0)

    def chunk(at, carry):
        these = pl.ds(pl.multiple_of(at * (step // slots), step // slots), step // slots)
        flat = pl.ds(pl.multiple_of(at * step, step), step)
        rows = rows_ref[these, 0].reshape(step, width)
        probs = softmax_lanes(dot_nn(rows, router_ref[...]))
        here = lax.broadcasted_iota(jnp.int32, probs.shape, 1) == expert
        gate = jnp.sum(jnp.where(here, probs, 0.0), axis=-1, keepdims=True)
        sg = (cot_ref[these, 0].reshape(step, width).astype(F32) * gate).astype(BF16)
        sg_ref[flat, :] = sg
        pre = dot_nn(rows, in_ref[0])
        square = pre * pre
        inner = jnp.tanh(pre * (ROOT_TWO_PI + ROOT_TWO_PI * CUBIC * square))
        half = 0.5 * (1.0 + inner)
        hidden = (pre * half).astype(BF16)
        hidden_ref[flat, :] = hidden
        slope = half + 0.5 * pre * (1.0 - inner * inner) * (
            ROOT_TWO_PI + 3.0 * ROOT_TWO_PI * CUBIC * square
        )
        gpre = (dot_nt(sg, out_ref[0]) * slope).astype(BF16)
        gpre_ref[flat, :] = gpre
        back_ref[these, 0] = dot_nn(hidden, out_ref[0]).astype(BF16).reshape(-1, slots, width)
        grows_ref[these, 0] = dot_nt(gpre, in_ref[0]).astype(BF16).reshape(-1, slots, width)
        return carry

    lax.fori_loop(0, total // step, chunk, 0)
    gout_ref[0] = dot_tn(hidden_ref[...], sg_ref[...])
    gin_ref[0] = dot_tn(rows_ref[:, 0].reshape(total, width), gpre_ref[...])


def remote(source, target, send, receive, device):
    return pltpu.make_async_remote_copy(
        src_ref=source,
        dst_ref=target,
        send_sem=send,
        recv_sem=receive,
        device_id=device,
        device_id_type=pl.DeviceIdType.MESH,
    )


def greet(devices):
    for device in devices:
        pl.semaphore_signal(
            pltpu.get_barrier_semaphore(), inc=1, device_id=device, device_id_type=pl.DeviceIdType.MESH
        )


def meet(devices):
    pl.semaphore_wait(pltpu.get_barrier_semaphore(), len(devices))


FORWARD_STEPS = {
    "first": (("send", 4, 0), ("start", 2, 0), ("start", 3, 0), ("send", 0, 0), ("start", 1, 0), ("spread", 4, 0),
        ("send", 1, 0), ("start", 0, 0), ("spread", 0, 0), ("send", 2, 0), ("start", 0, 2), ("forward", 1, 0),
        ("send", 3, 0), ("start", 1, 1), ("over_x", 4, 0), ("over_y", 4, 0), ("forward", 0, 0), ("spread", 1, 0),
        ("end", 4, 0), ("over_x", 0, 0), ("spread", 2, 0), ("start", 3, 2), ("over_y", 1, 0), ("forward", 3, 0),
        ("start", 3, 1), ("over_x", 1, 0), ("over_x", 2, 0), ("end", 0, 0), ("over_y", 0, 0), ("forward", 1, 1),
        ("start", 2, 2),),
    "N0": (("spread", 3, 0),),
    "A0": (("forward", 2, 0), ("pass", 1, 1), ("forward", 3, 1), ("pass", 3, 0), ("over_y", 2, 0),
        ("start", 1, 2), ("forward", 0, 2), ("forward", 3, 2), ("end", 1, 0),),
    "B0": (("start", 2, 1),),
    "A1": (("forward", 2, 2), ("end", 2, 0), ("start", 0, 1), ("over_x", 3, 0),),
    "A2": (("forward", 2, 1), ("forward", 1, 2), ("pass", 1, 0), ("pass", 2, 0), ("pass", 0, 0), ("pass", 3, 2),
        ("pass", 2, 2), ("pass", 0, 2), ("forward", 0, 1), ("end", 3, 0), ("over_y", 3, 0), ("pass", 3, 1),),
    "M0": (("pass", 1, 2), ("pass", 2, 1), ("pass", 0, 1),),
}

BACKWARD_STEPS = {
    "first": (("core", 3, 1), ("core", 2, 1), ("core", 2, 0),),
    "F0": (("go", 2, 1), ("core", 3, 0), ("near", 2, 0),),
    "O0": (("go", 3, 1),),
    "D0": (("core", 0, 1), ("core", 0, 0),),
    "Q0": (("go", 3, 2), ("near", 3, 0), ("core", 1, 1),),
    "S0": (("go", 2, 0), ("go", 0, 1), ("finish", 3, 1),),
    "A0": (("go", 1, 1), ("go", 0, 2), ("go", 2, 2), ("finish", 2, 1),),
    "B0": (("core", 1, 0),),
    "A1": (("near", 0, 0), ("finish", 3, 2), ("go", 1, 2), ("y", 3, 0), ("near", 1, 0),),
    "B1": (("finish", 0, 1), ("y", 0, 0), ("finish", 2, 2), ("finish", 2, 0), ("go", 0, 0), ("finish", 1, 2),),
    "B2": (("finish", 1, 1),),
    "P0": (("x", 3, 0), ("go", 3, 0), ("y", 1, 0), ("x", 0, 0), ("finish", 0, 2), ("y", 2, 0), ("finish", 0, 0),
        ("finish", 3, 0), ("x", 1, 0), ("x", 2, 0), ("go", 1, 0), ("small", 0, 0), ("small", 1, 0),
        ("small", 2, 0), ("finish", 1, 0), ("z", 0, 0), ("small", 3, 0), ("z", 3, 0), ("z", 1, 0), ("z", 2, 0),),
}

EXPERT_STEPS = {
    "first": (("start", 0, 0), ("start", 0, 2), ("start", 0, 1), ("forward", 0, 0), ("start", 1, 2),
        ("start", 1, 1), ("start", 1, 0), ("forward", 0, 2), ("start", 2, 2), ("forward", 0, 1), ("start", 3, 0),
        ("start", 2, 0), ("forward", 1, 0), ("pass", 0, 2), ("start", 2, 1), ("pass", 0, 1), ("pass", 0, 0),
        ("start", 3, 1), ("forward", 1, 2), ("forward", 1, 1),),
    "A0": (("pass", 1, 0), ("forward", 2, 0),),
    "B0": (("forward", 3, 0),),
    "C0": (("pass", 1, 2), ("forward", 2, 2), ("pass", 1, 1), ("go", 0, 1),),
    "A1": (("start", 3, 2),),
    "W0": (("forward", 2, 1),),
    "C1": (("sum", 0, 0), ("finish", 0, 1), ("pass", 2, 0), ("forward", 3, 1), ("go", 1, 1),),
    "D1": (("forward", 3, 2), ("sum", 1, 0), ("pass", 2, 2), ("pass", 2, 1), ("go", 0, 2),),
    "A2": (("go", 1, 0), ("go", 1, 2),),
    "B2": (("finish", 1, 1), ("go", 0, 0),),
    "W1": (("go", 2, 1), ("pass", 3, 2), ("pass", 3, 0), ("go", 2, 2),),
    "C2": (("finish", 0, 2),),
    "D2": (("pass", 3, 1),),
    "V1": (("sum", 2, 0), ("go", 2, 0), ("finish", 1, 2),),
    "B3": (("go", 3, 1), ("finish", 2, 1), ("go", 3, 2),),
    "W2": (("finish", 2, 2),),
    "D3": (("go", 3, 0), ("finish", 1, 0), ("finish", 0, 0), ("sum", 3, 0), ("finish", 3, 1),),
    "V2": (("finish", 3, 2), ("finish", 2, 0), ("finish", 3, 0),),
}


class Place:
    def __init__(self, wide):
        self.wide = wide
        self.run = wide // 2
        self.deep = wide // 2
        self.w, self.n = lax.axis_index("wide"), lax.axis_index("narrow")
        self.x, self.c = self.n // 2, lax.rem(self.n, 2)
        self.z, self.y = self.w // 2, lax.rem(self.w, 2)
        self.core = (self.w, self.x * 2 + 1 - self.c)
        self.side = (self.w, (1 - self.x) * 2 + self.c)
        self.row = (self.z * 2 + 1 - self.y, self.n)

    def flip(self, j):
        found, bit = self.w, 1
        while bit <= j:
            if j & bit:
                found = found + bit - 2 * bit * lax.rem(self.w // bit, 2)
            bit *= 2
        return found

    def peer(self, j):
        return (self.flip(j), self.n)

    def span(self, piece):
        half = self.w // self.run
        return pl.ds((1 - half if piece else half) * self.run, self.run)

    def steps(self, piece):
        return range(self.run, self.wide) if piece else range(1, self.run)

    def partners(self):
        return [self.peer(j) for j in range(1, self.wide)] + [self.core, self.side]


def slot_part(piece, slots):
    return pl.ds((piece - 1) * (slots // 2), slots // 2) if piece else pl.ds(0, slots)


PIECES = range(3)


class Spread:
    def __init__(self, place, sent, held, wide_s, wide_r, side_s, side_r, core_s, core_r):
        self.place, self.sent, self.held = place, sent, held
        self.wide_s, self.wide_r, self.side_s, self.side_r = wide_s, wide_r, side_s, side_r
        self.core_s, self.core_r = core_s, core_r
        self.slots = sent.shape[2]

    def hop(self, e, j, piece):
        p, part = self.place, slot_part(piece, self.slots)
        at = p.wide + j if piece == 2 else j
        return remote(
            self.sent.at[p.flip(j), e, part], self.held.at[e, p.n, p.w, part],
            self.wide_s.at[e, at], self.wide_r.at[e, at], p.peer(j),
        )

    def start(self, e, piece):
        for j in self.place.steps(piece):
            self.hop(e, j, piece).start()

    def beside(self, e, piece):
        p = self.place
        rows = self.held.at[e, p.n, p.span(piece), slot_part(piece, self.slots)]
        return remote(rows, rows, self.side_s.at[e, piece], self.side_r.at[e, piece], p.side)

    def over(self, e, other, piece):
        p = self.place
        m = (1 - p.x) * 2 + p.c if other else p.n
        rows = self.held.at[e, m, p.span(piece), slot_part(piece, self.slots)]
        at = 3 * other + piece
        return remote(rows, rows, self.core_s.at[e, at], self.core_r.at[e, at], p.core)

    def forward(self, e, piece):
        for j in self.place.steps(piece):
            self.hop(e, j, piece).wait_recv()
        self.beside(e, piece).start()
        self.over(e, 0, piece).start()

    def pass_on(self, e, piece):
        self.beside(e, piece).wait_recv()
        self.over(e, 1, piece).start()

    def arrive(self, e, other):
        for piece in PIECES:
            self.over(e, other, piece).wait_recv()

    def drain(self, e):
        for piece in PIECES:
            for j in self.place.steps(piece):
                self.hop(e, j, piece).wait_send()
            self.beside(e, piece).wait_send()
            self.over(e, 0, piece).wait_send()
            self.over(e, 1, piece).wait_send()

    @staticmethod
    def semaphores(local, wide):
        dma = pltpu.SemaphoreType.DMA
        return [dma((local, n)) for n in (2 * wide, 2 * wide, 3, 3, 6, 6)]


class Collect:
    def __init__(self, place, to_core, from_core, from_side, returned, semaphores):
        self.place, self.to_core, self.from_core = place, to_core, from_core
        self.from_side, self.returned = from_side, returned
        self.core_s, self.core_r, self.side_s, self.side_r, self.wide_s, self.wide_r = semaphores
        self.slots = from_side.shape[2]

    def core(self, e, other):
        return remote(
            self.to_core(e, other), self.from_core.at[e, other], self.core_s.at[e, other], self.core_r.at[e, other],
            self.place.core,
        )

    def beside(self, e, piece):
        rows, part = self.place.span(piece), slot_part(piece, self.slots)
        return remote(
            self.from_core.at[e, 1, rows, part], self.from_side.at[e, rows, part],
            self.side_s.at[e, piece], self.side_r.at[e, piece], self.place.side,
        )

    def back(self, e, j, piece):
        p, part = self.place, slot_part(piece, self.slots)
        at = p.wide + j if piece == 2 else j
        return remote(
            self.from_side.at[e, p.flip(j), part], self.returned.at[p.w, e, part],
            self.wide_s.at[e, at], self.wide_r.at[e, at], p.peer(j),
        )

    def go_beside(self, e, part):
        self.core(e, 1).wait_recv()
        held = self.from_core[e, 1].astype(F32)
        self.from_core[e, 1] = (part.astype(F32).reshape(held.shape) + held).astype(BF16)
        self.beside(e, 1).start()

    def finish(self, e, piece, own):
        p = self.place
        rows, part = p.span(piece), slot_part(piece, self.slots)
        self.beside(e, piece).wait_recv()
        total = own(rows, part) + self.from_side[e, rows, part].astype(F32)
        self.from_side[e, rows, part] = total.astype(BF16)
        for j in p.steps(piece):
            self.back(e, j, piece).start()
        if not piece:
            self.returned[p.w, e] = self.from_side[e, p.w]

    def drain(self, e):
        self.core(e, 0).wait_send()
        self.core(e, 1).wait_send()
        for piece in PIECES:
            self.beside(e, piece).wait_send()
            for j in self.place.steps(piece):
                self.back(e, j, piece).wait_send()

    def arrive(self, e):
        for piece in PIECES:
            for j in self.place.steps(piece):
                self.back(e, j, piece).wait_recv()

    @staticmethod
    def semaphores(local, wide):
        dma = pltpu.SemaphoreType.DMA
        return [dma((local, n)) for n in (2, 2, 3, 3, 2 * wide, 2 * wide)]


class Gather:
    def __init__(self, place, unit, held, halves, semaphores):
        self.p, self.u, self.held, self.halves = place, unit, held, halves
        self.s, self.r = semaphores

    def piece(self, *place):
        return self.held.at[self.u, self.p.c, *place] if self.halves else self.held.at[self.u, *place]

    def column(self, y, x):
        return self.piece(slice(None), y, x)

    def copy(self, piece, slot, device):
        return remote(piece, piece, self.s.at[self.u, slot], self.r.at[self.u, slot], device)

    def to_z(self, k):
        p = self.p
        z = lax.rem(p.z + k, p.deep)
        return self.copy(self.piece(p.z, p.y, p.x), k - 1, (z * 2 + p.y, p.n))

    def to_x(self):
        return self.copy(self.column(self.p.y, self.p.x), 3, self.p.side)

    def to_y(self):
        return self.copy(self.column(self.p.y, self.p.x), 4, self.p.row)

    def corner(self):
        return self.copy(self.column(self.p.y, 1 - self.p.x), 5, self.p.row)

    def to_core(self, at):
        p = self.p
        y, x = ((p.y, p.x), (p.y, 1 - p.x), (1 - p.y, p.x), (1 - p.y, 1 - p.x))[at]
        return self.copy(self.column(y, x), 6 + at, p.core)

    def hand(self, at):
        if self.halves:
            self.to_core(at).start()

    def start(self):
        for k in range(1, self.p.deep):
            self.to_z(k).start()

    def spread(self):
        for k in range(1, self.p.deep):
            self.to_z(k).wait_recv()
        self.to_x().start()
        self.to_y().start()
        self.hand(0)

    def over_x(self):
        self.to_x().wait_recv()
        self.corner().start()
        self.hand(1)

    def over_y(self):
        self.to_y().wait_recv()
        self.hand(2)

    def end(self):
        self.corner().wait_recv()
        self.hand(3)

    def arrive(self):
        if self.halves:
            for at in range(4):
                self.to_core(at).wait_recv()

    def drain(self):
        for k in range(1, self.p.deep):
            self.to_z(k).wait_send()
        for copy in (self.to_x(), self.to_y(), self.corner()):
            copy.wait_send()
        if self.halves:
            for at in range(4):
                self.to_core(at).wait_send()


def moving_forward_kernel(
    capacity_ref, x_ref, q_part, k_part, v_part, o_part, router_part, gain_a_part, gain_f_part, rel_ref, picks_ref, row_ref,
    cot_ref,
    normed_out, q_out, k_out, v_out, att_out, lse_out, mixed_out, normed_f_out, sent_out, weights_out, cot_out,
    slot_route, router_out, gains_out,
    normed_ref, q_ref, k_ref, v_ref, att_ref, lse_ref, mixed_ref, normed_f, sent_ref, store_s,
    near_ref, gain_lanes, small_lanes, small_part,
    held, small, pair_send, pair_got, small_got, cot_sent, weight_s, pair_s, pair_r,
    gs, gr, hs, hr, wide_s, wide_r, side_s, side_r, core_s, core_r,
):
    count, width = x_ref.shape
    wide, local, slots, _ = cot_sent.shape
    experts = router_out.shape[1]
    total = wide * local * slots
    units = HEADS // 4
    rows = pair_send.shape[2]
    p = Place(wide)
    greet(p.partners())

    def own_cols(u, half):
        if u == units:
            return o_part[:, half * (width // 2) : (half + 1) * (width // 2)]
        cols = slice((2 * u + half) * BLOCK, (2 * u + half + 1) * BLOCK)
        return jnp.concatenate([q_part[:, cols], k_part[:, cols], v_part[:, cols]], axis=1)

    def swap_copies():
        return [
            remote(pair_send.at[0], pair_got.at[0], pair_s.at[0], pair_r.at[0], p.core),
            remote(small_part, small_got, pair_s.at[1], pair_r.at[1], p.core),
        ]

    gain_lanes[...] = jnp.zeros_like(gain_lanes)
    gain_lanes[0:1, :rows] = gain_a_part[...].astype(F32)
    gain_lanes[1:2, :rows] = gain_f_part[...].astype(F32)
    gain_cols = gain_lanes[...].T[:rows, :]
    small_lanes[...] = jnp.zeros_like(small_lanes)
    small_lanes[:, :experts] = router_part[...].astype(F32)
    lanes = lax.broadcasted_iota(jnp.int32, small_lanes.shape, 1)
    others = jnp.where(lanes == experts + 1, gain_cols[:, 1:2], small_lanes[...])
    small_part[...] = jnp.where(lanes == experts, gain_cols[:, 0:1], others).astype(BF16)
    for u in range(units + 1):
        pair_send[0, u] = jnp.where(p.c == 0, own_cols(u, 1), own_cols(u, 0))
    limit = capacity_ref[0] * count // experts
    routes = jnp.broadcast_to(row_ref[...].astype(F32), (8, count)).T[:, :1].astype(jnp.int32)
    slot_col, slot_row = slot_places(routes, row_ref[...], limit, experts, slots, count)
    slot_route[:, 0:1] = slot_col
    slot_route[:, 1:2] = routes
    near_ref[...] = near_biases(rel_ref, picks_ref)
    cot_sent[...] = slot_rows(slot_row, cot_ref[...], total).reshape(cot_sent.shape)
    moves = Spread(p, cot_sent, cot_out, wide_s, wide_r, side_s, side_r, core_s, core_r)

    def own_rows(e):
        return pltpu.make_async_copy(cot_sent.at[p.w, e], cot_out.at[e, p.n, p.w], weight_s.at[1 + e])

    for e in range(local):
        own_rows(e).start()
    lse_ref[...] = jnp.zeros_like(lse_ref)
    for e in range(local):
        own_rows(e).wait()
    meet(p.partners())
    for copy in swap_copies():
        copy.start()
    for copy in swap_copies():
        copy.wait_recv()

    def joined(mine, other):
        mine, other = mine.astype(F32), other.astype(F32)
        return jnp.concatenate(
            [jnp.where(p.c == 0, mine, other), jnp.where(p.c == 0, other, mine)], axis=0
        ).astype(BF16)

    def gather(u):
        if isinstance(u, int) and u > units:
            return small_gather
        return Gather(p, u, held, True, (gs, gr))

    small_gather = Gather(p, 0, small, False, (hs, hr))
    small[0, p.z, p.y, p.x] = joined(small_part[...], small_got[...])
    for u in range(units + 1):
        mine = jnp.where(p.c == 0, own_cols(u, 0), own_cols(u, 1))
        held[u, p.c, p.z, p.y, p.x] = joined(mine, pair_got[0, u])

    acts = {
        "start": moves.start, "forward": moves.forward, "pass": moves.pass_on,
        "send": lambda u, piece: gather(u).start(), "spread": lambda u, piece: gather(u).spread(),
        "over_x": lambda u, piece: gather(u).over_x(), "over_y": lambda u, piece: gather(u).over_y(),
        "end": lambda u, piece: gather(u).end(),
    }

    def act(steps):
        for name, at, piece in steps:
            acts[name](at, piece)

    def after(u, part):
        for at in range(units):
            steps = FORWARD_STEPS.get(part + str(at), ())
            if steps:
                pl.when(u == at)(lambda steps=steps: act(steps))

    act(FORWARD_STEPS["first"])
    small_all = small[0].reshape(width, BLOCK)
    router_out[...] = small_all[:, :experts]
    gains_out[...] = small_all.astype(F32).T[experts : experts + 8, :]
    tokens = x_ref[...].astype(F32)
    normed_ref[...] = (tokens * inverse_rms(tokens) * gains_out[0:1, :]).astype(BF16)
    act(FORWARD_STEPS.get("N0", ()))

    def pair(at, weight):
        cols = pl.ds(pl.multiple_of(at * BLOCK, BLOCK), BLOCK)
        found = dot_nn(normed_ref[...], weight.reshape(width, 3 * BLOCK)).astype(BF16)
        q_ref[:, cols], k_ref[:, cols], v_ref[:, cols] = (found[:, i * BLOCK : (i + 1) * BLOCK] for i in range(3))
        pair_forward(at, near_ref, q_ref, k_ref, v_ref, att_ref, lse_ref)

    def pairs(u, carry):
        gather(u).arrive()
        pair(2 * u, held[u, 0])
        after(u, "A")
        pair(2 * u + 1, held[u, 1])
        after(u, "B")
        return carry

    lax.fori_loop(0, units, pairs, 0)
    stores = [
        pltpu.make_async_copy(source, target, store_s.at[at])
        for at, (source, target) in enumerate((
            (normed_ref, normed_out), (q_ref, q_out), (k_ref, k_out), (v_ref, v_out), (att_ref, att_out),
            (lse_ref, lse_out), (mixed_ref, mixed_out), (normed_f, normed_f_out), (sent_ref, sent_out),
        ))
    ]
    for copy in stores[:6]:
        copy.start()
    gather(units).arrive()
    weights_copy = pltpu.make_async_copy(held, weights_out, weight_s.at[0])
    weights_copy.start()
    mixed = tokens_again(x_ref) + jnp.concatenate(
        [dot_nn(att_ref[...], held[units, half].reshape(width, width // 2)) for half in range(2)], axis=1
    )
    mixed_ref[...] = mixed
    normed_2 = (mixed * inverse_rms(mixed) * gains_out[1:2, :]).astype(BF16)
    normed_f[...] = normed_2
    stores[6].start()
    stores[7].start()
    sent_ref[...] = slot_rows(slot_row, normed_2, total).reshape(sent_ref.shape)
    stores[8].start()
    act(FORWARD_STEPS.get("M0", ()))
    for copy in swap_copies():
        copy.wait_send()
    small_gather.drain()
    for u in range(units + 1):
        gather(u).drain()
    for e in range(local):
        moves.arrive(e, 0)
        moves.arrive(e, 1)
        moves.drain(e)
    weights_copy.wait()
    for copy in stores:
        copy.wait()


def tokens_again(x_ref):
    return x_ref[...].astype(F32)


def moving_forward(
    rel_bias, capacity, inputs, w_query, w_key, w_value, w_output, w_router, gain_attn, gain_ffn, routes, cotangent,
    wide, narrow, local, slots,
):
    count, width = inputs.shape
    experts = w_router.shape[1]
    shard = w_query.shape[0]
    deep, units = wide // 2, HEADS // 4
    half = width // 2
    sds = jax.ShapeDtypeStruct
    rows_t = lambda dtype, cols=width: sds((count, cols), dtype)
    smem, any_spec = pl.BlockSpec(memory_space=pltpu.SMEM), pl.BlockSpec(memory_space=pl.ANY)
    vmem = lambda *shape, dtype=BF16: pltpu.VMEM(shape, dtype)
    dma = pltpu.SemaphoreType.DMA
    picks = jnp.asarray(near_picks(rel_bias.shape[0], 1).T)
    return pl.pallas_call(
        moving_forward_kernel,
        out_shape=(
            rows_t(BF16), rows_t(BF16), rows_t(BF16), rows_t(BF16), rows_t(BF16), rows_t(F32, BLOCK), rows_t(F32),
            rows_t(BF16), sds((wide, local, slots, width), BF16),
            sds((units + 1, 2, deep, 2, 2, 2 * shard, half), BF16),
            sds((local, narrow, wide, slots, width), BF16), sds((count, 2), jnp.int32),
            sds((width, experts), BF16), sds((8, width), F32),
        ),
        in_specs=[smem] + in_vmem(12),
        out_specs=(any_spec,) * 11 + tuple(in_vmem(3)),
        scratch_shapes=[
            vmem(count, width), vmem(count, width), vmem(count, width), vmem(count, width), vmem(count, width),
            vmem(count, BLOCK, dtype=F32), vmem(count, width, dtype=F32), vmem(count, width),
            vmem(wide, local, slots, width), dma((9,)),
            vmem(HEADS, 4 * BLOCK, dtype=F32), vmem(8, BLOCK, dtype=F32), vmem(shard, BLOCK, dtype=F32), vmem(shard, BLOCK),
            vmem(units + 1, 2, deep, 2, 2, 2 * shard, half), vmem(1, deep, 2, 2, 2 * shard, BLOCK),
            vmem(1, units + 1, shard, half), vmem(1, units + 1, shard, half), vmem(shard, BLOCK),
            vmem(wide, local, slots, width), dma((1 + local,)), dma((2,)), dma((2,)),
            dma((units + 1, 10)), dma((units + 1, 10)), dma((1, 10)), dma((1, 10)),
            *Spread.semaphores(local, wide),
        ],
        compiler_params=pltpu.CompilerParams(collective_id=1, has_side_effects=True, vmem_limit_bytes=62 << 20),
        name="forward",
    )(
        capacity, inputs, w_query, w_key, w_value, w_output, w_router, gain_attn[None, :], gain_ffn[None, :], rel_bias, picks,
        routes.reshape(1, count), cotangent,
    )


def moving_expert_kernel(
    sent, cot_hbm, in_hbm, out_hbm, router_ref,
    outs_o, gin_o, gout_o, back_o, gate_o,
    held, cot, w_in, w_out, sg, hidden, gpre, outs, gin, gout, to_core, from_core, from_side, near_sum, far_sum,
    gate_sum, gate_core, gate_from_core, gate_side, gate_from_side, gate_ready,
    load_s, store_s, wide_s, wide_r, side_s, side_r, core_s, core_r,
    rc_s, rc_r, rx_s, rx_r, rw_s, rw_r, gc_s, gc_r, gx_s, gx_r, gw_s, gw_r,
):
    wide, local, slots, width = sent.shape
    narrow = held.shape[1]
    step = wide * slots
    hidden_width = in_hbm.shape[2]
    p = Place(wide)
    moves = Spread(p, sent, held, wide_s, wide_r, side_s, side_r, core_s, core_r)
    greet(p.partners())

    def loads(e):
        return [
            pltpu.make_async_copy(in_hbm.at[e], w_in.at[e], load_s.at[e, 0]),
            pltpu.make_async_copy(out_hbm.at[e], w_out.at[e], load_s.at[e, 1]),
            pltpu.make_async_copy(cot_hbm.at[e], cot.at[e], load_s.at[e, 2]),
        ]

    def store(e, at):
        source = (outs.at[lax.rem(e, 2)], gin, gout)[at]
        return pltpu.make_async_copy(source, (outs_o, gin_o, gout_o)[at].at[e], store_s.at[e, at])

    def grads_out(e):
        b = lax.rem(e, 2)

        @pl.when(e > 0)
        def _():
            store(e - 1, 2).wait()

        rows = narrow * step
        found = dot_tn(hidden[b].reshape(rows, hidden_width), sg[b].reshape(rows, width))
        gout[...] = found.astype(BF16)
        store(e, 2).start()

    def grads_in(e):
        b = lax.rem(e, 2)

        @pl.when(e > 0)
        def _():
            store(e - 1, 1).wait()

        rows = narrow * step
        found = dot_tn(held[e].reshape(rows, width), gpre[b].reshape(rows, hidden_width))
        gin[...] = found.astype(BF16)
        store(e, 1).start()

    for e in range(local):
        for copy in loads(e):
            copy.start()
        held[e, p.n, p.w] = sent[p.w, e]
    gate_sum[...] = jnp.zeros_like(gate_sum)
    meet(p.partners())

    def chunk(e, m):
        b = lax.rem(e, 2)
        rows = held[e, m].reshape(step, width)
        probs = softmax_lanes(dot_nn(rows, router_ref[...]))
        here = lax.broadcasted_iota(jnp.int32, probs.shape, 1) == p.w * local + e
        gate = jnp.sum(jnp.where(here, probs, 0.0), axis=-1, keepdims=True)
        cot_rows = cot[e, m].reshape(step, width).astype(F32)
        sg_rows = (cot_rows * gate).astype(BF16)
        sg[b, m] = sg_rows
        pre = dot_nn(rows, w_in[e])
        square = pre * pre
        inner = jnp.tanh(pre * (ROOT_TWO_PI + ROOT_TWO_PI * CUBIC * square))
        half = 0.5 * (1.0 + inner)
        hidden_rows = (pre * half).astype(BF16)
        hidden[b, m] = hidden_rows
        slope = half + 0.5 * pre * (1.0 - inner * inner) * (
            ROOT_TWO_PI + 3.0 * ROOT_TWO_PI * CUBIC * square
        )
        gpre_rows = (dot_nt(sg_rows, w_out[e]) * slope).astype(BF16)
        gpre[b, m] = gpre_rows
        out_rows = dot_nn(hidden_rows, w_out[e])
        outs[b, m] = out_rows.astype(BF16).reshape(wide, slots, width)
        gate_rows = jnp.sum(out_rows * cot_rows, axis=-1, keepdims=True)
        row = lax.broadcasted_iota(jnp.int32, (step, local * slots), 0)
        lane = lax.broadcasted_iota(jnp.int32, (step, local * slots), 1)
        spread = jnp.where(lane == e * slots + lax.rem(row, slots), gate_rows, 0.0)
        gate_sum[m] += jnp.sum(spread.reshape(wide, slots, local * slots), axis=1)
        return dot_nt(gpre_rows, w_in[e])

    back = Collect(
        p, lambda e, other: to_core.at[e, other], from_core, from_side, back_o, (rc_s, rc_r, rx_s, rx_r, rw_s, rw_r)
    )

    def go(e, piece):
        if piece == 1:
            back.go_beside(e, far_sum[...])
        else:
            back.beside(e, piece).start()

    def add_core(e, piece):
        back.core(e, 0).wait_recv()
        near_sum[e] = near_sum[e] + from_core[e, 0].astype(F32)

    acts = {
        "start": moves.start, "forward": moves.forward, "pass": moves.pass_on, "go": go, "sum": add_core,
        "finish": lambda e, piece: back.finish(e, piece, lambda rows, part: near_sum[e, rows, part]),
    }

    def after(e, part):
        for at in range(local):
            steps = EXPERT_STEPS.get(part + str(at), ())
            if steps:

                def run(steps=steps):
                    for name, expert, piece in steps:
                        acts[name](expert, piece)

                if not isinstance(e, int):
                    pl.when(e == at)(run)
                elif e == at:
                    run()

    for name, expert, piece in EXPERT_STEPS["first"]:
        acts[name](expert, piece)

    far_x = (1 - p.x) * 2

    gates_core = remote(gate_core, gate_from_core, gc_s, gc_r, p.core)

    def gates_core_start():
        gate_core[0] = gate_sum[p.x * 2 + 1 - p.c]
        gate_core[1] = gate_sum[far_x + 1 - p.c]
        gates_core.start()

    def expert(e, carry):
        for copy in loads(e):
            copy.wait()

        @pl.when(e >= 2)
        def _():
            store(e - 2, 0).wait()

        moves.arrive(e, 1)
        to_core[e, 1] = chunk(e, far_x + 1 - p.c).astype(BF16).reshape(wide, slots, width)
        back.core(e, 1).start()
        after(e, "A")
        far_sum[...] = chunk(e, far_x + p.c).reshape(wide, slots, width)
        after(e, "B")

        @pl.when(e > 0)
        def _():
            grads_out(e - 1)
            after(e - 1, "W")

        moves.arrive(e, 0)
        to_core[e, 0] = chunk(e, p.x * 2 + 1 - p.c).astype(BF16).reshape(wide, slots, width)
        back.core(e, 0).start()
        after(e, "C")
        near_sum[e] = chunk(e, p.n).reshape(wide, slots, width)
        store(e, 0).start()

        @pl.when(e == local - 1)
        def _():
            gates_core_start()

        after(e, "D")

        @pl.when(e > 0)
        def _():
            grads_in(e - 1)
            after(e - 1, "V")

        return carry

    lax.fori_loop(0, local, expert, 0)
    gates_core.wait_recv()
    gate_side[...] = gate_sum[far_x + p.c] + gate_from_core[1]
    gates_side = remote(gate_side, gate_from_side, gx_s, gx_r, p.side)
    gates_side.start()
    grads_out(local - 1)
    after(local - 1, "W")
    gates_side.wait_recv()
    gates = gate_sum[p.n] + gate_from_core[0] + gate_from_side[...]
    for v in range(wide):
        gate_ready[v] = gates[v : v + 1, :]
    gates_wide = [
        remote(gate_ready.at[p.flip(j)], gate_o.at[p.w], gw_s.at[j], gw_r.at[j], p.peer(j)) for j in range(1, wide)
    ]
    for copy in gates_wide:
        copy.start()
    gate_o[p.w] = gate_ready[p.w]
    grads_in(local - 1)
    after(local - 1, "V")
    gates_core.wait_send()
    gates_side.wait_send()

    def drain(e, carry):
        moves.drain(e)
        back.drain(e)
        back.arrive(e)

        @pl.when(e >= local - 2)
        def _():
            store(e, 0).wait()

        return carry

    lax.fori_loop(0, local, drain, 0)
    store(local - 1, 1).wait()
    store(local - 1, 2).wait()
    for copy in gates_wide:
        copy.wait()


def moving_experts(sent, cot_all, expert_in, expert_out, router, wide, narrow):
    _, local, slots, width = sent.shape
    hidden_width = expert_in.shape[2]
    step = wide * slots
    sds = jax.ShapeDtypeStruct
    any_spec, vmem_spec = pl.BlockSpec(memory_space=pl.ANY), pl.BlockSpec(memory_space=pltpu.VMEM)
    dma = pltpu.SemaphoreType.DMA
    outs, gin, gout, back, gates = pl.pallas_call(
        moving_expert_kernel,
        out_shape=(
            sds((local, narrow, wide, slots, width), BF16),
            sds(expert_in.shape, BF16),
            sds(expert_out.shape, BF16),
            sds((wide, local, slots, width), BF16),
            sds((wide, 1, local * slots), F32),
        ),
        in_specs=[vmem_spec, any_spec, any_spec, any_spec, vmem_spec],
        out_specs=(any_spec,) * 3 + (vmem_spec,) * 2,
        scratch_shapes=[
            pltpu.VMEM((local, narrow, wide, slots, width), BF16),
            pltpu.VMEM((local, narrow, wide, slots, width), BF16),
            pltpu.VMEM(expert_in.shape, BF16),
            pltpu.VMEM(expert_out.shape, BF16),
            pltpu.VMEM((2, narrow, step, width), BF16),
            pltpu.VMEM((2, narrow, step, hidden_width), BF16),
            pltpu.VMEM((2, narrow, step, hidden_width), BF16),
            pltpu.VMEM((2, narrow, wide, slots, width), BF16),
            pltpu.VMEM(expert_in.shape[1:], BF16),
            pltpu.VMEM(expert_out.shape[1:], BF16),
            pltpu.VMEM((local, 2, wide, slots, width), BF16),
            pltpu.VMEM((local, 2, wide, slots, width), BF16),
            pltpu.VMEM((local, wide, slots, width), BF16),
            pltpu.VMEM((local, wide, slots, width), F32),
            pltpu.VMEM((wide, slots, width), F32),
            pltpu.VMEM((narrow, wide, local * slots), F32),
            pltpu.VMEM((2, wide, local * slots), F32),
            pltpu.VMEM((2, wide, local * slots), F32),
            pltpu.VMEM((wide, local * slots), F32),
            pltpu.VMEM((wide, local * slots), F32),
            pltpu.VMEM((wide, 1, local * slots), F32),
            dma((local, 3)), dma((local, 3)), *Spread.semaphores(local, wide), *Collect.semaphores(local, wide),
            dma, dma, dma, dma, dma((wide,)), dma((wide,)),
        ],
        compiler_params=pltpu.CompilerParams(
            collective_id=2, has_side_effects=True, vmem_limit_bytes=62 << 20
        ),
        name="experts",
    )(sent, cot_all, expert_in, expert_out, router)
    return outs, back, gates, gin.astype(F32), gout.astype(F32)


def routed_gate(normed_f, router_ref, routes):
    probs = softmax_lanes(dot_nn(normed_f[...], router_ref[...]))
    chosen = lax.broadcasted_iota(jnp.int32, probs.shape, 1) == routes
    return probs, chosen, jnp.sum(jnp.where(chosen, probs, 0.0), axis=-1, keepdims=True)


def slot_owners(slot_col, total):
    return lax.broadcasted_iota(jnp.int32, (slot_col.shape[0], total), 1) == slot_col


def ffn_backward(probs, chosen, gate, owned, gates_ref, normed_f, router_ref, grows_ref, mixed, cot_ref, gain_f):
    grad_gate = jnp.sum(jnp.where(owned, gates_ref[...], 0.0), axis=-1, keepdims=True)
    grad_logits = (probs * (jnp.where(chosen, grad_gate, 0.0) - gate * grad_gate)).astype(BF16)
    grad_router = dot_tn(normed_f[...], grad_logits)
    grad_normed = dot_nt(grad_logits, router_ref[...]) + dot_nn(owned.astype(BF16), grows_ref[...])
    grad_norm, grad_gain = norm_backward(mixed, inverse_rms(mixed), gain_f[...], grad_normed)
    return grad_router, cot_ref[...].astype(F32) + grad_norm, grad_gain


def attention_setup(q_ref, k_ref, normed_ref, att_ref, lse_ref, q_t, k_t, normed_t, att_t, lse_t):
    head_dim = q_ref.shape[1] // HEADS
    att_t[...] = att_ref[...].T
    q_t[...] = (q_ref[...] * jnp.asarray(head_dim**-0.5, BF16)).T
    k_t[...] = k_ref[...].T
    normed_t[...] = normed_ref[...].T
    lse_t[...] = lse_ref[...].T


def attention_delta(datt, att_t, datt_t, delta):
    width, count = att_t.shape
    datt_t[...] = datt[...].T
    products = datt_t[...].astype(F32) * att_t[...].astype(F32)
    delta[...] = jnp.sum(products.reshape(HEADS, width // HEADS, count), axis=1)


def pair_backward(
    at, near_ref, q_ref, k_ref, v_ref, q_t, k_t, datt, datt_t, delta, lse_t, dst, gq, gk, gv, gnear_ref, gfar_ref
):
    count, width = q_ref.shape
    head_dim = width // HEADS
    blocks = count // BLOCK
    first = lax.broadcasted_iota(jnp.int32, (1, BLOCK), 1) < head_dim
    cols = pl.ds(pl.multiple_of(at * BLOCK, BLOCK), BLOCK)
    q_pair, datt_pair = q_ref[:, cols], datt[:, cols]
    gq_parts, gk_parts, gv_parts = [], [], []
    for half in range(2):
        head = 2 * at + half
        mask = first if half == 0 else jnp.logical_not(first)
        near_row = near_ref[pl.ds(head, 1), :]
        near = toeplitz_near(near_row)
        lse_row, delta_row = lse_t[pl.ds(head, 1), :], delta[pl.ds(head, 1), :]
        near_sum = jnp.zeros((BLOCK, 3 * BLOCK), F32)
        low_sum, high_sum = jnp.zeros((BLOCK, BLOCK), F32), jnp.zeros((BLOCK, BLOCK), F32)
        gk_rows, gv_rows = [], []
        for row in range(blocks):
            rows = slice(row * BLOCK, (row + 1) * BLOCK)
            k_rows, v_rows = k_ref[rows, cols], v_ref[rows, cols]
            zeros = jnp.zeros_like(k_rows)
            scores = dot_nn(jnp.where(mask, k_rows, zeros), q_t[cols, :])
            scores = scores + bias_rows(near, near_row, row, blocks)
            weights = jnp.exp(scores - lse_row)
            grad_weights = dot_nn(jnp.where(mask, v_rows, zeros), datt_t[cols, :])
            grad_scores = weights * (grad_weights - delta_row)
            gv_rows.append(dot_nn(weights.astype(BF16), datt_pair))
            low_bits = grad_scores.astype(BF16)
            dst[rows, :] = low_bits
            gk_rows.append(dot_nn(low_bits, q_pair))
            for column in range(blocks):
                piece = grad_scores[:, column * BLOCK : (column + 1) * BLOCK]
                distance = column - row
                if distance <= -2:
                    high_sum = high_sum + piece
                elif distance >= 2:
                    low_sum = low_sum + piece
                else:
                    pads = [jnp.zeros((BLOCK, BLOCK), F32)] * 3
                    pads[distance + 1] = piece
                    near_sum = near_sum + jnp.concatenate(pads, axis=1)
        gq_parts.append(
            dot_nn(k_t[pl.ds(pl.multiple_of(head * head_dim, head_dim), head_dim), :], dst[...])
        )
        gk_parts.append(jnp.concatenate(gk_rows, axis=0))
        gv_parts.append(jnp.concatenate(gv_rows, axis=0))
        gnear_ref[pl.ds(head, 1), :] = diagonal_sums(near_sum)
        gfar_ref[pl.ds(head, 1), :] = jnp.concatenate(
            [jnp.sum(low_sum, axis=0, keepdims=True), jnp.sum(high_sum, axis=0, keepdims=True)], axis=1
        )
    scale = head_dim**-0.5
    gq[:, cols] = (jnp.concatenate(gq_parts, axis=0).T * scale).astype(BF16)
    gk[:, cols] = (jnp.where(first, gk_parts[0], gk_parts[1]) * scale).astype(BF16)
    gv[:, cols] = jnp.where(first, gv_parts[0], gv_parts[1]).astype(BF16)


def input_backward(x_ref, w_ref, gain_a, gmixed, gq, gk, gv):
    count, width = x_ref.shape
    grad_normed = jnp.zeros((count, width), F32)
    for at, grad in enumerate((gq, gk, gv)):
        grad_normed = grad_normed + dot_nt(grad[...], w_ref[:, at * width : (at + 1) * width])
    tokens = x_ref[...].astype(F32)
    grad_norm, grad_gain = norm_backward(tokens, inverse_rms(tokens), gain_a[...], grad_normed)
    return gmixed[...] + grad_norm, grad_gain


def backward_kernel(
    x_ref, w_ref, gain_a, gain_f, router_ref, near_ref, slot_col, routes_ref,
    normed_ref, q_ref, k_ref, v_ref, att_ref, lse_ref, mixed_ref, normed_f, cot_ref, outs_ref, grows_ref, gates_ref,
    result_ref, gx_ref, gw_ref, grouter_ref, gnear_ref, gfar_ref, ggain_ref,
    q_t, k_t, normed_t, att_t, datt, datt_t, delta, lse_t, gq, gk, gv, gmixed, dst,
):
    width = x_ref.shape[1]
    probs, chosen, gate = routed_gate(normed_f, router_ref, routes_ref[...])
    owned = slot_owners(slot_col[...], outs_ref.shape[0])
    mixed = mixed_ref[...]
    result_ref[...] = (mixed + gate * dot_nn(owned.astype(BF16), outs_ref[...])).astype(BF16)
    grouter_ref[...], grad_mixed, ggain_ref[1:2, :] = ffn_backward(
        probs, chosen, gate, owned, gates_ref, normed_f, router_ref, grows_ref, mixed, cot_ref, gain_f
    )
    gmixed[...] = grad_mixed
    branch = grad_mixed.astype(BF16)
    gw_ref[:, 3 * width : 4 * width] = dot_tn(att_ref[...], branch).astype(BF16)
    datt[...] = dot_nt(branch, w_ref[:, 3 * width : 4 * width]).astype(BF16)
    attention_setup(q_ref, k_ref, normed_ref, att_ref, lse_ref, q_t, k_t, normed_t, att_t, lse_t)
    attention_delta(datt, att_t, datt_t, delta)

    def pair(at, carry):
        pair_backward(
            at, near_ref, q_ref, k_ref, v_ref, q_t, k_t, datt, datt_t, delta, lse_t, dst, gq, gk, gv,
            gnear_ref, gfar_ref,
        )
        return carry

    lax.fori_loop(0, HEADS // 2, pair, 0)
    for at, grad in enumerate((gq, gk, gv)):
        gw_ref[:, at * width : (at + 1) * width] = dot_nn(normed_t[...], grad[...]).astype(BF16)
    gx_ref[...], ggain_ref[0:1, :] = input_backward(x_ref, w_ref, gain_a, gmixed, gq, gk, gv)


class Sums:
    def __init__(self, place, unit, buffers, semaphores, out, split):
        self.p, self.unit, self.out, self.split = place, unit, out, split
        self.send, self.core, self.first_in, self.second_in, self.z_in, self.last = buffers
        self.s, self.r = semaphores
        self.deep = place.deep
        p, c = place, place.c * split
        self.first, self.second = p.y + c * (p.x - p.y), p.x + c * (p.y - p.x)
        row, side = p.row, p.side
        self.first_peer = tuple(a + c * (b - a) for a, b in zip(row, side))
        self.second_peer = tuple(b + c * (a - b) for a, b in zip(row, side))

    def store(self, buffer, part, core):
        rows, cols = buffer.shape[-2:]
        blocks = part.reshape(self.deep, 2, 2, rows, cols)
        c = core * self.split
        for y in range(2):
            for x in range(2):
                first, second = (y, x) if y == x else (y + c * (x - y), x + c * (y - x))
                buffer[self.unit, first, second] = blocks[:, y, x].astype(buffer.dtype)

    def to_core(self):
        u, p = self.unit, self.p
        return remote(self.send.at[u], self.core.at[u], self.s.at[u, 0], self.r.at[u, 0], p.core)

    def to_y(self):
        u = self.unit
        return remote(self.core.at[u, 1 - self.first], self.first_in.at[u], self.s.at[u, 1], self.r.at[u, 1], self.first_peer)

    def to_x(self):
        u = self.unit
        return remote(self.first_in.at[u, 1 - self.second], self.second_in.at[u], self.s.at[u, 2], self.r.at[u, 2], self.second_peer)

    def to_z(self, k):
        u, p = self.unit, self.p
        z = lax.rem(p.z + k, p.deep)
        return remote(
            self.second_in.at[u, z], self.z_in.at[u, k], self.s.at[u, 3 + k], self.r.at[u, 3 + k], (z * 2 + p.y, p.n)
        )

    def to_last(self):
        u, p = self.unit, self.p
        return remote(self.last.at[u, 1 - p.c], self.out.at[u, p.c], self.s.at[u, 3], self.r.at[u, 3], p.core)

    def begin(self, part):
        self.store(self.send, part, 1 - self.p.c)
        self.to_core().start()

    def stage_core(self, part):
        u = self.unit
        self.to_core().wait_recv()
        rows, cols = self.core.shape[-2:]
        blocks = part.reshape(self.deep, 2, 2, rows, cols)
        c = self.p.c * self.split
        for y in range(2):
            for x in range(2):
                first, second = (y, x) if y == x else (y + c * (x - y), x + c * (y - x))
                kept = blocks[:, y, x] + self.core[u, first, second].astype(F32)
                self.core[u, first, second] = kept.astype(BF16)
        self.to_y().start()

    def stage_y(self):
        u = self.unit
        self.to_y().wait_recv()
        self.first_in[u] = (self.core[u, self.first].astype(F32) + self.first_in[u].astype(F32)).astype(BF16)
        self.to_x().start()

    def stage_x(self):
        u = self.unit
        self.to_x().wait_recv()
        self.second_in[u] = (self.first_in[u, self.second].astype(F32) + self.second_in[u].astype(F32)).astype(BF16)
        for k in range(1, self.p.deep):
            self.to_z(k).start()

    def stage_z(self):
        u = self.unit
        total = self.second_in[u, self.p.z].astype(F32)
        for k in range(1, self.p.deep):
            self.to_z(k).wait_recv()
            total = total + self.z_in[u, k].astype(F32)
        self.last[u] = total.reshape(self.last.shape[1:])
        self.to_last().start()
        self.out[u, self.p.c] = self.last[u, self.p.c]

    def drain(self):
        for copy in (self.to_core(), self.to_y(), self.to_x()):
            copy.wait_send()
        for k in range(1, self.p.deep):
            self.to_z(k).wait_send()
        self.to_last().wait()


def sum_buffers(units, wide, rows, cols):
    deep = wide // 2
    vmem = lambda *shape, dtype=BF16: pltpu.VMEM((units, *shape), dtype)
    return [
        vmem(2, 2, deep, rows, cols), vmem(2, 2, deep, rows, cols), vmem(2, deep, rows, cols), vmem(deep, rows, cols),
        vmem(deep, rows, cols), vmem(2, rows // 2, cols, dtype=F32),
        pltpu.SemaphoreType.DMA((units, 3 + deep)), pltpu.SemaphoreType.DMA((units, 3 + deep)),
    ]


def moving_backward_kernel(
    x_hbm, w_hbm, normed_hbm, q_hbm, k_hbm, v_hbm, att_hbm, lse_hbm, outs_hbm,
    gains_ref, router_ref, rel_ref, slot_route, mixed_ref, normed_f, cot_ref, grows_ref, gates_ref, picks_ref,
    result_ref, gx_ref, gq_out, gk_out, gv_out, go_out, router_out, small_out,
    x_ref, w_ref, normed_ref, q_ref, k_ref, v_ref, att_ref, lse_ref, load_s, near_ref,
    q_t, k_t, normed_t, att_t, datt, datt_t, delta, lse_t, gq, gk, gv, gmixed, gnormed, dst, gnear, gfar,
    own, from_core, from_side, returned, own_s, rc_s, rc_r, rx_s, rx_r, rw_s, rw_r,
    u1, u2, u3, u4, u5, u6, us, ur, o1, o2, o3, o4, o5, o6, os, orr, pair_sums, o_out,
    small, small_in, ss, sr,
):
    count, width = x_hbm.shape
    wide, local, slots, _ = returned.shape
    total = wide * local * slots
    p = Place(wide)
    far_x = (1 - p.x) * 2
    units = HEADS // 4
    gain_a, gain_f = gains_ref.at[0:1, :], gains_ref.at[1:2, :]
    loads = [
        pltpu.make_async_copy(source, target, load_s.at[at])
        for at, (source, target) in enumerate((
            (att_hbm, att_ref), (q_hbm, q_ref), (k_hbm, k_ref), (normed_hbm, normed_ref), (lse_hbm, lse_ref),
            (w_hbm, w_ref), (v_hbm, v_ref), (x_hbm, x_ref),
        ))
    ]

    def partial(e, other, core):
        return outs_hbm.at[e, (far_x if other else p.x * 2) + core]

    back = Collect(
        p, lambda e, other: partial(e, other, 1 - p.c), from_core, from_side, returned, (rc_s, rc_r, rx_s, rx_r, rw_s, rw_r)
    )

    def own_copy(e, other):
        return pltpu.make_async_copy(partial(e, other, p.c), own.at[e, other], own_s.at[e, other])

    for copy in loads[:5]:
        copy.start()
    greet(p.partners())
    for other in (1, 0):
        for e in range(local):
            own_copy(e, other).start()
    for copy in loads[5:]:
        copy.start()

    def go(e, piece):
        if piece == 1:
            own_copy(e, 1).wait()
            back.go_beside(e, own[e, 1])
        else:
            back.beside(e, piece).start()

    def near(e, piece):
        back.core(e, 0).wait_recv()
        own_copy(e, 0).wait()

    def finish(e, piece):
        back.finish(
            e, piece, lambda rows, part: own[e, 0, rows, part].astype(F32) + from_core[e, 0, rows, part].astype(F32)
        )

    def unit(u):
        if isinstance(u, int) and u == units:
            return Sums(p, 0, (o1, o2, o3, o4, o5, o6), (os, orr), o_out, 0)
        return Sums(p, u, (u1, u2, u3, u4, u5, u6), (us, ur), pair_sums, (u + 1) // units)

    hops = [[p.core], [p.row], [p.side], [(lax.rem(p.z + k, p.deep) * 2 + p.y, p.n) for k in range(1, p.deep)]]
    copies, slot = [], 0
    for stage, devices in enumerate(hops):
        copies.append([
            remote(small.at[stage], small_in.at[slot + at], ss.at[slot + at], sr.at[slot + at], device)
            for at, device in enumerate(devices)
        ])
        slot += len(devices)

    def small_end(stage):
        slot = sum(len(c) for c in copies[:stage])
        found = small[stage]
        for at, copy in enumerate(copies[stage]):
            copy.wait_recv()
            found = found + small_in[slot + at]
        return found

    def small_step(stage, piece):
        if stage:
            small[stage] = small_end(stage - 1)
        for copy in copies[stage]:
            copy.start()

    acts = {
        "core": lambda e, other: back.core(e, other).start(), "go": go, "near": near, "finish": finish,
        "y": lambda u, piece: unit(u).stage_y(), "x": lambda u, piece: unit(u).stage_x(),
        "z": lambda u, piece: unit(u).stage_z(), "small": small_step,
    }

    def act(part):
        for name, at, piece in BACKWARD_STEPS.get(part, ()):
            acts[name](at, piece)

    def after(u, part):
        for at in range(units):
            if part + str(at) in BACKWARD_STEPS:
                pl.when(u == at)(lambda at=at: act(part + str(at)))

    probs, chosen, gate = routed_gate(normed_f, router_ref, slot_route[:, 1:2])
    owned = slot_owners(slot_route[:, 0:1], total)
    near_ref[...] = near_biases(rel_ref, picks_ref)
    for copy in loads[:5]:
        copy.wait()
    attention_setup(q_ref, k_ref, normed_ref, att_ref, lse_ref, q_t, k_t, normed_t, att_t, lse_t)
    meet(p.partners())
    act("first")
    grad_router, grad_mixed, grad_gain_f = ffn_backward(
        probs, chosen, gate, owned, gates_ref, normed_f, router_ref, grows_ref, mixed_ref[...], cot_ref, gain_f
    )
    gmixed[...] = grad_mixed
    small[0] = jnp.zeros_like(small[0])
    small[0, HEADS : HEADS + 1, :] = grad_gain_f
    act("F0")
    branch = grad_mixed.astype(BF16)
    half_cols = width // 2
    router_cols = o_out.shape[-1] - half_cols
    router_wide = jnp.concatenate(
        [grad_router, jnp.zeros((width, router_cols - grad_router.shape[1]), F32)], axis=1
    )

    def output_part(core):
        low, high = branch[:, :half_cols], branch[:, half_cols:]
        part = dot_nn(att_t[...], jnp.where(core == 0, low, high))
        return jnp.concatenate([part, jnp.where(core == 0, router_wide, 0.0)], axis=1)

    unit(units).begin(output_part(1 - p.c))
    act("O0")
    loads[5].wait()
    datt[...] = (
        dot_nt(branch[:, :half_cols], w_ref[units, 0]) + dot_nt(branch[:, half_cols:], w_ref[units, 1])
    ).astype(BF16)
    act("D0")
    unit(units).stage_core(output_part(p.c))
    act("Q0")
    attention_delta(datt, att_t, datt_t, delta)
    for copy in loads[6:]:
        copy.wait()
    act("S0")

    def pair(at):
        pair_backward(
            at, near_ref, q_ref, k_ref, v_ref, q_t, k_t, datt, datt_t, delta, lse_t, dst, gq, gk, gv,
            gnear, gfar,
        )
        cols = pl.ds(pl.multiple_of(at * BLOCK, BLOCK), BLOCK)
        grads = jnp.concatenate([gq[:, cols], gk[:, cols], gv[:, cols]], axis=1)
        gnormed[...] += dot_nt(grads, w_ref[at // 2, lax.rem(at, 2)])
        return dot_nn(normed_t[...], grads)

    gnormed[...] = jnp.zeros_like(gnormed)

    def pairs(u, carry):
        unit(u).begin(pair(2 * u + 1 - p.c))
        after(u, "A")
        unit(u).stage_core(pair(2 * u + p.c))
        after(u, "B")
        return carry

    lax.fori_loop(0, units, pairs, 0)
    near_grads = lax.dot_general(
        gnear[...], picks_ref[...], (((1,), (1,)), ((), ())), precision=HIGHEST, preferred_element_type=F32
    )
    buckets = lax.broadcasted_iota(jnp.int32, near_grads.shape, 1)
    low_sum = jnp.sum(gfar[:, :BLOCK], axis=1, keepdims=True)
    high_sum = jnp.sum(gfar[:, BLOCK:], axis=1, keepdims=True)
    bucket_count = rel_ref.shape[0]
    rel = near_grads + jnp.where(buckets == bucket_count // 2 - 1, low_sum, 0.0)
    small[0, :HEADS, :bucket_count] = rel + jnp.where(buckets == bucket_count - 1, high_sum, 0.0)
    tokens = x_ref[...].astype(F32)
    grad_norm, grad_gain_a = norm_backward(tokens, inverse_rms(tokens), gain_a[...], gnormed[...])
    gx_ref[...] = gmixed[...] + grad_norm
    small[0, HEADS + 1 : HEADS + 2, :] = grad_gain_a

    act("P0")
    for e in range(local):
        back.arrive(e)
    combined = dot_nn(owned.astype(BF16), returned[...].reshape(total, width))
    result_ref[...] = (mixed_ref[...] + gate * combined).astype(BF16)
    act("R0")
    small_out[...] = small_end(3)
    for e in range(local):
        back.drain(e)
    for u in range(units + 1):
        unit(u).drain()
    for half in range(2):
        for u in range(units):
            cols = slice((2 * u + half) * BLOCK, (2 * u + half + 1) * BLOCK)
            for at, out in enumerate((gq_out, gk_out, gv_out)):
                out[:, cols] = pair_sums[u, half, :, at * BLOCK : (at + 1) * BLOCK]
        go_out[:, half * half_cols : (half + 1) * half_cols] = o_out[0, half, :, :half_cols]
    router_out[...] = o_out[0, 0, :, half_cols : half_cols + router_out.shape[1]]
    for stage in copies:
        for copy in stage:
            copy.wait_send()


def moving_backward(
    rel_bias, inputs, weights, gains, router, slot_route,
    normed, q, k, v, att, lse, mixed, normed_f, cotangent, outs, grows, gates, wide, slots,
):
    count, width = inputs.shape
    local, narrow = outs.shape[:2]
    experts = router.shape[1]
    bucket_count = rel_bias.shape[0]
    deep, rows = wide // 2, width // (wide * 2)
    units = HEADS // 4
    pair_cols, out_cols = 3 * BLOCK, width // 2 + BLOCK * -(-experts // BLOCK)
    sds = jax.ShapeDtypeStruct
    any_spec = pl.BlockSpec(memory_space=pl.ANY)
    picks = jnp.asarray(near_picks(bucket_count, -1).T)
    wide_t = lambda dtype: pltpu.VMEM((width, count), dtype)
    tall = lambda dtype: pltpu.VMEM((count, width), dtype)
    vmem = lambda *shape, dtype=BF16: pltpu.VMEM(shape, dtype)
    dma = pltpu.SemaphoreType.DMA
    hops = 3 + deep - 1
    result, grad_inputs, grad_query, grad_key, grad_value, grad_output, grad_router, small = pl.pallas_call(
        moving_backward_kernel,
        out_shape=(
            sds((count, width), BF16), sds((count, width), F32), *[sds((rows // 2, width), F32)] * 4,
            sds((rows // 2, experts), F32), sds((16, width), F32),
        ),
        in_specs=[any_spec] * 9 + in_vmem(10),
        out_specs=tuple(in_vmem(8)),
        scratch_shapes=[
            tall(BF16), pltpu.VMEM(weights.shape, BF16), tall(BF16), tall(BF16), tall(BF16), tall(BF16), tall(BF16),
            vmem(count, BLOCK, dtype=F32), dma((8,)), vmem(HEADS, 4 * BLOCK, dtype=F32),
            wide_t(BF16), wide_t(BF16), wide_t(BF16), wide_t(BF16), tall(BF16), wide_t(BF16),
            vmem(HEADS, count, dtype=F32), vmem(BLOCK, count, dtype=F32),
            tall(BF16), tall(BF16), tall(BF16), tall(F32), tall(F32), vmem(count, count),
            vmem(HEADS, 4 * BLOCK, dtype=F32), vmem(HEADS, 2 * BLOCK, dtype=F32),
            vmem(local, 2, wide, slots, width), vmem(local, 2, wide, slots, width), vmem(local, wide, slots, width),
            vmem(wide, local, slots, width),
            dma((local, 2)), *Collect.semaphores(local, wide),
            *sum_buffers(units, wide, rows, pair_cols), *sum_buffers(1, wide, rows, out_cols),
            vmem(units, 2, rows // 2, pair_cols, dtype=F32), vmem(1, 2, rows // 2, out_cols, dtype=F32),
            vmem(4, 16, width, dtype=F32), vmem(hops, 16, width, dtype=F32), dma((hops,)), dma((hops,)),
        ],
        compiler_params=pltpu.CompilerParams(collective_id=3, has_side_effects=True, vmem_limit_bytes=62 << 20),
        name="backward",
    )(
        inputs, weights, normed, q, k, v, att, lse, outs,
        gains, router, rel_bias, slot_route, mixed, normed_f, cotangent, grows, gates, picks,
    )
    device = lax.axis_index("wide") * narrow + lax.axis_index("narrow")
    gain_grads = lax.dynamic_slice(small, (HEADS, device * (rows // 2)), (2, rows // 2))
    grad_rel = small[:HEADS, :bucket_count].T
    return result, grad_inputs, (grad_query, grad_key, grad_value), grad_output, grad_router, gain_grads[1], gain_grads[0], grad_rel


def in_vmem(count):
    return [pl.BlockSpec(memory_space=pltpu.VMEM)] * count


def shards(
    inputs, gain_attn, w_query, w_key, w_value, w_output, rel_bias, gain_ffn, w_router,
    expert_in, expert_out, routes, capacity, cotangent,
):
    count, width = inputs.shape
    experts = w_router.shape[1]
    local, _, hidden_width = expert_in.shape
    wide, narrow = lax.axis_size("wide"), lax.axis_size("narrow")
    slots = 2 * count // experts
    total = experts * slots
    bucket_count = rel_bias.shape[0]
    params = pltpu.CompilerParams(vmem_limit_bytes=60 << 20)
    smem = pl.BlockSpec(memory_space=pltpu.SMEM)

    moving = narrow == 4 and wide & (wide - 1) == 0 and local == HEADS // 4 + 1 and slots % 32 == 0 and local * slots % BLOCK == 0
    moving = moving and width % (wide * 2 * 16) == 0 and count == SEQ_LEN and experts + 8 <= BLOCK
    if moving:
        normed, q, k, v, att, lse, mixed, normed_f, sent, weights, cot_all, slot_route, router, gains = moving_forward(
            rel_bias, capacity, inputs, w_query, w_key, w_value, w_output, w_router, gain_attn, gain_ffn, routes,
            cotangent, wide, narrow, local, slots,
        )
        outs, back, gates, gin, gout = moving_experts(sent, cot_all, expert_in, expert_out, router, wide, narrow)
        result, grad_inputs, kinds, grad_output, grad_router, grad_gain_a, grad_gain_f, grad_rel = moving_backward(
            rel_bias, inputs, weights.reshape(HEADS // 4 + 1, 2, width, width // 2), gains, router, slot_route,
            normed, q, k, v, att, lse, mixed, normed_f, cotangent, outs,
            back.reshape(total, width), gates.reshape(1, total), wide, slots,
        )
        return (
            result, grad_inputs, grad_gain_a, *kinds, grad_output, grad_rel, grad_gain_f, grad_router, gin, gout,
        )

    near = jnp.dot(near_picks(bucket_count, 1), rel_bias, precision=HIGHEST).T
    near_back = jnp.dot(near_picks(bucket_count, -1), rel_bias, precision=HIGHEST).T

    packed = jnp.concatenate([w_query, w_key, w_value, w_output], axis=1)
    weights = lax.all_gather(packed, BOTH, axis=0, tiled=True)
    small = lax.all_gather(
        jnp.concatenate([w_router, gain_attn[:, None], gain_ffn[:, None]], axis=1), BOTH, axis=0, tiled=True
    )
    router = small[:, :experts]
    gain_a = small[:, experts].astype(F32)[None, :]
    gain_f = small[:, experts + 1].astype(F32)[None, :]
    slot_col, slot_row, cot_sent = pl.pallas_call(
        lambda *refs: place_kernel(slots, experts, *refs),
        out_shape=(
            jax.ShapeDtypeStruct((count, 1), jnp.int32),
            jax.ShapeDtypeStruct((1, count), jnp.int32),
            jax.ShapeDtypeStruct((total, width), BF16),
        ),
        in_specs=[smem] + in_vmem(3),
        out_specs=tuple(in_vmem(3)),
        compiler_params=params,
        name="places",
    )(capacity, routes, routes.reshape(1, count), cotangent)

    def spread(rows):
        taken = lax.all_to_all(
            rows.reshape(wide, local * slots, width), "wide", split_axis=0, concat_axis=0, tiled=True
        )
        held = lax.all_gather(taken, "narrow", axis=0, tiled=True)
        return held.reshape(wide * narrow, local, slots, width)

    def collect(rows):
        own = lax.psum_scatter(
            rows.reshape(wide * narrow, local * slots, width), "narrow", scatter_dimension=0, tiled=True
        )
        back = lax.all_to_all(own, "wide", split_axis=0, concat_axis=0, tiled=True)
        return back.reshape(total, width)

    cot_all = spread(cot_sent)

    rows_t = lambda dtype, cols=width: jax.ShapeDtypeStruct((count, cols), dtype)
    normed, q, k, v, att, lse, mixed, normed_f, sent = pl.pallas_call(
        forward_kernel,
        out_shape=(
            rows_t(BF16), rows_t(BF16), rows_t(BF16), rows_t(BF16), rows_t(BF16), rows_t(F32, BLOCK),
            rows_t(F32), rows_t(BF16), jax.ShapeDtypeStruct((total, width), BF16),
        ),
        in_specs=in_vmem(7),
        out_specs=tuple(in_vmem(9)),
        compiler_params=params,
        name="forward",
    )(inputs, weights, gain_a, gain_f, router, near, slot_row)

    rows_all = spread(sent)
    sources = wide * narrow
    block = pl.BlockSpec((sources, 1, slots, width), lambda e: (0, e, 0, 0))
    w_in_spec = pl.BlockSpec((1, width, hidden_width), lambda e: (e, 0, 0))
    w_out_spec = pl.BlockSpec((1, hidden_width, width), lambda e: (e, 0, 0))
    first_expert = (lax.axis_index("wide") * local).astype(jnp.int32)[None]
    back, grows, gin, gout = pl.pallas_call(
        expert_kernel,
        grid=(local,),
        out_shape=(
            jax.ShapeDtypeStruct(rows_all.shape, BF16),
            jax.ShapeDtypeStruct(rows_all.shape, BF16),
            jax.ShapeDtypeStruct(expert_in.shape, F32),
            jax.ShapeDtypeStruct(expert_out.shape, F32),
        ),
        in_specs=[
            smem, block, block, w_in_spec, w_out_spec, pl.BlockSpec((width, experts), lambda e: (0, 0)),
        ],
        out_specs=(block, block, w_in_spec, w_out_spec),
        scratch_shapes=[
            pltpu.VMEM((sources * slots, hidden_width), BF16),
            pltpu.VMEM((sources * slots, hidden_width), BF16),
            pltpu.VMEM((sources * slots, width), BF16),
        ],
        compiler_params=params,
        name="experts",
    )(first_expert, rows_all, cot_all, expert_in, expert_out, router)
    outs_back = collect(back)
    grows_back = collect(grows)
    gates = jnp.sum(outs_back.astype(F32) * cot_sent.astype(F32), axis=1)[None, :]

    wide_t = lambda dtype: pltpu.VMEM((width, count), dtype)
    tall = lambda dtype: pltpu.VMEM((count, width), dtype)
    result, grad_inputs, gw, grouter, gnear, gfar, ggain = pl.pallas_call(
        backward_kernel,
        out_shape=(
            rows_t(BF16), rows_t(F32), jax.ShapeDtypeStruct((width, 4 * width), BF16),
            jax.ShapeDtypeStruct((width, experts), F32), jax.ShapeDtypeStruct((HEADS, 4 * BLOCK), F32),
            jax.ShapeDtypeStruct((HEADS, 2 * BLOCK), F32), jax.ShapeDtypeStruct((2, width), F32),
        ),
        in_specs=in_vmem(20),
        out_specs=tuple(in_vmem(7)),
        scratch_shapes=[
            wide_t(BF16), wide_t(BF16), wide_t(BF16), wide_t(BF16), tall(BF16), wide_t(BF16),
            pltpu.VMEM((HEADS, count), F32), pltpu.VMEM((BLOCK, count), F32),
            tall(BF16), tall(BF16), tall(BF16), tall(F32), pltpu.VMEM((count, count), BF16),
        ],
        compiler_params=params,
        name="backward",
    )(
        inputs, weights, gain_a, gain_f, router, near_back, slot_col, routes,
        normed, q, k, v, att, lse, mixed, normed_f, cotangent, outs_back, grows_back, gates,
    )

    gw = lax.psum_scatter(gw, BOTH, scatter_dimension=0, tiled=True).astype(F32)
    grad_query, grad_key, grad_value, grad_output = (gw[:, i * width : (i + 1) * width] for i in range(4))
    gsmall = lax.psum_scatter(
        jnp.concatenate([grouter, ggain.T], axis=1), BOTH, scatter_dimension=0, tiled=True
    )
    grad_rel = jnp.dot(near_picks(bucket_count, -1).T, gnear.T, precision=HIGHEST)
    low, high = jnp.sum(gfar[:, :BLOCK], axis=1), jnp.sum(gfar[:, BLOCK:], axis=1)
    grad_rel = grad_rel.at[bucket_count // 2 - 1].add(low).at[bucket_count - 1].add(high)
    grad_rel = lax.psum(grad_rel, BOTH)
    return (
        result, grad_inputs, gsmall[:, experts], grad_query, grad_key, grad_value, grad_output,
        grad_rel, gsmall[:, experts + 1], gsmall[:, :experts], gin, gout,
    )


def solution(mesh):
    return jax.shard_map(
        shards,
        mesh=mesh,
        in_specs=(
            P(BOTH, None),
            P(BOTH),
            P(BOTH, None),
            P(BOTH, None),
            P(BOTH, None),
            P(BOTH, None),
            P(),
            P(BOTH),
            P(BOTH, None),
            P("wide", None, "narrow"),
            P("wide", "narrow", None),
            P(BOTH, None),
            P(BOTH),
            P(BOTH, None),
        ),
        out_specs=(
            P(BOTH, None),
            P(BOTH, None),
            P(BOTH),
            P(BOTH, None),
            P(BOTH, None),
            P(BOTH, None),
            P(BOTH, None),
            P(),
            P(BOTH),
            P(BOTH, None),
            P("wide", None, "narrow"),
            P("wide", "narrow", None),
        ),
        check_vma=False,
    )
```

```python
import jax
import jax.numpy as jnp
import numpy as np
from jax import lax
from jax.experimental import pallas as pl
from jax.experimental.pallas import tpu as pltpu
from jax.sharding import PartitionSpec as P

HEADS = 12
SEQ_LEN = 512
BLOCK = 128
EPSILON = 1e-06
HIGHEST = lax.Precision.HIGHEST
ROOT_TWO_PI = 0.7978845608028654
CUBIC = 0.044715
BOTH = ("wide", "narrow")
F32 = jnp.float32
BF16 = jnp.bfloat16


def bucket_of(offsets, bucket_count):
    half_count = bucket_count // 2
    exact_count = half_count // 2
    distance = np.abs(offsets)
    scaled = exact_count + np.floor(
        np.log(np.maximum(distance, 1) / exact_count)
        / np.log(128.0 / exact_count)
        * (half_count - exact_count)
    ).astype(np.int64)
    scaled = np.minimum(scaled, half_count - 1)
    return ((offsets > 0) * half_count + np.where(distance < exact_count, distance, scaled)).astype(
        np.int32
    )


def near_picks(bucket_count, sign):
    offsets = sign * (np.arange(4 * BLOCK) - (2 * BLOCK - 1))
    picks = (bucket_of(offsets, bucket_count)[:, None] == np.arange(bucket_count)[None, :]).astype(
        np.float32
    )
    picks[-1] = 0.0
    return picks


def dot_nn(left, right):
    return lax.dot_general(left, right, (((1,), (0,)), ((), ())), preferred_element_type=F32)


def dot_nt(left, right):
    return lax.dot_general(left, right, (((1,), (1,)), ((), ())), preferred_element_type=F32)


def dot_tn(left, right):
    return lax.dot_general(left, right, (((0,), (0,)), ((), ())), preferred_element_type=F32)


def inverse_rms(values):
    return lax.rsqrt(jnp.mean(values * values, axis=-1, keepdims=True) + EPSILON)


def norm_backward(values, inverse, gain, grad_normed):
    scaled = grad_normed * gain
    grad_gain = jnp.sum(grad_normed * values * inverse, axis=0, keepdims=True)
    inner = jnp.mean(scaled * values, axis=-1, keepdims=True)
    return (inverse * (scaled - values * inverse * inverse * inner), grad_gain)


def softmax_lanes(logits):
    peak = jnp.max(logits, axis=-1, keepdims=True)
    exponent = jnp.exp(logits - peak)
    return exponent / jnp.sum(exponent, axis=-1, keepdims=True)


def toeplitz_near(near_row):
    spread = jnp.broadcast_to(near_row, (BLOCK, 4 * BLOCK))
    return pltpu.roll(spread, 3 * BLOCK + 1, 1, stride=1, stride_axis=0)[:, : 3 * BLOCK]


def bias_rows(near, near_row, row, blocks):
    far_low, far_high = near_row[:, :1], near_row[:, 4 * BLOCK - 2 : 4 * BLOCK - 1]
    pieces = []
    for column in range(blocks):
        distance = column - row
        if distance <= -2:
            pieces.append(jnp.broadcast_to(far_low, (BLOCK, BLOCK)))
        elif distance >= 2:
            pieces.append(jnp.broadcast_to(far_high, (BLOCK, BLOCK)))
        else:
            pieces.append(near[:, (distance + 1) * BLOCK : (distance + 2) * BLOCK])
    return jnp.concatenate(pieces, axis=1)


def near_biases(rel_ref, picks_ref):
    return lax.dot_general(
        rel_ref[...], picks_ref[...], (((0,), (0,)), ((), ())), precision=HIGHEST, preferred_element_type=F32
    )


def diagonal_sums(near_sum):
    padded = jnp.concatenate([near_sum, jnp.zeros((BLOCK, BLOCK), F32)], axis=1)
    groups = jnp.zeros((8, 4 * BLOCK), F32)
    for at in range(0, BLOCK, 8):
        groups = groups + pltpu.roll(padded[at : at + 8, :], BLOCK - 8 - at, 1)
    sums = groups[7:8, :]
    for at in range(7):
        sums = sums + pltpu.roll(groups[at : at + 1, :], 7 - at, 1)
    return sums


def slot_places(col, row, limit, experts, slots, count):
    lower = lax.broadcasted_iota(jnp.int32, (count, count), 0)
    upper = lax.broadcasted_iota(jnp.int32, (count, count), 1)
    chosen = lax.broadcasted_iota(jnp.int32, (count, experts), 1) == col
    running = dot_nn((upper <= lower).astype(BF16), chosen.astype(BF16))
    place = jnp.sum(jnp.where(chosen, running, 0.0), axis=1, keepdims=True).astype(jnp.int32) - 1
    slot_col = jnp.where(place < limit, col * slots + place, -1)
    chosen_t = lax.broadcasted_iota(jnp.int32, (experts, count), 0) == row
    running_t = dot_nn(chosen_t.astype(BF16), (lower <= upper).astype(BF16))
    place_t = (
        jnp.sum(jnp.where(chosen_t, running_t, 0.0), axis=0, keepdims=True).astype(jnp.int32) - 1
    )
    slot_row = jnp.where(place_t < limit, row * slots + place_t, -1)
    return slot_col, slot_row


def place_kernel(slots, experts, capacity_ref, routes_ref, row_ref, cot_ref, slot_col, slot_row, cot_out):
    count = routes_ref.shape[0]
    limit = capacity_ref[0] * count // experts
    col, row = slot_places(routes_ref[...], row_ref[...], limit, experts, slots, count)
    slot_col[...] = col
    slot_row[...] = row
    picks = (lax.broadcasted_iota(jnp.int32, (experts * slots, count), 0) == row).astype(BF16)
    cot_out[...] = dot_nn(picks, cot_ref[...]).astype(BF16)


def pair_forward(at, near_ref, q_ref, k_ref, v_ref, att_ref, lse_ref):
    count, width = q_ref.shape
    head_dim = width // HEADS
    blocks = count // BLOCK
    lanes = lax.broadcasted_iota(jnp.int32, (1, BLOCK), 1)
    first = lanes < head_dim
    cols = pl.ds(pl.multiple_of(at * BLOCK, BLOCK), BLOCK)
    k_pair, v_pair = k_ref[:, cols], v_ref[:, cols]
    near_rows = [near_ref[pl.ds(2 * at + half, 1), :] for half in range(2)]
    nears = [toeplitz_near(near_row) for near_row in near_rows]
    for row in range(blocks):
        rows = slice(row * BLOCK, (row + 1) * BLOCK)
        q_rows = q_ref[rows, cols] * jnp.asarray(head_dim**-0.5, BF16)
        found = []
        log_sums = lse_ref[rows, :]
        for half in range(2):
            head = 2 * at + half
            mask = first if half == 0 else jnp.logical_not(first)
            scores = dot_nt(jnp.where(mask, q_rows, jnp.zeros_like(q_rows)), k_pair)
            scores = scores + bias_rows(nears[half], near_rows[half], row, blocks)
            peak = jnp.max(scores, axis=-1, keepdims=True)
            exponent = jnp.exp(scores - peak)
            total = jnp.sum(exponent, axis=-1, keepdims=True)
            found.append(dot_nn((exponent * (1.0 / total)).astype(BF16), v_pair))
            log_sums = jnp.where(lanes == head, peak + jnp.log(total), log_sums)
        lse_ref[rows, :] = log_sums
        att_ref[rows, cols] = jnp.where(first, found[0], found[1]).astype(BF16)


def slot_rows(slot_row, values, total):
    picks = lax.broadcasted_iota(jnp.int32, (total, slot_row.shape[1]), 0) == slot_row
    return dot_nn(picks.astype(BF16), values).astype(BF16)


def forward_kernel(
    x_ref, w_ref, gain_a, gain_f, router_ref, near_ref, slot_row,
    normed_ref, q_ref, k_ref, v_ref, att_ref, lse_ref, mixed_ref, normed_f, sent_ref,
):
    width = x_ref.shape[1]
    tokens = x_ref[...].astype(F32)
    normed = (tokens * inverse_rms(tokens) * gain_a[...]).astype(BF16)
    normed_ref[...] = normed
    for out, at in ((q_ref, 0), (k_ref, 1), (v_ref, 2)):
        out[...] = dot_nn(normed, w_ref[:, at * width : (at + 1) * width]).astype(BF16)
    lse_ref[...] = jnp.zeros_like(lse_ref)

    def pair(at, carry):
        pair_forward(at, near_ref, q_ref, k_ref, v_ref, att_ref, lse_ref)
        return carry

    lax.fori_loop(0, HEADS // 2, pair, 0)
    mixed = tokens + dot_nn(att_ref[...], w_ref[:, 3 * width : 4 * width])
    mixed_ref[...] = mixed
    normed_2 = (mixed * inverse_rms(mixed) * gain_f[...]).astype(BF16)
    normed_f[...] = normed_2
    sent_ref[...] = slot_rows(slot_row[...], normed_2, sent_ref.shape[0])


def expert_kernel(
    first_ref, rows_ref, cot_ref, in_ref, out_ref, router_ref,
    back_ref, grows_ref, gin_ref, gout_ref, hidden_ref, gpre_ref, sg_ref,
):
    sources, _, slots, width = rows_ref.shape
    total = sources * slots
    step = min(256, total)
    expert = first_ref[0] + pl.program_id(0)

    def chunk(at, carry):
        these = pl.ds(pl.multiple_of(at * (step // slots), step // slots), step // slots)
        flat = pl.ds(pl.multiple_of(at * step, step), step)
        rows = rows_ref[these, 0].reshape(step, width)
        probs = softmax_lanes(dot_nn(rows, router_ref[...]))
        here = lax.broadcasted_iota(jnp.int32, probs.shape, 1) == expert
        gate = jnp.sum(jnp.where(here, probs, 0.0), axis=-1, keepdims=True)
        sg = (cot_ref[these, 0].reshape(step, width).astype(F32) * gate).astype(BF16)
        sg_ref[flat, :] = sg
        pre = dot_nn(rows, in_ref[0])
        square = pre * pre
        inner = jnp.tanh(pre * (ROOT_TWO_PI + ROOT_TWO_PI * CUBIC * square))
        half = 0.5 * (1.0 + inner)
        hidden = (pre * half).astype(BF16)
        hidden_ref[flat, :] = hidden
        slope = half + 0.5 * pre * (1.0 - inner * inner) * (
            ROOT_TWO_PI + 3.0 * ROOT_TWO_PI * CUBIC * square
        )
        gpre = (dot_nt(sg, out_ref[0]) * slope).astype(BF16)
        gpre_ref[flat, :] = gpre
        back_ref[these, 0] = dot_nn(hidden, out_ref[0]).astype(BF16).reshape(-1, slots, width)
        grows_ref[these, 0] = dot_nt(gpre, in_ref[0]).astype(BF16).reshape(-1, slots, width)
        return carry

    lax.fori_loop(0, total // step, chunk, 0)
    gout_ref[0] = dot_tn(hidden_ref[...], sg_ref[...])
    gin_ref[0] = dot_tn(rows_ref[:, 0].reshape(total, width), gpre_ref[...])


def remote(source, target, send, receive, device):
    return pltpu.make_async_remote_copy(
        src_ref=source,
        dst_ref=target,
        send_sem=send,
        recv_sem=receive,
        device_id=device,
        device_id_type=pl.DeviceIdType.MESH,
    )


def greet(devices):
    for device in devices:
        pl.semaphore_signal(
            pltpu.get_barrier_semaphore(), inc=1, device_id=device, device_id_type=pl.DeviceIdType.MESH
        )


def meet(devices):
    pl.semaphore_wait(pltpu.get_barrier_semaphore(), len(devices))


FORWARD_STEPS = {
    "first": (("send", 4, 0), ("start", 2, 0), ("start", 3, 0), ("send", 0, 0), ("start", 1, 0), ("spread", 4, 0),
        ("send", 1, 0), ("start", 0, 0), ("spread", 0, 0), ("send", 2, 0), ("start", 0, 2), ("forward", 1, 0),
        ("send", 3, 0), ("start", 1, 1), ("over_x", 4, 0), ("over_y", 4, 0), ("forward", 0, 0), ("spread", 1, 0),
        ("end", 4, 0), ("over_x", 0, 0), ("spread", 2, 0), ("start", 3, 2), ("over_y", 1, 0), ("forward", 3, 0),
        ("start", 3, 1), ("over_x", 1, 0), ("over_x", 2, 0), ("end", 0, 0), ("over_y", 0, 0), ("forward", 1, 1),
        ("start", 2, 2),),
    "N0": (("spread", 3, 0),),
    "A0": (("forward", 2, 0), ("pass", 1, 1), ("forward", 3, 1), ("pass", 3, 0), ("over_y", 2, 0),
        ("start", 1, 2), ("forward", 0, 2), ("forward", 3, 2), ("end", 1, 0),),
    "B0": (("start", 2, 1),),
    "A1": (("forward", 2, 2), ("end", 2, 0), ("start", 0, 1), ("over_x", 3, 0),),
    "A2": (("forward", 2, 1), ("forward", 1, 2), ("pass", 1, 0), ("pass", 2, 0), ("pass", 0, 0), ("pass", 3, 2),
        ("pass", 2, 2), ("pass", 0, 2), ("forward", 0, 1), ("end", 3, 0), ("over_y", 3, 0), ("pass", 3, 1),),
    "M0": (("pass", 1, 2), ("pass", 2, 1), ("pass", 0, 1),),
}

BACKWARD_STEPS = {
    "first": (("core", 0, 1), ("core", 3, 0), ("core", 2, 1),),
    "O0": (("go", 2, 1), ("core", 1, 0), ("core", 2, 0), ("core", 0, 0), ("go", 0, 1),),
    "Q0": (("go", 2, 2), ("core", 3, 1),),
    "S0": (("core", 1, 1), ("near", 1, 0), ("near", 2, 0), ("go", 0, 2), ("near", 0, 0), ("finish", 2, 1),
        ("near", 3, 0), ("go", 3, 1),),
    "A0": (("go", 1, 1), ("finish", 0, 1), ("go", 3, 2), ("go", 0, 0), ("finish", 2, 2),),
    "A1": (("go", 3, 0), ("finish", 1, 1),),
    "B1": (("y", 3, 0), ("finish", 3, 1),),
    "A2": (("finish", 3, 2),),
    "P0": (("x", 3, 0), ("y", 0, 0), ("y", 1, 0), ("finish", 0, 2), ("go", 1, 0), ("finish", 0, 0),
        ("small", 0, 0), ("go", 1, 2), ("x", 0, 0), ("finish", 3, 0), ("x", 1, 0), ("y", 2, 0), ("z", 3, 0),
        ("small", 1, 0), ("go", 2, 0), ("finish", 1, 2), ("x", 2, 0), ("small", 2, 0), ("finish", 1, 0),
        ("finish", 2, 0), ("small", 3, 0), ("z", 0, 0), ("z", 1, 0), ("z", 2, 0),),
}

EXPERT_STEPS = {
    "first": (("start", 0, 0), ("start", 0, 1), ("start", 0, 2), ("forward", 0, 0), ("start", 1, 2),
        ("forward", 0, 1), ("start", 1, 0), ("forward", 0, 2), ("start", 1, 1), ("forward", 1, 0),
        ("start", 2, 0), ("pass", 0, 1), ("forward", 1, 2), ("start", 2, 1), ("pass", 0, 0), ("pass", 0, 2),),
    "A0": (("forward", 1, 1), ("start", 2, 2),),
    "B0": (("forward", 2, 0),),
    "C0": (("go", 0, 1), ("pass", 1, 0), ("forward", 2, 1), ("pass", 1, 2), ("start", 3, 0), ("pass", 1, 1),),
    "D0": (("start", 3, 2),),
    "A1": (("forward", 2, 2),),
    "B1": (("start", 3, 1), ("forward", 3, 0),),
    "W0": (("go", 1, 1), ("pass", 2, 0), ("pass", 2, 1), ("forward", 3, 2),),
    "D1": (("forward", 3, 1), ("go", 0, 2), ("go", 1, 2), ("pass", 2, 2), ("sum", 0, 0),),
    "V0": (("finish", 0, 1), ("sum", 1, 0),),
    "A2": (("finish", 1, 1),),
    "B2": (("go", 2, 1),),
    "W1": (("go", 0, 0), ("finish", 0, 2), ("pass", 3, 0), ("pass", 3, 2), ("go", 1, 0),),
    "C2": (("pass", 3, 1), ("go", 2, 2),),
    "D2": (("go", 2, 0),),
    "V1": (("sum", 2, 0), ("finish", 2, 1),),
    "B3": (("go", 3, 1), ("finish", 1, 2),),
    "W2": (("finish", 1, 0), ("finish", 2, 2),),
    "C3": (("finish", 0, 0), ("go", 3, 2),),
    "D3": (("sum", 3, 0), ("finish", 3, 1), ("go", 3, 0),),
    "V2": (("finish", 3, 2), ("finish", 2, 0),),
    "W3": (("finish", 3, 0),),
}


class Place:
    def __init__(self, wide):
        self.wide = wide
        self.run = wide // 2
        self.deep = wide // 2
        self.w, self.n = lax.axis_index("wide"), lax.axis_index("narrow")
        self.x, self.c = self.n // 2, lax.rem(self.n, 2)
        self.z, self.y = self.w // 2, lax.rem(self.w, 2)
        self.core = (self.w, self.x * 2 + 1 - self.c)
        self.side = (self.w, (1 - self.x) * 2 + self.c)
        self.row = (self.z * 2 + 1 - self.y, self.n)

    def flip(self, j):
        found, bit = self.w, 1
        while bit <= j:
            if j & bit:
                found = found + bit - 2 * bit * lax.rem(self.w // bit, 2)
            bit *= 2
        return found

    def peer(self, j):
        return (self.flip(j), self.n)

    def span(self, piece):
        half = self.w // self.run
        return pl.ds((1 - half if piece else half) * self.run, self.run)

    def steps(self, piece):
        return range(self.run, self.wide) if piece else range(1, self.run)

    def partners(self):
        return [self.peer(j) for j in range(1, self.wide)] + [self.core, self.side]


def slot_part(piece, slots):
    return pl.ds((piece - 1) * (slots // 2), slots // 2) if piece else pl.ds(0, slots)


PIECES = range(3)


class Spread:
    def __init__(self, place, sent, held, wide_s, wide_r, side_s, side_r, core_s, core_r):
        self.place, self.sent, self.held = place, sent, held
        self.wide_s, self.wide_r, self.side_s, self.side_r = wide_s, wide_r, side_s, side_r
        self.core_s, self.core_r = core_s, core_r
        self.slots = sent.shape[2]

    def hop(self, e, j, piece):
        p, part = self.place, slot_part(piece, self.slots)
        at = p.wide + j if piece == 2 else j
        return remote(
            self.sent.at[p.flip(j), e, part], self.held.at[e, p.n, p.w, part],
            self.wide_s.at[e, at], self.wide_r.at[e, at], p.peer(j),
        )

    def start(self, e, piece):
        for j in self.place.steps(piece):
            self.hop(e, j, piece).start()

    def beside(self, e, piece):
        p = self.place
        rows = self.held.at[e, p.n, p.span(piece), slot_part(piece, self.slots)]
        return remote(rows, rows, self.side_s.at[e, piece], self.side_r.at[e, piece], p.side)

    def over(self, e, other, piece):
        p = self.place
        m = (1 - p.x) * 2 + p.c if other else p.n
        rows = self.held.at[e, m, p.span(piece), slot_part(piece, self.slots)]
        at = 3 * other + piece
        return remote(rows, rows, self.core_s.at[e, at], self.core_r.at[e, at], p.core)

    def forward(self, e, piece):
        for j in self.place.steps(piece):
            self.hop(e, j, piece).wait_recv()
        self.beside(e, piece).start()
        self.over(e, 0, piece).start()

    def pass_on(self, e, piece):
        self.beside(e, piece).wait_recv()
        self.over(e, 1, piece).start()

    def arrive(self, e, other):
        for piece in PIECES:
            self.over(e, other, piece).wait_recv()

    def drain(self, e):
        for piece in PIECES:
            for j in self.place.steps(piece):
                self.hop(e, j, piece).wait_send()
            self.beside(e, piece).wait_send()
            self.over(e, 0, piece).wait_send()
            self.over(e, 1, piece).wait_send()

    @staticmethod
    def semaphores(local, wide):
        dma = pltpu.SemaphoreType.DMA
        return [dma((local, n)) for n in (2 * wide, 2 * wide, 3, 3, 6, 6)]


class Collect:
    def __init__(self, place, to_core, from_core, from_side, returned, semaphores):
        self.place, self.to_core, self.from_core = place, to_core, from_core
        self.from_side, self.returned = from_side, returned
        self.core_s, self.core_r, self.side_s, self.side_r, self.wide_s, self.wide_r = semaphores
        self.slots = from_side.shape[2]

    def core(self, e, other):
        return remote(
            self.to_core(e, other), self.from_core.at[e, other], self.core_s.at[e, other], self.core_r.at[e, other],
            self.place.core,
        )

    def beside(self, e, piece):
        rows, part = self.place.span(piece), slot_part(piece, self.slots)
        return remote(
            self.from_core.at[e, 1, rows, part], self.from_side.at[e, rows, part],
            self.side_s.at[e, piece], self.side_r.at[e, piece], self.place.side,
        )

    def back(self, e, j, piece):
        p, part = self.place, slot_part(piece, self.slots)
        at = p.wide + j if piece == 2 else j
        return remote(
            self.from_side.at[e, p.flip(j), part], self.returned.at[p.w, e, part],
            self.wide_s.at[e, at], self.wide_r.at[e, at], p.peer(j),
        )

    def go_beside(self, e, part):
        self.core(e, 1).wait_recv()
        held = self.from_core[e, 1].astype(F32)
        self.from_core[e, 1] = (part.astype(F32).reshape(held.shape) + held).astype(BF16)
        self.beside(e, 1).start()

    def finish(self, e, piece, own):
        p = self.place
        rows, part = p.span(piece), slot_part(piece, self.slots)
        self.beside(e, piece).wait_recv()
        total = own(rows, part) + self.from_side[e, rows, part].astype(F32)
        self.from_side[e, rows, part] = total.astype(BF16)
        for j in p.steps(piece):
            self.back(e, j, piece).start()
        if not piece:
            self.returned[p.w, e] = self.from_side[e, p.w]

    def drain(self, e):
        self.core(e, 0).wait_send()
        self.core(e, 1).wait_send()
        for piece in PIECES:
            self.beside(e, piece).wait_send()
            for j in self.place.steps(piece):
                self.back(e, j, piece).wait_send()

    def arrive(self, e):
        for piece in PIECES:
            for j in self.place.steps(piece):
                self.back(e, j, piece).wait_recv()

    @staticmethod
    def semaphores(local, wide):
        dma = pltpu.SemaphoreType.DMA
        return [dma((local, n)) for n in (2, 2, 3, 3, 2 * wide, 2 * wide)]


class Gather:
    def __init__(self, place, unit, held, halves, semaphores):
        self.p, self.u, self.held, self.halves = place, unit, held, halves
        self.s, self.r = semaphores

    def piece(self, *place):
        return self.held.at[self.u, self.p.c, *place] if self.halves else self.held.at[self.u, *place]

    def column(self, y, x):
        return self.piece(slice(None), y, x)

    def copy(self, piece, slot, device):
        return remote(piece, piece, self.s.at[self.u, slot], self.r.at[self.u, slot], device)

    def to_z(self, k):
        p = self.p
        z = lax.rem(p.z + k, p.deep)
        return self.copy(self.piece(p.z, p.y, p.x), k - 1, (z * 2 + p.y, p.n))

    def to_x(self):
        return self.copy(self.column(self.p.y, self.p.x), 3, self.p.side)

    def to_y(self):
        return self.copy(self.column(self.p.y, self.p.x), 4, self.p.row)

    def corner(self):
        return self.copy(self.column(self.p.y, 1 - self.p.x), 5, self.p.row)

    def to_core(self, at):
        p = self.p
        y, x = ((p.y, p.x), (p.y, 1 - p.x), (1 - p.y, p.x), (1 - p.y, 1 - p.x))[at]
        return self.copy(self.column(y, x), 6 + at, p.core)

    def hand(self, at):
        if self.halves:
            self.to_core(at).start()

    def start(self):
        for k in range(1, self.p.deep):
            self.to_z(k).start()

    def spread(self):
        for k in range(1, self.p.deep):
            self.to_z(k).wait_recv()
        self.to_x().start()
        self.to_y().start()
        self.hand(0)

    def over_x(self):
        self.to_x().wait_recv()
        self.corner().start()
        self.hand(1)

    def over_y(self):
        self.to_y().wait_recv()
        self.hand(2)

    def end(self):
        self.corner().wait_recv()
        self.hand(3)

    def arrive(self):
        if self.halves:
            for at in range(4):
                self.to_core(at).wait_recv()

    def drain(self):
        for k in range(1, self.p.deep):
            self.to_z(k).wait_send()
        for copy in (self.to_x(), self.to_y(), self.corner()):
            copy.wait_send()
        if self.halves:
            for at in range(4):
                self.to_core(at).wait_send()


def moving_forward_kernel(
    capacity_ref, x_ref, q_part, k_part, v_part, o_part, router_part, gain_a_part, gain_f_part, rel_ref, picks_ref, row_ref,
    cot_ref,
    normed_out, q_out, k_out, v_out, att_out, lse_out, mixed_out, normed_f_out, sent_out, weights_out, cot_out,
    slot_route, router_out, gains_out,
    normed_ref, q_ref, k_ref, v_ref, att_ref, lse_ref, mixed_ref, normed_f, sent_ref, store_s,
    near_ref, gain_lanes, small_lanes, small_part,
    held, small, pair_send, pair_got, small_got, cot_sent, weight_s, pair_s, pair_r,
    gs, gr, hs, hr, wide_s, wide_r, side_s, side_r, core_s, core_r,
):
    count, width = x_ref.shape
    wide, local, slots, _ = cot_sent.shape
    experts = router_out.shape[1]
    total = wide * local * slots
    units = HEADS // 4
    rows = pair_send.shape[2]
    p = Place(wide)
    greet(p.partners())

    def own_cols(u, half):
        if u == units:
            return o_part[:, half * (width // 2) : (half + 1) * (width // 2)]
        cols = slice((2 * u + half) * BLOCK, (2 * u + half + 1) * BLOCK)
        return jnp.concatenate([q_part[:, cols], k_part[:, cols], v_part[:, cols]], axis=1)

    def swap_copies():
        return [
            remote(pair_send.at[0], pair_got.at[0], pair_s.at[0], pair_r.at[0], p.core),
            remote(small_part, small_got, pair_s.at[1], pair_r.at[1], p.core),
        ]

    gain_lanes[...] = jnp.zeros_like(gain_lanes)
    gain_lanes[0:1, :rows] = gain_a_part[...].astype(F32)
    gain_lanes[1:2, :rows] = gain_f_part[...].astype(F32)
    gain_cols = gain_lanes[...].T[:rows, :]
    small_lanes[...] = jnp.zeros_like(small_lanes)
    small_lanes[:, :experts] = router_part[...].astype(F32)
    lanes = lax.broadcasted_iota(jnp.int32, small_lanes.shape, 1)
    others = jnp.where(lanes == experts + 1, gain_cols[:, 1:2], small_lanes[...])
    small_part[...] = jnp.where(lanes == experts, gain_cols[:, 0:1], others).astype(BF16)
    for u in range(units + 1):
        pair_send[0, u] = jnp.where(p.c == 0, own_cols(u, 1), own_cols(u, 0))
    limit = capacity_ref[0] * count // experts
    routes = jnp.broadcast_to(row_ref[...].astype(F32), (8, count)).T[:, :1].astype(jnp.int32)
    slot_col, slot_row = slot_places(routes, row_ref[...], limit, experts, slots, count)
    slot_route[:, 0:1] = slot_col
    slot_route[:, 1:2] = routes
    near_ref[...] = near_biases(rel_ref, picks_ref)
    cot_sent[...] = slot_rows(slot_row, cot_ref[...], total).reshape(cot_sent.shape)
    moves = Spread(p, cot_sent, cot_out, wide_s, wide_r, side_s, side_r, core_s, core_r)

    def own_rows(e):
        return pltpu.make_async_copy(cot_sent.at[p.w, e], cot_out.at[e, p.n, p.w], weight_s.at[1 + e])

    for e in range(local):
        own_rows(e).start()
    lse_ref[...] = jnp.zeros_like(lse_ref)
    for e in range(local):
        own_rows(e).wait()
    meet(p.partners())
    for copy in swap_copies():
        copy.start()
    for copy in swap_copies():
        copy.wait_recv()

    def joined(mine, other):
        mine, other = mine.astype(F32), other.astype(F32)
        return jnp.concatenate(
            [jnp.where(p.c == 0, mine, other), jnp.where(p.c == 0, other, mine)], axis=0
        ).astype(BF16)

    def gather(u):
        if isinstance(u, int) and u > units:
            return small_gather
        return Gather(p, u, held, True, (gs, gr))

    small_gather = Gather(p, 0, small, False, (hs, hr))
    small[0, p.z, p.y, p.x] = joined(small_part[...], small_got[...])
    for u in range(units + 1):
        mine = jnp.where(p.c == 0, own_cols(u, 0), own_cols(u, 1))
        held[u, p.c, p.z, p.y, p.x] = joined(mine, pair_got[0, u])

    acts = {
        "start": moves.start, "forward": moves.forward, "pass": moves.pass_on,
        "send": lambda u, piece: gather(u).start(), "spread": lambda u, piece: gather(u).spread(),
        "over_x": lambda u, piece: gather(u).over_x(), "over_y": lambda u, piece: gather(u).over_y(),
        "end": lambda u, piece: gather(u).end(),
    }

    def act(steps):
        for name, at, piece in steps:
            acts[name](at, piece)

    def after(u, part):
        for at in range(units):
            steps = FORWARD_STEPS.get(part + str(at), ())
            if steps:
                pl.when(u == at)(lambda steps=steps: act(steps))

    act(FORWARD_STEPS["first"])
    small_all = small[0].reshape(width, BLOCK)
    router_out[...] = small_all[:, :experts]
    gains_out[...] = small_all.astype(F32).T[experts : experts + 8, :]
    tokens = x_ref[...].astype(F32)
    normed_ref[...] = (tokens * inverse_rms(tokens) * gains_out[0:1, :]).astype(BF16)
    act(FORWARD_STEPS.get("N0", ()))

    def pair(at, weight):
        cols = pl.ds(pl.multiple_of(at * BLOCK, BLOCK), BLOCK)
        found = dot_nn(normed_ref[...], weight.reshape(width, 3 * BLOCK)).astype(BF16)
        q_ref[:, cols], k_ref[:, cols], v_ref[:, cols] = (found[:, i * BLOCK : (i + 1) * BLOCK] for i in range(3))
        pair_forward(at, near_ref, q_ref, k_ref, v_ref, att_ref, lse_ref)

    def pairs(u, carry):
        gather(u).arrive()
        pair(2 * u, held[u, 0])
        after(u, "A")
        pair(2 * u + 1, held[u, 1])
        after(u, "B")
        return carry

    lax.fori_loop(0, units, pairs, 0)
    stores = [
        pltpu.make_async_copy(source, target, store_s.at[at])
        for at, (source, target) in enumerate((
            (normed_ref, normed_out), (q_ref, q_out), (k_ref, k_out), (v_ref, v_out), (att_ref, att_out),
            (lse_ref, lse_out), (mixed_ref, mixed_out), (normed_f, normed_f_out), (sent_ref, sent_out),
        ))
    ]
    for copy in stores[:6]:
        copy.start()
    gather(units).arrive()
    weights_copy = pltpu.make_async_copy(held, weights_out, weight_s.at[0])
    weights_copy.start()
    mixed = tokens_again(x_ref) + jnp.concatenate(
        [dot_nn(att_ref[...], held[units, half].reshape(width, width // 2)) for half in range(2)], axis=1
    )
    mixed_ref[...] = mixed
    normed_2 = (mixed * inverse_rms(mixed) * gains_out[1:2, :]).astype(BF16)
    normed_f[...] = normed_2
    stores[6].start()
    stores[7].start()
    sent_ref[...] = slot_rows(slot_row, normed_2, total).reshape(sent_ref.shape)
    stores[8].start()
    act(FORWARD_STEPS.get("M0", ()))
    for copy in swap_copies():
        copy.wait_send()
    small_gather.drain()
    for u in range(units + 1):
        gather(u).drain()
    for e in range(local):
        moves.arrive(e, 0)
        moves.arrive(e, 1)
        moves.drain(e)
    weights_copy.wait()
    for copy in stores:
        copy.wait()


def tokens_again(x_ref):
    return x_ref[...].astype(F32)


def moving_forward(
    rel_bias, capacity, inputs, w_query, w_key, w_value, w_output, w_router, gain_attn, gain_ffn, routes, cotangent,
    wide, narrow, local, slots,
):
    count, width = inputs.shape
    experts = w_router.shape[1]
    shard = w_query.shape[0]
    deep, units = wide // 2, HEADS // 4
    half = width // 2
    sds = jax.ShapeDtypeStruct
    rows_t = lambda dtype, cols=width: sds((count, cols), dtype)
    smem, any_spec = pl.BlockSpec(memory_space=pltpu.SMEM), pl.BlockSpec(memory_space=pl.ANY)
    vmem = lambda *shape, dtype=BF16: pltpu.VMEM(shape, dtype)
    dma = pltpu.SemaphoreType.DMA
    picks = jnp.asarray(near_picks(rel_bias.shape[0], 1).T)
    return pl.pallas_call(
        moving_forward_kernel,
        out_shape=(
            rows_t(BF16), rows_t(BF16), rows_t(BF16), rows_t(BF16), rows_t(BF16), rows_t(F32, BLOCK), rows_t(F32),
            rows_t(BF16), sds((wide, local, slots, width), BF16),
            sds((units + 1, 2, deep, 2, 2, 2 * shard, half), BF16),
            sds((local, narrow, wide, slots, width), BF16), sds((count, 2), jnp.int32),
            sds((width, experts), BF16), sds((8, width), F32),
        ),
        in_specs=[smem] + in_vmem(12),
        out_specs=(any_spec,) * 11 + tuple(in_vmem(3)),
        scratch_shapes=[
            vmem(count, width), vmem(count, width), vmem(count, width), vmem(count, width), vmem(count, width),
            vmem(count, BLOCK, dtype=F32), vmem(count, width, dtype=F32), vmem(count, width),
            vmem(wide, local, slots, width), dma((9,)),
            vmem(HEADS, 4 * BLOCK, dtype=F32), vmem(8, BLOCK, dtype=F32), vmem(shard, BLOCK, dtype=F32), vmem(shard, BLOCK),
            vmem(units + 1, 2, deep, 2, 2, 2 * shard, half), vmem(1, deep, 2, 2, 2 * shard, BLOCK),
            vmem(1, units + 1, shard, half), vmem(1, units + 1, shard, half), vmem(shard, BLOCK),
            vmem(wide, local, slots, width), dma((1 + local,)), dma((2,)), dma((2,)),
            dma((units + 1, 10)), dma((units + 1, 10)), dma((1, 10)), dma((1, 10)),
            *Spread.semaphores(local, wide),
        ],
        compiler_params=pltpu.CompilerParams(collective_id=1, has_side_effects=True, vmem_limit_bytes=62 << 20),
        name="forward",
    )(
        capacity, inputs, w_query, w_key, w_value, w_output, w_router, gain_attn[None, :], gain_ffn[None, :], rel_bias, picks,
        routes.reshape(1, count), cotangent,
    )


def moving_expert_kernel(
    sent, cot_hbm, in_hbm, out_hbm, router_ref,
    outs_o, gin_o, gout_o, back_o, gate_o,
    held, cot, w_in, w_out, sg, hidden, gpre, outs, gin, gout, to_core, from_core, from_side, near_sum, far_sum,
    gate_sum, gate_core, gate_from_core, gate_side, gate_from_side, gate_ready,
    load_s, store_s, wide_s, wide_r, side_s, side_r, core_s, core_r,
    rc_s, rc_r, rx_s, rx_r, rw_s, rw_r, gc_s, gc_r, gx_s, gx_r, gw_s, gw_r,
):
    wide, local, slots, width = sent.shape
    narrow = held.shape[1]
    step = wide * slots
    hidden_width = in_hbm.shape[2]
    p = Place(wide)
    moves = Spread(p, sent, held, wide_s, wide_r, side_s, side_r, core_s, core_r)
    greet(p.partners())

    def loads(e):
        return [
            pltpu.make_async_copy(in_hbm.at[e], w_in.at[e], load_s.at[e, 0]),
            pltpu.make_async_copy(out_hbm.at[e], w_out.at[e], load_s.at[e, 1]),
            pltpu.make_async_copy(cot_hbm.at[e], cot.at[e], load_s.at[e, 2]),
        ]

    def store(e, at):
        source = (outs.at[lax.rem(e, 2)], gin, gout)[at]
        return pltpu.make_async_copy(source, (outs_o, gin_o, gout_o)[at].at[e], store_s.at[e, at])

    def grads_out(e):
        b = lax.rem(e, 2)

        @pl.when(e > 0)
        def _():
            store(e - 1, 2).wait()

        rows = narrow * step
        found = dot_tn(hidden[b].reshape(rows, hidden_width), sg[b].reshape(rows, width))
        gout[...] = found.astype(BF16)
        store(e, 2).start()

    def grads_in(e):
        b = lax.rem(e, 2)

        @pl.when(e > 0)
        def _():
            store(e - 1, 1).wait()

        rows = narrow * step
        found = dot_tn(held[e].reshape(rows, width), gpre[b].reshape(rows, hidden_width))
        gin[...] = found.astype(BF16)
        store(e, 1).start()

    for e in range(local):
        for copy in loads(e):
            copy.start()
        held[e, p.n, p.w] = sent[p.w, e]
    gate_sum[...] = jnp.zeros_like(gate_sum)
    meet(p.partners())

    def chunk(e, m):
        b = lax.rem(e, 2)
        rows = held[e, m].reshape(step, width)
        probs = softmax_lanes(dot_nn(rows, router_ref[...]))
        here = lax.broadcasted_iota(jnp.int32, probs.shape, 1) == p.w * local + e
        gate = jnp.sum(jnp.where(here, probs, 0.0), axis=-1, keepdims=True)
        cot_rows = cot[e, m].reshape(step, width).astype(F32)
        sg_rows = (cot_rows * gate).astype(BF16)
        sg[b, m] = sg_rows
        pre = dot_nn(rows, w_in[e])
        square = pre * pre
        inner = jnp.tanh(pre * (ROOT_TWO_PI + ROOT_TWO_PI * CUBIC * square))
        half = 0.5 * (1.0 + inner)
        hidden_rows = (pre * half).astype(BF16)
        hidden[b, m] = hidden_rows
        slope = half + 0.5 * pre * (1.0 - inner * inner) * (
            ROOT_TWO_PI + 3.0 * ROOT_TWO_PI * CUBIC * square
        )
        gpre_rows = (dot_nt(sg_rows, w_out[e]) * slope).astype(BF16)
        gpre[b, m] = gpre_rows
        out_rows = dot_nn(hidden_rows, w_out[e])
        outs[b, m] = out_rows.astype(BF16).reshape(wide, slots, width)
        gate_rows = jnp.sum(out_rows * cot_rows, axis=-1, keepdims=True)
        row = lax.broadcasted_iota(jnp.int32, (step, local * slots), 0)
        lane = lax.broadcasted_iota(jnp.int32, (step, local * slots), 1)
        spread = jnp.where(lane == e * slots + lax.rem(row, slots), gate_rows, 0.0)
        gate_sum[m] += jnp.sum(spread.reshape(wide, slots, local * slots), axis=1)
        return dot_nt(gpre_rows, w_in[e])

    back = Collect(
        p, lambda e, other: to_core.at[e, other], from_core, from_side, back_o, (rc_s, rc_r, rx_s, rx_r, rw_s, rw_r)
    )

    def go(e, piece):
        if piece == 1:
            back.go_beside(e, far_sum[...])
        else:
            back.beside(e, piece).start()

    def add_core(e, piece):
        back.core(e, 0).wait_recv()
        near_sum[e] = near_sum[e] + from_core[e, 0].astype(F32)

    acts = {
        "start": moves.start, "forward": moves.forward, "pass": moves.pass_on, "go": go, "sum": add_core,
        "finish": lambda e, piece: back.finish(e, piece, lambda rows, part: near_sum[e, rows, part]),
    }

    def after(e, part):
        for at in range(local):
            steps = EXPERT_STEPS.get(part + str(at), ())
            if steps:

                def run(steps=steps):
                    for name, expert, piece in steps:
                        acts[name](expert, piece)

                if not isinstance(e, int):
                    pl.when(e == at)(run)
                elif e == at:
                    run()

    for name, expert, piece in EXPERT_STEPS["first"]:
        acts[name](expert, piece)

    far_x = (1 - p.x) * 2

    gates_core = remote(gate_core, gate_from_core, gc_s, gc_r, p.core)

    def gates_core_start():
        gate_core[0] = gate_sum[p.x * 2 + 1 - p.c]
        gate_core[1] = gate_sum[far_x + 1 - p.c]
        gates_core.start()

    def expert(e, carry):
        for copy in loads(e):
            copy.wait()

        @pl.when(e >= 2)
        def _():
            store(e - 2, 0).wait()

        moves.arrive(e, 1)
        to_core[e, 1] = chunk(e, far_x + 1 - p.c).astype(BF16).reshape(wide, slots, width)
        back.core(e, 1).start()
        after(e, "A")
        far_sum[...] = chunk(e, far_x + p.c).reshape(wide, slots, width)
        after(e, "B")

        @pl.when(e > 0)
        def _():
            grads_out(e - 1)
            after(e - 1, "W")

        moves.arrive(e, 0)
        to_core[e, 0] = chunk(e, p.x * 2 + 1 - p.c).astype(BF16).reshape(wide, slots, width)
        back.core(e, 0).start()
        after(e, "C")
        near_sum[e] = chunk(e, p.n).reshape(wide, slots, width)
        store(e, 0).start()

        @pl.when(e == local - 1)
        def _():
            gates_core_start()

        after(e, "D")

        @pl.when(e > 0)
        def _():
            grads_in(e - 1)
            after(e - 1, "V")

        return carry

    lax.fori_loop(0, local, expert, 0)
    gates_core.wait_recv()
    gate_side[...] = gate_sum[far_x + p.c] + gate_from_core[1]
    gates_side = remote(gate_side, gate_from_side, gx_s, gx_r, p.side)
    gates_side.start()
    grads_out(local - 1)
    after(local - 1, "W")
    gates_side.wait_recv()
    gates = gate_sum[p.n] + gate_from_core[0] + gate_from_side[...]
    for v in range(wide):
        gate_ready[v] = gates[v : v + 1, :]
    gates_wide = [
        remote(gate_ready.at[p.flip(j)], gate_o.at[p.w], gw_s.at[j], gw_r.at[j], p.peer(j)) for j in range(1, wide)
    ]
    for copy in gates_wide:
        copy.start()
    gate_o[p.w] = gate_ready[p.w]
    grads_in(local - 1)
    after(local - 1, "V")
    gates_core.wait_send()
    gates_side.wait_send()

    def drain(e, carry):
        moves.drain(e)
        back.drain(e)
        back.arrive(e)

        @pl.when(e >= local - 2)
        def _():
            store(e, 0).wait()

        return carry

    lax.fori_loop(0, local, drain, 0)
    store(local - 1, 1).wait()
    store(local - 1, 2).wait()
    for copy in gates_wide:
        copy.wait()


def moving_experts(sent, cot_all, expert_in, expert_out, router, wide, narrow):
    _, local, slots, width = sent.shape
    hidden_width = expert_in.shape[2]
    step = wide * slots
    sds = jax.ShapeDtypeStruct
    any_spec, vmem_spec = pl.BlockSpec(memory_space=pl.ANY), pl.BlockSpec(memory_space=pltpu.VMEM)
    dma = pltpu.SemaphoreType.DMA
    outs, gin, gout, back, gates = pl.pallas_call(
        moving_expert_kernel,
        out_shape=(
            sds((local, narrow, wide, slots, width), BF16),
            sds(expert_in.shape, BF16),
            sds(expert_out.shape, BF16),
            sds((wide, local, slots, width), BF16),
            sds((wide, 1, local * slots), F32),
        ),
        in_specs=[vmem_spec, any_spec, any_spec, any_spec, vmem_spec],
        out_specs=(any_spec,) * 3 + (vmem_spec,) * 2,
        scratch_shapes=[
            pltpu.VMEM((local, narrow, wide, slots, width), BF16),
            pltpu.VMEM((local, narrow, wide, slots, width), BF16),
            pltpu.VMEM(expert_in.shape, BF16),
            pltpu.VMEM(expert_out.shape, BF16),
            pltpu.VMEM((2, narrow, step, width), BF16),
            pltpu.VMEM((2, narrow, step, hidden_width), BF16),
            pltpu.VMEM((2, narrow, step, hidden_width), BF16),
            pltpu.VMEM((2, narrow, wide, slots, width), BF16),
            pltpu.VMEM(expert_in.shape[1:], BF16),
            pltpu.VMEM(expert_out.shape[1:], BF16),
            pltpu.VMEM((local, 2, wide, slots, width), BF16),
            pltpu.VMEM((local, 2, wide, slots, width), BF16),
            pltpu.VMEM((local, wide, slots, width), BF16),
            pltpu.VMEM((local, wide, slots, width), F32),
            pltpu.VMEM((wide, slots, width), F32),
            pltpu.VMEM((narrow, wide, local * slots), F32),
            pltpu.VMEM((2, wide, local * slots), F32),
            pltpu.VMEM((2, wide, local * slots), F32),
            pltpu.VMEM((wide, local * slots), F32),
            pltpu.VMEM((wide, local * slots), F32),
            pltpu.VMEM((wide, 1, local * slots), F32),
            dma((local, 3)), dma((local, 3)), *Spread.semaphores(local, wide), *Collect.semaphores(local, wide),
            dma, dma, dma, dma, dma((wide,)), dma((wide,)),
        ],
        compiler_params=pltpu.CompilerParams(
            collective_id=2, has_side_effects=True, vmem_limit_bytes=62 << 20
        ),
        name="experts",
    )(sent, cot_all, expert_in, expert_out, router)
    return outs, back, gates, gin.astype(F32), gout.astype(F32)


def routed_gate(normed_f, router_ref, routes):
    probs = softmax_lanes(dot_nn(normed_f[...], router_ref[...]))
    chosen = lax.broadcasted_iota(jnp.int32, probs.shape, 1) == routes
    return probs, chosen, jnp.sum(jnp.where(chosen, probs, 0.0), axis=-1, keepdims=True)


def slot_owners(slot_col, total):
    return lax.broadcasted_iota(jnp.int32, (slot_col.shape[0], total), 1) == slot_col


def ffn_backward(probs, chosen, gate, owned, gates_ref, normed_f, router_ref, grows_ref, mixed, cot_ref, gain_f):
    grad_gate = jnp.sum(jnp.where(owned, gates_ref[...], 0.0), axis=-1, keepdims=True)
    grad_logits = (probs * (jnp.where(chosen, grad_gate, 0.0) - gate * grad_gate)).astype(BF16)
    grad_router = dot_tn(normed_f[...], grad_logits)
    grad_normed = dot_nt(grad_logits, router_ref[...]) + dot_nn(owned.astype(BF16), grows_ref[...])
    grad_norm, grad_gain = norm_backward(mixed, inverse_rms(mixed), gain_f[...], grad_normed)
    return grad_router, cot_ref[...].astype(F32) + grad_norm, grad_gain


def attention_setup(q_ref, k_ref, normed_ref, att_ref, lse_ref, q_t, k_t, normed_t, att_t, lse_t):
    head_dim = q_ref.shape[1] // HEADS
    att_t[...] = att_ref[...].T
    q_t[...] = (q_ref[...] * jnp.asarray(head_dim**-0.5, BF16)).T
    k_t[...] = k_ref[...].T
    normed_t[...] = normed_ref[...].T
    lse_t[...] = lse_ref[...].T


def attention_delta(datt, att_t, datt_t, delta):
    width, count = att_t.shape
    datt_t[...] = datt[...].T
    products = datt_t[...].astype(F32) * att_t[...].astype(F32)
    delta[...] = jnp.sum(products.reshape(HEADS, width // HEADS, count), axis=1)


def pair_backward(
    at, near_ref, q_ref, k_ref, v_ref, q_t, k_t, datt, datt_t, delta, lse_t, dst, gq, gk, gv, gnear_ref, gfar_ref
):
    count, width = q_ref.shape
    head_dim = width // HEADS
    blocks = count // BLOCK
    first = lax.broadcasted_iota(jnp.int32, (1, BLOCK), 1) < head_dim
    cols = pl.ds(pl.multiple_of(at * BLOCK, BLOCK), BLOCK)
    q_pair, datt_pair = q_ref[:, cols], datt[:, cols]
    gq_parts, gk_parts, gv_parts = [], [], []
    for half in range(2):
        head = 2 * at + half
        mask = first if half == 0 else jnp.logical_not(first)
        near_row = near_ref[pl.ds(head, 1), :]
        near = toeplitz_near(near_row)
        lse_row, delta_row = lse_t[pl.ds(head, 1), :], delta[pl.ds(head, 1), :]
        near_sum = jnp.zeros((BLOCK, 3 * BLOCK), F32)
        low_sum, high_sum = jnp.zeros((BLOCK, BLOCK), F32), jnp.zeros((BLOCK, BLOCK), F32)
        gk_rows, gv_rows = [], []
        for row in range(blocks):
            rows = slice(row * BLOCK, (row + 1) * BLOCK)
            k_rows, v_rows = k_ref[rows, cols], v_ref[rows, cols]
            zeros = jnp.zeros_like(k_rows)
            scores = dot_nn(jnp.where(mask, k_rows, zeros), q_t[cols, :])
            scores = scores + bias_rows(near, near_row, row, blocks)
            weights = jnp.exp(scores - lse_row)
            grad_weights = dot_nn(jnp.where(mask, v_rows, zeros), datt_t[cols, :])
            grad_scores = weights * (grad_weights - delta_row)
            gv_rows.append(dot_nn(weights.astype(BF16), datt_pair))
            low_bits = grad_scores.astype(BF16)
            dst[rows, :] = low_bits
            gk_rows.append(dot_nn(low_bits, q_pair))
            for column in range(blocks):
                piece = grad_scores[:, column * BLOCK : (column + 1) * BLOCK]
                distance = column - row
                if distance <= -2:
                    high_sum = high_sum + piece
                elif distance >= 2:
                    low_sum = low_sum + piece
                else:
                    pads = [jnp.zeros((BLOCK, BLOCK), F32)] * 3
                    pads[distance + 1] = piece
                    near_sum = near_sum + jnp.concatenate(pads, axis=1)
        gq_parts.append(
            dot_nn(k_t[pl.ds(pl.multiple_of(head * head_dim, head_dim), head_dim), :], dst[...])
        )
        gk_parts.append(jnp.concatenate(gk_rows, axis=0))
        gv_parts.append(jnp.concatenate(gv_rows, axis=0))
        gnear_ref[pl.ds(head, 1), :] = diagonal_sums(near_sum)
        gfar_ref[pl.ds(head, 1), :] = jnp.concatenate(
            [jnp.sum(low_sum, axis=0, keepdims=True), jnp.sum(high_sum, axis=0, keepdims=True)], axis=1
        )
    scale = head_dim**-0.5
    gq[:, cols] = (jnp.concatenate(gq_parts, axis=0).T * scale).astype(BF16)
    gk[:, cols] = (jnp.where(first, gk_parts[0], gk_parts[1]) * scale).astype(BF16)
    gv[:, cols] = jnp.where(first, gv_parts[0], gv_parts[1]).astype(BF16)


def input_backward(x_ref, w_ref, gain_a, gmixed, gq, gk, gv):
    count, width = x_ref.shape
    grad_normed = jnp.zeros((count, width), F32)
    for at, grad in enumerate((gq, gk, gv)):
        grad_normed = grad_normed + dot_nt(grad[...], w_ref[:, at * width : (at + 1) * width])
    tokens = x_ref[...].astype(F32)
    grad_norm, grad_gain = norm_backward(tokens, inverse_rms(tokens), gain_a[...], grad_normed)
    return gmixed[...] + grad_norm, grad_gain


def backward_kernel(
    x_ref, w_ref, gain_a, gain_f, router_ref, near_ref, slot_col, routes_ref,
    normed_ref, q_ref, k_ref, v_ref, att_ref, lse_ref, mixed_ref, normed_f, cot_ref, outs_ref, grows_ref, gates_ref,
    result_ref, gx_ref, gw_ref, grouter_ref, gnear_ref, gfar_ref, ggain_ref,
    q_t, k_t, normed_t, att_t, datt, datt_t, delta, lse_t, gq, gk, gv, gmixed, dst,
):
    width = x_ref.shape[1]
    probs, chosen, gate = routed_gate(normed_f, router_ref, routes_ref[...])
    owned = slot_owners(slot_col[...], outs_ref.shape[0])
    mixed = mixed_ref[...]
    result_ref[...] = (mixed + gate * dot_nn(owned.astype(BF16), outs_ref[...])).astype(BF16)
    grouter_ref[...], grad_mixed, ggain_ref[1:2, :] = ffn_backward(
        probs, chosen, gate, owned, gates_ref, normed_f, router_ref, grows_ref, mixed, cot_ref, gain_f
    )
    gmixed[...] = grad_mixed
    branch = grad_mixed.astype(BF16)
    gw_ref[:, 3 * width : 4 * width] = dot_tn(att_ref[...], branch).astype(BF16)
    datt[...] = dot_nt(branch, w_ref[:, 3 * width : 4 * width]).astype(BF16)
    attention_setup(q_ref, k_ref, normed_ref, att_ref, lse_ref, q_t, k_t, normed_t, att_t, lse_t)
    attention_delta(datt, att_t, datt_t, delta)

    def pair(at, carry):
        pair_backward(
            at, near_ref, q_ref, k_ref, v_ref, q_t, k_t, datt, datt_t, delta, lse_t, dst, gq, gk, gv,
            gnear_ref, gfar_ref,
        )
        return carry

    lax.fori_loop(0, HEADS // 2, pair, 0)
    for at, grad in enumerate((gq, gk, gv)):
        gw_ref[:, at * width : (at + 1) * width] = dot_nn(normed_t[...], grad[...]).astype(BF16)
    gx_ref[...], ggain_ref[0:1, :] = input_backward(x_ref, w_ref, gain_a, gmixed, gq, gk, gv)


class Sums:
    def __init__(self, place, unit, buffers, semaphores, out, split):
        self.p, self.unit, self.out, self.split = place, unit, out, split
        self.send, self.core, self.first_in, self.second_in, self.z_in, self.last = buffers
        self.s, self.r = semaphores
        self.deep = place.deep
        p, c = place, place.c * split
        self.first, self.second = p.y + c * (p.x - p.y), p.x + c * (p.y - p.x)
        row, side = p.row, p.side
        self.first_peer = tuple(a + c * (b - a) for a, b in zip(row, side))
        self.second_peer = tuple(b + c * (a - b) for a, b in zip(row, side))

    def store(self, buffer, part, core):
        rows, cols = buffer.shape[-2:]
        blocks = part.reshape(self.deep, 2, 2, rows, cols)
        c = core * self.split
        for y in range(2):
            for x in range(2):
                first, second = (y, x) if y == x else (y + c * (x - y), x + c * (y - x))
                buffer[self.unit, first, second] = blocks[:, y, x].astype(buffer.dtype)

    def to_core(self):
        u, p = self.unit, self.p
        return remote(self.send.at[u], self.core.at[u], self.s.at[u, 0], self.r.at[u, 0], p.core)

    def to_y(self):
        u = self.unit
        return remote(self.core.at[u, 1 - self.first], self.first_in.at[u], self.s.at[u, 1], self.r.at[u, 1], self.first_peer)

    def to_x(self):
        u = self.unit
        return remote(self.first_in.at[u, 1 - self.second], self.second_in.at[u], self.s.at[u, 2], self.r.at[u, 2], self.second_peer)

    def to_z(self, k):
        u, p = self.unit, self.p
        z = lax.rem(p.z + k, p.deep)
        return remote(
            self.second_in.at[u, z], self.z_in.at[u, k], self.s.at[u, 3 + k], self.r.at[u, 3 + k], (z * 2 + p.y, p.n)
        )

    def to_last(self):
        u, p = self.unit, self.p
        return remote(self.last.at[u, 1 - p.c], self.out.at[u, p.c], self.s.at[u, 3], self.r.at[u, 3], p.core)

    def begin(self, part):
        self.store(self.send, part, 1 - self.p.c)
        self.to_core().start()

    def stage_core(self, part):
        u = self.unit
        self.to_core().wait_recv()
        rows, cols = self.core.shape[-2:]
        blocks = part.reshape(self.deep, 2, 2, rows, cols)
        c = self.p.c * self.split
        for y in range(2):
            for x in range(2):
                first, second = (y, x) if y == x else (y + c * (x - y), x + c * (y - x))
                kept = blocks[:, y, x] + self.core[u, first, second].astype(F32)
                self.core[u, first, second] = kept.astype(BF16)
        self.to_y().start()

    def stage_y(self):
        u = self.unit
        self.to_y().wait_recv()
        self.first_in[u] = (self.core[u, self.first].astype(F32) + self.first_in[u].astype(F32)).astype(BF16)
        self.to_x().start()

    def stage_x(self):
        u = self.unit
        self.to_x().wait_recv()
        self.second_in[u] = (self.first_in[u, self.second].astype(F32) + self.second_in[u].astype(F32)).astype(BF16)
        for k in range(1, self.p.deep):
            self.to_z(k).start()

    def stage_z(self):
        u = self.unit
        total = self.second_in[u, self.p.z].astype(F32)
        for k in range(1, self.p.deep):
            self.to_z(k).wait_recv()
            total = total + self.z_in[u, k].astype(F32)
        self.last[u] = total.reshape(self.last.shape[1:])
        self.to_last().start()
        self.out[u, self.p.c] = self.last[u, self.p.c]

    def drain(self):
        for copy in (self.to_core(), self.to_y(), self.to_x()):
            copy.wait_send()
        for k in range(1, self.p.deep):
            self.to_z(k).wait_send()
        self.to_last().wait()


def sum_buffers(units, wide, rows, cols):
    deep = wide // 2
    vmem = lambda *shape, dtype=BF16: pltpu.VMEM((units, *shape), dtype)
    return [
        vmem(2, 2, deep, rows, cols), vmem(2, 2, deep, rows, cols), vmem(2, deep, rows, cols), vmem(deep, rows, cols),
        vmem(deep, rows, cols), vmem(2, rows // 2, cols, dtype=F32),
        pltpu.SemaphoreType.DMA((units, 3 + deep)), pltpu.SemaphoreType.DMA((units, 3 + deep)),
    ]


def moving_backward_kernel(
    x_hbm, w_hbm, normed_hbm, q_hbm, k_hbm, v_hbm, att_hbm, lse_hbm, outs_hbm, mixed_hbm, cot_hbm, grows_hbm,
    gains_ref, router_ref, rel_ref, slot_route, normed_f, gates_ref, picks_ref,
    gx_ref, result_ref, gq_out, gk_out, gv_out, go_out, router_out, small_out,
    x_ref, w_ref, normed_ref, q_ref, k_ref, v_ref, att_ref, lse_ref, mixed_ref, cot_ref, grows_ref, load_s, near_ref,
    q_t, k_t, normed_t, att_t, datt, datt_t, delta, lse_t, gq, gk, gv, gmixed, gnormed, dst, gnear, gfar,
    own, from_core, from_side, returned, own_s, rc_s, rc_r, rx_s, rx_r, rw_s, rw_r,
    u1, u2, u3, u4, u5, u6, us, ur, o1, o2, o3, o4, o5, o6, os, orr, pair_sums, o_out,
    small, small_in, ss, sr,
):
    count, width = x_hbm.shape
    wide, local, slots, _ = returned.shape
    total = wide * local * slots
    p = Place(wide)
    far_x = (1 - p.x) * 2
    units = HEADS // 4
    gain_a, gain_f = gains_ref.at[0:1, :], gains_ref.at[1:2, :]
    loads = [
        pltpu.make_async_copy(source, target, load_s.at[at])
        for at, (source, target) in enumerate((
            (att_hbm, att_ref), (q_hbm, q_ref), (k_hbm, k_ref), (normed_hbm, normed_ref), (lse_hbm, lse_ref),
            (mixed_hbm, mixed_ref), (cot_hbm, cot_ref), (grows_hbm, grows_ref),
            (w_hbm, w_ref), (v_hbm, v_ref), (x_hbm, x_ref),
        ))
    ]

    def partial(e, other, core):
        return outs_hbm.at[e, (far_x if other else p.x * 2) + core]

    back = Collect(
        p, lambda e, other: partial(e, other, 1 - p.c), from_core, from_side, returned, (rc_s, rc_r, rx_s, rx_r, rw_s, rw_r)
    )

    def own_copy(e, other):
        return pltpu.make_async_copy(partial(e, other, p.c), own.at[e, other], own_s.at[e, other])

    for copy in loads[:5]:
        copy.start()
    greet(p.partners())
    for other in (1, 0):
        for e in range(local):
            own_copy(e, other).start()
    for copy in loads[5:11]:
        copy.start()

    def go(e, piece):
        if piece == 1:
            own_copy(e, 1).wait()
            back.go_beside(e, own[e, 1])
        else:
            back.beside(e, piece).start()

    def near(e, piece):
        back.core(e, 0).wait_recv()
        own_copy(e, 0).wait()

    def finish(e, piece):
        back.finish(
            e, piece, lambda rows, part: own[e, 0, rows, part].astype(F32) + from_core[e, 0, rows, part].astype(F32)
        )

    def unit(u):
        if isinstance(u, int) and u == units:
            return Sums(p, 0, (o1, o2, o3, o4, o5, o6), (os, orr), o_out, 0)
        return Sums(p, u, (u1, u2, u3, u4, u5, u6), (us, ur), pair_sums, (u + 1) // units)

    hops = [[p.core], [p.row], [p.side], [(lax.rem(p.z + k, p.deep) * 2 + p.y, p.n) for k in range(1, p.deep)]]
    copies, slot = [], 0
    for stage, devices in enumerate(hops):
        copies.append([
            remote(small.at[stage], small_in.at[slot + at], ss.at[slot + at], sr.at[slot + at], device)
            for at, device in enumerate(devices)
        ])
        slot += len(devices)

    def small_end(stage):
        slot = sum(len(c) for c in copies[:stage])
        found = small[stage]
        for at, copy in enumerate(copies[stage]):
            copy.wait_recv()
            found = found + small_in[slot + at]
        return found

    def small_step(stage, piece):
        if stage:
            small[stage] = small_end(stage - 1)
        for copy in copies[stage]:
            copy.start()

    acts = {
        "core": lambda e, other: back.core(e, other).start(), "go": go, "near": near, "finish": finish,
        "y": lambda u, piece: unit(u).stage_y(), "x": lambda u, piece: unit(u).stage_x(),
        "z": lambda u, piece: unit(u).stage_z(), "small": small_step,
    }

    def act(part):
        for name, at, piece in BACKWARD_STEPS.get(part, ()):
            acts[name](at, piece)

    def after(u, part):
        for at in range(units):
            if part + str(at) in BACKWARD_STEPS:
                pl.when(u == at)(lambda at=at: act(part + str(at)))

    probs, chosen, gate = routed_gate(normed_f, router_ref, slot_route[:, 1:2])
    owned = slot_owners(slot_route[:, 0:1], total)
    near_ref[...] = near_biases(rel_ref, picks_ref)
    for copy in loads[:5]:
        copy.wait()
    attention_setup(q_ref, k_ref, normed_ref, att_ref, lse_ref, q_t, k_t, normed_t, att_t, lse_t)
    meet(p.partners())
    act("first")
    for copy in loads[5:8]:
        copy.wait()
    grad_router, grad_mixed, grad_gain_f = ffn_backward(
        probs, chosen, gate, owned, gates_ref, normed_f, router_ref, grows_ref, mixed_ref[...], cot_ref, gain_f
    )
    gmixed[...] = grad_mixed
    small[0] = jnp.zeros_like(small[0])
    small[0, HEADS : HEADS + 1, :] = grad_gain_f
    act("F0")
    branch = grad_mixed.astype(BF16)
    half_cols = width // 2
    router_cols = o_out.shape[-1] - half_cols
    router_wide = jnp.concatenate(
        [grad_router, jnp.zeros((width, router_cols - grad_router.shape[1]), F32)], axis=1
    )

    def output_part(core):
        low, high = branch[:, :half_cols], branch[:, half_cols:]
        part = dot_nn(att_t[...], jnp.where(core == 0, low, high))
        return jnp.concatenate([part, jnp.where(core == 0, router_wide, 0.0)], axis=1)

    unit(units).begin(output_part(1 - p.c))
    act("O0")
    loads[8].wait()
    datt[...] = (
        dot_nt(branch[:, :half_cols], w_ref[units, 0]) + dot_nt(branch[:, half_cols:], w_ref[units, 1])
    ).astype(BF16)
    act("D0")
    unit(units).stage_core(output_part(p.c))
    act("Q0")
    attention_delta(datt, att_t, datt_t, delta)
    for copy in loads[9:11]:
        copy.wait()
    act("S0")

    def pair(at):
        pair_backward(
            at, near_ref, q_ref, k_ref, v_ref, q_t, k_t, datt, datt_t, delta, lse_t, dst, gq, gk, gv,
            gnear, gfar,
        )
        cols = pl.ds(pl.multiple_of(at * BLOCK, BLOCK), BLOCK)
        grads = jnp.concatenate([gq[:, cols], gk[:, cols], gv[:, cols]], axis=1)
        gnormed[...] += dot_nt(grads, w_ref[at // 2, lax.rem(at, 2)])
        return dot_nn(normed_t[...], grads)

    gnormed[...] = jnp.zeros_like(gnormed)

    def pairs(u, carry):
        unit(u).begin(pair(2 * u + 1 - p.c))
        after(u, "A")
        unit(u).stage_core(pair(2 * u + p.c))
        after(u, "B")
        return carry

    lax.fori_loop(0, units, pairs, 0)
    near_grads = lax.dot_general(
        gnear[...], picks_ref[...], (((1,), (1,)), ((), ())), precision=HIGHEST, preferred_element_type=F32
    )
    buckets = lax.broadcasted_iota(jnp.int32, near_grads.shape, 1)
    low_sum = jnp.sum(gfar[:, :BLOCK], axis=1, keepdims=True)
    high_sum = jnp.sum(gfar[:, BLOCK:], axis=1, keepdims=True)
    bucket_count = rel_ref.shape[0]
    rel = near_grads + jnp.where(buckets == bucket_count // 2 - 1, low_sum, 0.0)
    small[0, :HEADS, :bucket_count] = rel + jnp.where(buckets == bucket_count - 1, high_sum, 0.0)
    tokens = x_ref[...].astype(F32)
    grad_norm, grad_gain_a = norm_backward(tokens, inverse_rms(tokens), gain_a[...], gnormed[...])
    gx_ref[...] = gmixed[...] + grad_norm
    small[0, HEADS + 1 : HEADS + 2, :] = grad_gain_a

    act("P0")
    for e in range(local):
        back.arrive(e)
    combined = dot_nn(owned.astype(BF16), returned[...].reshape(total, width))
    result_ref[...] = (mixed_ref[...] + gate * combined).astype(BF16)
    act("R0")
    small_out[...] = small_end(3)
    for e in range(local):
        back.drain(e)
    for u in range(units + 1):
        unit(u).drain()
    for half in range(2):
        for u in range(units):
            cols = slice((2 * u + half) * BLOCK, (2 * u + half + 1) * BLOCK)
            for at, out in enumerate((gq_out, gk_out, gv_out)):
                out[:, cols] = pair_sums[u, half, :, at * BLOCK : (at + 1) * BLOCK]
        go_out[:, half * half_cols : (half + 1) * half_cols] = o_out[0, half, :, :half_cols]
    router_out[...] = o_out[0, 0, :, half_cols : half_cols + router_out.shape[1]]
    for stage in copies:
        for copy in stage:
            copy.wait_send()


def moving_backward(
    rel_bias, inputs, weights, gains, router, slot_route,
    normed, q, k, v, att, lse, mixed, normed_f, cotangent, outs, grows, gates, wide, slots,
):
    count, width = inputs.shape
    local, narrow = outs.shape[:2]
    experts = router.shape[1]
    bucket_count = rel_bias.shape[0]
    deep, rows = wide // 2, width // (wide * 2)
    units = HEADS // 4
    pair_cols, out_cols = 3 * BLOCK, width // 2 + BLOCK * -(-experts // BLOCK)
    sds = jax.ShapeDtypeStruct
    any_spec = pl.BlockSpec(memory_space=pl.ANY)
    picks = jnp.asarray(near_picks(bucket_count, -1).T)
    wide_t = lambda dtype: pltpu.VMEM((width, count), dtype)
    tall = lambda dtype: pltpu.VMEM((count, width), dtype)
    vmem = lambda *shape, dtype=BF16: pltpu.VMEM(shape, dtype)
    dma = pltpu.SemaphoreType.DMA
    hops = 3 + deep - 1
    grad_inputs, result, grad_query, grad_key, grad_value, grad_output, grad_router, small = pl.pallas_call(
        moving_backward_kernel,
        out_shape=(
            sds((count, width), F32), sds((count, width), BF16), *[sds((rows // 2, width), F32)] * 4,
            sds((rows // 2, experts), F32), sds((16, width), F32),
        ),
        in_specs=[any_spec] * 12 + in_vmem(7),
        out_specs=tuple(in_vmem(8)),
        scratch_shapes=[
            tall(BF16), pltpu.VMEM(weights.shape, BF16), tall(BF16), tall(BF16), tall(BF16), tall(BF16), tall(BF16),
            vmem(count, BLOCK, dtype=F32), tall(F32), tall(BF16), vmem(wide * local * slots, width),
            dma((11,)), vmem(HEADS, 4 * BLOCK, dtype=F32),
            wide_t(BF16), wide_t(BF16), wide_t(BF16), wide_t(BF16), tall(BF16), wide_t(BF16),
            vmem(HEADS, count, dtype=F32), vmem(BLOCK, count, dtype=F32),
            tall(BF16), tall(BF16), tall(BF16), tall(F32), tall(F32), vmem(count, count),
            vmem(HEADS, 4 * BLOCK, dtype=F32), vmem(HEADS, 2 * BLOCK, dtype=F32),
            vmem(local, 2, wide, slots, width), vmem(local, 2, wide, slots, width), vmem(local, wide, slots, width),
            vmem(wide, local, slots, width),
            dma((local, 2)), *Collect.semaphores(local, wide),
            *sum_buffers(units, wide, rows, pair_cols), *sum_buffers(1, wide, rows, out_cols),
            vmem(units, 2, rows // 2, pair_cols, dtype=F32), vmem(1, 2, rows // 2, out_cols, dtype=F32),
            vmem(4, 16, width, dtype=F32), vmem(hops, 16, width, dtype=F32), dma((hops,)), dma((hops,)),
        ],
        compiler_params=pltpu.CompilerParams(collective_id=3, has_side_effects=True, vmem_limit_bytes=62 << 20),
        name="backward",
    )(
        inputs, weights, normed, q, k, v, att, lse, outs, mixed, cotangent, grows,
        gains, router, rel_bias, slot_route, normed_f, gates, picks,
    )
    device = lax.axis_index("wide") * narrow + lax.axis_index("narrow")
    gain_grads = lax.dynamic_slice(small, (HEADS, device * (rows // 2)), (2, rows // 2))
    grad_rel = small[:HEADS, :bucket_count].T
    return result, grad_inputs, (grad_query, grad_key, grad_value), grad_output, grad_router, gain_grads[1], gain_grads[0], grad_rel


def in_vmem(count):
    return [pl.BlockSpec(memory_space=pltpu.VMEM)] * count


def shards(
    inputs, gain_attn, w_query, w_key, w_value, w_output, rel_bias, gain_ffn, w_router,
    expert_in, expert_out, routes, capacity, cotangent,
):
    count, width = inputs.shape
    experts = w_router.shape[1]
    local, _, hidden_width = expert_in.shape
    wide, narrow = lax.axis_size("wide"), lax.axis_size("narrow")
    slots = 2 * count // experts
    total = experts * slots
    bucket_count = rel_bias.shape[0]
    params = pltpu.CompilerParams(vmem_limit_bytes=60 << 20)
    smem = pl.BlockSpec(memory_space=pltpu.SMEM)

    moving = narrow == 4 and wide & (wide - 1) == 0 and local == HEADS // 4 + 1 and slots % 32 == 0 and local * slots % BLOCK == 0
    moving = moving and width % (wide * 2 * 16) == 0 and count == SEQ_LEN and experts + 8 <= BLOCK
    if moving:
        normed, q, k, v, att, lse, mixed, normed_f, sent, weights, cot_all, slot_route, router, gains = moving_forward(
            rel_bias, capacity, inputs, w_query, w_key, w_value, w_output, w_router, gain_attn, gain_ffn, routes,
            cotangent, wide, narrow, local, slots,
        )
        outs, back, gates, gin, gout = moving_experts(sent, cot_all, expert_in, expert_out, router, wide, narrow)
        result, grad_inputs, kinds, grad_output, grad_router, grad_gain_a, grad_gain_f, grad_rel = moving_backward(
            rel_bias, inputs, weights.reshape(HEADS // 4 + 1, 2, width, width // 2), gains, router, slot_route,
            normed, q, k, v, att, lse, mixed, normed_f, cotangent, outs,
            back.reshape(total, width), gates.reshape(1, total), wide, slots,
        )
        return (
            result, grad_inputs, grad_gain_a, *kinds, grad_output, grad_rel, grad_gain_f, grad_router, gin, gout,
        )

    near = jnp.dot(near_picks(bucket_count, 1), rel_bias, precision=HIGHEST).T
    near_back = jnp.dot(near_picks(bucket_count, -1), rel_bias, precision=HIGHEST).T

    packed = jnp.concatenate([w_query, w_key, w_value, w_output], axis=1)
    weights = lax.all_gather(packed, BOTH, axis=0, tiled=True)
    small = lax.all_gather(
        jnp.concatenate([w_router, gain_attn[:, None], gain_ffn[:, None]], axis=1), BOTH, axis=0, tiled=True
    )
    router = small[:, :experts]
    gain_a = small[:, experts].astype(F32)[None, :]
    gain_f = small[:, experts + 1].astype(F32)[None, :]
    slot_col, slot_row, cot_sent = pl.pallas_call(
        lambda *refs: place_kernel(slots, experts, *refs),
        out_shape=(
            jax.ShapeDtypeStruct((count, 1), jnp.int32),
            jax.ShapeDtypeStruct((1, count), jnp.int32),
            jax.ShapeDtypeStruct((total, width), BF16),
        ),
        in_specs=[smem] + in_vmem(3),
        out_specs=tuple(in_vmem(3)),
        compiler_params=params,
        name="places",
    )(capacity, routes, routes.reshape(1, count), cotangent)

    def spread(rows):
        taken = lax.all_to_all(
            rows.reshape(wide, local * slots, width), "wide", split_axis=0, concat_axis=0, tiled=True
        )
        held = lax.all_gather(taken, "narrow", axis=0, tiled=True)
        return held.reshape(wide * narrow, local, slots, width)

    def collect(rows):
        own = lax.psum_scatter(
            rows.reshape(wide * narrow, local * slots, width), "narrow", scatter_dimension=0, tiled=True
        )
        back = lax.all_to_all(own, "wide", split_axis=0, concat_axis=0, tiled=True)
        return back.reshape(total, width)

    cot_all = spread(cot_sent)

    rows_t = lambda dtype, cols=width: jax.ShapeDtypeStruct((count, cols), dtype)
    normed, q, k, v, att, lse, mixed, normed_f, sent = pl.pallas_call(
        forward_kernel,
        out_shape=(
            rows_t(BF16), rows_t(BF16), rows_t(BF16), rows_t(BF16), rows_t(BF16), rows_t(F32, BLOCK),
            rows_t(F32), rows_t(BF16), jax.ShapeDtypeStruct((total, width), BF16),
        ),
        in_specs=in_vmem(7),
        out_specs=tuple(in_vmem(9)),
        compiler_params=params,
        name="forward",
    )(inputs, weights, gain_a, gain_f, router, near, slot_row)

    rows_all = spread(sent)
    sources = wide * narrow
    block = pl.BlockSpec((sources, 1, slots, width), lambda e: (0, e, 0, 0))
    w_in_spec = pl.BlockSpec((1, width, hidden_width), lambda e: (e, 0, 0))
    w_out_spec = pl.BlockSpec((1, hidden_width, width), lambda e: (e, 0, 0))
    first_expert = (lax.axis_index("wide") * local).astype(jnp.int32)[None]
    back, grows, gin, gout = pl.pallas_call(
        expert_kernel,
        grid=(local,),
        out_shape=(
            jax.ShapeDtypeStruct(rows_all.shape, BF16),
            jax.ShapeDtypeStruct(rows_all.shape, BF16),
            jax.ShapeDtypeStruct(expert_in.shape, F32),
            jax.ShapeDtypeStruct(expert_out.shape, F32),
        ),
        in_specs=[
            smem, block, block, w_in_spec, w_out_spec, pl.BlockSpec((width, experts), lambda e: (0, 0)),
        ],
        out_specs=(block, block, w_in_spec, w_out_spec),
        scratch_shapes=[
            pltpu.VMEM((sources * slots, hidden_width), BF16),
            pltpu.VMEM((sources * slots, hidden_width), BF16),
            pltpu.VMEM((sources * slots, width), BF16),
        ],
        compiler_params=params,
        name="experts",
    )(first_expert, rows_all, cot_all, expert_in, expert_out, router)
    outs_back = collect(back)
    grows_back = collect(grows)
    gates = jnp.sum(outs_back.astype(F32) * cot_sent.astype(F32), axis=1)[None, :]

    wide_t = lambda dtype: pltpu.VMEM((width, count), dtype)
    tall = lambda dtype: pltpu.VMEM((count, width), dtype)
    result, grad_inputs, gw, grouter, gnear, gfar, ggain = pl.pallas_call(
        backward_kernel,
        out_shape=(
            rows_t(BF16), rows_t(F32), jax.ShapeDtypeStruct((width, 4 * width), BF16),
            jax.ShapeDtypeStruct((width, experts), F32), jax.ShapeDtypeStruct((HEADS, 4 * BLOCK), F32),
            jax.ShapeDtypeStruct((HEADS, 2 * BLOCK), F32), jax.ShapeDtypeStruct((2, width), F32),
        ),
        in_specs=in_vmem(20),
        out_specs=tuple(in_vmem(7)),
        scratch_shapes=[
            wide_t(BF16), wide_t(BF16), wide_t(BF16), wide_t(BF16), tall(BF16), wide_t(BF16),
            pltpu.VMEM((HEADS, count), F32), pltpu.VMEM((BLOCK, count), F32),
            tall(BF16), tall(BF16), tall(BF16), tall(F32), pltpu.VMEM((count, count), BF16),
        ],
        compiler_params=params,
        name="backward",
    )(
        inputs, weights, gain_a, gain_f, router, near_back, slot_col, routes,
        normed, q, k, v, att, lse, mixed, normed_f, cotangent, outs_back, grows_back, gates,
    )

    gw = lax.psum_scatter(gw, BOTH, scatter_dimension=0, tiled=True).astype(F32)
    grad_query, grad_key, grad_value, grad_output = (gw[:, i * width : (i + 1) * width] for i in range(4))
    gsmall = lax.psum_scatter(
        jnp.concatenate([grouter, ggain.T], axis=1), BOTH, scatter_dimension=0, tiled=True
    )
    grad_rel = jnp.dot(near_picks(bucket_count, -1).T, gnear.T, precision=HIGHEST)
    low, high = jnp.sum(gfar[:, :BLOCK], axis=1), jnp.sum(gfar[:, BLOCK:], axis=1)
    grad_rel = grad_rel.at[bucket_count // 2 - 1].add(low).at[bucket_count - 1].add(high)
    grad_rel = lax.psum(grad_rel, BOTH)
    return (
        result, grad_inputs, gsmall[:, experts], grad_query, grad_key, grad_value, grad_output,
        grad_rel, gsmall[:, experts + 1], gsmall[:, :experts], gin, gout,
    )


def solution(mesh):
    return jax.shard_map(
        shards,
        mesh=mesh,
        in_specs=(
            P(BOTH, None),
            P(BOTH),
            P(BOTH, None),
            P(BOTH, None),
            P(BOTH, None),
            P(BOTH, None),
            P(),
            P(BOTH),
            P(BOTH, None),
            P("wide", None, "narrow"),
            P("wide", "narrow", None),
            P(BOTH, None),
            P(BOTH),
            P(BOTH, None),
        ),
        out_specs=(
            P(BOTH, None),
            P(BOTH, None),
            P(BOTH),
            P(BOTH, None),
            P(BOTH, None),
            P(BOTH, None),
            P(BOTH, None),
            P(),
            P(BOTH),
            P(BOTH, None),
            P("wide", None, "narrow"),
            P("wide", "narrow", None),
        ),
        check_vma=False,
    )
```

```python
import jax
import jax.numpy as jnp
import numpy as np
from jax import lax
from jax.experimental import pallas as pl
from jax.experimental.pallas import tpu as pltpu
from jax.sharding import PartitionSpec as P

HEADS = 12
SEQ_LEN = 512
BLOCK = 128
EPSILON = 1e-06
HIGHEST = lax.Precision.HIGHEST
ROOT_TWO_PI = 0.7978845608028654
CUBIC = 0.044715
BOTH = ("wide", "narrow")
F32 = jnp.float32
BF16 = jnp.bfloat16


def bucket_of(offsets, bucket_count):
    half_count = bucket_count // 2
    exact_count = half_count // 2
    distance = np.abs(offsets)
    scaled = exact_count + np.floor(
        np.log(np.maximum(distance, 1) / exact_count)
        / np.log(128.0 / exact_count)
        * (half_count - exact_count)
    ).astype(np.int64)
    scaled = np.minimum(scaled, half_count - 1)
    return ((offsets > 0) * half_count + np.where(distance < exact_count, distance, scaled)).astype(
        np.int32
    )


def near_picks(bucket_count, sign):
    offsets = sign * (np.arange(4 * BLOCK) - (2 * BLOCK - 1))
    picks = (bucket_of(offsets, bucket_count)[:, None] == np.arange(bucket_count)[None, :]).astype(
        np.float32
    )
    picks[-1] = 0.0
    return picks


def dot_nn(left, right):
    return lax.dot_general(left, right, (((1,), (0,)), ((), ())), preferred_element_type=F32)


def dot_nt(left, right):
    return lax.dot_general(left, right, (((1,), (1,)), ((), ())), preferred_element_type=F32)


def dot_tn(left, right):
    return lax.dot_general(left, right, (((0,), (0,)), ((), ())), preferred_element_type=F32)


def inverse_rms(values):
    return lax.rsqrt(jnp.mean(values * values, axis=-1, keepdims=True) + EPSILON)


def norm_backward(values, inverse, gain, grad_normed):
    scaled = grad_normed * gain
    grad_gain = jnp.sum(grad_normed * values * inverse, axis=0, keepdims=True)
    inner = jnp.mean(scaled * values, axis=-1, keepdims=True)
    return (inverse * (scaled - values * inverse * inverse * inner), grad_gain)


def softmax_lanes(logits):
    peak = jnp.max(logits, axis=-1, keepdims=True)
    exponent = jnp.exp(logits - peak)
    return exponent / jnp.sum(exponent, axis=-1, keepdims=True)


def toeplitz_near(near_row):
    spread = jnp.broadcast_to(near_row, (BLOCK, 4 * BLOCK))
    return pltpu.roll(spread, 3 * BLOCK + 1, 1, stride=1, stride_axis=0)[:, : 3 * BLOCK]


def bias_rows(near, near_row, row, blocks):
    far_low, far_high = near_row[:, :1], near_row[:, 4 * BLOCK - 2 : 4 * BLOCK - 1]
    pieces = []
    for column in range(blocks):
        distance = column - row
        if distance <= -2:
            pieces.append(jnp.broadcast_to(far_low, (BLOCK, BLOCK)))
        elif distance >= 2:
            pieces.append(jnp.broadcast_to(far_high, (BLOCK, BLOCK)))
        else:
            pieces.append(near[:, (distance + 1) * BLOCK : (distance + 2) * BLOCK])
    return jnp.concatenate(pieces, axis=1)


def near_biases(rel_ref, picks_ref):
    return lax.dot_general(
        rel_ref[...], picks_ref[...], (((1,), (0,)), ((), ())), precision=HIGHEST, preferred_element_type=F32
    )


def diagonal_sums(near_sum):
    padded = jnp.concatenate([near_sum, jnp.zeros((BLOCK, BLOCK), F32)], axis=1)
    groups = jnp.zeros((8, 4 * BLOCK), F32)
    for at in range(0, BLOCK, 8):
        groups = groups + pltpu.roll(padded[at : at + 8, :], BLOCK - 8 - at, 1)
    sums = groups[7:8, :]
    for at in range(7):
        sums = sums + pltpu.roll(groups[at : at + 1, :], 7 - at, 1)
    return sums


def slot_places(col, row, limit, experts, slots, count):
    lower = lax.broadcasted_iota(jnp.int32, (count, count), 0)
    upper = lax.broadcasted_iota(jnp.int32, (count, count), 1)
    chosen = lax.broadcasted_iota(jnp.int32, (count, experts), 1) == col
    running = dot_nn((upper <= lower).astype(BF16), chosen.astype(BF16))
    place = jnp.sum(jnp.where(chosen, running, 0.0), axis=1, keepdims=True).astype(jnp.int32) - 1
    slot_col = jnp.where(place < limit, col * slots + place, -1)
    chosen_t = lax.broadcasted_iota(jnp.int32, (experts, count), 0) == row
    running_t = dot_nn(chosen_t.astype(BF16), (lower <= upper).astype(BF16))
    place_t = (
        jnp.sum(jnp.where(chosen_t, running_t, 0.0), axis=0, keepdims=True).astype(jnp.int32) - 1
    )
    slot_row = jnp.where(place_t < limit, row * slots + place_t, -1)
    return slot_col, slot_row


def place_kernel(slots, experts, capacity_ref, routes_ref, row_ref, cot_ref, slot_col, slot_row, cot_out):
    count = routes_ref.shape[0]
    limit = capacity_ref[0] * count // experts
    col, row = slot_places(routes_ref[...], row_ref[...], limit, experts, slots, count)
    slot_col[...] = col
    slot_row[...] = row
    picks = (lax.broadcasted_iota(jnp.int32, (experts * slots, count), 0) == row).astype(BF16)
    cot_out[...] = dot_nn(picks, cot_ref[...]).astype(BF16)


def pair_forward(at, near_ref, q_ref, k_ref, v_ref, att_ref, lse_ref):
    count, width = q_ref.shape
    head_dim = width // HEADS
    blocks = count // BLOCK
    lanes = lax.broadcasted_iota(jnp.int32, (1, BLOCK), 1)
    first = lanes < head_dim
    cols = pl.ds(pl.multiple_of(at * BLOCK, BLOCK), BLOCK)
    k_pair, v_pair = k_ref[:, cols], v_ref[:, cols]
    near_rows = [near_ref[pl.ds(2 * at + half, 1), :] for half in range(2)]
    nears = [toeplitz_near(near_row) for near_row in near_rows]
    for row in range(blocks):
        rows = slice(row * BLOCK, (row + 1) * BLOCK)
        q_rows = q_ref[rows, cols] * jnp.asarray(head_dim**-0.5, BF16)
        found = []
        log_sums = lse_ref[rows, :]
        for half in range(2):
            head = 2 * at + half
            mask = first if half == 0 else jnp.logical_not(first)
            scores = dot_nt(jnp.where(mask, q_rows, jnp.zeros_like(q_rows)), k_pair)
            scores = scores + bias_rows(nears[half], near_rows[half], row, blocks)
            peak = jnp.max(scores, axis=-1, keepdims=True)
            exponent = jnp.exp(scores - peak)
            total = jnp.sum(exponent, axis=-1, keepdims=True)
            found.append(dot_nn((exponent * (1.0 / total)).astype(BF16), v_pair))
            log_sums = jnp.where(lanes == head, peak + jnp.log(total), log_sums)
        lse_ref[rows, :] = log_sums
        att_ref[rows, cols] = jnp.where(first, found[0], found[1]).astype(BF16)


def slot_rows(slot_row, values, total):
    picks = lax.broadcasted_iota(jnp.int32, (total, slot_row.shape[1]), 0) == slot_row
    return dot_nn(picks.astype(BF16), values).astype(BF16)


def forward_kernel(
    x_ref, w_ref, gain_a, gain_f, router_ref, near_ref, slot_row,
    normed_ref, q_ref, k_ref, v_ref, att_ref, lse_ref, mixed_ref, normed_f, sent_ref,
):
    width = x_ref.shape[1]
    tokens = x_ref[...].astype(F32)
    normed = (tokens * inverse_rms(tokens) * gain_a[...]).astype(BF16)
    normed_ref[...] = normed
    for out, at in ((q_ref, 0), (k_ref, 1), (v_ref, 2)):
        out[...] = dot_nn(normed, w_ref[:, at * width : (at + 1) * width]).astype(BF16)
    lse_ref[...] = jnp.zeros_like(lse_ref)

    def pair(at, carry):
        pair_forward(at, near_ref, q_ref, k_ref, v_ref, att_ref, lse_ref)
        return carry

    lax.fori_loop(0, HEADS // 2, pair, 0)
    mixed = tokens + dot_nn(att_ref[...], w_ref[:, 3 * width : 4 * width])
    mixed_ref[...] = mixed
    normed_2 = (mixed * inverse_rms(mixed) * gain_f[...]).astype(BF16)
    normed_f[...] = normed_2
    sent_ref[...] = slot_rows(slot_row[...], normed_2, sent_ref.shape[0])


def expert_kernel(
    first_ref, rows_ref, cot_ref, in_ref, out_ref, router_ref,
    back_ref, grows_ref, gin_ref, gout_ref, hidden_ref, gpre_ref, sg_ref,
):
    sources, _, slots, width = rows_ref.shape
    total = sources * slots
    step = min(256, total)
    expert = first_ref[0] + pl.program_id(0)

    def chunk(at, carry):
        these = pl.ds(pl.multiple_of(at * (step // slots), step // slots), step // slots)
        flat = pl.ds(pl.multiple_of(at * step, step), step)
        rows = rows_ref[these, 0].reshape(step, width)
        probs = softmax_lanes(dot_nn(rows, router_ref[...]))
        here = lax.broadcasted_iota(jnp.int32, probs.shape, 1) == expert
        gate = jnp.sum(jnp.where(here, probs, 0.0), axis=-1, keepdims=True)
        sg = (cot_ref[these, 0].reshape(step, width).astype(F32) * gate).astype(BF16)
        sg_ref[flat, :] = sg
        pre = dot_nn(rows, in_ref[0])
        square = pre * pre
        inner = jnp.tanh(pre * (ROOT_TWO_PI + ROOT_TWO_PI * CUBIC * square))
        half = 0.5 * (1.0 + inner)
        hidden = (pre * half).astype(BF16)
        hidden_ref[flat, :] = hidden
        slope = half + 0.5 * pre * (1.0 - inner * inner) * (
            ROOT_TWO_PI + 3.0 * ROOT_TWO_PI * CUBIC * square
        )
        gpre = (dot_nt(sg, out_ref[0]) * slope).astype(BF16)
        gpre_ref[flat, :] = gpre
        back_ref[these, 0] = dot_nn(hidden, out_ref[0]).astype(BF16).reshape(-1, slots, width)
        grows_ref[these, 0] = dot_nt(gpre, in_ref[0]).astype(BF16).reshape(-1, slots, width)
        return carry

    lax.fori_loop(0, total // step, chunk, 0)
    gout_ref[0] = dot_tn(hidden_ref[...], sg_ref[...])
    gin_ref[0] = dot_tn(rows_ref[:, 0].reshape(total, width), gpre_ref[...])


def remote(source, target, send, receive, device):
    return pltpu.make_async_remote_copy(
        src_ref=source,
        dst_ref=target,
        send_sem=send,
        recv_sem=receive,
        device_id=device,
        device_id_type=pl.DeviceIdType.MESH,
    )


def greet(devices):
    for device in devices:
        pl.semaphore_signal(
            pltpu.get_barrier_semaphore(), inc=1, device_id=device, device_id_type=pl.DeviceIdType.MESH
        )


def meet(devices):
    pl.semaphore_wait(pltpu.get_barrier_semaphore(), len(devices))


FORWARD_STEPS = {
    "first": (("send", 4, 0), ("start", 2, 0), ("start", 3, 0), ("send", 0, 0), ("start", 1, 0), ("spread", 4, 0),
        ("send", 1, 0), ("start", 0, 0), ("spread", 0, 0), ("send", 2, 0), ("start", 0, 2), ("forward", 1, 0),
        ("send", 3, 0), ("start", 1, 1), ("over_x", 4, 0), ("over_y", 4, 0), ("forward", 0, 0), ("spread", 1, 0),
        ("end", 4, 0), ("over_x", 0, 0), ("spread", 2, 0), ("start", 3, 2), ("over_y", 1, 0), ("forward", 3, 0),
        ("start", 3, 1), ("over_x", 1, 0), ("over_x", 2, 0), ("end", 0, 0), ("over_y", 0, 0), ("forward", 1, 1),
        ("start", 2, 2),),
    "N0": (("spread", 3, 0),),
    "A0": (("forward", 2, 0), ("pass", 1, 1), ("forward", 3, 1), ("pass", 3, 0), ("over_y", 2, 0),
        ("start", 1, 2), ("forward", 0, 2), ("forward", 3, 2), ("end", 1, 0),),
    "B0": (("start", 2, 1),),
    "A1": (("forward", 2, 2), ("end", 2, 0), ("start", 0, 1), ("over_x", 3, 0),),
    "A2": (("forward", 2, 1), ("forward", 1, 2), ("pass", 1, 0), ("pass", 2, 0), ("pass", 0, 0), ("pass", 3, 2),
        ("pass", 2, 2), ("pass", 0, 2), ("forward", 0, 1), ("end", 3, 0), ("over_y", 3, 0), ("pass", 3, 1),),
    "M0": (("pass", 1, 2), ("pass", 2, 1), ("pass", 0, 1),),
}

BACKWARD_STEPS = {
    "first": (("core", 0, 1), ("core", 3, 0), ("core", 2, 1),),
    "O0": (("go", 2, 1), ("core", 1, 0), ("core", 2, 0), ("core", 0, 0), ("go", 0, 1),),
    "Q0": (("go", 2, 2), ("core", 3, 1),),
    "S0": (("core", 1, 1), ("near", 1, 0), ("near", 2, 0), ("go", 0, 2), ("near", 0, 0), ("finish", 2, 1),
        ("near", 3, 0), ("go", 3, 1),),
    "A0": (("go", 1, 1), ("finish", 0, 1), ("go", 3, 2), ("go", 0, 0), ("finish", 2, 2),),
    "A1": (("go", 3, 0), ("finish", 1, 1),),
    "B1": (("y", 3, 0), ("finish", 3, 1),),
    "A2": (("finish", 3, 2),),
    "P0": (("x", 3, 0), ("y", 0, 0), ("y", 1, 0), ("finish", 0, 2), ("go", 1, 0), ("finish", 0, 0),
        ("small", 0, 0), ("go", 1, 2), ("x", 0, 0), ("finish", 3, 0), ("x", 1, 0), ("y", 2, 0), ("z", 3, 0),
        ("small", 1, 0), ("go", 2, 0), ("finish", 1, 2), ("x", 2, 0), ("small", 2, 0), ("finish", 1, 0),
        ("finish", 2, 0), ("small", 3, 0), ("z", 0, 0), ("z", 1, 0), ("z", 2, 0),),
}

EXPERT_STEPS = {
    "first": (("start", 0, 0), ("start", 0, 1), ("start", 0, 2), ("forward", 0, 0), ("start", 1, 2),
        ("forward", 0, 1), ("start", 1, 0), ("forward", 0, 2), ("start", 1, 1), ("forward", 1, 0),
        ("start", 2, 0), ("pass", 0, 1), ("forward", 1, 2), ("start", 2, 1), ("pass", 0, 0), ("pass", 0, 2),),
    "A0": (("forward", 1, 1), ("start", 2, 2),),
    "B0": (("forward", 2, 0),),
    "C0": (("go", 0, 1), ("pass", 1, 0), ("forward", 2, 1), ("pass", 1, 2), ("start", 3, 0), ("pass", 1, 1),),
    "D0": (("start", 3, 2),),
    "A1": (("forward", 2, 2),),
    "B1": (("start", 3, 1), ("forward", 3, 0),),
    "W0": (("go", 1, 1), ("pass", 2, 0), ("pass", 2, 1), ("forward", 3, 2),),
    "D1": (("forward", 3, 1), ("go", 0, 2), ("go", 1, 2), ("pass", 2, 2), ("sum", 0, 0),),
    "V0": (("finish", 0, 1), ("sum", 1, 0),),
    "A2": (("finish", 1, 1),),
    "B2": (("go", 2, 1),),
    "W1": (("go", 0, 0), ("finish", 0, 2), ("pass", 3, 0), ("pass", 3, 2), ("go", 1, 0),),
    "C2": (("pass", 3, 1), ("go", 2, 2),),
    "D2": (("go", 2, 0),),
    "V1": (("sum", 2, 0), ("finish", 2, 1),),
    "B3": (("go", 3, 1), ("finish", 1, 2),),
    "W2": (("finish", 1, 0), ("finish", 2, 2),),
    "C3": (("finish", 0, 0), ("go", 3, 2),),
    "D3": (("sum", 3, 0), ("finish", 3, 1), ("go", 3, 0),),
    "V2": (("finish", 3, 2), ("finish", 2, 0),),
    "W3": (("finish", 3, 0),),
}


class Place:
    def __init__(self, wide):
        self.wide = wide
        self.run = wide // 2
        self.deep = wide // 2
        self.w, self.n = lax.axis_index("wide"), lax.axis_index("narrow")
        self.x, self.c = self.n // 2, lax.rem(self.n, 2)
        self.z, self.y = self.w // 2, lax.rem(self.w, 2)
        self.core = (self.w, self.x * 2 + 1 - self.c)
        self.side = (self.w, (1 - self.x) * 2 + self.c)
        self.row = (self.z * 2 + 1 - self.y, self.n)

    def flip(self, j):
        found, bit = self.w, 1
        while bit <= j:
            if j & bit:
                found = found + bit - 2 * bit * lax.rem(self.w // bit, 2)
            bit *= 2
        return found

    def peer(self, j):
        return (self.flip(j), self.n)

    def span(self, piece):
        half = self.w // self.run
        return pl.ds((1 - half if piece else half) * self.run, self.run)

    def steps(self, piece):
        return range(self.run, self.wide) if piece else range(1, self.run)

    def partners(self):
        return [self.peer(j) for j in range(1, self.wide)] + [self.core, self.side]


def slot_part(piece, slots):
    return pl.ds((piece - 1) * (slots // 2), slots // 2) if piece else pl.ds(0, slots)


PIECES = range(3)


class Spread:
    def __init__(self, place, sent, held, wide_s, wide_r, side_s, side_r, core_s, core_r):
        self.place, self.sent, self.held = place, sent, held
        self.wide_s, self.wide_r, self.side_s, self.side_r = wide_s, wide_r, side_s, side_r
        self.core_s, self.core_r = core_s, core_r
        self.slots = sent.shape[2]

    def hop(self, e, j, piece):
        p, part = self.place, slot_part(piece, self.slots)
        at = p.wide + j if piece == 2 else j
        return remote(
            self.sent.at[p.flip(j), e, part], self.held.at[e, p.n, p.w, part],
            self.wide_s.at[e, at], self.wide_r.at[e, at], p.peer(j),
        )

    def start(self, e, piece):
        for j in self.place.steps(piece):
            self.hop(e, j, piece).start()

    def beside(self, e, piece):
        p = self.place
        rows = self.held.at[e, p.n, p.span(piece), slot_part(piece, self.slots)]
        return remote(rows, rows, self.side_s.at[e, piece], self.side_r.at[e, piece], p.side)

    def over(self, e, other, piece):
        p = self.place
        m = (1 - p.x) * 2 + p.c if other else p.n
        rows = self.held.at[e, m, p.span(piece), slot_part(piece, self.slots)]
        at = 3 * other + piece
        return remote(rows, rows, self.core_s.at[e, at], self.core_r.at[e, at], p.core)

    def forward(self, e, piece):
        for j in self.place.steps(piece):
            self.hop(e, j, piece).wait_recv()
        self.beside(e, piece).start()
        self.over(e, 0, piece).start()

    def pass_on(self, e, piece):
        self.beside(e, piece).wait_recv()
        self.over(e, 1, piece).start()

    def arrive(self, e, other):
        for piece in PIECES:
            self.over(e, other, piece).wait_recv()

    def drain(self, e):
        for piece in PIECES:
            for j in self.place.steps(piece):
                self.hop(e, j, piece).wait_send()
            self.beside(e, piece).wait_send()
            self.over(e, 0, piece).wait_send()
            self.over(e, 1, piece).wait_send()

    @staticmethod
    def semaphores(local, wide):
        dma = pltpu.SemaphoreType.DMA
        return [dma((local, n)) for n in (2 * wide, 2 * wide, 3, 3, 6, 6)]


class Collect:
    def __init__(self, place, to_core, from_core, from_side, returned, semaphores):
        self.place, self.to_core, self.from_core = place, to_core, from_core
        self.from_side, self.returned = from_side, returned
        self.core_s, self.core_r, self.side_s, self.side_r, self.wide_s, self.wide_r = semaphores
        self.slots = from_side.shape[2]

    def core(self, e, other):
        return remote(
            self.to_core(e, other), self.from_core.at[e, other], self.core_s.at[e, other], self.core_r.at[e, other],
            self.place.core,
        )

    def beside(self, e, piece):
        rows, part = self.place.span(piece), slot_part(piece, self.slots)
        return remote(
            self.from_core.at[e, 1, rows, part], self.from_side.at[e, rows, part],
            self.side_s.at[e, piece], self.side_r.at[e, piece], self.place.side,
        )

    def back(self, e, j, piece):
        p, part = self.place, slot_part(piece, self.slots)
        at = p.wide + j if piece == 2 else j
        return remote(
            self.from_side.at[e, p.flip(j), part], self.returned.at[p.w, e, part],
            self.wide_s.at[e, at], self.wide_r.at[e, at], p.peer(j),
        )

    def go_beside(self, e, part):
        self.core(e, 1).wait_recv()
        held = self.from_core[e, 1].astype(F32)
        self.from_core[e, 1] = (part.astype(F32).reshape(held.shape) + held).astype(BF16)
        self.beside(e, 1).start()

    def finish(self, e, piece, own):
        p = self.place
        rows, part = p.span(piece), slot_part(piece, self.slots)
        self.beside(e, piece).wait_recv()
        total = own(rows, part) + self.from_side[e, rows, part].astype(F32)
        self.from_side[e, rows, part] = total.astype(BF16)
        for j in p.steps(piece):
            self.back(e, j, piece).start()
        if not piece:
            self.returned[p.w, e] = self.from_side[e, p.w]

    def drain(self, e):
        self.core(e, 0).wait_send()
        self.core(e, 1).wait_send()
        for piece in PIECES:
            self.beside(e, piece).wait_send()
            for j in self.place.steps(piece):
                self.back(e, j, piece).wait_send()

    def arrive(self, e):
        for piece in PIECES:
            for j in self.place.steps(piece):
                self.back(e, j, piece).wait_recv()

    @staticmethod
    def semaphores(local, wide):
        dma = pltpu.SemaphoreType.DMA
        return [dma((local, n)) for n in (2, 2, 3, 3, 2 * wide, 2 * wide)]


class Gather:
    def __init__(self, place, unit, held, halves, semaphores):
        self.p, self.u, self.held, self.halves = place, unit, held, halves
        self.s, self.r = semaphores

    def piece(self, *place):
        return self.held.at[self.u, self.p.c, *place] if self.halves else self.held.at[self.u, *place]

    def column(self, y, x):
        return self.piece(slice(None), y, x)

    def copy(self, piece, slot, device):
        return remote(piece, piece, self.s.at[self.u, slot], self.r.at[self.u, slot], device)

    def to_z(self, k):
        p = self.p
        z = lax.rem(p.z + k, p.deep)
        return self.copy(self.piece(p.z, p.y, p.x), k - 1, (z * 2 + p.y, p.n))

    def to_x(self):
        return self.copy(self.column(self.p.y, self.p.x), 3, self.p.side)

    def to_y(self):
        return self.copy(self.column(self.p.y, self.p.x), 4, self.p.row)

    def corner(self):
        return self.copy(self.column(self.p.y, 1 - self.p.x), 5, self.p.row)

    def to_core(self, at):
        p = self.p
        y, x = ((p.y, p.x), (p.y, 1 - p.x), (1 - p.y, p.x), (1 - p.y, 1 - p.x))[at]
        return self.copy(self.column(y, x), 6 + at, p.core)

    def hand(self, at):
        if self.halves:
            self.to_core(at).start()

    def start(self):
        for k in range(1, self.p.deep):
            self.to_z(k).start()

    def spread(self):
        for k in range(1, self.p.deep):
            self.to_z(k).wait_recv()
        self.to_x().start()
        self.to_y().start()
        self.hand(0)

    def over_x(self):
        self.to_x().wait_recv()
        self.corner().start()
        self.hand(1)

    def over_y(self):
        self.to_y().wait_recv()
        self.hand(2)

    def end(self):
        self.corner().wait_recv()
        self.hand(3)

    def arrive(self):
        if self.halves:
            for at in range(4):
                self.to_core(at).wait_recv()

    def drain(self):
        for k in range(1, self.p.deep):
            self.to_z(k).wait_send()
        for copy in (self.to_x(), self.to_y(), self.corner()):
            copy.wait_send()
        if self.halves:
            for at in range(4):
                self.to_core(at).wait_send()


def moving_forward_kernel(
    capacity_ref, x_ref, q_part, k_part, v_part, o_part, router_part, gain_a_part, gain_f_part, rel_ref, picks_ref, row_ref,
    cot_ref,
    normed_out, q_out, k_out, v_out, att_out, lse_out, mixed_out, normed_f_out, sent_out, weights_out, cot_out,
    slot_route, router_out, gains_out,
    normed_ref, q_ref, k_ref, v_ref, att_ref, lse_ref, mixed_ref, normed_f, sent_ref, store_s,
    near_ref, gain_lanes, small_lanes, small_part,
    held, small, pair_send, pair_got, small_got, cot_sent, weight_s, pair_s, pair_r,
    gs, gr, hs, hr, wide_s, wide_r, side_s, side_r, core_s, core_r,
):
    count, width = x_ref.shape
    wide, local, slots, _ = cot_sent.shape
    experts = router_out.shape[1]
    total = wide * local * slots
    units = HEADS // 4
    rows = pair_send.shape[2]
    p = Place(wide)
    greet(p.partners())

    def own_cols(u, half):
        if u == units:
            return o_part[:, half * (width // 2) : (half + 1) * (width // 2)]
        cols = slice((2 * u + half) * BLOCK, (2 * u + half + 1) * BLOCK)
        return jnp.concatenate([q_part[:, cols], k_part[:, cols], v_part[:, cols]], axis=1)

    def swap_copies():
        return [
            remote(pair_send.at[0], pair_got.at[0], pair_s.at[0], pair_r.at[0], p.core),
            remote(small_part, small_got, pair_s.at[1], pair_r.at[1], p.core),
        ]

    gain_lanes[...] = jnp.zeros_like(gain_lanes)
    gain_lanes[0:1, :rows] = gain_a_part[...].astype(F32)
    gain_lanes[1:2, :rows] = gain_f_part[...].astype(F32)
    gain_cols = gain_lanes[...].T[:rows, :]
    small_lanes[...] = jnp.zeros_like(small_lanes)
    small_lanes[:, :experts] = router_part[...].astype(F32)
    lanes = lax.broadcasted_iota(jnp.int32, small_lanes.shape, 1)
    others = jnp.where(lanes == experts + 1, gain_cols[:, 1:2], small_lanes[...])
    small_part[...] = jnp.where(lanes == experts, gain_cols[:, 0:1], others).astype(BF16)
    for u in range(units + 1):
        pair_send[0, u] = jnp.where(p.c == 0, own_cols(u, 1), own_cols(u, 0))
    limit = capacity_ref[0] * count // experts
    routes = jnp.broadcast_to(row_ref[...].astype(F32), (8, count)).T[:, :1].astype(jnp.int32)
    slot_col, slot_row = slot_places(routes, row_ref[...], limit, experts, slots, count)
    slot_route[:, 0:1] = slot_col
    slot_route[:, 1:2] = routes
    near_ref[...] = near_biases(rel_ref, picks_ref)
    cot_sent[...] = slot_rows(slot_row, cot_ref[...], total).reshape(cot_sent.shape)
    moves = Spread(p, cot_sent, cot_out, wide_s, wide_r, side_s, side_r, core_s, core_r)

    def own_rows(e):
        return pltpu.make_async_copy(cot_sent.at[p.w, e], cot_out.at[e, p.n, p.w], weight_s.at[1 + e])

    for e in range(local):
        own_rows(e).start()
    lse_ref[...] = jnp.zeros_like(lse_ref)
    for e in range(local):
        own_rows(e).wait()
    meet(p.partners())
    for copy in swap_copies():
        copy.start()
    for copy in swap_copies():
        copy.wait_recv()

    def joined(mine, other):
        mine, other = mine.astype(F32), other.astype(F32)
        return jnp.concatenate(
            [jnp.where(p.c == 0, mine, other), jnp.where(p.c == 0, other, mine)], axis=0
        ).astype(BF16)

    def gather(u):
        if isinstance(u, int) and u > units:
            return small_gather
        return Gather(p, u, held, True, (gs, gr))

    small_gather = Gather(p, 0, small, False, (hs, hr))
    small[0, p.z, p.y, p.x] = joined(small_part[...], small_got[...])
    for u in range(units + 1):
        mine = jnp.where(p.c == 0, own_cols(u, 0), own_cols(u, 1))
        held[u, p.c, p.z, p.y, p.x] = joined(mine, pair_got[0, u])

    acts = {
        "start": moves.start, "forward": moves.forward, "pass": moves.pass_on,
        "send": lambda u, piece: gather(u).start(), "spread": lambda u, piece: gather(u).spread(),
        "over_x": lambda u, piece: gather(u).over_x(), "over_y": lambda u, piece: gather(u).over_y(),
        "end": lambda u, piece: gather(u).end(),
    }

    def act(steps):
        for name, at, piece in steps:
            acts[name](at, piece)

    def after(u, part):
        for at in range(units):
            steps = FORWARD_STEPS.get(part + str(at), ())
            if steps:
                pl.when(u == at)(lambda steps=steps: act(steps))

    act(FORWARD_STEPS["first"])
    small_all = small[0].reshape(width, BLOCK)
    router_out[...] = small_all[:, :experts]
    gains_out[...] = small_all.astype(F32).T[experts : experts + 8, :]
    tokens = x_ref[...].astype(F32)
    normed_ref[...] = (tokens * inverse_rms(tokens) * gains_out[0:1, :]).astype(BF16)
    act(FORWARD_STEPS.get("N0", ()))

    def pair(at, weight):
        cols = pl.ds(pl.multiple_of(at * BLOCK, BLOCK), BLOCK)
        found = dot_nn(normed_ref[...], weight.reshape(width, 3 * BLOCK)).astype(BF16)
        q_ref[:, cols], k_ref[:, cols], v_ref[:, cols] = (found[:, i * BLOCK : (i + 1) * BLOCK] for i in range(3))
        pair_forward(at, near_ref, q_ref, k_ref, v_ref, att_ref, lse_ref)

    def pairs(u, carry):
        gather(u).arrive()
        pair(2 * u, held[u, 0])
        after(u, "A")
        pair(2 * u + 1, held[u, 1])
        after(u, "B")
        return carry

    lax.fori_loop(0, units, pairs, 0)
    stores = [
        pltpu.make_async_copy(source, target, store_s.at[at])
        for at, (source, target) in enumerate((
            (normed_ref, normed_out), (q_ref, q_out), (k_ref, k_out), (v_ref, v_out), (att_ref, att_out),
            (lse_ref, lse_out), (mixed_ref, mixed_out), (normed_f, normed_f_out), (sent_ref, sent_out),
        ))
    ]
    for copy in stores[:6]:
        copy.start()
    gather(units).arrive()
    weights_copy = pltpu.make_async_copy(held, weights_out, weight_s.at[0])
    weights_copy.start()
    mixed = tokens_again(x_ref) + jnp.concatenate(
        [dot_nn(att_ref[...], held[units, half].reshape(width, width // 2)) for half in range(2)], axis=1
    )
    mixed_ref[...] = mixed
    normed_2 = (mixed * inverse_rms(mixed) * gains_out[1:2, :]).astype(BF16)
    normed_f[...] = normed_2
    stores[6].start()
    stores[7].start()
    sent_ref[...] = slot_rows(slot_row, normed_2, total).reshape(sent_ref.shape)
    stores[8].start()
    act(FORWARD_STEPS.get("M0", ()))
    for copy in swap_copies():
        copy.wait_send()
    small_gather.drain()
    for u in range(units + 1):
        gather(u).drain()
    for e in range(local):
        moves.arrive(e, 0)
        moves.arrive(e, 1)
        moves.drain(e)
    weights_copy.wait()
    for copy in stores:
        copy.wait()


def tokens_again(x_ref):
    return x_ref[...].astype(F32)


def moving_forward(
    rel_bias, capacity, inputs, w_query, w_key, w_value, w_output, w_router, gain_attn, gain_ffn, routes, cotangent,
    wide, narrow, local, slots,
):
    count, width = inputs.shape
    experts = w_router.shape[1]
    shard = w_query.shape[0]
    deep, units = wide // 2, HEADS // 4
    half = width // 2
    sds = jax.ShapeDtypeStruct
    rows_t = lambda dtype, cols=width: sds((count, cols), dtype)
    smem, any_spec = pl.BlockSpec(memory_space=pltpu.SMEM), pl.BlockSpec(memory_space=pl.ANY)
    vmem = lambda *shape, dtype=BF16: pltpu.VMEM(shape, dtype)
    dma = pltpu.SemaphoreType.DMA
    picks = jnp.asarray(near_picks(rel_bias.shape[0], 1).T)
    return pl.pallas_call(
        moving_forward_kernel,
        out_shape=(
            rows_t(BF16), rows_t(BF16), rows_t(BF16), rows_t(BF16), rows_t(BF16), rows_t(F32, BLOCK), rows_t(F32),
            rows_t(BF16), sds((wide, local, slots, width), BF16),
            sds((units + 1, 2, deep, 2, 2, 2 * shard, half), BF16),
            sds((local, narrow, wide, slots, width), BF16), sds((count, 2), jnp.int32),
            sds((width, experts), BF16), sds((8, width), F32),
        ),
        in_specs=[smem] + in_vmem(12),
        out_specs=(any_spec,) * 11 + tuple(in_vmem(3)),
        scratch_shapes=[
            vmem(count, width), vmem(count, width), vmem(count, width), vmem(count, width), vmem(count, width),
            vmem(count, BLOCK, dtype=F32), vmem(count, width, dtype=F32), vmem(count, width),
            vmem(wide, local, slots, width), dma((9,)),
            vmem(HEADS, 4 * BLOCK, dtype=F32), vmem(8, BLOCK, dtype=F32), vmem(shard, BLOCK, dtype=F32), vmem(shard, BLOCK),
            vmem(units + 1, 2, deep, 2, 2, 2 * shard, half), vmem(1, deep, 2, 2, 2 * shard, BLOCK),
            vmem(1, units + 1, shard, half), vmem(1, units + 1, shard, half), vmem(shard, BLOCK),
            vmem(wide, local, slots, width), dma((1 + local,)), dma((2,)), dma((2,)),
            dma((units + 1, 10)), dma((units + 1, 10)), dma((1, 10)), dma((1, 10)),
            *Spread.semaphores(local, wide),
        ],
        compiler_params=pltpu.CompilerParams(collective_id=1, has_side_effects=True, vmem_limit_bytes=62 << 20),
        name="forward",
    )(
        capacity, inputs, w_query, w_key, w_value, w_output, w_router, gain_attn[None, :], gain_ffn[None, :], rel_bias.T, picks,
        routes.reshape(1, count), cotangent,
    )


def moving_expert_kernel(
    sent, cot_hbm, in_hbm, out_hbm, router_ref,
    outs_o, gin_o, gout_o, back_o, gate_o,
    held, cot, w_in, w_out, sg, hidden, gpre, outs, gin, gout, to_core, from_core, from_side, near_sum, far_sum,
    gate_sum, gate_core, gate_from_core, gate_side, gate_from_side, gate_ready,
    load_s, store_s, wide_s, wide_r, side_s, side_r, core_s, core_r,
    rc_s, rc_r, rx_s, rx_r, rw_s, rw_r, gc_s, gc_r, gx_s, gx_r, gw_s, gw_r,
):
    wide, local, slots, width = sent.shape
    narrow = held.shape[1]
    step = wide * slots
    hidden_width = in_hbm.shape[2]
    p = Place(wide)
    moves = Spread(p, sent, held, wide_s, wide_r, side_s, side_r, core_s, core_r)
    greet(p.partners())

    def loads(e):
        return [
            pltpu.make_async_copy(in_hbm.at[e], w_in.at[e], load_s.at[e, 0]),
            pltpu.make_async_copy(out_hbm.at[e], w_out.at[e], load_s.at[e, 1]),
            pltpu.make_async_copy(cot_hbm.at[e], cot.at[e], load_s.at[e, 2]),
        ]

    def store(e, at):
        source = (outs.at[lax.rem(e, 2)], gin, gout)[at]
        return pltpu.make_async_copy(source, (outs_o, gin_o, gout_o)[at].at[e], store_s.at[e, at])

    def grads_out(e):
        b = lax.rem(e, 2)

        @pl.when(e > 0)
        def _():
            store(e - 1, 2).wait()

        rows = narrow * step
        found = dot_tn(hidden[b].reshape(rows, hidden_width), sg[b].reshape(rows, width))
        gout[...] = found.astype(BF16)
        store(e, 2).start()

    def grads_in(e):
        b = lax.rem(e, 2)

        @pl.when(e > 0)
        def _():
            store(e - 1, 1).wait()

        rows = narrow * step
        found = dot_tn(held[e].reshape(rows, width), gpre[b].reshape(rows, hidden_width))
        gin[...] = found.astype(BF16)
        store(e, 1).start()

    for e in range(local):
        for copy in loads(e):
            copy.start()
        held[e, p.n, p.w] = sent[p.w, e]
    gate_sum[...] = jnp.zeros_like(gate_sum)
    meet(p.partners())

    def chunk(e, m):
        b = lax.rem(e, 2)
        rows = held[e, m].reshape(step, width)
        probs = softmax_lanes(dot_nn(rows, router_ref[...]))
        here = lax.broadcasted_iota(jnp.int32, probs.shape, 1) == p.w * local + e
        gate = jnp.sum(jnp.where(here, probs, 0.0), axis=-1, keepdims=True)
        cot_rows = cot[e, m].reshape(step, width).astype(F32)
        sg_rows = (cot_rows * gate).astype(BF16)
        sg[b, m] = sg_rows
        pre = dot_nn(rows, w_in[e])
        square = pre * pre
        inner = jnp.tanh(pre * (ROOT_TWO_PI + ROOT_TWO_PI * CUBIC * square))
        half = 0.5 * (1.0 + inner)
        hidden_rows = (pre * half).astype(BF16)
        hidden[b, m] = hidden_rows
        slope = half + 0.5 * pre * (1.0 - inner * inner) * (
            ROOT_TWO_PI + 3.0 * ROOT_TWO_PI * CUBIC * square
        )
        gpre_rows = (dot_nt(sg_rows, w_out[e]) * slope).astype(BF16)
        gpre[b, m] = gpre_rows
        out_rows = dot_nn(hidden_rows, w_out[e])
        outs[b, m] = out_rows.astype(BF16).reshape(wide, slots, width)
        gate_rows = jnp.sum(out_rows * cot_rows, axis=-1, keepdims=True)
        row = lax.broadcasted_iota(jnp.int32, (step, local * slots), 0)
        lane = lax.broadcasted_iota(jnp.int32, (step, local * slots), 1)
        spread = jnp.where(lane == e * slots + lax.rem(row, slots), gate_rows, 0.0)
        gate_sum[m] += jnp.sum(spread.reshape(wide, slots, local * slots), axis=1)
        return dot_nt(gpre_rows, w_in[e])

    back = Collect(
        p, lambda e, other: to_core.at[e, other], from_core, from_side, back_o, (rc_s, rc_r, rx_s, rx_r, rw_s, rw_r)
    )

    def go(e, piece):
        if piece == 1:
            back.go_beside(e, far_sum[...])
        else:
            back.beside(e, piece).start()

    def add_core(e, piece):
        back.core(e, 0).wait_recv()
        near_sum[e] = near_sum[e] + from_core[e, 0].astype(F32)

    acts = {
        "start": moves.start, "forward": moves.forward, "pass": moves.pass_on, "go": go, "sum": add_core,
        "finish": lambda e, piece: back.finish(e, piece, lambda rows, part: near_sum[e, rows, part]),
    }

    def after(e, part):
        for at in range(local):
            steps = EXPERT_STEPS.get(part + str(at), ())
            if steps:

                def run(steps=steps):
                    for name, expert, piece in steps:
                        acts[name](expert, piece)

                if not isinstance(e, int):
                    pl.when(e == at)(run)
                elif e == at:
                    run()

    for name, expert, piece in EXPERT_STEPS["first"]:
        acts[name](expert, piece)

    far_x = (1 - p.x) * 2

    gates_core = remote(gate_core, gate_from_core, gc_s, gc_r, p.core)

    def gates_core_start():
        gate_core[0] = gate_sum[p.x * 2 + 1 - p.c]
        gate_core[1] = gate_sum[far_x + 1 - p.c]
        gates_core.start()

    def expert(e, carry):
        for copy in loads(e):
            copy.wait()

        @pl.when(e >= 2)
        def _():
            store(e - 2, 0).wait()

        moves.arrive(e, 1)
        to_core[e, 1] = chunk(e, far_x + 1 - p.c).astype(BF16).reshape(wide, slots, width)
        back.core(e, 1).start()
        after(e, "A")
        far_sum[...] = chunk(e, far_x + p.c).reshape(wide, slots, width)
        after(e, "B")

        @pl.when(e > 0)
        def _():
            grads_out(e - 1)
            after(e - 1, "W")

        moves.arrive(e, 0)
        to_core[e, 0] = chunk(e, p.x * 2 + 1 - p.c).astype(BF16).reshape(wide, slots, width)
        back.core(e, 0).start()
        after(e, "C")
        near_sum[e] = chunk(e, p.n).reshape(wide, slots, width)
        store(e, 0).start()

        @pl.when(e == local - 1)
        def _():
            gates_core_start()

        after(e, "D")

        @pl.when(e > 0)
        def _():
            grads_in(e - 1)
            after(e - 1, "V")

        return carry

    lax.fori_loop(0, local, expert, 0)
    gates_core.wait_recv()
    gate_side[...] = gate_sum[far_x + p.c] + gate_from_core[1]
    gates_side = remote(gate_side, gate_from_side, gx_s, gx_r, p.side)
    gates_side.start()
    grads_out(local - 1)
    after(local - 1, "W")
    gates_side.wait_recv()
    gates = gate_sum[p.n] + gate_from_core[0] + gate_from_side[...]
    for v in range(wide):
        gate_ready[v] = gates[v : v + 1, :]
    gates_wide = [
        remote(gate_ready.at[p.flip(j)], gate_o.at[p.w], gw_s.at[j], gw_r.at[j], p.peer(j)) for j in range(1, wide)
    ]
    for copy in gates_wide:
        copy.start()
    gate_o[p.w] = gate_ready[p.w]
    grads_in(local - 1)
    after(local - 1, "V")
    gates_core.wait_send()
    gates_side.wait_send()

    def drain(e, carry):
        moves.drain(e)
        back.drain(e)
        back.arrive(e)

        @pl.when(e >= local - 2)
        def _():
            store(e, 0).wait()

        return carry

    lax.fori_loop(0, local, drain, 0)
    store(local - 1, 1).wait()
    store(local - 1, 2).wait()
    for copy in gates_wide:
        copy.wait()


def moving_experts(sent, cot_all, expert_in, expert_out, router, wide, narrow):
    _, local, slots, width = sent.shape
    hidden_width = expert_in.shape[2]
    step = wide * slots
    sds = jax.ShapeDtypeStruct
    any_spec, vmem_spec = pl.BlockSpec(memory_space=pl.ANY), pl.BlockSpec(memory_space=pltpu.VMEM)
    dma = pltpu.SemaphoreType.DMA
    outs, gin, gout, back, gates = pl.pallas_call(
        moving_expert_kernel,
        out_shape=(
            sds((local, narrow, wide, slots, width), BF16),
            sds(expert_in.shape, BF16),
            sds(expert_out.shape, BF16),
            sds((wide, local, slots, width), BF16),
            sds((wide, 1, local * slots), F32),
        ),
        in_specs=[vmem_spec, any_spec, any_spec, any_spec, vmem_spec],
        out_specs=(any_spec,) * 3 + (vmem_spec,) * 2,
        scratch_shapes=[
            pltpu.VMEM((local, narrow, wide, slots, width), BF16),
            pltpu.VMEM((local, narrow, wide, slots, width), BF16),
            pltpu.VMEM(expert_in.shape, BF16),
            pltpu.VMEM(expert_out.shape, BF16),
            pltpu.VMEM((2, narrow, step, width), BF16),
            pltpu.VMEM((2, narrow, step, hidden_width), BF16),
            pltpu.VMEM((2, narrow, step, hidden_width), BF16),
            pltpu.VMEM((2, narrow, wide, slots, width), BF16),
            pltpu.VMEM(expert_in.shape[1:], BF16),
            pltpu.VMEM(expert_out.shape[1:], BF16),
            pltpu.VMEM((local, 2, wide, slots, width), BF16),
            pltpu.VMEM((local, 2, wide, slots, width), BF16),
            pltpu.VMEM((local, wide, slots, width), BF16),
            pltpu.VMEM((local, wide, slots, width), F32),
            pltpu.VMEM((wide, slots, width), F32),
            pltpu.VMEM((narrow, wide, local * slots), F32),
            pltpu.VMEM((2, wide, local * slots), F32),
            pltpu.VMEM((2, wide, local * slots), F32),
            pltpu.VMEM((wide, local * slots), F32),
            pltpu.VMEM((wide, local * slots), F32),
            pltpu.VMEM((wide, 1, local * slots), F32),
            dma((local, 3)), dma((local, 3)), *Spread.semaphores(local, wide), *Collect.semaphores(local, wide),
            dma, dma, dma, dma, dma((wide,)), dma((wide,)),
        ],
        compiler_params=pltpu.CompilerParams(
            collective_id=2, has_side_effects=True, vmem_limit_bytes=62 << 20
        ),
        name="experts",
    )(sent, cot_all, expert_in, expert_out, router)
    return outs, back, gates, gin.astype(F32), gout.astype(F32)


def routed_gate(normed_f, router_ref, routes):
    probs = softmax_lanes(dot_nn(normed_f[...], router_ref[...]))
    chosen = lax.broadcasted_iota(jnp.int32, probs.shape, 1) == routes
    return probs, chosen, jnp.sum(jnp.where(chosen, probs, 0.0), axis=-1, keepdims=True)


def slot_owners(slot_col, total):
    return lax.broadcasted_iota(jnp.int32, (slot_col.shape[0], total), 1) == slot_col


def ffn_backward(probs, chosen, gate, owned, gates_ref, normed_f, router_ref, grows_ref, mixed, cot_ref, gain_f):
    grad_gate = jnp.sum(jnp.where(owned, gates_ref[...], 0.0), axis=-1, keepdims=True)
    grad_logits = (probs * (jnp.where(chosen, grad_gate, 0.0) - gate * grad_gate)).astype(BF16)
    grad_router = dot_tn(normed_f[...], grad_logits)
    grad_normed = dot_nt(grad_logits, router_ref[...]) + dot_nn(owned.astype(BF16), grows_ref[...])
    grad_norm, grad_gain = norm_backward(mixed, inverse_rms(mixed), gain_f[...], grad_normed)
    return grad_router, cot_ref[...].astype(F32) + grad_norm, grad_gain


def attention_setup(q_ref, k_ref, normed_ref, att_ref, lse_ref, q_t, k_t, normed_t, att_t, lse_t):
    head_dim = q_ref.shape[1] // HEADS
    att_t[...] = att_ref[...].T
    q_t[...] = (q_ref[...] * jnp.asarray(head_dim**-0.5, BF16)).T
    k_t[...] = k_ref[...].T
    normed_t[...] = normed_ref[...].T
    lse_t[...] = lse_ref[...].T


def attention_delta(datt, att_t, datt_t, delta):
    width, count = att_t.shape
    datt_t[...] = datt[...].T
    products = datt_t[...].astype(F32) * att_t[...].astype(F32)
    delta[...] = jnp.sum(products.reshape(HEADS, width // HEADS, count), axis=1)


def pair_backward(
    at, near_ref, q_ref, k_ref, v_ref, q_t, k_t, datt, datt_t, delta, lse_t, dst, gq, gk, gv, gnear_ref, gfar_ref
):
    count, width = q_ref.shape
    head_dim = width // HEADS
    blocks = count // BLOCK
    first = lax.broadcasted_iota(jnp.int32, (1, BLOCK), 1) < head_dim
    cols = pl.ds(pl.multiple_of(at * BLOCK, BLOCK), BLOCK)
    q_pair, datt_pair = q_ref[:, cols], datt[:, cols]
    gq_parts, gk_parts, gv_parts = [], [], []
    for half in range(2):
        head = 2 * at + half
        mask = first if half == 0 else jnp.logical_not(first)
        near_row = near_ref[pl.ds(head, 1), :]
        near = toeplitz_near(near_row)
        lse_row, delta_row = lse_t[pl.ds(head, 1), :], delta[pl.ds(head, 1), :]
        near_sum = jnp.zeros((BLOCK, 3 * BLOCK), F32)
        low_sum, high_sum = jnp.zeros((BLOCK, BLOCK), F32), jnp.zeros((BLOCK, BLOCK), F32)
        gk_rows, gv_rows = [], []
        for row in range(blocks):
            rows = slice(row * BLOCK, (row + 1) * BLOCK)
            k_rows, v_rows = k_ref[rows, cols], v_ref[rows, cols]
            zeros = jnp.zeros_like(k_rows)
            scores = dot_nn(jnp.where(mask, k_rows, zeros), q_t[cols, :])
            scores = scores + bias_rows(near, near_row, row, blocks)
            weights = jnp.exp(scores - lse_row)
            grad_weights = dot_nn(jnp.where(mask, v_rows, zeros), datt_t[cols, :])
            grad_scores = weights * (grad_weights - delta_row)
            gv_rows.append(dot_nn(weights.astype(BF16), datt_pair))
            low_bits = grad_scores.astype(BF16)
            dst[rows, :] = low_bits
            gk_rows.append(dot_nn(low_bits, q_pair))
            for column in range(blocks):
                piece = grad_scores[:, column * BLOCK : (column + 1) * BLOCK]
                distance = column - row
                if distance <= -2:
                    high_sum = high_sum + piece
                elif distance >= 2:
                    low_sum = low_sum + piece
                else:
                    pads = [jnp.zeros((BLOCK, BLOCK), F32)] * 3
                    pads[distance + 1] = piece
                    near_sum = near_sum + jnp.concatenate(pads, axis=1)
        gq_parts.append(
            dot_nn(k_t[pl.ds(pl.multiple_of(head * head_dim, head_dim), head_dim), :], dst[...])
        )
        gk_parts.append(jnp.concatenate(gk_rows, axis=0))
        gv_parts.append(jnp.concatenate(gv_rows, axis=0))
        gnear_ref[pl.ds(head, 1), :] = diagonal_sums(near_sum)
        gfar_ref[pl.ds(head, 1), :] = jnp.concatenate(
            [jnp.sum(low_sum, axis=0, keepdims=True), jnp.sum(high_sum, axis=0, keepdims=True)], axis=1
        )
    scale = head_dim**-0.5
    gq[:, cols] = (jnp.concatenate(gq_parts, axis=0).T * scale).astype(BF16)
    gk[:, cols] = (jnp.where(first, gk_parts[0], gk_parts[1]) * scale).astype(BF16)
    gv[:, cols] = jnp.where(first, gv_parts[0], gv_parts[1]).astype(BF16)


def input_backward(x_ref, w_ref, gain_a, gmixed, gq, gk, gv):
    count, width = x_ref.shape
    grad_normed = jnp.zeros((count, width), F32)
    for at, grad in enumerate((gq, gk, gv)):
        grad_normed = grad_normed + dot_nt(grad[...], w_ref[:, at * width : (at + 1) * width])
    tokens = x_ref[...].astype(F32)
    grad_norm, grad_gain = norm_backward(tokens, inverse_rms(tokens), gain_a[...], grad_normed)
    return gmixed[...] + grad_norm, grad_gain


def backward_kernel(
    x_ref, w_ref, gain_a, gain_f, router_ref, near_ref, slot_col, routes_ref,
    normed_ref, q_ref, k_ref, v_ref, att_ref, lse_ref, mixed_ref, normed_f, cot_ref, outs_ref, grows_ref, gates_ref,
    result_ref, gx_ref, gw_ref, grouter_ref, gnear_ref, gfar_ref, ggain_ref,
    q_t, k_t, normed_t, att_t, datt, datt_t, delta, lse_t, gq, gk, gv, gmixed, dst,
):
    width = x_ref.shape[1]
    probs, chosen, gate = routed_gate(normed_f, router_ref, routes_ref[...])
    owned = slot_owners(slot_col[...], outs_ref.shape[0])
    mixed = mixed_ref[...]
    result_ref[...] = (mixed + gate * dot_nn(owned.astype(BF16), outs_ref[...])).astype(BF16)
    grouter_ref[...], grad_mixed, ggain_ref[1:2, :] = ffn_backward(
        probs, chosen, gate, owned, gates_ref, normed_f, router_ref, grows_ref, mixed, cot_ref, gain_f
    )
    gmixed[...] = grad_mixed
    branch = grad_mixed.astype(BF16)
    gw_ref[:, 3 * width : 4 * width] = dot_tn(att_ref[...], branch).astype(BF16)
    datt[...] = dot_nt(branch, w_ref[:, 3 * width : 4 * width]).astype(BF16)
    attention_setup(q_ref, k_ref, normed_ref, att_ref, lse_ref, q_t, k_t, normed_t, att_t, lse_t)
    attention_delta(datt, att_t, datt_t, delta)

    def pair(at, carry):
        pair_backward(
            at, near_ref, q_ref, k_ref, v_ref, q_t, k_t, datt, datt_t, delta, lse_t, dst, gq, gk, gv,
            gnear_ref, gfar_ref,
        )
        return carry

    lax.fori_loop(0, HEADS // 2, pair, 0)
    for at, grad in enumerate((gq, gk, gv)):
        gw_ref[:, at * width : (at + 1) * width] = dot_nn(normed_t[...], grad[...]).astype(BF16)
    gx_ref[...], ggain_ref[0:1, :] = input_backward(x_ref, w_ref, gain_a, gmixed, gq, gk, gv)


class Sums:
    def __init__(self, place, unit, buffers, semaphores, out, split):
        self.p, self.unit, self.out, self.split = place, unit, out, split
        self.send, self.core, self.first_in, self.second_in, self.z_in, self.last = buffers
        self.s, self.r = semaphores
        self.deep = place.deep
        p, c = place, place.c * split
        self.first, self.second = p.y + c * (p.x - p.y), p.x + c * (p.y - p.x)
        row, side = p.row, p.side
        self.first_peer = tuple(a + c * (b - a) for a, b in zip(row, side))
        self.second_peer = tuple(b + c * (a - b) for a, b in zip(row, side))

    def store(self, buffer, part, core):
        rows, cols = buffer.shape[-2:]
        blocks = part.reshape(self.deep, 2, 2, rows, cols)
        c = core * self.split
        for y in range(2):
            for x in range(2):
                first, second = (y, x) if y == x else (y + c * (x - y), x + c * (y - x))
                buffer[self.unit, first, second] = blocks[:, y, x].astype(buffer.dtype)

    def to_core(self):
        u, p = self.unit, self.p
        return remote(self.send.at[u], self.core.at[u], self.s.at[u, 0], self.r.at[u, 0], p.core)

    def to_y(self):
        u = self.unit
        return remote(self.core.at[u, 1 - self.first], self.first_in.at[u], self.s.at[u, 1], self.r.at[u, 1], self.first_peer)

    def to_x(self):
        u = self.unit
        return remote(self.first_in.at[u, 1 - self.second], self.second_in.at[u], self.s.at[u, 2], self.r.at[u, 2], self.second_peer)

    def to_z(self, k):
        u, p = self.unit, self.p
        z = lax.rem(p.z + k, p.deep)
        return remote(
            self.second_in.at[u, z], self.z_in.at[u, k], self.s.at[u, 3 + k], self.r.at[u, 3 + k], (z * 2 + p.y, p.n)
        )

    def to_last(self):
        u, p = self.unit, self.p
        return remote(self.last.at[u, 1 - p.c], self.out.at[u, p.c], self.s.at[u, 3], self.r.at[u, 3], p.core)

    def begin(self, part):
        self.store(self.send, part, 1 - self.p.c)
        self.to_core().start()

    def stage_core(self, part):
        u = self.unit
        self.to_core().wait_recv()
        rows, cols = self.core.shape[-2:]
        blocks = part.reshape(self.deep, 2, 2, rows, cols)
        c = self.p.c * self.split
        for y in range(2):
            for x in range(2):
                first, second = (y, x) if y == x else (y + c * (x - y), x + c * (y - x))
                kept = blocks[:, y, x] + self.core[u, first, second].astype(F32)
                self.core[u, first, second] = kept.astype(BF16)
        self.to_y().start()

    def stage_y(self):
        u = self.unit
        self.to_y().wait_recv()
        self.first_in[u] = (self.core[u, self.first].astype(F32) + self.first_in[u].astype(F32)).astype(BF16)
        self.to_x().start()

    def stage_x(self):
        u = self.unit
        self.to_x().wait_recv()
        self.second_in[u] = (self.first_in[u, self.second].astype(F32) + self.second_in[u].astype(F32)).astype(BF16)
        for k in range(1, self.p.deep):
            self.to_z(k).start()

    def stage_z(self):
        u = self.unit
        total = self.second_in[u, self.p.z].astype(F32)
        for k in range(1, self.p.deep):
            self.to_z(k).wait_recv()
            total = total + self.z_in[u, k].astype(F32)
        self.last[u] = total.reshape(self.last.shape[1:])
        self.to_last().start()
        self.out[u, self.p.c] = self.last[u, self.p.c]

    def drain(self):
        for copy in (self.to_core(), self.to_y(), self.to_x()):
            copy.wait_send()
        for k in range(1, self.p.deep):
            self.to_z(k).wait_send()
        self.to_last().wait()


def sum_buffers(units, wide, rows, cols):
    deep = wide // 2
    vmem = lambda *shape, dtype=BF16: pltpu.VMEM((units, *shape), dtype)
    return [
        vmem(2, 2, deep, rows, cols), vmem(2, 2, deep, rows, cols), vmem(2, deep, rows, cols), vmem(deep, rows, cols),
        vmem(deep, rows, cols), vmem(2, rows // 2, cols, dtype=F32),
        pltpu.SemaphoreType.DMA((units, 3 + deep)), pltpu.SemaphoreType.DMA((units, 3 + deep)),
    ]


def moving_backward_kernel(
    x_hbm, w_hbm, normed_hbm, q_hbm, k_hbm, v_hbm, att_hbm, lse_hbm, outs_hbm, mixed_hbm, cot_hbm, grows_hbm,
    gains_ref, router_ref, rel_ref, slot_route, normed_f, gates_ref, picks_ref,
    gx_ref, result_ref, gq_out, gk_out, gv_out, go_out, router_out, rel_out, small_out,
    x_ref, w_ref, normed_ref, q_ref, k_ref, v_ref, att_ref, lse_ref, mixed_ref, cot_ref, grows_ref, load_s, near_ref,
    q_t, k_t, normed_t, att_t, datt, datt_t, delta, lse_t, gq, gk, gv, gmixed, gnormed, dst, gnear, gfar,
    own, from_core, from_side, returned, own_s, rc_s, rc_r, rx_s, rx_r, rw_s, rw_r,
    u1, u2, u3, u4, u5, u6, us, ur, o1, o2, o3, o4, o5, o6, os, orr, pair_sums, o_out,
    small, small_in, ss, sr,
):
    count, width = x_hbm.shape
    wide, local, slots, _ = returned.shape
    total = wide * local * slots
    p = Place(wide)
    far_x = (1 - p.x) * 2
    units = HEADS // 4
    gain_a, gain_f = gains_ref.at[0:1, :], gains_ref.at[1:2, :]
    loads = [
        pltpu.make_async_copy(source, target, load_s.at[at])
        for at, (source, target) in enumerate((
            (att_hbm, att_ref), (q_hbm, q_ref), (k_hbm, k_ref), (normed_hbm, normed_ref), (lse_hbm, lse_ref),
            (mixed_hbm, mixed_ref), (cot_hbm, cot_ref), (grows_hbm, grows_ref),
            (w_hbm, w_ref), (v_hbm, v_ref), (x_hbm, x_ref),
        ))
    ]

    def partial(e, other, core):
        return outs_hbm.at[e, (far_x if other else p.x * 2) + core]

    back = Collect(
        p, lambda e, other: partial(e, other, 1 - p.c), from_core, from_side, returned, (rc_s, rc_r, rx_s, rx_r, rw_s, rw_r)
    )

    def own_copy(e, other):
        return pltpu.make_async_copy(partial(e, other, p.c), own.at[e, other], own_s.at[e, other])

    for copy in loads[:5]:
        copy.start()
    greet(p.partners())
    for other in (1, 0):
        for e in range(local):
            own_copy(e, other).start()
    for copy in loads[5:11]:
        copy.start()

    def go(e, piece):
        if piece == 1:
            own_copy(e, 1).wait()
            back.go_beside(e, own[e, 1])
        else:
            back.beside(e, piece).start()

    def near(e, piece):
        back.core(e, 0).wait_recv()
        own_copy(e, 0).wait()

    def finish(e, piece):
        back.finish(
            e, piece, lambda rows, part: own[e, 0, rows, part].astype(F32) + from_core[e, 0, rows, part].astype(F32)
        )

    def unit(u):
        if isinstance(u, int) and u == units:
            return Sums(p, 0, (o1, o2, o3, o4, o5, o6), (os, orr), o_out, 0)
        return Sums(p, u, (u1, u2, u3, u4, u5, u6), (us, ur), pair_sums, (u + 1) // units)

    hops = [[p.core], [p.row], [p.side], [(lax.rem(p.z + k, p.deep) * 2 + p.y, p.n) for k in range(1, p.deep)]]
    copies, slot = [], 0
    for stage, devices in enumerate(hops):
        copies.append([
            remote(small.at[stage], small_in.at[slot + at], ss.at[slot + at], sr.at[slot + at], device)
            for at, device in enumerate(devices)
        ])
        slot += len(devices)

    def small_end(stage):
        slot = sum(len(c) for c in copies[:stage])
        found = small[stage]
        for at, copy in enumerate(copies[stage]):
            copy.wait_recv()
            found = found + small_in[slot + at]
        return found

    def small_step(stage, piece):
        if stage:
            small[stage] = small_end(stage - 1)
        for copy in copies[stage]:
            copy.start()

    acts = {
        "core": lambda e, other: back.core(e, other).start(), "go": go, "near": near, "finish": finish,
        "y": lambda u, piece: unit(u).stage_y(), "x": lambda u, piece: unit(u).stage_x(),
        "z": lambda u, piece: unit(u).stage_z(), "small": small_step,
    }

    def act(part):
        for name, at, piece in BACKWARD_STEPS.get(part, ()):
            acts[name](at, piece)

    def after(u, part):
        for at in range(units):
            if part + str(at) in BACKWARD_STEPS:
                pl.when(u == at)(lambda at=at: act(part + str(at)))

    probs, chosen, gate = routed_gate(normed_f, router_ref, slot_route[:, 1:2])
    owned = slot_owners(slot_route[:, 0:1], total)
    near_ref[...] = near_biases(rel_ref, picks_ref)
    for copy in loads[:5]:
        copy.wait()
    attention_setup(q_ref, k_ref, normed_ref, att_ref, lse_ref, q_t, k_t, normed_t, att_t, lse_t)
    meet(p.partners())
    act("first")
    for copy in loads[5:8]:
        copy.wait()
    grad_router, grad_mixed, grad_gain_f = ffn_backward(
        probs, chosen, gate, owned, gates_ref, normed_f, router_ref, grows_ref, mixed_ref[...], cot_ref, gain_f
    )
    gmixed[...] = grad_mixed
    small[0] = jnp.zeros_like(small[0])
    small[0, HEADS : HEADS + 1, :] = grad_gain_f
    act("F0")
    branch = grad_mixed.astype(BF16)
    half_cols = width // 2
    router_cols = o_out.shape[-1] - half_cols
    router_wide = jnp.concatenate(
        [grad_router, jnp.zeros((width, router_cols - grad_router.shape[1]), F32)], axis=1
    )

    def output_part(core):
        low, high = branch[:, :half_cols], branch[:, half_cols:]
        part = dot_nn(att_t[...], jnp.where(core == 0, low, high))
        return jnp.concatenate([part, jnp.where(core == 0, router_wide, 0.0)], axis=1)

    unit(units).begin(output_part(1 - p.c))
    act("O0")
    loads[8].wait()
    datt[...] = (
        dot_nt(branch[:, :half_cols], w_ref[units, 0]) + dot_nt(branch[:, half_cols:], w_ref[units, 1])
    ).astype(BF16)
    act("D0")
    unit(units).stage_core(output_part(p.c))
    act("Q0")
    attention_delta(datt, att_t, datt_t, delta)
    for copy in loads[9:11]:
        copy.wait()
    act("S0")

    def pair(at):
        pair_backward(
            at, near_ref, q_ref, k_ref, v_ref, q_t, k_t, datt, datt_t, delta, lse_t, dst, gq, gk, gv,
            gnear, gfar,
        )
        cols = pl.ds(pl.multiple_of(at * BLOCK, BLOCK), BLOCK)
        grads = jnp.concatenate([gq[:, cols], gk[:, cols], gv[:, cols]], axis=1)
        gnormed[...] += dot_nt(grads, w_ref[at // 2, lax.rem(at, 2)])
        return dot_nn(normed_t[...], grads)

    gnormed[...] = jnp.zeros_like(gnormed)

    def pairs(u, carry):
        unit(u).begin(pair(2 * u + 1 - p.c))
        after(u, "A")
        unit(u).stage_core(pair(2 * u + p.c))
        after(u, "B")
        return carry

    lax.fori_loop(0, units, pairs, 0)
    near_grads = lax.dot_general(
        gnear[...], picks_ref[...], (((1,), (1,)), ((), ())), precision=HIGHEST, preferred_element_type=F32
    )
    buckets = lax.broadcasted_iota(jnp.int32, near_grads.shape, 1)
    low_sum = jnp.sum(gfar[:, :BLOCK], axis=1, keepdims=True)
    high_sum = jnp.sum(gfar[:, BLOCK:], axis=1, keepdims=True)
    bucket_count = rel_ref.shape[1]
    rel = near_grads + jnp.where(buckets == bucket_count // 2 - 1, low_sum, 0.0)
    small[0, :HEADS, :bucket_count] = rel + jnp.where(buckets == bucket_count - 1, high_sum, 0.0)
    tokens = x_ref[...].astype(F32)
    grad_norm, grad_gain_a = norm_backward(tokens, inverse_rms(tokens), gain_a[...], gnormed[...])
    gx_ref[...] = gmixed[...] + grad_norm
    small[0, HEADS + 1 : HEADS + 2, :] = grad_gain_a

    act("P0")
    for e in range(local):
        back.arrive(e)
    combined = dot_nn(owned.astype(BF16), returned[...].reshape(total, width))
    result_ref[...] = (mixed_ref[...] + gate * combined).astype(BF16)
    act("R0")
    small_all = small_end(3)
    small_out[...] = small_all
    rel_out[...] = small_all[:HEADS, : rel_out.shape[1]]
    for e in range(local):
        back.drain(e)
    for u in range(units + 1):
        unit(u).drain()
    for half in range(2):
        for u in range(units):
            cols = slice((2 * u + half) * BLOCK, (2 * u + half + 1) * BLOCK)
            for at, out in enumerate((gq_out, gk_out, gv_out)):
                out[:, cols] = pair_sums[u, half, :, at * BLOCK : (at + 1) * BLOCK]
        go_out[:, half * half_cols : (half + 1) * half_cols] = o_out[0, half, :, :half_cols]
    router_out[...] = o_out[0, 0, :, half_cols : half_cols + router_out.shape[1]]
    for stage in copies:
        for copy in stage:
            copy.wait_send()


def moving_backward(
    rel_bias, inputs, weights, gains, router, slot_route,
    normed, q, k, v, att, lse, mixed, normed_f, cotangent, outs, grows, gates, wide, slots,
):
    count, width = inputs.shape
    local, narrow = outs.shape[:2]
    experts = router.shape[1]
    bucket_count = rel_bias.shape[0]
    deep, rows = wide // 2, width // (wide * 2)
    units = HEADS // 4
    pair_cols, out_cols = 3 * BLOCK, width // 2 + BLOCK * -(-experts // BLOCK)
    sds = jax.ShapeDtypeStruct
    any_spec = pl.BlockSpec(memory_space=pl.ANY)
    picks = jnp.asarray(near_picks(bucket_count, -1).T)
    wide_t = lambda dtype: pltpu.VMEM((width, count), dtype)
    tall = lambda dtype: pltpu.VMEM((count, width), dtype)
    vmem = lambda *shape, dtype=BF16: pltpu.VMEM(shape, dtype)
    dma = pltpu.SemaphoreType.DMA
    hops = 3 + deep - 1
    grad_inputs, result, grad_query, grad_key, grad_value, grad_output, grad_router, grad_rel, small = pl.pallas_call(
        moving_backward_kernel,
        out_shape=(
            sds((count, width), F32), sds((count, width), BF16), *[sds((rows // 2, width), F32)] * 4,
            sds((rows // 2, experts), F32), sds((HEADS, bucket_count), F32), sds((16, width), F32),
        ),
        in_specs=[any_spec] * 12 + in_vmem(7),
        out_specs=tuple(in_vmem(9)),
        scratch_shapes=[
            tall(BF16), pltpu.VMEM(weights.shape, BF16), tall(BF16), tall(BF16), tall(BF16), tall(BF16), tall(BF16),
            vmem(count, BLOCK, dtype=F32), tall(F32), tall(BF16), vmem(wide * local * slots, width),
            dma((11,)), vmem(HEADS, 4 * BLOCK, dtype=F32),
            wide_t(BF16), wide_t(BF16), wide_t(BF16), wide_t(BF16), tall(BF16), wide_t(BF16),
            vmem(HEADS, count, dtype=F32), vmem(BLOCK, count, dtype=F32),
            tall(BF16), tall(BF16), tall(BF16), tall(F32), tall(F32), vmem(count, count),
            vmem(HEADS, 4 * BLOCK, dtype=F32), vmem(HEADS, 2 * BLOCK, dtype=F32),
            vmem(local, 2, wide, slots, width), vmem(local, 2, wide, slots, width), vmem(local, wide, slots, width),
            vmem(wide, local, slots, width),
            dma((local, 2)), *Collect.semaphores(local, wide),
            *sum_buffers(units, wide, rows, pair_cols), *sum_buffers(1, wide, rows, out_cols),
            vmem(units, 2, rows // 2, pair_cols, dtype=F32), vmem(1, 2, rows // 2, out_cols, dtype=F32),
            vmem(4, 16, width, dtype=F32), vmem(hops, 16, width, dtype=F32), dma((hops,)), dma((hops,)),
        ],
        compiler_params=pltpu.CompilerParams(collective_id=3, has_side_effects=True, vmem_limit_bytes=62 << 20),
        name="backward",
    )(
        inputs, weights, normed, q, k, v, att, lse, outs, mixed, cotangent, grows,
        gains, router, rel_bias.T, slot_route, normed_f, gates, picks,
    )
    device = lax.axis_index("wide") * narrow + lax.axis_index("narrow")
    gain_grads = lax.dynamic_slice(small, (HEADS, device * (rows // 2)), (2, rows // 2))
    return result, grad_inputs, (grad_query, grad_key, grad_value), grad_output, grad_router, gain_grads[1], gain_grads[0], grad_rel.T


def in_vmem(count):
    return [pl.BlockSpec(memory_space=pltpu.VMEM)] * count


def shards(
    inputs, gain_attn, w_query, w_key, w_value, w_output, rel_bias, gain_ffn, w_router,
    expert_in, expert_out, routes, capacity, cotangent,
):
    count, width = inputs.shape
    experts = w_router.shape[1]
    local, _, hidden_width = expert_in.shape
    wide, narrow = lax.axis_size("wide"), lax.axis_size("narrow")
    slots = 2 * count // experts
    total = experts * slots
    bucket_count = rel_bias.shape[0]
    params = pltpu.CompilerParams(vmem_limit_bytes=60 << 20)
    smem = pl.BlockSpec(memory_space=pltpu.SMEM)

    moving = narrow == 4 and wide & (wide - 1) == 0 and local == HEADS // 4 + 1 and slots % 32 == 0 and local * slots % BLOCK == 0
    moving = moving and width % (wide * 2 * 16) == 0 and count == SEQ_LEN and experts + 8 <= BLOCK
    if moving:
        normed, q, k, v, att, lse, mixed, normed_f, sent, weights, cot_all, slot_route, router, gains = moving_forward(
            rel_bias, capacity, inputs, w_query, w_key, w_value, w_output, w_router, gain_attn, gain_ffn, routes,
            cotangent, wide, narrow, local, slots,
        )
        outs, back, gates, gin, gout = moving_experts(sent, cot_all, expert_in, expert_out, router, wide, narrow)
        result, grad_inputs, kinds, grad_output, grad_router, grad_gain_a, grad_gain_f, grad_rel = moving_backward(
            rel_bias, inputs, weights.reshape(HEADS // 4 + 1, 2, width, width // 2), gains, router, slot_route,
            normed, q, k, v, att, lse, mixed, normed_f, cotangent, outs,
            back.reshape(total, width), gates.reshape(1, total), wide, slots,
        )
        return (
            result, grad_inputs, grad_gain_a, *kinds, grad_output, grad_rel, grad_gain_f, grad_router, gin, gout,
        )

    near = jnp.dot(near_picks(bucket_count, 1), rel_bias, precision=HIGHEST).T
    near_back = jnp.dot(near_picks(bucket_count, -1), rel_bias, precision=HIGHEST).T

    packed = jnp.concatenate([w_query, w_key, w_value, w_output], axis=1)
    weights = lax.all_gather(packed, BOTH, axis=0, tiled=True)
    small = lax.all_gather(
        jnp.concatenate([w_router, gain_attn[:, None], gain_ffn[:, None]], axis=1), BOTH, axis=0, tiled=True
    )
    router = small[:, :experts]
    gain_a = small[:, experts].astype(F32)[None, :]
    gain_f = small[:, experts + 1].astype(F32)[None, :]
    slot_col, slot_row, cot_sent = pl.pallas_call(
        lambda *refs: place_kernel(slots, experts, *refs),
        out_shape=(
            jax.ShapeDtypeStruct((count, 1), jnp.int32),
            jax.ShapeDtypeStruct((1, count), jnp.int32),
            jax.ShapeDtypeStruct((total, width), BF16),
        ),
        in_specs=[smem] + in_vmem(3),
        out_specs=tuple(in_vmem(3)),
        compiler_params=params,
        name="places",
    )(capacity, routes, routes.reshape(1, count), cotangent)

    def spread(rows):
        taken = lax.all_to_all(
            rows.reshape(wide, local * slots, width), "wide", split_axis=0, concat_axis=0, tiled=True
        )
        held = lax.all_gather(taken, "narrow", axis=0, tiled=True)
        return held.reshape(wide * narrow, local, slots, width)

    def collect(rows):
        own = lax.psum_scatter(
            rows.reshape(wide * narrow, local * slots, width), "narrow", scatter_dimension=0, tiled=True
        )
        back = lax.all_to_all(own, "wide", split_axis=0, concat_axis=0, tiled=True)
        return back.reshape(total, width)

    cot_all = spread(cot_sent)

    rows_t = lambda dtype, cols=width: jax.ShapeDtypeStruct((count, cols), dtype)
    normed, q, k, v, att, lse, mixed, normed_f, sent = pl.pallas_call(
        forward_kernel,
        out_shape=(
            rows_t(BF16), rows_t(BF16), rows_t(BF16), rows_t(BF16), rows_t(BF16), rows_t(F32, BLOCK),
            rows_t(F32), rows_t(BF16), jax.ShapeDtypeStruct((total, width), BF16),
        ),
        in_specs=in_vmem(7),
        out_specs=tuple(in_vmem(9)),
        compiler_params=params,
        name="forward",
    )(inputs, weights, gain_a, gain_f, router, near, slot_row)

    rows_all = spread(sent)
    sources = wide * narrow
    block = pl.BlockSpec((sources, 1, slots, width), lambda e: (0, e, 0, 0))
    w_in_spec = pl.BlockSpec((1, width, hidden_width), lambda e: (e, 0, 0))
    w_out_spec = pl.BlockSpec((1, hidden_width, width), lambda e: (e, 0, 0))
    first_expert = (lax.axis_index("wide") * local).astype(jnp.int32)[None]
    back, grows, gin, gout = pl.pallas_call(
        expert_kernel,
        grid=(local,),
        out_shape=(
            jax.ShapeDtypeStruct(rows_all.shape, BF16),
            jax.ShapeDtypeStruct(rows_all.shape, BF16),
            jax.ShapeDtypeStruct(expert_in.shape, F32),
            jax.ShapeDtypeStruct(expert_out.shape, F32),
        ),
        in_specs=[
            smem, block, block, w_in_spec, w_out_spec, pl.BlockSpec((width, experts), lambda e: (0, 0)),
        ],
        out_specs=(block, block, w_in_spec, w_out_spec),
        scratch_shapes=[
            pltpu.VMEM((sources * slots, hidden_width), BF16),
            pltpu.VMEM((sources * slots, hidden_width), BF16),
            pltpu.VMEM((sources * slots, width), BF16),
        ],
        compiler_params=params,
        name="experts",
    )(first_expert, rows_all, cot_all, expert_in, expert_out, router)
    outs_back = collect(back)
    grows_back = collect(grows)
    gates = jnp.sum(outs_back.astype(F32) * cot_sent.astype(F32), axis=1)[None, :]

    wide_t = lambda dtype: pltpu.VMEM((width, count), dtype)
    tall = lambda dtype: pltpu.VMEM((count, width), dtype)
    result, grad_inputs, gw, grouter, gnear, gfar, ggain = pl.pallas_call(
        backward_kernel,
        out_shape=(
            rows_t(BF16), rows_t(F32), jax.ShapeDtypeStruct((width, 4 * width), BF16),
            jax.ShapeDtypeStruct((width, experts), F32), jax.ShapeDtypeStruct((HEADS, 4 * BLOCK), F32),
            jax.ShapeDtypeStruct((HEADS, 2 * BLOCK), F32), jax.ShapeDtypeStruct((2, width), F32),
        ),
        in_specs=in_vmem(20),
        out_specs=tuple(in_vmem(7)),
        scratch_shapes=[
            wide_t(BF16), wide_t(BF16), wide_t(BF16), wide_t(BF16), tall(BF16), wide_t(BF16),
            pltpu.VMEM((HEADS, count), F32), pltpu.VMEM((BLOCK, count), F32),
            tall(BF16), tall(BF16), tall(BF16), tall(F32), pltpu.VMEM((count, count), BF16),
        ],
        compiler_params=params,
        name="backward",
    )(
        inputs, weights, gain_a, gain_f, router, near_back, slot_col, routes,
        normed, q, k, v, att, lse, mixed, normed_f, cotangent, outs_back, grows_back, gates,
    )

    gw = lax.psum_scatter(gw, BOTH, scatter_dimension=0, tiled=True).astype(F32)
    grad_query, grad_key, grad_value, grad_output = (gw[:, i * width : (i + 1) * width] for i in range(4))
    gsmall = lax.psum_scatter(
        jnp.concatenate([grouter, ggain.T], axis=1), BOTH, scatter_dimension=0, tiled=True
    )
    grad_rel = jnp.dot(near_picks(bucket_count, -1).T, gnear.T, precision=HIGHEST)
    low, high = jnp.sum(gfar[:, :BLOCK], axis=1), jnp.sum(gfar[:, BLOCK:], axis=1)
    grad_rel = grad_rel.at[bucket_count // 2 - 1].add(low).at[bucket_count - 1].add(high)
    grad_rel = lax.psum(grad_rel, BOTH)
    return (
        result, grad_inputs, gsmall[:, experts], grad_query, grad_key, grad_value, grad_output,
        grad_rel, gsmall[:, experts + 1], gsmall[:, :experts], gin, gout,
    )


def solution(mesh):
    return jax.shard_map(
        shards,
        mesh=mesh,
        in_specs=(
            P(BOTH, None),
            P(BOTH),
            P(BOTH, None),
            P(BOTH, None),
            P(BOTH, None),
            P(BOTH, None),
            P(),
            P(BOTH),
            P(BOTH, None),
            P("wide", None, "narrow"),
            P("wide", "narrow", None),
            P(BOTH, None),
            P(BOTH),
            P(BOTH, None),
        ),
        out_specs=(
            P(BOTH, None),
            P(BOTH, None),
            P(BOTH),
            P(BOTH, None),
            P(BOTH, None),
            P(BOTH, None),
            P(BOTH, None),
            P(),
            P(BOTH),
            P(BOTH, None),
            P("wide", None, "narrow"),
            P("wide", "narrow", None),
        ),
        check_vma=False,
    )
```

```python
import jax
import jax.numpy as jnp
import numpy as np
from jax import lax
from jax.experimental import pallas as pl
from jax.experimental.pallas import tpu as pltpu
from jax.sharding import PartitionSpec as P

HEADS = 12
SEQ_LEN = 512
BLOCK = 128
EPSILON = 1e-06
HIGHEST = lax.Precision.HIGHEST
ROOT_TWO_PI = 0.7978845608028654
CUBIC = 0.044715
BOTH = ("wide", "narrow")
F32 = jnp.float32
BF16 = jnp.bfloat16


def bucket_of(offsets, bucket_count):
    half_count = bucket_count // 2
    exact_count = half_count // 2
    distance = np.abs(offsets)
    scaled = exact_count + np.floor(
        np.log(np.maximum(distance, 1) / exact_count)
        / np.log(128.0 / exact_count)
        * (half_count - exact_count)
    ).astype(np.int64)
    scaled = np.minimum(scaled, half_count - 1)
    return ((offsets > 0) * half_count + np.where(distance < exact_count, distance, scaled)).astype(
        np.int32
    )


def near_picks(bucket_count, sign):
    offsets = sign * (np.arange(4 * BLOCK) - (2 * BLOCK - 1))
    picks = (bucket_of(offsets, bucket_count)[:, None] == np.arange(bucket_count)[None, :]).astype(
        np.float32
    )
    picks[-1] = 0.0
    return picks


def dot_nn(left, right):
    return lax.dot_general(left, right, (((1,), (0,)), ((), ())), preferred_element_type=F32)


def dot_nt(left, right):
    return lax.dot_general(left, right, (((1,), (1,)), ((), ())), preferred_element_type=F32)


def dot_tn(left, right):
    return lax.dot_general(left, right, (((0,), (0,)), ((), ())), preferred_element_type=F32)


def inverse_rms(values):
    return lax.rsqrt(jnp.mean(values * values, axis=-1, keepdims=True) + EPSILON)


def norm_backward(values, inverse, gain, grad_normed):
    scaled = grad_normed * gain
    grad_gain = jnp.sum(grad_normed * values * inverse, axis=0, keepdims=True)
    inner = jnp.mean(scaled * values, axis=-1, keepdims=True)
    return (inverse * (scaled - values * inverse * inverse * inner), grad_gain)


def softmax_lanes(logits):
    peak = jnp.max(logits, axis=-1, keepdims=True)
    exponent = jnp.exp(logits - peak)
    return exponent / jnp.sum(exponent, axis=-1, keepdims=True)


def toeplitz_near(near_row):
    spread = jnp.broadcast_to(near_row, (BLOCK, 4 * BLOCK))
    return pltpu.roll(spread, 3 * BLOCK + 1, 1, stride=1, stride_axis=0)[:, : 3 * BLOCK]


def bias_rows(near, near_row, row, blocks):
    far_low, far_high = near_row[:, :1], near_row[:, 4 * BLOCK - 2 : 4 * BLOCK - 1]
    pieces = []
    for column in range(blocks):
        distance = column - row
        if distance <= -2:
            pieces.append(jnp.broadcast_to(far_low, (BLOCK, BLOCK)))
        elif distance >= 2:
            pieces.append(jnp.broadcast_to(far_high, (BLOCK, BLOCK)))
        else:
            pieces.append(near[:, (distance + 1) * BLOCK : (distance + 2) * BLOCK])
    return jnp.concatenate(pieces, axis=1)


def near_biases(rel_ref, picks_ref):
    return lax.dot_general(
        rel_ref[...], picks_ref[...], (((1,), (0,)), ((), ())), precision=HIGHEST, preferred_element_type=F32
    )


def diagonal_sums(near_sum):
    padded = jnp.concatenate([near_sum, jnp.zeros((BLOCK, BLOCK), F32)], axis=1)
    groups = jnp.zeros((8, 4 * BLOCK), F32)
    for at in range(0, BLOCK, 8):
        groups = groups + pltpu.roll(padded[at : at + 8, :], BLOCK - 8 - at, 1)
    sums = groups[7:8, :]
    for at in range(7):
        sums = sums + pltpu.roll(groups[at : at + 1, :], 7 - at, 1)
    return sums


def slot_places(col, row, limit, experts, slots, count):
    lower = lax.broadcasted_iota(jnp.int32, (count, count), 0)
    upper = lax.broadcasted_iota(jnp.int32, (count, count), 1)
    chosen = lax.broadcasted_iota(jnp.int32, (count, experts), 1) == col
    running = dot_nn((upper <= lower).astype(BF16), chosen.astype(BF16))
    place = jnp.sum(jnp.where(chosen, running, 0.0), axis=1, keepdims=True).astype(jnp.int32) - 1
    slot_col = jnp.where(place < limit, col * slots + place, -1)
    chosen_t = lax.broadcasted_iota(jnp.int32, (experts, count), 0) == row
    running_t = dot_nn(chosen_t.astype(BF16), (lower <= upper).astype(BF16))
    place_t = (
        jnp.sum(jnp.where(chosen_t, running_t, 0.0), axis=0, keepdims=True).astype(jnp.int32) - 1
    )
    slot_row = jnp.where(place_t < limit, row * slots + place_t, -1)
    return slot_col, slot_row


def place_kernel(slots, experts, capacity_ref, routes_ref, row_ref, cot_ref, slot_col, slot_row, cot_out):
    count = routes_ref.shape[0]
    limit = capacity_ref[0] * count // experts
    col, row = slot_places(routes_ref[...], row_ref[...], limit, experts, slots, count)
    slot_col[...] = col
    slot_row[...] = row
    picks = (lax.broadcasted_iota(jnp.int32, (experts * slots, count), 0) == row).astype(BF16)
    cot_out[...] = dot_nn(picks, cot_ref[...]).astype(BF16)


def pair_forward(at, near_ref, q_ref, k_ref, v_ref, att_ref, lse_ref):
    count, width = q_ref.shape
    head_dim = width // HEADS
    blocks = count // BLOCK
    lanes = lax.broadcasted_iota(jnp.int32, (1, BLOCK), 1)
    first = lanes < head_dim
    cols = pl.ds(pl.multiple_of(at * BLOCK, BLOCK), BLOCK)
    k_pair, v_pair = k_ref[:, cols], v_ref[:, cols]
    near_rows = [near_ref[pl.ds(2 * at + half, 1), :] for half in range(2)]
    nears = [toeplitz_near(near_row) for near_row in near_rows]
    for row in range(blocks):
        rows = slice(row * BLOCK, (row + 1) * BLOCK)
        q_rows = q_ref[rows, cols] * jnp.asarray(head_dim**-0.5, BF16)
        found = []
        log_sums = lse_ref[rows, :]
        for half in range(2):
            head = 2 * at + half
            mask = first if half == 0 else jnp.logical_not(first)
            scores = dot_nt(jnp.where(mask, q_rows, jnp.zeros_like(q_rows)), k_pair)
            scores = scores + bias_rows(nears[half], near_rows[half], row, blocks)
            peak = jnp.max(scores, axis=-1, keepdims=True)
            exponent = jnp.exp(scores - peak)
            total = jnp.sum(exponent, axis=-1, keepdims=True)
            found.append(dot_nn((exponent * (1.0 / total)).astype(BF16), v_pair))
            log_sums = jnp.where(lanes == head, peak + jnp.log(total), log_sums)
        lse_ref[rows, :] = log_sums
        att_ref[rows, cols] = jnp.where(first, found[0], found[1]).astype(BF16)


def slot_rows(slot_row, values, total):
    picks = lax.broadcasted_iota(jnp.int32, (total, slot_row.shape[1]), 0) == slot_row
    return dot_nn(picks.astype(BF16), values).astype(BF16)


def forward_kernel(
    x_ref, w_ref, gain_a, gain_f, router_ref, near_ref, slot_row,
    normed_ref, q_ref, k_ref, v_ref, att_ref, lse_ref, mixed_ref, normed_f, sent_ref,
):
    width = x_ref.shape[1]
    tokens = x_ref[...].astype(F32)
    normed = (tokens * inverse_rms(tokens) * gain_a[...]).astype(BF16)
    normed_ref[...] = normed
    for out, at in ((q_ref, 0), (k_ref, 1), (v_ref, 2)):
        out[...] = dot_nn(normed, w_ref[:, at * width : (at + 1) * width]).astype(BF16)
    lse_ref[...] = jnp.zeros_like(lse_ref)

    def pair(at, carry):
        pair_forward(at, near_ref, q_ref, k_ref, v_ref, att_ref, lse_ref)
        return carry

    lax.fori_loop(0, HEADS // 2, pair, 0)
    mixed = tokens + dot_nn(att_ref[...], w_ref[:, 3 * width : 4 * width])
    mixed_ref[...] = mixed
    normed_2 = (mixed * inverse_rms(mixed) * gain_f[...]).astype(BF16)
    normed_f[...] = normed_2
    sent_ref[...] = slot_rows(slot_row[...], normed_2, sent_ref.shape[0])


def expert_kernel(
    first_ref, rows_ref, cot_ref, in_ref, out_ref, router_ref,
    back_ref, grows_ref, gin_ref, gout_ref, hidden_ref, gpre_ref, sg_ref,
):
    sources, _, slots, width = rows_ref.shape
    total = sources * slots
    step = min(256, total)
    expert = first_ref[0] + pl.program_id(0)

    def chunk(at, carry):
        these = pl.ds(pl.multiple_of(at * (step // slots), step // slots), step // slots)
        flat = pl.ds(pl.multiple_of(at * step, step), step)
        rows = rows_ref[these, 0].reshape(step, width)
        probs = softmax_lanes(dot_nn(rows, router_ref[...]))
        here = lax.broadcasted_iota(jnp.int32, probs.shape, 1) == expert
        gate = jnp.sum(jnp.where(here, probs, 0.0), axis=-1, keepdims=True)
        sg = (cot_ref[these, 0].reshape(step, width).astype(F32) * gate).astype(BF16)
        sg_ref[flat, :] = sg
        pre = dot_nn(rows, in_ref[0])
        square = pre * pre
        inner = jnp.tanh(pre * (ROOT_TWO_PI + ROOT_TWO_PI * CUBIC * square))
        half = 0.5 * (1.0 + inner)
        hidden = (pre * half).astype(BF16)
        hidden_ref[flat, :] = hidden
        slope = half + 0.5 * pre * (1.0 - inner * inner) * (
            ROOT_TWO_PI + 3.0 * ROOT_TWO_PI * CUBIC * square
        )
        gpre = (dot_nt(sg, out_ref[0]) * slope).astype(BF16)
        gpre_ref[flat, :] = gpre
        back_ref[these, 0] = dot_nn(hidden, out_ref[0]).astype(BF16).reshape(-1, slots, width)
        grows_ref[these, 0] = dot_nt(gpre, in_ref[0]).astype(BF16).reshape(-1, slots, width)
        return carry

    lax.fori_loop(0, total // step, chunk, 0)
    gout_ref[0] = dot_tn(hidden_ref[...], sg_ref[...])
    gin_ref[0] = dot_tn(rows_ref[:, 0].reshape(total, width), gpre_ref[...])


def remote(source, target, send, receive, device):
    return pltpu.make_async_remote_copy(
        src_ref=source,
        dst_ref=target,
        send_sem=send,
        recv_sem=receive,
        device_id=device,
        device_id_type=pl.DeviceIdType.MESH,
    )


def greet(devices):
    for device in devices:
        pl.semaphore_signal(
            pltpu.get_barrier_semaphore(), inc=1, device_id=device, device_id_type=pl.DeviceIdType.MESH
        )


def meet(devices):
    pl.semaphore_wait(pltpu.get_barrier_semaphore(), len(devices))


FORWARD_STEPS = {
    "first": (("send", 4, 0), ("start", 2, 0), ("start", 3, 0), ("send", 0, 0), ("start", 1, 0), ("spread", 4, 0),
        ("send", 1, 0), ("start", 0, 0), ("spread", 0, 0), ("send", 2, 0), ("start", 0, 2), ("forward", 1, 0),
        ("send", 3, 0), ("start", 1, 1), ("over_x", 4, 0), ("over_y", 4, 0), ("forward", 0, 0), ("spread", 1, 0),
        ("end", 4, 0), ("over_x", 0, 0), ("spread", 2, 0), ("start", 3, 2), ("over_y", 1, 0), ("forward", 3, 0),
        ("start", 3, 1), ("over_x", 1, 0), ("over_x", 2, 0), ("end", 0, 0), ("over_y", 0, 0), ("forward", 1, 1),
        ("start", 2, 2),),
    "N0": (("spread", 3, 0),),
    "A0": (("forward", 2, 0), ("pass", 1, 1), ("forward", 3, 1), ("pass", 3, 0), ("over_y", 2, 0),
        ("start", 1, 2), ("forward", 0, 2), ("forward", 3, 2), ("end", 1, 0),),
    "B0": (("start", 2, 1),),
    "A1": (("forward", 2, 2), ("end", 2, 0), ("start", 0, 1), ("over_x", 3, 0),),
    "A2": (("forward", 2, 1), ("forward", 1, 2), ("pass", 1, 0), ("pass", 2, 0), ("pass", 0, 0), ("pass", 3, 2),
        ("pass", 2, 2), ("pass", 0, 2), ("forward", 0, 1), ("end", 3, 0), ("over_y", 3, 0), ("pass", 3, 1),),
    "M0": (("pass", 1, 2), ("pass", 2, 1), ("pass", 0, 1),),
}

BACKWARD_STEPS = {
    "first": (("core", 0, 1), ("core", 3, 0), ("core", 2, 1),),
    "O0": (("go", 2, 1), ("core", 1, 0), ("core", 2, 0), ("core", 0, 0), ("go", 0, 1),),
    "Q0": (("go", 2, 2), ("core", 3, 1),),
    "S0": (("core", 1, 1), ("near", 1, 0), ("near", 2, 0), ("go", 0, 2), ("near", 0, 0), ("finish", 2, 1),
        ("near", 3, 0), ("go", 3, 1),),
    "A0": (("go", 1, 1), ("finish", 0, 1), ("go", 3, 2), ("go", 0, 0), ("finish", 2, 2),),
    "A1": (("go", 3, 0), ("finish", 1, 1),),
    "B1": (("y", 3, 0), ("finish", 3, 1),),
    "A2": (("finish", 3, 2),),
    "P0": (("x", 3, 0), ("y", 0, 0), ("y", 1, 0), ("finish", 0, 2), ("go", 1, 0), ("finish", 0, 0),
        ("small", 0, 0), ("go", 1, 2), ("x", 0, 0), ("finish", 3, 0), ("x", 1, 0), ("y", 2, 0), ("z", 3, 0),
        ("small", 1, 0), ("go", 2, 0), ("finish", 1, 2), ("x", 2, 0), ("small", 2, 0), ("finish", 1, 0),
        ("finish", 2, 0), ("small", 3, 0), ("z", 0, 0), ("z", 1, 0), ("z", 2, 0),),
}

EXPERT_STEPS = {
    "first": (("start", 0, 0), ("start", 0, 1), ("start", 0, 2), ("forward", 0, 0), ("start", 1, 2),
        ("forward", 0, 1), ("start", 1, 0), ("forward", 0, 2), ("start", 1, 1), ("forward", 1, 0),
        ("start", 2, 0), ("pass", 0, 1), ("forward", 1, 2), ("start", 2, 1), ("pass", 0, 0), ("pass", 0, 2),),
    "A0": (("forward", 1, 1), ("start", 2, 2),),
    "B0": (("forward", 2, 0),),
    "C0": (("go", 0, 1), ("pass", 1, 0), ("forward", 2, 1), ("pass", 1, 2), ("start", 3, 0), ("pass", 1, 1),),
    "D0": (("start", 3, 2),),
    "A1": (("forward", 2, 2),),
    "B1": (("start", 3, 1), ("forward", 3, 0),),
    "W0": (("go", 1, 1), ("pass", 2, 0), ("pass", 2, 1), ("forward", 3, 2),),
    "D1": (("forward", 3, 1), ("go", 0, 2), ("go", 1, 2), ("pass", 2, 2), ("sum", 0, 0),),
    "V0": (("finish", 0, 1), ("sum", 1, 0),),
    "A2": (("finish", 1, 1),),
    "B2": (("go", 2, 1),),
    "W1": (("go", 0, 0), ("finish", 0, 2), ("pass", 3, 0), ("pass", 3, 2), ("go", 1, 0),),
    "C2": (("pass", 3, 1), ("go", 2, 2),),
    "D2": (("go", 2, 0),),
    "V1": (("sum", 2, 0), ("finish", 2, 1),),
    "B3": (("go", 3, 1), ("finish", 1, 2),),
    "W2": (("finish", 1, 0), ("finish", 2, 2),),
    "C3": (("finish", 0, 0), ("go", 3, 2),),
    "D3": (("sum", 3, 0), ("finish", 3, 1), ("go", 3, 0),),
    "V2": (("finish", 3, 2), ("finish", 2, 0),),
    "W3": (("finish", 3, 0),),
}


class Place:
    def __init__(self, wide):
        self.wide = wide
        self.run = wide // 2
        self.deep = wide // 2
        self.w, self.n = lax.axis_index("wide"), lax.axis_index("narrow")
        self.x, self.c = self.n // 2, lax.rem(self.n, 2)
        self.z, self.y = self.w // 2, lax.rem(self.w, 2)
        self.core = (self.w, self.x * 2 + 1 - self.c)
        self.side = (self.w, (1 - self.x) * 2 + self.c)
        self.row = (self.z * 2 + 1 - self.y, self.n)

    def flip(self, j):
        found, bit = self.w, 1
        while bit <= j:
            if j & bit:
                found = found + bit - 2 * bit * lax.rem(self.w // bit, 2)
            bit *= 2
        return found

    def peer(self, j):
        return (self.flip(j), self.n)

    def span(self, piece):
        half = self.w // self.run
        return pl.ds((1 - half if piece else half) * self.run, self.run)

    def steps(self, piece):
        return range(self.run, self.wide) if piece else range(1, self.run)

    def partners(self):
        return [self.peer(j) for j in range(1, self.wide)] + [self.core, self.side]


def slot_part(piece, slots):
    return pl.ds((piece - 1) * (slots // 2), slots // 2) if piece else pl.ds(0, slots)


PIECES = range(3)


class Spread:
    def __init__(self, place, sent, held, wide_s, wide_r, side_s, side_r, core_s, core_r):
        self.place, self.sent, self.held = place, sent, held
        self.wide_s, self.wide_r, self.side_s, self.side_r = wide_s, wide_r, side_s, side_r
        self.core_s, self.core_r = core_s, core_r
        self.slots = sent.shape[2]

    def hop(self, e, j, piece):
        p, part = self.place, slot_part(piece, self.slots)
        at = p.wide + j if piece == 2 else j
        return remote(
            self.sent.at[p.flip(j), e, part], self.held.at[e, p.n, p.w, part],
            self.wide_s.at[e, at], self.wide_r.at[e, at], p.peer(j),
        )

    def start(self, e, piece):
        for j in self.place.steps(piece):
            self.hop(e, j, piece).start()

    def beside(self, e, piece):
        p = self.place
        rows = self.held.at[e, p.n, p.span(piece), slot_part(piece, self.slots)]
        return remote(rows, rows, self.side_s.at[e, piece], self.side_r.at[e, piece], p.side)

    def over(self, e, other, piece):
        p = self.place
        m = (1 - p.x) * 2 + p.c if other else p.n
        rows = self.held.at[e, m, p.span(piece), slot_part(piece, self.slots)]
        at = 3 * other + piece
        return remote(rows, rows, self.core_s.at[e, at], self.core_r.at[e, at], p.core)

    def forward(self, e, piece):
        for j in self.place.steps(piece):
            self.hop(e, j, piece).wait_recv()
        self.beside(e, piece).start()
        self.over(e, 0, piece).start()

    def pass_on(self, e, piece):
        self.beside(e, piece).wait_recv()
        self.over(e, 1, piece).start()

    def arrive(self, e, other):
        for piece in PIECES:
            self.over(e, other, piece).wait_recv()

    def drain(self, e):
        for piece in PIECES:
            for j in self.place.steps(piece):
                self.hop(e, j, piece).wait_send()
            self.beside(e, piece).wait_send()
            self.over(e, 0, piece).wait_send()
            self.over(e, 1, piece).wait_send()

    @staticmethod
    def semaphores(local, wide):
        dma = pltpu.SemaphoreType.DMA
        return [dma((local, n)) for n in (2 * wide, 2 * wide, 3, 3, 6, 6)]


class Collect:
    def __init__(self, place, to_core, from_core, from_side, returned, semaphores):
        self.place, self.to_core, self.from_core = place, to_core, from_core
        self.from_side, self.returned = from_side, returned
        self.core_s, self.core_r, self.side_s, self.side_r, self.wide_s, self.wide_r = semaphores
        self.slots = from_side.shape[2]

    def core(self, e, other):
        return remote(
            self.to_core(e, other), self.from_core.at[e, other], self.core_s.at[e, other], self.core_r.at[e, other],
            self.place.core,
        )

    def beside(self, e, piece):
        rows, part = self.place.span(piece), slot_part(piece, self.slots)
        return remote(
            self.from_core.at[e, 1, rows, part], self.from_side.at[e, rows, part],
            self.side_s.at[e, piece], self.side_r.at[e, piece], self.place.side,
        )

    def back(self, e, j, piece):
        p, part = self.place, slot_part(piece, self.slots)
        at = p.wide + j if piece == 2 else j
        return remote(
            self.from_side.at[e, p.flip(j), part], self.returned.at[p.w, e, part],
            self.wide_s.at[e, at], self.wide_r.at[e, at], p.peer(j),
        )

    def go_beside(self, e, part):
        self.core(e, 1).wait_recv()
        held = self.from_core[e, 1].astype(F32)
        self.from_core[e, 1] = (part.astype(F32).reshape(held.shape) + held).astype(BF16)
        self.beside(e, 1).start()

    def finish(self, e, piece, own):
        p = self.place
        rows, part = p.span(piece), slot_part(piece, self.slots)
        self.beside(e, piece).wait_recv()
        total = own(rows, part) + self.from_side[e, rows, part].astype(F32)
        self.from_side[e, rows, part] = total.astype(BF16)
        for j in p.steps(piece):
            self.back(e, j, piece).start()
        if not piece:
            self.returned[p.w, e] = self.from_side[e, p.w]

    def drain(self, e):
        self.core(e, 0).wait_send()
        self.core(e, 1).wait_send()
        for piece in PIECES:
            self.beside(e, piece).wait_send()
            for j in self.place.steps(piece):
                self.back(e, j, piece).wait_send()

    def arrive(self, e):
        for piece in PIECES:
            for j in self.place.steps(piece):
                self.back(e, j, piece).wait_recv()

    @staticmethod
    def semaphores(local, wide):
        dma = pltpu.SemaphoreType.DMA
        return [dma((local, n)) for n in (2, 2, 3, 3, 2 * wide, 2 * wide)]


class Gather:
    def __init__(self, place, unit, held, halves, semaphores):
        self.p, self.u, self.held, self.halves = place, unit, held, halves
        self.s, self.r = semaphores

    def piece(self, *place):
        return self.held.at[self.u, self.p.c, *place] if self.halves else self.held.at[self.u, *place]

    def column(self, y, x):
        return self.piece(slice(None), y, x)

    def copy(self, piece, slot, device):
        return remote(piece, piece, self.s.at[self.u, slot], self.r.at[self.u, slot], device)

    def to_z(self, k):
        p = self.p
        z = lax.rem(p.z + k, p.deep)
        return self.copy(self.piece(p.z, p.y, p.x), k - 1, (z * 2 + p.y, p.n))

    def to_x(self):
        return self.copy(self.column(self.p.y, self.p.x), 3, self.p.side)

    def to_y(self):
        return self.copy(self.column(self.p.y, self.p.x), 4, self.p.row)

    def corner(self):
        return self.copy(self.column(self.p.y, 1 - self.p.x), 5, self.p.row)

    def to_core(self, at):
        p = self.p
        y, x = ((p.y, p.x), (p.y, 1 - p.x), (1 - p.y, p.x), (1 - p.y, 1 - p.x))[at]
        return self.copy(self.column(y, x), 6 + at, p.core)

    def hand(self, at):
        if self.halves:
            self.to_core(at).start()

    def start(self):
        for k in range(1, self.p.deep):
            self.to_z(k).start()

    def spread(self):
        for k in range(1, self.p.deep):
            self.to_z(k).wait_recv()
        self.to_x().start()
        self.to_y().start()
        self.hand(0)

    def over_x(self):
        self.to_x().wait_recv()
        self.corner().start()
        self.hand(1)

    def over_y(self):
        self.to_y().wait_recv()
        self.hand(2)

    def end(self):
        self.corner().wait_recv()
        self.hand(3)

    def arrive(self):
        if self.halves:
            for at in range(4):
                self.to_core(at).wait_recv()

    def drain(self):
        for k in range(1, self.p.deep):
            self.to_z(k).wait_send()
        for copy in (self.to_x(), self.to_y(), self.corner()):
            copy.wait_send()
        if self.halves:
            for at in range(4):
                self.to_core(at).wait_send()


def moving_forward_kernel(
    capacity_ref, x_ref, q_part, k_part, v_part, o_part, router_part, gain_a_part, gain_f_part, rel_ref, picks_ref, row_ref,
    cot_ref,
    normed_out, q_out, k_out, v_out, att_out, lse_out, mixed_out, normed_f_out, sent_out, weights_out, cot_out,
    slot_route, router_out, gains_out,
    normed_ref, q_ref, k_ref, v_ref, att_ref, lse_ref, mixed_ref, normed_f, sent_ref, store_s,
    near_ref, gain_lanes, small_lanes, small_part,
    held, small, pair_send, pair_got, small_got, cot_sent, weight_s, pair_s, pair_r,
    gs, gr, hs, hr, wide_s, wide_r, side_s, side_r, core_s, core_r,
):
    count, width = x_ref.shape
    wide, local, slots, _ = cot_sent.shape
    experts = router_out.shape[1]
    total = wide * local * slots
    units = HEADS // 4
    rows = pair_send.shape[2]
    p = Place(wide)
    greet(p.partners())

    def own_cols(u, half):
        if u == units:
            return o_part[:, half * (width // 2) : (half + 1) * (width // 2)]
        cols = slice((2 * u + half) * BLOCK, (2 * u + half + 1) * BLOCK)
        return jnp.concatenate([q_part[:, cols], k_part[:, cols], v_part[:, cols]], axis=1)

    def swap_copies():
        return [
            remote(pair_send.at[0], pair_got.at[0], pair_s.at[0], pair_r.at[0], p.core),
            remote(small_part, small_got, pair_s.at[1], pair_r.at[1], p.core),
        ]

    gain_lanes[...] = jnp.zeros_like(gain_lanes)
    gain_lanes[0:1, :rows] = gain_a_part[...].astype(F32)
    gain_lanes[1:2, :rows] = gain_f_part[...].astype(F32)
    gain_cols = gain_lanes[...].T[:rows, :]
    small_lanes[...] = jnp.zeros_like(small_lanes)
    small_lanes[:, :experts] = router_part[...].astype(F32)
    lanes = lax.broadcasted_iota(jnp.int32, small_lanes.shape, 1)
    others = jnp.where(lanes == experts + 1, gain_cols[:, 1:2], small_lanes[...])
    small_part[...] = jnp.where(lanes == experts, gain_cols[:, 0:1], others).astype(BF16)
    for u in range(units + 1):
        pair_send[0, u] = jnp.where(p.c == 0, own_cols(u, 1), own_cols(u, 0))
    limit = capacity_ref[0] * count // experts
    routes = jnp.broadcast_to(row_ref[...].astype(F32), (8, count)).T[:, :1].astype(jnp.int32)
    slot_col, slot_row = slot_places(routes, row_ref[...], limit, experts, slots, count)
    slot_route[:, 0:1] = slot_col
    slot_route[:, 1:2] = routes
    near_ref[...] = near_biases(rel_ref, picks_ref)
    cot_sent[...] = slot_rows(slot_row, cot_ref[...], total).reshape(cot_sent.shape)
    moves = Spread(p, cot_sent, cot_out, wide_s, wide_r, side_s, side_r, core_s, core_r)

    def own_rows(e):
        return pltpu.make_async_copy(cot_sent.at[p.w, e], cot_out.at[e, p.n, p.w], weight_s.at[1 + e])

    for e in range(local):
        own_rows(e).start()
    lse_ref[...] = jnp.zeros_like(lse_ref)
    for e in range(local):
        own_rows(e).wait()
    meet(p.partners())
    for copy in swap_copies():
        copy.start()
    for copy in swap_copies():
        copy.wait_recv()

    def joined(mine, other):
        mine, other = mine.astype(F32), other.astype(F32)
        return jnp.concatenate(
            [jnp.where(p.c == 0, mine, other), jnp.where(p.c == 0, other, mine)], axis=0
        ).astype(BF16)

    def gather(u):
        if isinstance(u, int) and u > units:
            return small_gather
        return Gather(p, u, held, True, (gs, gr))

    small_gather = Gather(p, 0, small, False, (hs, hr))
    small[0, p.z, p.y, p.x] = joined(small_part[...], small_got[...])
    for u in range(units + 1):
        mine = jnp.where(p.c == 0, own_cols(u, 0), own_cols(u, 1))
        held[u, p.c, p.z, p.y, p.x] = joined(mine, pair_got[0, u])

    acts = {
        "start": moves.start, "forward": moves.forward, "pass": moves.pass_on,
        "send": lambda u, piece: gather(u).start(), "spread": lambda u, piece: gather(u).spread(),
        "over_x": lambda u, piece: gather(u).over_x(), "over_y": lambda u, piece: gather(u).over_y(),
        "end": lambda u, piece: gather(u).end(),
    }

    def act(steps):
        for name, at, piece in steps:
            acts[name](at, piece)

    def after(u, part):
        for at in range(units):
            steps = FORWARD_STEPS.get(part + str(at), ())
            if steps:
                pl.when(u == at)(lambda steps=steps: act(steps))

    act(FORWARD_STEPS["first"])
    small_all = small[0].reshape(width, BLOCK)
    router_out[...] = small_all[:, :experts]
    gains_out[...] = small_all.astype(F32).T[experts : experts + 8, :]
    tokens = x_ref[...].astype(F32)
    normed_ref[...] = (tokens * inverse_rms(tokens) * gains_out[0:1, :]).astype(BF16)
    act(FORWARD_STEPS.get("N0", ()))

    def pair(at, weight):
        cols = pl.ds(pl.multiple_of(at * BLOCK, BLOCK), BLOCK)
        found = dot_nn(normed_ref[...], weight.reshape(width, 3 * BLOCK)).astype(BF16)
        q_ref[:, cols], k_ref[:, cols], v_ref[:, cols] = (found[:, i * BLOCK : (i + 1) * BLOCK] for i in range(3))
        pair_forward(at, near_ref, q_ref, k_ref, v_ref, att_ref, lse_ref)

    def pairs(u, carry):
        gather(u).arrive()
        pair(2 * u, held[u, 0])
        after(u, "A")
        pair(2 * u + 1, held[u, 1])
        after(u, "B")
        return carry

    lax.fori_loop(0, units, pairs, 0)
    stores = [
        pltpu.make_async_copy(source, target, store_s.at[at])
        for at, (source, target) in enumerate((
            (normed_ref, normed_out), (q_ref, q_out), (k_ref, k_out), (v_ref, v_out), (att_ref, att_out),
            (lse_ref, lse_out), (mixed_ref, mixed_out), (normed_f, normed_f_out), (sent_ref, sent_out),
        ))
    ]
    for copy in stores[:6]:
        copy.start()
    gather(units).arrive()
    weights_copy = pltpu.make_async_copy(held, weights_out, weight_s.at[0])
    weights_copy.start()
    mixed = tokens_again(x_ref) + jnp.concatenate(
        [dot_nn(att_ref[...], held[units, half].reshape(width, width // 2)) for half in range(2)], axis=1
    )
    mixed_ref[...] = mixed
    normed_2 = (mixed * inverse_rms(mixed) * gains_out[1:2, :]).astype(BF16)
    normed_f[...] = normed_2
    stores[6].start()
    stores[7].start()
    sent_ref[...] = slot_rows(slot_row, normed_2, total).reshape(sent_ref.shape)
    stores[8].start()
    act(FORWARD_STEPS.get("M0", ()))
    for copy in swap_copies():
        copy.wait_send()
    small_gather.drain()
    for u in range(units + 1):
        gather(u).drain()
    for e in range(local):
        moves.arrive(e, 0)
        moves.arrive(e, 1)
        moves.drain(e)
    weights_copy.wait()
    for copy in stores:
        copy.wait()


def tokens_again(x_ref):
    return x_ref[...].astype(F32)


def moving_forward(
    rel_bias, capacity, inputs, w_query, w_key, w_value, w_output, w_router, gain_attn, gain_ffn, routes, cotangent,
    wide, narrow, local, slots,
):
    count, width = inputs.shape
    experts = w_router.shape[1]
    shard = w_query.shape[0]
    deep, units = wide // 2, HEADS // 4
    half = width // 2
    sds = jax.ShapeDtypeStruct
    rows_t = lambda dtype, cols=width: sds((count, cols), dtype)
    smem, any_spec = pl.BlockSpec(memory_space=pltpu.SMEM), pl.BlockSpec(memory_space=pl.ANY)
    vmem = lambda *shape, dtype=BF16: pltpu.VMEM(shape, dtype)
    dma = pltpu.SemaphoreType.DMA
    picks = jnp.asarray(near_picks(rel_bias.shape[0], 1).T)
    return pl.pallas_call(
        moving_forward_kernel,
        out_shape=(
            rows_t(BF16), rows_t(BF16), rows_t(BF16), rows_t(BF16), rows_t(BF16), rows_t(F32, BLOCK), rows_t(F32),
            rows_t(BF16), sds((wide, local, slots, width), BF16),
            sds((units + 1, 2, deep, 2, 2, 2 * shard, half), BF16),
            sds((local, narrow, wide, slots, width), BF16), sds((count, 2), jnp.int32),
            sds((width, experts), BF16), sds((8, width), F32),
        ),
        in_specs=[smem] + in_vmem(12),
        out_specs=(any_spec,) * 11 + tuple(in_vmem(3)),
        scratch_shapes=[
            vmem(count, width), vmem(count, width), vmem(count, width), vmem(count, width), vmem(count, width),
            vmem(count, BLOCK, dtype=F32), vmem(count, width, dtype=F32), vmem(count, width),
            vmem(wide, local, slots, width), dma((9,)),
            vmem(HEADS, 4 * BLOCK, dtype=F32), vmem(8, BLOCK, dtype=F32), vmem(shard, BLOCK, dtype=F32), vmem(shard, BLOCK),
            vmem(units + 1, 2, deep, 2, 2, 2 * shard, half), vmem(1, deep, 2, 2, 2 * shard, BLOCK),
            vmem(1, units + 1, shard, half), vmem(1, units + 1, shard, half), vmem(shard, BLOCK),
            vmem(wide, local, slots, width), dma((1 + local,)), dma((2,)), dma((2,)),
            dma((units + 1, 10)), dma((units + 1, 10)), dma((1, 10)), dma((1, 10)),
            *Spread.semaphores(local, wide),
        ],
        compiler_params=pltpu.CompilerParams(collective_id=1, has_side_effects=True, vmem_limit_bytes=62 << 20),
        name="forward",
    )(
        capacity, inputs, w_query, w_key, w_value, w_output, w_router, gain_attn[None, :], gain_ffn[None, :], rel_bias.T, picks,
        routes.reshape(1, count), cotangent,
    )


def moving_expert_kernel(
    sent, cot_hbm, in_hbm, out_hbm, router_ref,
    outs_o, gin_o, gout_o, back_o, gate_o,
    held, cot, w_in, w_out, sg, hidden, gpre, outs, gin, gout, to_core, from_core, from_side, near_sum, far_sum,
    gate_sum, gate_core, gate_from_core, gate_side, gate_from_side, gate_ready,
    load_s, store_s, wide_s, wide_r, side_s, side_r, core_s, core_r,
    rc_s, rc_r, rx_s, rx_r, rw_s, rw_r, gc_s, gc_r, gx_s, gx_r, gw_s, gw_r,
):
    wide, local, slots, width = sent.shape
    narrow = held.shape[1]
    step = wide * slots
    hidden_width = in_hbm.shape[2]
    p = Place(wide)
    moves = Spread(p, sent, held, wide_s, wide_r, side_s, side_r, core_s, core_r)
    greet(p.partners())

    def loads(e):
        return [
            pltpu.make_async_copy(in_hbm.at[e], w_in.at[e], load_s.at[e, 0]),
            pltpu.make_async_copy(out_hbm.at[e], w_out.at[e], load_s.at[e, 1]),
            pltpu.make_async_copy(cot_hbm.at[e], cot.at[e], load_s.at[e, 2]),
        ]

    def own_rows(e):
        return pltpu.make_async_copy(sent.at[p.w, e], held.at[e, p.n, p.w], load_s.at[e, 3])

    def store(e, at):
        source = (outs.at[lax.rem(e, 2)], gin, gout)[at]
        return pltpu.make_async_copy(source, (outs_o, gin_o, gout_o)[at].at[e], store_s.at[e, at])

    def grads_out(e):
        b = lax.rem(e, 2)

        @pl.when(e > 0)
        def _():
            store(e - 1, 2).wait()

        rows = narrow * step
        found = dot_tn(hidden[b].reshape(rows, hidden_width), sg[b].reshape(rows, width))
        gout[...] = found.astype(BF16)
        store(e, 2).start()

    def grads_in(e):
        b = lax.rem(e, 2)

        @pl.when(e > 0)
        def _():
            store(e - 1, 1).wait()

        rows = narrow * step
        found = dot_tn(held[e].reshape(rows, width), gpre[b].reshape(rows, hidden_width))
        gin[...] = found.astype(BF16)
        store(e, 1).start()

    for e in range(local):
        for copy in loads(e):
            copy.start()
        own_rows(e).start()
    gate_sum[...] = jnp.zeros_like(gate_sum)
    for e in range(local):
        own_rows(e).wait()
    meet(p.partners())

    def chunk(e, m):
        b = lax.rem(e, 2)
        rows = held[e, m].reshape(step, width)
        probs = softmax_lanes(dot_nn(rows, router_ref[...]))
        here = lax.broadcasted_iota(jnp.int32, probs.shape, 1) == p.w * local + e
        gate = jnp.sum(jnp.where(here, probs, 0.0), axis=-1, keepdims=True)
        cot_rows = cot[e, m].reshape(step, width).astype(F32)
        sg_rows = (cot_rows * gate).astype(BF16)
        sg[b, m] = sg_rows
        pre = dot_nn(rows, w_in[e])
        square = pre * pre
        inner = jnp.tanh(pre * (ROOT_TWO_PI + ROOT_TWO_PI * CUBIC * square))
        half = 0.5 * (1.0 + inner)
        hidden_rows = (pre * half).astype(BF16)
        hidden[b, m] = hidden_rows
        slope = half + 0.5 * pre * (1.0 - inner * inner) * (
            ROOT_TWO_PI + 3.0 * ROOT_TWO_PI * CUBIC * square
        )
        gpre_rows = (dot_nt(sg_rows, w_out[e]) * slope).astype(BF16)
        gpre[b, m] = gpre_rows
        out_rows = dot_nn(hidden_rows, w_out[e])
        outs[b, m] = out_rows.astype(BF16).reshape(wide, slots, width)
        gate_rows = jnp.sum(out_rows * cot_rows, axis=-1, keepdims=True)
        row = lax.broadcasted_iota(jnp.int32, (step, local * slots), 0)
        lane = lax.broadcasted_iota(jnp.int32, (step, local * slots), 1)
        spread = jnp.where(lane == e * slots + lax.rem(row, slots), gate_rows, 0.0)
        gate_sum[m] += jnp.sum(spread.reshape(wide, slots, local * slots), axis=1)
        return dot_nt(gpre_rows, w_in[e])

    back = Collect(
        p, lambda e, other: to_core.at[e, other], from_core, from_side, back_o, (rc_s, rc_r, rx_s, rx_r, rw_s, rw_r)
    )

    def go(e, piece):
        if piece == 1:
            back.go_beside(e, far_sum[...])
        else:
            back.beside(e, piece).start()

    def add_core(e, piece):
        back.core(e, 0).wait_recv()
        near_sum[e] = near_sum[e] + from_core[e, 0].astype(F32)

    acts = {
        "start": moves.start, "forward": moves.forward, "pass": moves.pass_on, "go": go, "sum": add_core,
        "finish": lambda e, piece: back.finish(e, piece, lambda rows, part: near_sum[e, rows, part]),
    }

    def after(e, part):
        for at in range(local):
            steps = EXPERT_STEPS.get(part + str(at), ())
            if steps:

                def run(steps=steps):
                    for name, expert, piece in steps:
                        acts[name](expert, piece)

                if not isinstance(e, int):
                    pl.when(e == at)(run)
                elif e == at:
                    run()

    for name, expert, piece in EXPERT_STEPS["first"]:
        acts[name](expert, piece)

    far_x = (1 - p.x) * 2

    gates_core = remote(gate_core, gate_from_core, gc_s, gc_r, p.core)

    def gates_core_start():
        gate_core[0] = gate_sum[p.x * 2 + 1 - p.c]
        gate_core[1] = gate_sum[far_x + 1 - p.c]
        gates_core.start()

    def expert(e, carry):
        for copy in loads(e):
            copy.wait()

        @pl.when(e >= 2)
        def _():
            store(e - 2, 0).wait()

        moves.arrive(e, 1)
        to_core[e, 1] = chunk(e, far_x + 1 - p.c).astype(BF16).reshape(wide, slots, width)
        back.core(e, 1).start()
        after(e, "A")
        far_sum[...] = chunk(e, far_x + p.c).reshape(wide, slots, width)
        after(e, "B")

        @pl.when(e > 0)
        def _():
            grads_out(e - 1)
            after(e - 1, "W")

        moves.arrive(e, 0)
        to_core[e, 0] = chunk(e, p.x * 2 + 1 - p.c).astype(BF16).reshape(wide, slots, width)
        back.core(e, 0).start()
        after(e, "C")
        near_sum[e] = chunk(e, p.n).reshape(wide, slots, width)
        store(e, 0).start()

        @pl.when(e == local - 1)
        def _():
            gates_core_start()

        after(e, "D")

        @pl.when(e > 0)
        def _():
            grads_in(e - 1)
            after(e - 1, "V")

        return carry

    lax.fori_loop(0, local, expert, 0)
    gates_core.wait_recv()
    gate_side[...] = gate_sum[far_x + p.c] + gate_from_core[1]
    gates_side = remote(gate_side, gate_from_side, gx_s, gx_r, p.side)
    gates_side.start()
    grads_out(local - 1)
    after(local - 1, "W")
    gates_side.wait_recv()
    gates = gate_sum[p.n] + gate_from_core[0] + gate_from_side[...]
    for v in range(wide):
        gate_ready[v] = gates[v : v + 1, :]
    gates_wide = [
        remote(gate_ready.at[p.flip(j)], gate_o.at[p.w], gw_s.at[j], gw_r.at[j], p.peer(j)) for j in range(1, wide)
    ]
    for copy in gates_wide:
        copy.start()
    gate_o[p.w] = gate_ready[p.w]
    grads_in(local - 1)
    after(local - 1, "V")
    gates_core.wait_send()
    gates_side.wait_send()

    def drain(e, carry):
        moves.drain(e)
        back.drain(e)
        back.arrive(e)

        @pl.when(e >= local - 2)
        def _():
            store(e, 0).wait()

        return carry

    lax.fori_loop(0, local, drain, 0)
    store(local - 1, 1).wait()
    store(local - 1, 2).wait()
    for copy in gates_wide:
        copy.wait()


def moving_experts(sent, cot_all, expert_in, expert_out, router, wide, narrow):
    _, local, slots, width = sent.shape
    hidden_width = expert_in.shape[2]
    step = wide * slots
    sds = jax.ShapeDtypeStruct
    any_spec, vmem_spec = pl.BlockSpec(memory_space=pl.ANY), pl.BlockSpec(memory_space=pltpu.VMEM)
    dma = pltpu.SemaphoreType.DMA
    outs, gin, gout, back, gates = pl.pallas_call(
        moving_expert_kernel,
        out_shape=(
            sds((local, narrow, wide, slots, width), BF16),
            sds(expert_in.shape, BF16),
            sds(expert_out.shape, BF16),
            sds((wide, local, slots, width), BF16),
            sds((wide, 1, local * slots), F32),
        ),
        in_specs=[any_spec, any_spec, any_spec, any_spec, vmem_spec],
        out_specs=(any_spec,) * 3 + (vmem_spec,) * 2,
        scratch_shapes=[
            pltpu.VMEM((local, narrow, wide, slots, width), BF16),
            pltpu.VMEM((local, narrow, wide, slots, width), BF16),
            pltpu.VMEM(expert_in.shape, BF16),
            pltpu.VMEM(expert_out.shape, BF16),
            pltpu.VMEM((2, narrow, step, width), BF16),
            pltpu.VMEM((2, narrow, step, hidden_width), BF16),
            pltpu.VMEM((2, narrow, step, hidden_width), BF16),
            pltpu.VMEM((2, narrow, wide, slots, width), BF16),
            pltpu.VMEM(expert_in.shape[1:], BF16),
            pltpu.VMEM(expert_out.shape[1:], BF16),
            pltpu.VMEM((local, 2, wide, slots, width), BF16),
            pltpu.VMEM((local, 2, wide, slots, width), BF16),
            pltpu.VMEM((local, wide, slots, width), BF16),
            pltpu.VMEM((local, wide, slots, width), F32),
            pltpu.VMEM((wide, slots, width), F32),
            pltpu.VMEM((narrow, wide, local * slots), F32),
            pltpu.VMEM((2, wide, local * slots), F32),
            pltpu.VMEM((2, wide, local * slots), F32),
            pltpu.VMEM((wide, local * slots), F32),
            pltpu.VMEM((wide, local * slots), F32),
            pltpu.VMEM((wide, 1, local * slots), F32),
            dma((local, 4)), dma((local, 3)), *Spread.semaphores(local, wide), *Collect.semaphores(local, wide),
            dma, dma, dma, dma, dma((wide,)), dma((wide,)),
        ],
        compiler_params=pltpu.CompilerParams(
            collective_id=2, has_side_effects=True, vmem_limit_bytes=62 << 20
        ),
        name="experts",
    )(sent, cot_all, expert_in, expert_out, router)
    return outs, back, gates, gin.astype(F32), gout.astype(F32)


def routed_gate(normed_f, router_ref, routes):
    probs = softmax_lanes(dot_nn(normed_f[...], router_ref[...]))
    chosen = lax.broadcasted_iota(jnp.int32, probs.shape, 1) == routes
    return probs, chosen, jnp.sum(jnp.where(chosen, probs, 0.0), axis=-1, keepdims=True)


def slot_owners(slot_col, total):
    return lax.broadcasted_iota(jnp.int32, (slot_col.shape[0], total), 1) == slot_col


def ffn_backward(probs, chosen, gate, owned, gates_ref, normed_f, router_ref, grows_ref, mixed, cot_ref, gain_f):
    grad_gate = jnp.sum(jnp.where(owned, gates_ref[...], 0.0), axis=-1, keepdims=True)
    grad_logits = (probs * (jnp.where(chosen, grad_gate, 0.0) - gate * grad_gate)).astype(BF16)
    grad_router = dot_tn(normed_f[...], grad_logits)
    grad_normed = dot_nt(grad_logits, router_ref[...]) + dot_nn(owned.astype(BF16), grows_ref[...])
    grad_norm, grad_gain = norm_backward(mixed, inverse_rms(mixed), gain_f[...], grad_normed)
    return grad_router, cot_ref[...].astype(F32) + grad_norm, grad_gain


def attention_setup(q_ref, k_ref, normed_ref, att_ref, lse_ref, q_t, k_t, normed_t, att_t, lse_t):
    head_dim = q_ref.shape[1] // HEADS
    att_t[...] = att_ref[...].T
    q_t[...] = (q_ref[...] * jnp.asarray(head_dim**-0.5, BF16)).T
    k_t[...] = k_ref[...].T
    normed_t[...] = normed_ref[...].T
    lse_t[...] = lse_ref[...].T


def attention_delta(datt, att_t, datt_t, delta):
    width, count = att_t.shape
    datt_t[...] = datt[...].T
    products = datt_t[...].astype(F32) * att_t[...].astype(F32)
    delta[...] = jnp.sum(products.reshape(HEADS, width // HEADS, count), axis=1)


def pair_backward(
    at, near_ref, q_ref, k_ref, v_ref, q_t, k_t, datt, datt_t, delta, lse_t, dst, gq, gk, gv, gnear_ref, gfar_ref
):
    count, width = q_ref.shape
    head_dim = width // HEADS
    blocks = count // BLOCK
    first = lax.broadcasted_iota(jnp.int32, (1, BLOCK), 1) < head_dim
    cols = pl.ds(pl.multiple_of(at * BLOCK, BLOCK), BLOCK)
    q_pair, datt_pair = q_ref[:, cols], datt[:, cols]
    gq_parts, gk_parts, gv_parts = [], [], []
    for half in range(2):
        head = 2 * at + half
        mask = first if half == 0 else jnp.logical_not(first)
        near_row = near_ref[pl.ds(head, 1), :]
        near = toeplitz_near(near_row)
        lse_row, delta_row = lse_t[pl.ds(head, 1), :], delta[pl.ds(head, 1), :]
        near_sum = jnp.zeros((BLOCK, 3 * BLOCK), F32)
        low_sum, high_sum = jnp.zeros((BLOCK, BLOCK), F32), jnp.zeros((BLOCK, BLOCK), F32)
        gk_rows, gv_rows = [], []
        for row in range(blocks):
            rows = slice(row * BLOCK, (row + 1) * BLOCK)
            k_rows, v_rows = k_ref[rows, cols], v_ref[rows, cols]
            zeros = jnp.zeros_like(k_rows)
            scores = dot_nn(jnp.where(mask, k_rows, zeros), q_t[cols, :])
            scores = scores + bias_rows(near, near_row, row, blocks)
            weights = jnp.exp(scores - lse_row)
            grad_weights = dot_nn(jnp.where(mask, v_rows, zeros), datt_t[cols, :])
            grad_scores = weights * (grad_weights - delta_row)
            gv_rows.append(dot_nn(weights.astype(BF16), datt_pair))
            low_bits = grad_scores.astype(BF16)
            dst[rows, :] = low_bits
            gk_rows.append(dot_nn(low_bits, q_pair))
            for column in range(blocks):
                piece = grad_scores[:, column * BLOCK : (column + 1) * BLOCK]
                distance = column - row
                if distance <= -2:
                    high_sum = high_sum + piece
                elif distance >= 2:
                    low_sum = low_sum + piece
                else:
                    pads = [jnp.zeros((BLOCK, BLOCK), F32)] * 3
                    pads[distance + 1] = piece
                    near_sum = near_sum + jnp.concatenate(pads, axis=1)
        gq_parts.append(
            dot_nn(k_t[pl.ds(pl.multiple_of(head * head_dim, head_dim), head_dim), :], dst[...])
        )
        gk_parts.append(jnp.concatenate(gk_rows, axis=0))
        gv_parts.append(jnp.concatenate(gv_rows, axis=0))
        gnear_ref[pl.ds(head, 1), :] = diagonal_sums(near_sum)
        gfar_ref[pl.ds(head, 1), :] = jnp.concatenate(
            [jnp.sum(low_sum, axis=0, keepdims=True), jnp.sum(high_sum, axis=0, keepdims=True)], axis=1
        )
    scale = head_dim**-0.5
    gq[:, cols] = (jnp.concatenate(gq_parts, axis=0).T * scale).astype(BF16)
    gk[:, cols] = (jnp.where(first, gk_parts[0], gk_parts[1]) * scale).astype(BF16)
    gv[:, cols] = jnp.where(first, gv_parts[0], gv_parts[1]).astype(BF16)


def input_backward(x_ref, w_ref, gain_a, gmixed, gq, gk, gv):
    count, width = x_ref.shape
    grad_normed = jnp.zeros((count, width), F32)
    for at, grad in enumerate((gq, gk, gv)):
        grad_normed = grad_normed + dot_nt(grad[...], w_ref[:, at * width : (at + 1) * width])
    tokens = x_ref[...].astype(F32)
    grad_norm, grad_gain = norm_backward(tokens, inverse_rms(tokens), gain_a[...], grad_normed)
    return gmixed[...] + grad_norm, grad_gain


def backward_kernel(
    x_ref, w_ref, gain_a, gain_f, router_ref, near_ref, slot_col, routes_ref,
    normed_ref, q_ref, k_ref, v_ref, att_ref, lse_ref, mixed_ref, normed_f, cot_ref, outs_ref, grows_ref, gates_ref,
    result_ref, gx_ref, gw_ref, grouter_ref, gnear_ref, gfar_ref, ggain_ref,
    q_t, k_t, normed_t, att_t, datt, datt_t, delta, lse_t, gq, gk, gv, gmixed, dst,
):
    width = x_ref.shape[1]
    probs, chosen, gate = routed_gate(normed_f, router_ref, routes_ref[...])
    owned = slot_owners(slot_col[...], outs_ref.shape[0])
    mixed = mixed_ref[...]
    result_ref[...] = (mixed + gate * dot_nn(owned.astype(BF16), outs_ref[...])).astype(BF16)
    grouter_ref[...], grad_mixed, ggain_ref[1:2, :] = ffn_backward(
        probs, chosen, gate, owned, gates_ref, normed_f, router_ref, grows_ref, mixed, cot_ref, gain_f
    )
    gmixed[...] = grad_mixed
    branch = grad_mixed.astype(BF16)
    gw_ref[:, 3 * width : 4 * width] = dot_tn(att_ref[...], branch).astype(BF16)
    datt[...] = dot_nt(branch, w_ref[:, 3 * width : 4 * width]).astype(BF16)
    attention_setup(q_ref, k_ref, normed_ref, att_ref, lse_ref, q_t, k_t, normed_t, att_t, lse_t)
    attention_delta(datt, att_t, datt_t, delta)

    def pair(at, carry):
        pair_backward(
            at, near_ref, q_ref, k_ref, v_ref, q_t, k_t, datt, datt_t, delta, lse_t, dst, gq, gk, gv,
            gnear_ref, gfar_ref,
        )
        return carry

    lax.fori_loop(0, HEADS // 2, pair, 0)
    for at, grad in enumerate((gq, gk, gv)):
        gw_ref[:, at * width : (at + 1) * width] = dot_nn(normed_t[...], grad[...]).astype(BF16)
    gx_ref[...], ggain_ref[0:1, :] = input_backward(x_ref, w_ref, gain_a, gmixed, gq, gk, gv)


class Sums:
    def __init__(self, place, unit, buffers, semaphores, out, split):
        self.p, self.unit, self.out, self.split = place, unit, out, split
        self.send, self.core, self.first_in, self.second_in, self.z_in, self.last = buffers
        self.s, self.r = semaphores
        self.deep = place.deep
        p, c = place, place.c * split
        self.first, self.second = p.y + c * (p.x - p.y), p.x + c * (p.y - p.x)
        row, side = p.row, p.side
        self.first_peer = tuple(a + c * (b - a) for a, b in zip(row, side))
        self.second_peer = tuple(b + c * (a - b) for a, b in zip(row, side))

    def store(self, buffer, part, core):
        rows, cols = buffer.shape[-2:]
        blocks = part.reshape(self.deep, 2, 2, rows, cols)
        c = core * self.split
        for y in range(2):
            for x in range(2):
                first, second = (y, x) if y == x else (y + c * (x - y), x + c * (y - x))
                buffer[self.unit, first, second] = blocks[:, y, x].astype(buffer.dtype)

    def to_core(self):
        u, p = self.unit, self.p
        return remote(self.send.at[u], self.core.at[u], self.s.at[u, 0], self.r.at[u, 0], p.core)

    def to_y(self):
        u = self.unit
        return remote(self.core.at[u, 1 - self.first], self.first_in.at[u], self.s.at[u, 1], self.r.at[u, 1], self.first_peer)

    def to_x(self):
        u = self.unit
        return remote(self.first_in.at[u, 1 - self.second], self.second_in.at[u], self.s.at[u, 2], self.r.at[u, 2], self.second_peer)

    def to_z(self, k):
        u, p = self.unit, self.p
        z = lax.rem(p.z + k, p.deep)
        return remote(
            self.second_in.at[u, z], self.z_in.at[u, k], self.s.at[u, 3 + k], self.r.at[u, 3 + k], (z * 2 + p.y, p.n)
        )

    def to_last(self):
        u, p = self.unit, self.p
        return remote(self.last.at[u, 1 - p.c], self.out.at[u, p.c], self.s.at[u, 3], self.r.at[u, 3], p.core)

    def begin(self, part):
        self.store(self.send, part, 1 - self.p.c)
        self.to_core().start()

    def stage_core(self, part):
        u = self.unit
        self.to_core().wait_recv()
        rows, cols = self.core.shape[-2:]
        blocks = part.reshape(self.deep, 2, 2, rows, cols)
        c = self.p.c * self.split
        for y in range(2):
            for x in range(2):
                first, second = (y, x) if y == x else (y + c * (x - y), x + c * (y - x))
                kept = blocks[:, y, x] + self.core[u, first, second].astype(F32)
                self.core[u, first, second] = kept.astype(BF16)
        self.to_y().start()

    def stage_y(self):
        u = self.unit
        self.to_y().wait_recv()
        self.first_in[u] = (self.core[u, self.first].astype(F32) + self.first_in[u].astype(F32)).astype(BF16)
        self.to_x().start()

    def stage_x(self):
        u = self.unit
        self.to_x().wait_recv()
        self.second_in[u] = (self.first_in[u, self.second].astype(F32) + self.second_in[u].astype(F32)).astype(BF16)
        for k in range(1, self.p.deep):
            self.to_z(k).start()

    def stage_z(self):
        u = self.unit
        total = self.second_in[u, self.p.z].astype(F32)
        for k in range(1, self.p.deep):
            self.to_z(k).wait_recv()
            total = total + self.z_in[u, k].astype(F32)
        self.last[u] = total.reshape(self.last.shape[1:])
        self.to_last().start()
        self.out[u, self.p.c] = self.last[u, self.p.c]

    def drain(self):
        for copy in (self.to_core(), self.to_y(), self.to_x()):
            copy.wait_send()
        for k in range(1, self.p.deep):
            self.to_z(k).wait_send()
        self.to_last().wait()


def sum_buffers(units, wide, rows, cols):
    deep = wide // 2
    vmem = lambda *shape, dtype=BF16: pltpu.VMEM((units, *shape), dtype)
    return [
        vmem(2, 2, deep, rows, cols), vmem(2, 2, deep, rows, cols), vmem(2, deep, rows, cols), vmem(deep, rows, cols),
        vmem(deep, rows, cols), vmem(2, rows // 2, cols, dtype=F32),
        pltpu.SemaphoreType.DMA((units, 3 + deep)), pltpu.SemaphoreType.DMA((units, 3 + deep)),
    ]


def moving_backward_kernel(
    x_hbm, w_hbm, normed_hbm, q_hbm, k_hbm, v_hbm, att_hbm, lse_hbm, outs_hbm, mixed_hbm, cot_hbm, grows_hbm,
    gains_ref, router_ref, rel_ref, slot_route, normed_f, gates_ref, picks_ref,
    gx_ref, result_ref, gq_out, gk_out, gv_out, go_out, router_out, rel_out, small_out,
    x_ref, w_ref, normed_ref, q_ref, k_ref, v_ref, att_ref, lse_ref, mixed_ref, cot_ref, grows_ref, load_s, near_ref,
    q_t, k_t, normed_t, att_t, datt, datt_t, delta, lse_t, gq, gk, gv, gmixed, gnormed, dst, gnear, gfar,
    own, from_core, from_side, returned, own_s, rc_s, rc_r, rx_s, rx_r, rw_s, rw_r,
    u1, u2, u3, u4, u5, u6, us, ur, o1, o2, o3, o4, o5, o6, os, orr, pair_sums, o_out,
    small, small_in, ss, sr,
):
    count, width = x_hbm.shape
    wide, local, slots, _ = returned.shape
    total = wide * local * slots
    p = Place(wide)
    far_x = (1 - p.x) * 2
    units = HEADS // 4
    gain_a, gain_f = gains_ref.at[0:1, :], gains_ref.at[1:2, :]
    loads = [
        pltpu.make_async_copy(source, target, load_s.at[at])
        for at, (source, target) in enumerate((
            (att_hbm, att_ref), (q_hbm, q_ref), (k_hbm, k_ref), (normed_hbm, normed_ref), (lse_hbm, lse_ref),
            (mixed_hbm, mixed_ref), (cot_hbm, cot_ref), (grows_hbm, grows_ref),
            (w_hbm, w_ref), (v_hbm, v_ref), (x_hbm, x_ref),
        ))
    ]

    def partial(e, other, core):
        return outs_hbm.at[e, (far_x if other else p.x * 2) + core]

    back = Collect(
        p, lambda e, other: partial(e, other, 1 - p.c), from_core, from_side, returned, (rc_s, rc_r, rx_s, rx_r, rw_s, rw_r)
    )

    def own_copy(e, other):
        return pltpu.make_async_copy(partial(e, other, p.c), own.at[e, other], own_s.at[e, other])

    for copy in loads[:5]:
        copy.start()
    greet(p.partners())
    for other in (1, 0):
        for e in range(local):
            own_copy(e, other).start()
    for copy in loads[5:11]:
        copy.start()

    def go(e, piece):
        if piece == 1:
            own_copy(e, 1).wait()
            back.go_beside(e, own[e, 1])
        else:
            back.beside(e, piece).start()

    def near(e, piece):
        back.core(e, 0).wait_recv()
        own_copy(e, 0).wait()

    def finish(e, piece):
        back.finish(
            e, piece, lambda rows, part: own[e, 0, rows, part].astype(F32) + from_core[e, 0, rows, part].astype(F32)
        )

    def unit(u):
        if isinstance(u, int) and u == units:
            return Sums(p, 0, (o1, o2, o3, o4, o5, o6), (os, orr), o_out, 0)
        return Sums(p, u, (u1, u2, u3, u4, u5, u6), (us, ur), pair_sums, (u + 1) // units)

    hops = [[p.core], [p.row], [p.side], [(lax.rem(p.z + k, p.deep) * 2 + p.y, p.n) for k in range(1, p.deep)]]
    copies, slot = [], 0
    for stage, devices in enumerate(hops):
        copies.append([
            remote(small.at[stage], small_in.at[slot + at], ss.at[slot + at], sr.at[slot + at], device)
            for at, device in enumerate(devices)
        ])
        slot += len(devices)

    def small_end(stage):
        slot = sum(len(c) for c in copies[:stage])
        found = small[stage]
        for at, copy in enumerate(copies[stage]):
            copy.wait_recv()
            found = found + small_in[slot + at]
        return found

    def small_step(stage, piece):
        if stage:
            small[stage] = small_end(stage - 1)
        for copy in copies[stage]:
            copy.start()

    acts = {
        "core": lambda e, other: back.core(e, other).start(), "go": go, "near": near, "finish": finish,
        "y": lambda u, piece: unit(u).stage_y(), "x": lambda u, piece: unit(u).stage_x(),
        "z": lambda u, piece: unit(u).stage_z(), "small": small_step,
    }

    def act(part):
        for name, at, piece in BACKWARD_STEPS.get(part, ()):
            acts[name](at, piece)

    def after(u, part):
        for at in range(units):
            if part + str(at) in BACKWARD_STEPS:
                pl.when(u == at)(lambda at=at: act(part + str(at)))

    probs, chosen, gate = routed_gate(normed_f, router_ref, slot_route[:, 1:2])
    owned = slot_owners(slot_route[:, 0:1], total)
    near_ref[...] = near_biases(rel_ref, picks_ref)
    for copy in loads[:5]:
        copy.wait()
    attention_setup(q_ref, k_ref, normed_ref, att_ref, lse_ref, q_t, k_t, normed_t, att_t, lse_t)
    meet(p.partners())
    act("first")
    for copy in loads[5:8]:
        copy.wait()
    grad_router, grad_mixed, grad_gain_f = ffn_backward(
        probs, chosen, gate, owned, gates_ref, normed_f, router_ref, grows_ref, mixed_ref[...], cot_ref, gain_f
    )
    gmixed[...] = grad_mixed
    small[0] = jnp.zeros_like(small[0])
    small[0, HEADS : HEADS + 1, :] = grad_gain_f
    act("F0")
    branch = grad_mixed.astype(BF16)
    half_cols = width // 2
    router_cols = o_out.shape[-1] - half_cols
    router_wide = jnp.concatenate(
        [grad_router, jnp.zeros((width, router_cols - grad_router.shape[1]), F32)], axis=1
    )

    def output_part(core):
        low, high = branch[:, :half_cols], branch[:, half_cols:]
        part = dot_nn(att_t[...], jnp.where(core == 0, low, high))
        return jnp.concatenate([part, jnp.where(core == 0, router_wide, 0.0)], axis=1)

    unit(units).begin(output_part(1 - p.c))
    act("O0")
    loads[8].wait()
    datt[...] = (
        dot_nt(branch[:, :half_cols], w_ref[units, 0]) + dot_nt(branch[:, half_cols:], w_ref[units, 1])
    ).astype(BF16)
    act("D0")
    unit(units).stage_core(output_part(p.c))
    act("Q0")
    attention_delta(datt, att_t, datt_t, delta)
    for copy in loads[9:11]:
        copy.wait()
    act("S0")

    def pair(at):
        pair_backward(
            at, near_ref, q_ref, k_ref, v_ref, q_t, k_t, datt, datt_t, delta, lse_t, dst, gq, gk, gv,
            gnear, gfar,
        )
        cols = pl.ds(pl.multiple_of(at * BLOCK, BLOCK), BLOCK)
        grads = jnp.concatenate([gq[:, cols], gk[:, cols], gv[:, cols]], axis=1)
        gnormed[...] += dot_nt(grads, w_ref[at // 2, lax.rem(at, 2)])
        return dot_nn(normed_t[...], grads)

    gnormed[...] = jnp.zeros_like(gnormed)

    def pairs(u, carry):
        unit(u).begin(pair(2 * u + 1 - p.c))
        after(u, "A")
        unit(u).stage_core(pair(2 * u + p.c))
        after(u, "B")
        return carry

    lax.fori_loop(0, units, pairs, 0)
    near_grads = lax.dot_general(
        gnear[...], picks_ref[...], (((1,), (1,)), ((), ())), precision=HIGHEST, preferred_element_type=F32
    )
    buckets = lax.broadcasted_iota(jnp.int32, near_grads.shape, 1)
    low_sum = jnp.sum(gfar[:, :BLOCK], axis=1, keepdims=True)
    high_sum = jnp.sum(gfar[:, BLOCK:], axis=1, keepdims=True)
    bucket_count = rel_ref.shape[1]
    rel = near_grads + jnp.where(buckets == bucket_count // 2 - 1, low_sum, 0.0)
    small[0, :HEADS, :bucket_count] = rel + jnp.where(buckets == bucket_count - 1, high_sum, 0.0)
    tokens = x_ref[...].astype(F32)
    grad_norm, grad_gain_a = norm_backward(tokens, inverse_rms(tokens), gain_a[...], gnormed[...])
    gx_ref[...] = gmixed[...] + grad_norm
    small[0, HEADS + 1 : HEADS + 2, :] = grad_gain_a

    act("P0")
    for e in range(local):
        back.arrive(e)
    combined = dot_nn(owned.astype(BF16), returned[...].reshape(total, width))
    result_ref[...] = (mixed_ref[...] + gate * combined).astype(BF16)
    act("R0")
    small_all = small_end(3)
    small_out[...] = small_all
    rel_out[...] = small_all[:HEADS, : rel_out.shape[1]]
    for e in range(local):
        back.drain(e)
    for u in range(units + 1):
        unit(u).drain()
    for half in range(2):
        for u in range(units):
            cols = slice((2 * u + half) * BLOCK, (2 * u + half + 1) * BLOCK)
            for at, out in enumerate((gq_out, gk_out, gv_out)):
                out[:, cols] = pair_sums[u, half, :, at * BLOCK : (at + 1) * BLOCK]
        go_out[:, half * half_cols : (half + 1) * half_cols] = o_out[0, half, :, :half_cols]
    router_out[...] = o_out[0, 0, :, half_cols : half_cols + router_out.shape[1]]
    for stage in copies:
        for copy in stage:
            copy.wait_send()


def moving_backward(
    rel_bias, inputs, weights, gains, router, slot_route,
    normed, q, k, v, att, lse, mixed, normed_f, cotangent, outs, grows, gates, wide, slots,
):
    count, width = inputs.shape
    local, narrow = outs.shape[:2]
    experts = router.shape[1]
    bucket_count = rel_bias.shape[0]
    deep, rows = wide // 2, width // (wide * 2)
    units = HEADS // 4
    pair_cols, out_cols = 3 * BLOCK, width // 2 + BLOCK * -(-experts // BLOCK)
    sds = jax.ShapeDtypeStruct
    any_spec = pl.BlockSpec(memory_space=pl.ANY)
    picks = jnp.asarray(near_picks(bucket_count, -1).T)
    wide_t = lambda dtype: pltpu.VMEM((width, count), dtype)
    tall = lambda dtype: pltpu.VMEM((count, width), dtype)
    vmem = lambda *shape, dtype=BF16: pltpu.VMEM(shape, dtype)
    dma = pltpu.SemaphoreType.DMA
    hops = 3 + deep - 1
    grad_inputs, result, grad_query, grad_key, grad_value, grad_output, grad_router, grad_rel, small = pl.pallas_call(
        moving_backward_kernel,
        out_shape=(
            sds((count, width), F32), sds((count, width), BF16), *[sds((rows // 2, width), F32)] * 4,
            sds((rows // 2, experts), F32), sds((HEADS, bucket_count), F32), sds((16, width), F32),
        ),
        in_specs=[any_spec] * 12 + in_vmem(7),
        out_specs=tuple(in_vmem(9)),
        scratch_shapes=[
            tall(BF16), pltpu.VMEM(weights.shape, BF16), tall(BF16), tall(BF16), tall(BF16), tall(BF16), tall(BF16),
            vmem(count, BLOCK, dtype=F32), tall(F32), tall(BF16), vmem(wide * local * slots, width),
            dma((11,)), vmem(HEADS, 4 * BLOCK, dtype=F32),
            wide_t(BF16), wide_t(BF16), wide_t(BF16), wide_t(BF16), tall(BF16), wide_t(BF16),
            vmem(HEADS, count, dtype=F32), vmem(BLOCK, count, dtype=F32),
            tall(BF16), tall(BF16), tall(BF16), tall(F32), tall(F32), vmem(count, count),
            vmem(HEADS, 4 * BLOCK, dtype=F32), vmem(HEADS, 2 * BLOCK, dtype=F32),
            vmem(local, 2, wide, slots, width), vmem(local, 2, wide, slots, width), vmem(local, wide, slots, width),
            vmem(wide, local, slots, width),
            dma((local, 2)), *Collect.semaphores(local, wide),
            *sum_buffers(units, wide, rows, pair_cols), *sum_buffers(1, wide, rows, out_cols),
            vmem(units, 2, rows // 2, pair_cols, dtype=F32), vmem(1, 2, rows // 2, out_cols, dtype=F32),
            vmem(4, 16, width, dtype=F32), vmem(hops, 16, width, dtype=F32), dma((hops,)), dma((hops,)),
        ],
        compiler_params=pltpu.CompilerParams(collective_id=3, has_side_effects=True, vmem_limit_bytes=62 << 20),
        name="backward",
    )(
        inputs, weights, normed, q, k, v, att, lse, outs, mixed, cotangent, grows,
        gains, router, rel_bias.T, slot_route, normed_f, gates, picks,
    )
    device = lax.axis_index("wide") * narrow + lax.axis_index("narrow")
    gain_grads = lax.dynamic_slice(small, (HEADS, device * (rows // 2)), (2, rows // 2))
    return result, grad_inputs, (grad_query, grad_key, grad_value), grad_output, grad_router, gain_grads[1], gain_grads[0], grad_rel.T


def in_vmem(count):
    return [pl.BlockSpec(memory_space=pltpu.VMEM)] * count


def shards(
    inputs, gain_attn, w_query, w_key, w_value, w_output, rel_bias, gain_ffn, w_router,
    expert_in, expert_out, routes, capacity, cotangent,
):
    count, width = inputs.shape
    experts = w_router.shape[1]
    local, _, hidden_width = expert_in.shape
    wide, narrow = lax.axis_size("wide"), lax.axis_size("narrow")
    slots = 2 * count // experts
    total = experts * slots
    bucket_count = rel_bias.shape[0]
    params = pltpu.CompilerParams(vmem_limit_bytes=60 << 20)
    smem = pl.BlockSpec(memory_space=pltpu.SMEM)

    moving = narrow == 4 and wide & (wide - 1) == 0 and local == HEADS // 4 + 1 and slots % 32 == 0 and local * slots % BLOCK == 0
    moving = moving and width % (wide * 2 * 16) == 0 and count == SEQ_LEN and experts + 8 <= BLOCK
    if moving:
        normed, q, k, v, att, lse, mixed, normed_f, sent, weights, cot_all, slot_route, router, gains = moving_forward(
            rel_bias, capacity, inputs, w_query, w_key, w_value, w_output, w_router, gain_attn, gain_ffn, routes,
            cotangent, wide, narrow, local, slots,
        )
        outs, back, gates, gin, gout = moving_experts(sent, cot_all, expert_in, expert_out, router, wide, narrow)
        result, grad_inputs, kinds, grad_output, grad_router, grad_gain_a, grad_gain_f, grad_rel = moving_backward(
            rel_bias, inputs, weights.reshape(HEADS // 4 + 1, 2, width, width // 2), gains, router, slot_route,
            normed, q, k, v, att, lse, mixed, normed_f, cotangent, outs,
            back.reshape(total, width), gates.reshape(1, total), wide, slots,
        )
        return (
            result, grad_inputs, grad_gain_a, *kinds, grad_output, grad_rel, grad_gain_f, grad_router, gin, gout,
        )

    near = jnp.dot(near_picks(bucket_count, 1), rel_bias, precision=HIGHEST).T
    near_back = jnp.dot(near_picks(bucket_count, -1), rel_bias, precision=HIGHEST).T

    packed = jnp.concatenate([w_query, w_key, w_value, w_output], axis=1)
    weights = lax.all_gather(packed, BOTH, axis=0, tiled=True)
    small = lax.all_gather(
        jnp.concatenate([w_router, gain_attn[:, None], gain_ffn[:, None]], axis=1), BOTH, axis=0, tiled=True
    )
    router = small[:, :experts]
    gain_a = small[:, experts].astype(F32)[None, :]
    gain_f = small[:, experts + 1].astype(F32)[None, :]
    slot_col, slot_row, cot_sent = pl.pallas_call(
        lambda *refs: place_kernel(slots, experts, *refs),
        out_shape=(
            jax.ShapeDtypeStruct((count, 1), jnp.int32),
            jax.ShapeDtypeStruct((1, count), jnp.int32),
            jax.ShapeDtypeStruct((total, width), BF16),
        ),
        in_specs=[smem] + in_vmem(3),
        out_specs=tuple(in_vmem(3)),
        compiler_params=params,
        name="places",
    )(capacity, routes, routes.reshape(1, count), cotangent)

    def spread(rows):
        taken = lax.all_to_all(
            rows.reshape(wide, local * slots, width), "wide", split_axis=0, concat_axis=0, tiled=True
        )
        held = lax.all_gather(taken, "narrow", axis=0, tiled=True)
        return held.reshape(wide * narrow, local, slots, width)

    def collect(rows):
        own = lax.psum_scatter(
            rows.reshape(wide * narrow, local * slots, width), "narrow", scatter_dimension=0, tiled=True
        )
        back = lax.all_to_all(own, "wide", split_axis=0, concat_axis=0, tiled=True)
        return back.reshape(total, width)

    cot_all = spread(cot_sent)

    rows_t = lambda dtype, cols=width: jax.ShapeDtypeStruct((count, cols), dtype)
    normed, q, k, v, att, lse, mixed, normed_f, sent = pl.pallas_call(
        forward_kernel,
        out_shape=(
            rows_t(BF16), rows_t(BF16), rows_t(BF16), rows_t(BF16), rows_t(BF16), rows_t(F32, BLOCK),
            rows_t(F32), rows_t(BF16), jax.ShapeDtypeStruct((total, width), BF16),
        ),
        in_specs=in_vmem(7),
        out_specs=tuple(in_vmem(9)),
        compiler_params=params,
        name="forward",
    )(inputs, weights, gain_a, gain_f, router, near, slot_row)

    rows_all = spread(sent)
    sources = wide * narrow
    block = pl.BlockSpec((sources, 1, slots, width), lambda e: (0, e, 0, 0))
    w_in_spec = pl.BlockSpec((1, width, hidden_width), lambda e: (e, 0, 0))
    w_out_spec = pl.BlockSpec((1, hidden_width, width), lambda e: (e, 0, 0))
    first_expert = (lax.axis_index("wide") * local).astype(jnp.int32)[None]
    back, grows, gin, gout = pl.pallas_call(
        expert_kernel,
        grid=(local,),
        out_shape=(
            jax.ShapeDtypeStruct(rows_all.shape, BF16),
            jax.ShapeDtypeStruct(rows_all.shape, BF16),
            jax.ShapeDtypeStruct(expert_in.shape, F32),
            jax.ShapeDtypeStruct(expert_out.shape, F32),
        ),
        in_specs=[
            smem, block, block, w_in_spec, w_out_spec, pl.BlockSpec((width, experts), lambda e: (0, 0)),
        ],
        out_specs=(block, block, w_in_spec, w_out_spec),
        scratch_shapes=[
            pltpu.VMEM((sources * slots, hidden_width), BF16),
            pltpu.VMEM((sources * slots, hidden_width), BF16),
            pltpu.VMEM((sources * slots, width), BF16),
        ],
        compiler_params=params,
        name="experts",
    )(first_expert, rows_all, cot_all, expert_in, expert_out, router)
    outs_back = collect(back)
    grows_back = collect(grows)
    gates = jnp.sum(outs_back.astype(F32) * cot_sent.astype(F32), axis=1)[None, :]

    wide_t = lambda dtype: pltpu.VMEM((width, count), dtype)
    tall = lambda dtype: pltpu.VMEM((count, width), dtype)
    result, grad_inputs, gw, grouter, gnear, gfar, ggain = pl.pallas_call(
        backward_kernel,
        out_shape=(
            rows_t(BF16), rows_t(F32), jax.ShapeDtypeStruct((width, 4 * width), BF16),
            jax.ShapeDtypeStruct((width, experts), F32), jax.ShapeDtypeStruct((HEADS, 4 * BLOCK), F32),
            jax.ShapeDtypeStruct((HEADS, 2 * BLOCK), F32), jax.ShapeDtypeStruct((2, width), F32),
        ),
        in_specs=in_vmem(20),
        out_specs=tuple(in_vmem(7)),
        scratch_shapes=[
            wide_t(BF16), wide_t(BF16), wide_t(BF16), wide_t(BF16), tall(BF16), wide_t(BF16),
            pltpu.VMEM((HEADS, count), F32), pltpu.VMEM((BLOCK, count), F32),
            tall(BF16), tall(BF16), tall(BF16), tall(F32), pltpu.VMEM((count, count), BF16),
        ],
        compiler_params=params,
        name="backward",
    )(
        inputs, weights, gain_a, gain_f, router, near_back, slot_col, routes,
        normed, q, k, v, att, lse, mixed, normed_f, cotangent, outs_back, grows_back, gates,
    )

    gw = lax.psum_scatter(gw, BOTH, scatter_dimension=0, tiled=True).astype(F32)
    grad_query, grad_key, grad_value, grad_output = (gw[:, i * width : (i + 1) * width] for i in range(4))
    gsmall = lax.psum_scatter(
        jnp.concatenate([grouter, ggain.T], axis=1), BOTH, scatter_dimension=0, tiled=True
    )
    grad_rel = jnp.dot(near_picks(bucket_count, -1).T, gnear.T, precision=HIGHEST)
    low, high = jnp.sum(gfar[:, :BLOCK], axis=1), jnp.sum(gfar[:, BLOCK:], axis=1)
    grad_rel = grad_rel.at[bucket_count // 2 - 1].add(low).at[bucket_count - 1].add(high)
    grad_rel = lax.psum(grad_rel, BOTH)
    return (
        result, grad_inputs, gsmall[:, experts], grad_query, grad_key, grad_value, grad_output,
        grad_rel, gsmall[:, experts + 1], gsmall[:, :experts], gin, gout,
    )


def solution(mesh):
    return jax.shard_map(
        shards,
        mesh=mesh,
        in_specs=(
            P(BOTH, None),
            P(BOTH),
            P(BOTH, None),
            P(BOTH, None),
            P(BOTH, None),
            P(BOTH, None),
            P(),
            P(BOTH),
            P(BOTH, None),
            P("wide", None, "narrow"),
            P("wide", "narrow", None),
            P(BOTH, None),
            P(BOTH),
            P(BOTH, None),
        ),
        out_specs=(
            P(BOTH, None),
            P(BOTH, None),
            P(BOTH),
            P(BOTH, None),
            P(BOTH, None),
            P(BOTH, None),
            P(BOTH, None),
            P(),
            P(BOTH),
            P(BOTH, None),
            P("wide", None, "narrow"),
            P("wide", "narrow", None),
        ),
        check_vma=False,
    )
```
